32 devices in a mesh: expert: 8 (over y, x, core), head: 4 (over z).
Axes of the slice: x: 2, y: 2, z: 4, core: 2. Of those that a mesh axis runs over, the one named last changes fastest.
Arguments:
- short_x: bfloat16 [256, 64, 512], P('expert'), may hold values from -45 to 45
- long_x: bfloat16 [64, 256, 512], P('expert'), may hold values from -45 to 45
- short_cot: bfloat16 [256, 64, 512], P('expert'), may hold values from -10 to 10
- long_cot: bfloat16 [64, 256, 512], P('expert'), may hold values from -10 to 10
- short_len: int32 [256], P('expert'), may hold values from 9 to 64, as said below
- long_len: int32 [64], P('expert'), may hold values from 33 to 256, as said below
- short_task: int32 [256], P('expert'), may hold values from 0 to 7, as said below
- long_task: int32 [64], P('expert'), may hold values from 0 to 7, as said below
- expert_ids: int32 [8, 2], replicated, may hold values from 0 to 7, as said below
- ln_gain: float32 [2, 512], replicated, may hold values from 0.5 to 1.5
- ln_bias: float32 [2, 512], replicated, may hold values from -1.75 to 1.75
- w_qkv: bfloat16 [3, 512, 512], P(None, None, 'head'), may hold values from -0.25 to 0.25
- b_qv: float32 [2, 512], P(None, 'head'), may hold values from -1.75 to 1.75
- w_attn_out: bfloat16 [512, 512], P('head'), may hold values from -1 to 1
- b_attn_out: float32 [512], replicated, may hold values from -1.75 to 1.75
- w_up: bfloat16 [8, 512, 2048], P('expert'), may hold values from -0.25 to 0.25
- b_up: float32 [8, 2048], P('expert'), may hold values from -0.625 to 0.625
- w_down: bfloat16 [8, 2048, 512], P('expert'), may hold values from -0.125 to 0.125
- b_down: float32 [8, 512], P('expert'), may hold values from -0.625 to 0.625
- task_emb: float32 [8, 512], replicated, may hold values from -6 to 6
- gate_w: float32 [512, 8], replicated, may hold values from -0.1875 to 0.1875
Outputs:
- short_out: bfloat16 [256, 64, 512], P(('expert', 'head'))
- long_out: bfloat16 [64, 256, 512], P(('expert', 'head'))
- short_dx: float32 [256, 64, 512], P(('expert', 'head'))
- long_dx: float32 [64, 256, 512], P(('expert', 'head'))
- grad_ln_gain: float32 [2, 512], replicated
- grad_ln_bias: float32 [2, 512], replicated
- grad_w_qkv: float32 [3, 512, 512], P(None, None, 'head')
- grad_b_qv: float32 [2, 512], P(None, 'head')
- grad_w_attn_out: float32 [512, 512], P('head')
- grad_b_attn_out: float32 [512], replicated
- grad_w_up: float32 [8, 512, 2048], P('expert', None, 'head')
- grad_b_up: float32 [8, 2048], P('expert', 'head')
- grad_w_down: float32 [8, 2048, 512], P('expert', 'head')
- grad_b_down: float32 [8, 512], P('expert', 'head')
- grad_task_emb: float32 [8, 512], replicated
- grad_gate_w: float32 [512, 8], replicated
The draws below stay inside these ranges and needn't reach their ends.
Inputs may be any that keep to these rules, and one draw needn't show every extreme that they name: `short_len`: in every block of 32 consecutive short sentences one has length 64. `long_len`: in every block of 8 consecutive long sentences one has length 256. `short_task`: in every block of 32 consecutive short sentences every task occurs exactly 32 / 8 times. `long_task`: in every block of 8 consecutive long sentences the tasks are all even or all odd, and each task of that parity occurs exactly 2 * 8 / 8 times. The first column is a permutation of the experts and expert_ids[t, 1] = expert_ids[(t + 1) % 8, 0]; so in every block of sentences above each expert is named by exactly 8 short and 2 long sentences.
All inputs are finite; a program needn't handle non-finite values.
Results may differ from the reference program's by a relative error of at most 0.018.
Values may be sent and summed in bfloat16 or wider, within the bound.
No kernel may reach another device: no remote copies, remote signals or barrier semaphores. Data moves between devices by JAX's collectives and lax.ppermute only.
A program may use at most 256 MiB of HBM per device.

```python
import jax
import jax.numpy as jnp
from jax import lax

D = 512
HEADS = 8
HEAD_DIM = 64
FF = 2048
EXPERTS = 8
TASKS = 8
SHORT_LEN = 64
LONG_LEN = 256
SHORT_GROUP = 32
LONG_GROUP = 8
SHORTS = 256
LONGS = 64
N_EXPERT = 8


def draw_short_x(key, part):
    key = jax.random.fold_in(key, 11)
    first, second, third = jax.random.split(key, 3)
    base = jnp.clip(jax.random.normal(first, (SHORTS, SHORT_LEN, D)), -4.0, 4.0)
    columns = jnp.exp(jax.random.uniform(second, (D,), minval=-1.2, maxval=1.2))
    scales = jnp.exp(jax.random.uniform(third, (SHORTS, SHORT_LEN, 1), minval=-1.2, maxval=1.2))
    return (base * columns * scales).astype(jnp.bfloat16)


def draw_long_x(key, part):
    key = jax.random.fold_in(key, 12)
    first, second, third = jax.random.split(key, 3)
    base = jnp.clip(jax.random.normal(first, (LONGS, LONG_LEN, D)), -4.0, 4.0)
    columns = jnp.exp(jax.random.uniform(second, (D,), minval=-1.2, maxval=1.2))
    scales = jnp.exp(jax.random.uniform(third, (LONGS, LONG_LEN, 1), minval=-1.2, maxval=1.2))
    return (base * columns * scales).astype(jnp.bfloat16)


def draw_short_cot(key, part):
    key = jax.random.fold_in(key, 13)
    first, second = jax.random.split(key, 2)
    base = jnp.clip(jax.random.normal(first, (SHORTS, SHORT_LEN, D)), -4.0, 4.0)
    ramp = jnp.arange(SHORTS, dtype=jnp.float32) / max(SHORTS - 1, 1)
    rising = jnp.exp((ramp - 0.5) * jnp.log(3.0))
    factor = jnp.exp(jax.random.uniform(second, (SHORTS,), minval=jnp.log(0.7), maxval=jnp.log(1.4)))
    return (base * (rising * factor)[:, None, None]).astype(jnp.bfloat16)


def draw_long_cot(key, part):
    key = jax.random.fold_in(key, 14)
    first, second = jax.random.split(key, 2)
    base = jnp.clip(jax.random.normal(first, (LONGS, LONG_LEN, D)), -4.0, 4.0)
    ramp = jnp.arange(LONGS, dtype=jnp.float32) / max(LONGS - 1, 1)
    rising = jnp.exp((ramp - 0.5) * jnp.log(3.0))
    factor = jnp.exp(jax.random.uniform(second, (LONGS,), minval=jnp.log(0.7), maxval=jnp.log(1.4)))
    return (base * (rising * factor)[:, None, None]).astype(jnp.bfloat16)


def draw_short_len(key, part):
    key = jax.random.fold_in(key, 17)
    first, second = jax.random.split(key)
    lengths = jax.random.randint(first, (SHORTS,), SHORT_LEN // 8 + 1, SHORT_LEN + 1)
    longest = jax.random.randint(second, (SHORTS // SHORT_GROUP,), 0, SHORT_GROUP)
    members = jnp.arange(SHORTS, dtype=jnp.int32)
    marked = members % SHORT_GROUP == longest[members // SHORT_GROUP]
    return jnp.where(marked, SHORT_LEN, lengths).astype(jnp.int32)


def draw_long_len(key, part):
    key = jax.random.fold_in(key, 18)
    first, second = jax.random.split(key)
    lengths = jax.random.randint(first, (LONGS,), LONG_LEN // 8 + 1, LONG_LEN + 1)
    longest = jax.random.randint(second, (LONGS // LONG_GROUP,), 0, LONG_GROUP)
    members = jnp.arange(LONGS, dtype=jnp.int32)
    marked = members % LONG_GROUP == longest[members // LONG_GROUP]
    return jnp.where(marked, LONG_LEN, lengths).astype(jnp.int32)


def draw_short_task(key, part):
    key = jax.random.fold_in(key, 19)
    pattern = jnp.tile(jnp.arange(TASKS, dtype=jnp.int32), SHORT_GROUP // TASKS)
    shuffled = jax.vmap(lambda single: jax.random.permutation(single, pattern))(jax.random.split(key, SHORTS // SHORT_GROUP))
    return shuffled.reshape(-1).astype(jnp.int32)


def draw_long_task(key, part):
    key = jax.random.fold_in(key, 23)
    first, second = jax.random.split(key)
    halves = TASKS // 2
    pattern = 2 * jnp.tile(jnp.arange(halves, dtype=jnp.int32), LONG_GROUP // halves)
    shuffled = jax.vmap(lambda single: jax.random.permutation(single, pattern))(jax.random.split(first, LONGS // LONG_GROUP))
    parity = jax.random.randint(second, (LONGS // LONG_GROUP, 1), 0, 2)
    return (shuffled + parity).reshape(-1).astype(jnp.int32)


def draw_expert_ids(key, part):
    key = jax.random.fold_in(key, 29)
    order = jax.random.permutation(key, EXPERTS).astype(jnp.int32)
    return jnp.stack([order, jnp.roll(order, -1)], axis=1)


def steps_of(own_key, extent, cuts, smallest, high):
    loudness = 1.0
    for position, shards_of in cuts:
        heights = jax.random.uniform(jax.random.fold_in(jax.random.fold_in(own_key, 6), position), (shards_of,), jnp.float32, smallest / len(cuts), high / len(cuts))
        loudness = loudness * jnp.repeat(jnp.exp(heights), extent[position] // shards_of).reshape((-1,) + (1,) * (len(extent) - 1 - position))
    return loudness


def noise(stream_key, shape, scale, most, cuts=(), held_as=jnp.bfloat16):
    factor_of = steps_of(stream_key, shape, cuts, -0.22, 0.18) if cuts else 1.0
    values = jax.random.normal(stream_key, shape, jnp.float32) * scale * factor_of
    return jnp.minimum(jnp.maximum(values, -most), most).astype(held_as)


def setup_inputs(seed: int = 0) -> dict:
    keys = jax.random.split(jax.random.key(seed), 22)
    return {
        "short_x": draw_short_x(jax.random.fold_in(keys[21], 71), 0),
        "long_x": draw_long_x(jax.random.fold_in(keys[21], 71), 0),
        "short_cot": draw_short_cot(jax.random.fold_in(keys[21], 71), 0),
        "long_cot": draw_long_cot(jax.random.fold_in(keys[21], 71), 0),
        "short_len": draw_short_len(jax.random.fold_in(keys[21], 71), 0),
        "long_len": draw_long_len(jax.random.fold_in(keys[21], 71), 0),
        "short_task": draw_short_task(jax.random.fold_in(keys[21], 71), 0),
        "long_task": draw_long_task(jax.random.fold_in(keys[21], 71), 0),
        "expert_ids": draw_expert_ids(jax.random.fold_in(keys[21], 71), 0),
        "ln_gain": jnp.clip(1.0 + 0.1 * jax.random.normal(keys[9], (2, D), jnp.float32), 0.5, 1.5),
        "ln_bias": noise(keys[10], (2, D), 0.3, 1.75, (), jnp.float32),
        "w_qkv": noise(keys[11], (3, D, D), D ** -0.5, 0.25, ((2, 4),)),
        "b_qv": noise(keys[12], (2, D), 0.3, 1.75, ((1, 4),), jnp.float32),
        "w_attn_out": noise(keys[13], (D, D), (D // 16) ** -0.5, 1.0, ((0, 4),)),
        "b_attn_out": noise(keys[14], (D,), 0.3, 1.75, (), jnp.float32),
        "w_up": noise(keys[15], (EXPERTS, D, FF), D ** -0.5, 0.25, ((0, 8),)),
        "b_up": noise(keys[16], (EXPERTS, FF), 0.1, 0.625, ((0, 8),), jnp.float32),
        "w_down": noise(keys[17], (EXPERTS, FF, D), FF ** -0.5, 0.125, ((0, 8),)),
        "b_down": noise(keys[18], (EXPERTS, D), 0.1, 0.625, ((0, 8),), jnp.float32),
        "task_emb": noise(keys[19], (TASKS, D), 1.0, 6.0, (), jnp.float32),
        "gate_w": noise(keys[20], (D, EXPERTS), (2 * D) ** -0.5, 0.1875, (), jnp.float32),
    }


HIGHEST = lax.Precision.HIGHEST

@jax.custom_vjp
def low(v):
    return lax.optimization_barrier(v.astype(jnp.bfloat16)).astype(jnp.float32)

@jax.custom_vjp
def low_back(v):
    return v

def low_keep(v):
    return (low(v), None)

def low_pass(kept, grad):
    return (grad,)

def back_keep(v):
    return (v, None)

def back_low(kept, grad):
    return (low(grad),)
low.defvjp(low_keep, low_pass)
low_back.defvjp(back_keep, back_low)

def layer_norm(values, gain, shift):
    centred = values - lax.optimization_barrier(jnp.mean(values, axis=-1, keepdims=True))
    spread = lax.optimization_barrier(jnp.mean(centred * centred, axis=-1, keepdims=True))
    return centred * lax.rsqrt(spread + 1e-05) * gain + shift

def heads_attend(normed, lengths, qkv_weight, qv_bias, out_weight):
    sentences, positions, features = normed.shape

    def project(matrix, offset):
        return jnp.einsum('bld,de->ble', normed, matrix, precision=HIGHEST) + offset
    shape_heads = (sentences, positions, HEADS, HEAD_DIM)
    queries = low_back(low(project(qkv_weight[0], qv_bias[0]))).reshape(shape_heads)
    key_rows = low_back(low(project(qkv_weight[1], 0.0))).reshape(shape_heads)
    values = low_back(low(project(qkv_weight[2], qv_bias[1]))).reshape(shape_heads)
    scores = low_back(jnp.einsum('blhd,bmhd->bhlm', queries, key_rows, precision=HIGHEST) * HEAD_DIM ** (-0.5))
    visible = jnp.arange(positions, dtype=jnp.int32)[None, None, None, :] < lengths[:, None, None, None]
    scores = jnp.where(visible, scores, -1e+30)
    attn_probs = low(jax.nn.softmax(scores, axis=-1))
    context = low_back(low(jnp.einsum('bhlm,bmhd->blhd', attn_probs, values, precision=HIGHEST)))
    return jnp.einsum('ble,ed->bld', context.reshape(sentences, positions, features), out_weight, precision=HIGHEST)

def expert_apply(packed):
    weight_up, bias_up, weight_down, bias_down, short_rows, long_rows = packed
    features = short_rows.shape[-1]
    inputs = jnp.concatenate([short_rows.reshape(-1, features), long_rows.reshape(-1, features)], axis=0)
    gelu_in = low_back(jnp.dot(inputs, weight_up, precision=HIGHEST) + bias_up)
    hidden = low(jax.nn.gelu(gelu_in))
    output = low_back(low(jnp.dot(hidden, weight_down, precision=HIGHEST) + bias_down))
    split_at = short_rows.shape[0] * short_rows.shape[1]
    return (output[:split_at].reshape(short_rows.shape), output[split_at:].reshape(long_rows.shape))

def route_order(tasks, expert_ids):
    chosen = expert_ids[tasks].reshape(-1).astype(jnp.int32)
    count = chosen.shape[0]
    sort_keys = chosen * count + jnp.arange(count, dtype=jnp.int32)
    order = jnp.argsort(sort_keys).astype(jnp.int32)
    inverse = jnp.argsort(order).astype(jnp.int32)
    return (order, inverse)

def reference(short_x, long_x, short_cot, long_cot, short_len, long_len, short_task, long_task, expert_ids, ln_gain, ln_bias, w_qkv, b_qv, w_attn_out, b_attn_out, w_up, b_up, w_down, b_down, task_emb, gate_w):
    short_order, short_inverse = route_order(short_task, expert_ids)
    long_order, long_inverse = route_order(long_task, expert_ids)
    short_mask = (jnp.arange(SHORT_LEN, dtype=jnp.int32)[None, :] < short_len[:, None]).astype(jnp.float32)[:, :, None]
    long_mask = (jnp.arange(LONG_LEN, dtype=jnp.int32)[None, :] < long_len[:, None]).astype(jnp.float32)[:, :, None]

    def forward(short_in, long_in, gains, shifts, qkv_weight, qv_bias, out_weight, out_bias, up_weight, up_bias, down_weight, down_bias, task_table, gate_table):

        def attention(normed, lengths):

            def one_group(pair):
                return heads_attend(pair[0], pair[1], qkv_weight, qv_bias, out_weight)
            grouped = normed.reshape((N_EXPERT, -1) + normed.shape[1:])
            result = lax.map(jax.checkpoint(one_group), (grouped, lengths.reshape(N_EXPERT, -1)))
            return result.reshape(normed.shape)
        short_normed = low(layer_norm(short_in, gains[0], shifts[0]))
        long_normed = low(layer_norm(long_in, gains[0], shifts[0]))
        short_mid = short_in + short_mask * (attention(short_normed, short_len) + out_bias)
        long_mid = long_in + long_mask * (attention(long_normed, long_len) + out_bias)
        short_mixin = low(layer_norm(short_mid, gains[1], shifts[1]))
        long_mixin = low(layer_norm(long_mid, gains[1], shifts[1]))
        logits = lax.optimization_barrier(jnp.sum(task_table[:, None, :] * gate_table.T[expert_ids], axis=-1))
        gate_probs = jax.nn.softmax(logits, axis=-1)
        short_routed = low_back(short_mixin[short_order // 2]).reshape((EXPERTS, -1, SHORT_LEN, D))
        long_routed = low_back(long_mixin[long_order // 2]).reshape((EXPERTS, -1, LONG_LEN, D))
        short_back, long_back = lax.map(jax.checkpoint(expert_apply), (up_weight, up_bias, down_weight, down_bias, short_routed, long_routed))
        short_each = short_back.reshape(-1, SHORT_LEN, D)[short_inverse].reshape(SHORTS, 2, SHORT_LEN, D)
        long_each = long_back.reshape(-1, LONG_LEN, D)[long_inverse].reshape(LONGS, 2, LONG_LEN, D)
        short_moe = lax.optimization_barrier(jnp.sum(gate_probs[short_task][:, :, None, None] * short_each, axis=1))
        long_moe = lax.optimization_barrier(jnp.sum(gate_probs[long_task][:, :, None, None] * long_each, axis=1))
        return (short_mid + short_mask * short_moe, long_mid + long_mask * long_moe)
    inputs = (short_x.astype(jnp.float32), long_x.astype(jnp.float32), ln_gain, ln_bias, w_qkv.astype(jnp.float32), b_qv, w_attn_out.astype(jnp.float32), b_attn_out, w_up.astype(jnp.float32), b_up, w_down.astype(jnp.float32), b_down, task_emb, gate_w)
    outputs, pullback = jax.vjp(forward, *inputs)
    grads = pullback((short_cot.astype(jnp.float32), long_cot.astype(jnp.float32)))
    return (outputs[0].astype(jnp.bfloat16), outputs[1].astype(jnp.bfloat16), grads[0], grads[1], grads[2], grads[3], grads[4], grads[5], grads[6], grads[7], grads[8], grads[9], grads[10], grads[11], grads[12], grads[13])
```

```python
import functools

import jax
import jax.numpy as jnp
from jax import lax
from jax.experimental import pallas as pl
from jax.experimental.pallas import tpu as pltpu
from jax.sharding import PartitionSpec as P

HEAD_DIM = 64


HIGHEST = lax.Precision.HIGHEST
CONTRACT_ROWS = (((0,), (0,)), ((), ()))
CONTRACT_COLS = (((1,), (1,)), ((), ()))


def layer_norm(values, gain, shift):
    centred = values - jnp.mean(values, axis=-1, keepdims=True)
    spread = jnp.mean(centred * centred, axis=-1, keepdims=True)
    return centred * lax.rsqrt(spread + 1e-05) * gain + shift


def lookup(table, index):
    hits = index[..., None] == jnp.arange(table.shape[0], dtype=jnp.int32)
    return jnp.sum(jnp.where(hits, table, jnp.zeros((), table.dtype)), axis=-1)


def route_slots(tasks, expert_ids, capacity, experts):
    task_hits = tasks[:, None] == jnp.arange(expert_ids.shape[0], dtype=jnp.int32)
    chosen = jnp.sum(jnp.where(task_hits[:, :, None], expert_ids[None, :, :], 0), axis=1).reshape(
        -1
    )
    routes = chosen.shape[0]
    owner_hits = (chosen[:, None] == jnp.arange(experts, dtype=jnp.int32)).astype(jnp.int32)
    earlier = jnp.cumsum(owner_hits, axis=0) - owner_hits
    ranking = jnp.sum(earlier * owner_hits, axis=1)
    slot_key = chosen * capacity + ranking
    slot_hits = slot_key[:, None] == jnp.arange(experts * capacity, dtype=jnp.int32)
    return jnp.sum(jnp.where(slot_hits, jnp.arange(routes, dtype=jnp.int32)[:, None], 0), axis=0)


def masked_scores(queries, key_rows, lengths):
    positions = key_rows.shape[1]
    scores = jnp.einsum(
        "blhd,bmhd->bhlm", queries, key_rows, preferred_element_type=jnp.float32
    ) * HEAD_DIM ** (-0.5)
    visible = (
        jnp.arange(positions, dtype=jnp.int32)[None, None, None, :] < lengths[:, None, None, None]
    )
    return jnp.where(visible, scores, -1e30)


def attend(normed, lengths, weights, biases, head_count):
    sentences, positions, features = normed.shape
    flattened = normed.reshape(-1, features)
    shape_heads = (sentences, positions, head_count, HEAD_DIM)

    def project(index, offset):
        return (
            (jnp.dot(flattened, weights[index], preferred_element_type=jnp.float32) + offset)
            .astype(jnp.bfloat16)
            .reshape(shape_heads)
        )

    queries = project(0, biases[0])
    key_rows = project(1, 0.0)
    values = project(2, biases[1])
    scores = masked_scores(queries, key_rows, lengths)
    highest = jnp.max(scores, axis=-1, keepdims=True)
    shifted = jnp.exp(scores - highest)
    totals = jnp.sum(shifted, axis=-1, keepdims=True)
    attn_probs = (shifted / totals).astype(jnp.bfloat16)
    log_total = highest + jnp.log(totals)
    context = jnp.einsum(
        "bhlm,bmhd->blhd", attn_probs, values, preferred_element_type=jnp.float32
    ).astype(jnp.bfloat16)
    return (queries, key_rows, values, context.reshape(sentences, positions, -1), log_total)


def attend_back(normed, lengths, kept, grad_out, weights, out_weight):
    queries, key_rows, values, context, log_total = kept
    features = normed.shape[-1]
    head_cols = context.shape[-1]
    grad_flat = grad_out.reshape(-1, features)
    context_flat = context.reshape(-1, head_cols)
    grad_context = (
        lax.dot_general(grad_flat, out_weight, CONTRACT_COLS, preferred_element_type=jnp.float32)
        .astype(jnp.bfloat16)
        .reshape(queries.shape)
    )
    grad_out_weight = lax.dot_general(
        context_flat, grad_flat, CONTRACT_ROWS, preferred_element_type=jnp.float32
    )
    probs = jnp.exp(masked_scores(queries, key_rows, lengths) - log_total)
    grad_probs = jnp.einsum(
        "blhd,bmhd->bhlm", grad_context, values, preferred_element_type=jnp.float32
    )
    grad_values = jnp.einsum(
        "bhlm,blhd->bmhd",
        probs.astype(jnp.bfloat16),
        grad_context,
        preferred_element_type=jnp.float32,
    ).astype(jnp.bfloat16)
    grad_scores = (
        probs * (grad_probs - jnp.sum(probs * grad_probs, axis=-1, keepdims=True))
    ).astype(jnp.bfloat16)
    scaling = HEAD_DIM ** (-0.5)
    grad_queries = (
        jnp.einsum("bhlm,bmhd->blhd", grad_scores, key_rows, preferred_element_type=jnp.float32)
        * scaling
    ).astype(jnp.bfloat16)
    grad_keys = (
        jnp.einsum("bhlm,blhd->bmhd", grad_scores, queries, preferred_element_type=jnp.float32)
        * scaling
    ).astype(jnp.bfloat16)
    normed_flat = normed.reshape(-1, features)
    members = [member.reshape(-1, head_cols) for member in (grad_queries, grad_keys, grad_values)]
    grad_weights = jnp.stack(
        [
            lax.dot_general(normed_flat, member, CONTRACT_ROWS, preferred_element_type=jnp.float32)
            for member in members
        ]
    )
    grad_biases = jnp.stack(
        [
            jnp.sum(members[0].astype(jnp.float32), axis=0),
            jnp.sum(members[2].astype(jnp.float32), axis=0),
        ]
    )
    grad_normed = lax.dot_general(
        members[0], weights[0], CONTRACT_COLS, preferred_element_type=jnp.float32
    )
    grad_normed = grad_normed + lax.dot_general(
        members[1], weights[1], CONTRACT_COLS, preferred_element_type=jnp.float32
    )
    grad_normed = grad_normed + lax.dot_general(
        members[2], weights[2], CONTRACT_COLS, preferred_element_type=jnp.float32
    )
    return (grad_normed.reshape(normed.shape), grad_weights, grad_out_weight, grad_biases)


def group_rows(first_rows, second_rows):
    return (
        lax.all_gather(first_rows, "head", axis=0, tiled=True),
        lax.all_gather(second_rows, "head", axis=0, tiled=True),
    )


def per_device_wide(
    short_x,
    long_x,
    short_cot,
    long_cot,
    short_len,
    long_len,
    short_task,
    long_task,
    expert_ids,
    ln_gain,
    ln_bias,
    w_qkv,
    b_qv,
    w_attn_out,
    b_attn_out,
    w_up,
    b_up,
    w_down,
    b_down,
    task_emb,
    gate_w,
):
    heads_here = lax.axis_size("head")
    head_place = lax.axis_index("head")
    experts = lax.axis_size("expert")
    short_group, short_span, features = short_x.shape
    long_group, long_span = (long_x.shape[0], long_x.shape[1])
    short_dev = short_group // heads_here
    long_dev = long_group // heads_here
    hidden_width = w_up.shape[2]
    tasks_total = expert_ids.shape[0]
    cap_short = 2 * short_group // experts
    cap_long = 2 * long_group // experts
    piece_rows = (cap_short * short_span + cap_long * long_span) // heads_here
    short_total = short_group * short_span
    all_rows = short_total + long_group * long_span
    expert_hits = (expert_ids[:, :, None] == jnp.arange(experts, dtype=jnp.int32)).astype(
        jnp.float32
    )
    chosen_cols = jnp.einsum("tke,de->tkd", expert_hits, gate_w, precision=HIGHEST)
    gate_probs = jax.nn.softmax(jnp.sum(task_emb[:, None, :] * chosen_cols, axis=-1), axis=-1)
    short_slots = route_slots(short_task, expert_ids, cap_short, experts)
    long_slots = route_slots(long_task, expert_ids, cap_long, experts)
    offsets = head_place * piece_rows + jnp.arange(piece_rows, dtype=jnp.int32)
    owners = jnp.arange(experts, dtype=jnp.int32)[:, None]
    in_short = jnp.broadcast_to(offsets < cap_short * short_span, (experts, piece_rows))
    short_pos = offsets % short_span
    long_offset = jnp.maximum(offsets - cap_short * short_span, 0)
    long_pos = long_offset % long_span
    short_route = lookup(
        short_slots, owners * cap_short + jnp.minimum(offsets // short_span, cap_short - 1)
    )
    long_route = lookup(
        long_slots, owners * cap_long + jnp.minimum(long_offset // long_span, cap_long - 1)
    )
    short_sent = short_route // 2
    long_sent = long_route // 2
    position = jnp.where(in_short, short_pos, long_pos)
    target = jnp.where(
        in_short,
        short_sent * short_span + short_pos,
        short_total + long_sent * long_span + long_pos,
    )
    task_rows = jnp.where(in_short, lookup(short_task, short_sent), lookup(long_task, long_sent))
    length_rows = jnp.where(in_short, lookup(short_len, short_sent), lookup(long_len, long_sent))
    live_rows = (position < length_rows).astype(jnp.float32)
    gate_index = task_rows * 2 + jnp.where(in_short, short_route % 2, long_route % 2)
    gate_rows = lookup(gate_probs.reshape(-1), gate_index)
    short_mask = (jnp.arange(short_span, dtype=jnp.int32)[None, :] < short_len[:, None]).astype(
        jnp.float32
    )[:, :, None]
    long_mask = (jnp.arange(long_span, dtype=jnp.int32)[None, :] < long_len[:, None]).astype(
        jnp.float32
    )[:, :, None]
    short_start = head_place * short_dev
    long_start = head_place * long_dev
    own_short_mask = lax.dynamic_slice_in_dim(short_mask, short_start, short_dev, 0)
    own_long_mask = lax.dynamic_slice_in_dim(long_mask, long_start, long_dev, 0)
    short_in = short_x.astype(jnp.float32)
    long_in = long_x.astype(jnp.float32)
    own_short_in = lax.dynamic_slice_in_dim(short_in, short_start, short_dev, 0)
    own_long_in = lax.dynamic_slice_in_dim(long_in, long_start, long_dev, 0)
    attn_qkv, attn_qv, attn_out_w = (w_qkv, b_qv, w_attn_out)
    short_src, long_src = (short_in, long_in)
    short_lens, long_lens = (short_len, long_len)
    head_cols = attn_qkv.shape[2]
    head_count = head_cols // HEAD_DIM
    short_normed = layer_norm(short_src, ln_gain[0], ln_bias[0]).astype(jnp.bfloat16)
    long_normed = layer_norm(long_src, ln_gain[0], ln_bias[0]).astype(jnp.bfloat16)
    short_kept = attend(short_normed, short_lens, attn_qkv, attn_qv, head_count)
    long_kept = attend(long_normed, long_lens, attn_qkv, attn_qv, head_count)
    short_part = jnp.dot(
        short_kept[3].reshape(-1, head_cols), attn_out_w, preferred_element_type=jnp.float32
    ).reshape(short_src.shape)
    long_part = jnp.dot(
        long_kept[3].reshape(-1, head_cols), attn_out_w, preferred_element_type=jnp.float32
    ).reshape(long_src.shape)
    short_sum, long_sum = (
        lax.psum(short_part.astype(jnp.bfloat16), "head").astype(jnp.float32),
        lax.psum(long_part.astype(jnp.bfloat16), "head").astype(jnp.float32),
    )
    short_mid = short_in + short_mask * (short_sum + b_attn_out)
    long_mid = long_in + long_mask * (long_sum + b_attn_out)
    short_mixin = layer_norm(short_mid, ln_gain[1], ln_bias[1]).astype(jnp.bfloat16)
    long_mixin = layer_norm(long_mid, ln_gain[1], ln_bias[1]).astype(jnp.bfloat16)
    own_short_mid = lax.dynamic_slice_in_dim(short_mid, short_start, short_dev, 0)
    own_long_mid = lax.dynamic_slice_in_dim(long_mid, long_start, long_dev, 0)
    mixin_rows = jnp.concatenate(
        [short_mixin.reshape(-1, features), long_mixin.reshape(-1, features)], axis=0
    )
    outgoing = mixin_rows[target]
    received = lax.all_to_all(outgoing, "expert", split_axis=0, concat_axis=0, tiled=True)
    inputs = received.reshape(-1, features)
    gelu_in = jnp.dot(inputs, w_up[0], preferred_element_type=jnp.float32) + b_up[0]
    hidden = jax.nn.gelu(gelu_in).astype(jnp.bfloat16)
    output = (jnp.dot(hidden, w_down[0], preferred_element_type=jnp.float32) + b_down[0]).astype(
        jnp.bfloat16
    )
    returned = lax.all_to_all(
        output.reshape(received.shape), "expert", split_axis=0, concat_axis=0, tiled=True
    )
    wide_shape = received.shape[:2] + (hidden_width,)
    packed = (returned, received, hidden.reshape(wide_shape), gelu_in.reshape(wide_shape))
    returned = packed[0]
    received = packed[1]
    contrib = (gate_rows[:, :, None] * returned.astype(jnp.float32)).reshape(-1, features)
    mixed_rows = jnp.zeros((all_rows, features), jnp.float32).at[target.reshape(-1)].add(contrib)
    short_moe, long_moe = (
        lax.psum_scatter(
            mixed_rows[:short_total].reshape(short_in.shape).astype(jnp.bfloat16),
            "head",
            scatter_dimension=0,
            tiled=True,
        ).astype(jnp.float32),
        lax.psum_scatter(
            mixed_rows[short_total:].reshape(long_in.shape).astype(jnp.bfloat16),
            "head",
            scatter_dimension=0,
            tiled=True,
        ).astype(jnp.float32),
    )
    short_out = (own_short_mid + own_short_mask * short_moe).astype(jnp.bfloat16)
    long_out = (own_long_mid + own_long_mask * long_moe).astype(jnp.bfloat16)
    cot_rows = jnp.concatenate(
        [short_cot.reshape(-1, features), long_cot.reshape(-1, features)], axis=0
    )
    cot_picked = cot_rows[target].astype(jnp.float32)
    grad_sent = ((gate_rows * live_rows)[:, :, None] * cot_picked).astype(jnp.bfloat16)
    gate_terms = live_rows * jnp.sum(cot_picked * returned.astype(jnp.float32), axis=-1)
    gate_part = jnp.sum(
        jnp.where(
            gate_index[:, :, None] == jnp.arange(2 * tasks_total, dtype=jnp.int32),
            gate_terms[:, :, None],
            0.0,
        ),
        axis=(0, 1),
    )
    grad_arrived = lax.all_to_all(grad_sent, "expert", split_axis=0, concat_axis=0, tiled=True)
    inputs = received.reshape(-1, features)
    hidden = packed[2].reshape(-1, hidden_width)
    gelu_in = packed[3].reshape(-1, hidden_width)
    grad_output = grad_arrived.reshape(-1, features)
    grad_hidden = lax.dot_general(
        grad_output, w_down[0], CONTRACT_COLS, preferred_element_type=jnp.float32
    )
    grad_gelu = jax.vjp(jax.nn.gelu, gelu_in)[1](grad_hidden)[0].astype(jnp.bfloat16)
    grad_up_w = lax.dot_general(
        inputs, grad_gelu, CONTRACT_ROWS, preferred_element_type=jnp.float32
    )
    grad_up_b = jnp.sum(grad_gelu.astype(jnp.float32), axis=0)
    grad_down_w = lax.dot_general(
        hidden, grad_output, CONTRACT_ROWS, preferred_element_type=jnp.float32
    )
    grad_down_b = jnp.sum(grad_output.astype(jnp.float32), axis=0)
    grad_inputs = (
        lax.dot_general(grad_gelu, w_up[0], CONTRACT_COLS, preferred_element_type=jnp.float32)
        .astype(jnp.bfloat16)
        .reshape(received.shape)
    )
    grad_home = lax.all_to_all(grad_inputs, "expert", split_axis=0, concat_axis=0, tiled=True)
    shard_up_w, shard_up_b, shard_down_w, shard_down_b = (
        lax.psum_scatter(
            grad_up_w[None].astype(jnp.bfloat16), "head", scatter_dimension=2, tiled=True
        ).astype(jnp.float32),
        lax.psum_scatter(
            grad_up_b[None].astype(jnp.bfloat16), "head", scatter_dimension=1, tiled=True
        ).astype(jnp.float32),
        lax.psum_scatter(
            grad_down_w[None].astype(jnp.bfloat16), "head", scatter_dimension=1, tiled=True
        ).astype(jnp.float32),
        lax.psum_scatter(
            grad_down_b[None].astype(jnp.bfloat16), "head", scatter_dimension=1, tiled=True
        ).astype(jnp.float32),
    )
    grad_mixin = (
        jnp.zeros((all_rows, features), jnp.float32)
        .at[target.reshape(-1)]
        .add(grad_home.reshape(-1, features).astype(jnp.float32))
    )
    short_dmix, long_dmix = (
        lax.psum_scatter(
            grad_mixin[:short_total].reshape(short_in.shape).astype(jnp.bfloat16),
            "head",
            scatter_dimension=0,
            tiled=True,
        ).astype(jnp.float32),
        lax.psum_scatter(
            grad_mixin[short_total:].reshape(long_in.shape).astype(jnp.bfloat16),
            "head",
            scatter_dimension=0,
            tiled=True,
        ).astype(jnp.float32),
    )
    short_dmid, short_gain_two, short_shift_two = jax.vjp(
        layer_norm, own_short_mid, ln_gain[1], ln_bias[1]
    )[1](short_dmix)
    long_dmid, long_gain_two, long_shift_two = jax.vjp(
        layer_norm, own_long_mid, ln_gain[1], ln_bias[1]
    )[1](long_dmix)
    short_dmid = short_dmid + lax.dynamic_slice_in_dim(short_cot, short_start, short_dev, 0).astype(
        jnp.float32
    )
    long_dmid = long_dmid + lax.dynamic_slice_in_dim(long_cot, long_start, long_dev, 0).astype(
        jnp.float32
    )
    short_dattn = (own_short_mask * short_dmid).astype(jnp.bfloat16)
    long_dattn = (own_long_mask * long_dmid).astype(jnp.bfloat16)
    bias_out_grad = jnp.sum(short_dattn.astype(jnp.float32), axis=(0, 1)) + jnp.sum(
        long_dattn.astype(jnp.float32), axis=(0, 1)
    )
    attn_short_grad, attn_long_grad = group_rows(short_dattn, long_dattn)
    short_back = attend_back(
        short_normed, short_lens, short_kept, attn_short_grad, attn_qkv, attn_out_w
    )
    long_back = attend_back(long_normed, long_lens, long_kept, attn_long_grad, attn_qkv, attn_out_w)
    short_dnormed, long_dnormed = (
        lax.psum_scatter(
            short_back[0].astype(jnp.bfloat16), "head", scatter_dimension=0, tiled=True
        ).astype(jnp.float32),
        lax.psum_scatter(
            long_back[0].astype(jnp.bfloat16), "head", scatter_dimension=0, tiled=True
        ).astype(jnp.float32),
    )
    short_dln, short_gain_one, short_shift_one = jax.vjp(
        layer_norm, own_short_in, ln_gain[0], ln_bias[0]
    )[1](short_dnormed)
    long_dln, long_gain_one, long_shift_one = jax.vjp(
        layer_norm, own_long_in, ln_gain[0], ln_bias[0]
    )[1](long_dnormed)
    short_dx = short_dmid + short_dln
    long_dx = long_dmid + long_dln
    qkv_terms = short_back[1] + long_back[1]
    out_terms = short_back[2] + long_back[2]
    bias_terms = short_back[3] + long_back[3]
    grad_qkv, grad_attn_weight, grad_qv = (
        lax.psum(qkv_terms.astype(jnp.bfloat16), "expert").astype(jnp.float32),
        lax.psum(out_terms.astype(jnp.bfloat16), "expert").astype(jnp.float32),
        lax.psum(bias_terms.astype(jnp.bfloat16), "expert").astype(jnp.float32),
    )
    gain_grads = jnp.stack([short_gain_one + long_gain_one, short_gain_two + long_gain_two])
    shift_grads = jnp.stack([short_shift_one + long_shift_one, short_shift_two + long_shift_two])
    grad_gain, grad_shift, grad_bias_out, gate_total = lax.psum(
        (gain_grads, shift_grads, bias_out_grad, gate_part), ("expert", "head")
    )
    gate_grad = gate_total.reshape(tasks_total, 2)
    logit_grad = gate_probs * (gate_grad - jnp.sum(gate_probs * gate_grad, axis=-1, keepdims=True))
    grad_task = jnp.sum(logit_grad[:, :, None] * chosen_cols, axis=1)
    grad_gate = jnp.einsum("tke,tk,td->de", expert_hits, logit_grad, task_emb, precision=HIGHEST)
    return (
        short_out,
        long_out,
        short_dx,
        long_dx,
        grad_gain,
        grad_shift,
        grad_qkv,
        grad_qv,
        grad_attn_weight,
        grad_bias_out,
        shard_up_w,
        shard_up_b,
        shard_down_w,
        shard_down_b,
        grad_task,
        grad_gate,
    )


BF16 = jnp.bfloat16
F32 = jnp.float32
VMEM_LIMIT = 56 * 1024 * 1024
SLICE_ROWS = 272
HALF_PACK = 1088
QKV_ROWS = 1536
MISC_ROW = 2048
GRAD_ROWS = 1040


def mm(a, b):
    return lax.dot_general(a, b, (((1,), (0,)), ((), ())), preferred_element_type=F32)


def mm_nt(a, b):
    return lax.dot_general(a, b, (((1,), (1,)), ((), ())), preferred_element_type=F32)


def mm_tn(a, b):
    return lax.dot_general(a, b, (((0,), (0,)), ((), ())), preferred_element_type=F32)


def iota(shape, dim):
    return lax.broadcasted_iota(jnp.int32, shape, dim)


def params(**kw):
    return pltpu.CompilerParams(vmem_limit_bytes=VMEM_LIMIT, **kw)


def cost(micros):
    return pl.CostEstimate(flops=0, bytes_accessed=int(micros * 3.7e6), transcendentals=0)


VM = pl.BlockSpec(memory_space=pltpu.VMEM)
SM = pl.BlockSpec(memory_space=pltpu.SMEM)
ANY = pl.BlockSpec(memory_space=pl.ANY)


def pack_kernel(qkv, qv, wo, out):
    core = lax.axis_index("expert") % 2
    feats = qkv.shape[1]
    split = HALF_PACK - 2 * feats

    @pl.when(core == 0)
    def _():
        out[0:feats, :] = qkv[0]
        out[feats : 2 * feats, :] = qkv[1]
        out[2 * feats :, :] = qkv[2, 0:split, :]

    @pl.when(core != 0)
    def _():
        at = feats - split
        out[0:at, :] = qkv[2, split:, :]
        for c in range(4):
            out[at + 128 * c : at + 128 * (c + 1), :] = wo[:, 128 * c : 128 * (c + 1)]
        at += 4 * 128
        out[at:, :] = jnp.zeros((HALF_PACK - at, 128), BF16)
        high = qv[...].astype(BF16)
        low = (qv[...] - high.astype(F32)).astype(BF16)
        out[at : at + 2, :] = high
        out[at + 2 : at + 4, :] = low


def split_cycles(pair_left, pair_right, eye, count):
    step = mm(pair_left.astype(BF16), pair_right.astype(BF16))
    reach = jnp.minimum(eye + step, 1.0)
    hops = 1
    while hops < count // 2:
        wide = reach.astype(BF16)
        reach = jnp.minimum(mm(wide, wide), 1.0)
        hops *= 2
    lanes = iota((count, count), 1).astype(F32)
    lowest = jnp.min(jnp.where(reach > 0.5, lanes, float(count)), axis=1, keepdims=True)
    lowest_row = jnp.sum(eye * lowest, axis=0, keepdims=True)
    other = jnp.sum(pair_left * lowest_row, axis=1, keepdims=True)
    return (lowest > other).astype(F32)


def route_kernel(st_ref, sl_ref, lt_ref, ll_ref, ids_ref, temb_ref, gw_ref, tab_ref, gate_ref):
    here = lax.axis_index("head").astype(jnp.int32)
    group = lax.axis_index("expert").astype(jnp.int32)
    shorts = st_ref.shape[1]
    longs = lt_ref.shape[1]
    tasks = ids_ref.shape[1]
    per_owner = shorts // 4
    mine = here.astype(F32)

    def eye_of(n):
        return (iota((n, n), 0) == iota((n, n), 1)).astype(F32)

    def col(row, eye):
        return jnp.sum(eye * row, axis=1, keepdims=True)

    def row(column, eye):
        return jnp.sum(eye * column, axis=0, keepdims=True)

    eye = eye_of(shorts)
    at_sub, at_lane = iota((shorts, shorts), 0), iota((shorts, shorts), 1)
    off_diag = 1.0 - eye
    task_row = st_ref[...].astype(F32)
    task_col = col(task_row, eye)
    same_task = (task_col == task_row).astype(F32)
    earlier = (at_lane < at_sub).astype(F32)
    later = (at_lane > at_sub).astype(F32)
    rank_col = jnp.sum(same_task * earlier, axis=1, keepdims=True)
    rank_row = jnp.sum(same_task * later, axis=0, keepdims=True)
    first_of_pair = jnp.floor(rank_col * 0.5) == jnp.floor(rank_row * 0.5)
    pair_right = same_task * first_of_pair.astype(F32) * off_diag
    pair_left = ((at_sub // 2) == (at_lane // 2)).astype(F32) * off_diag
    major = split_cycles(pair_left, pair_right, eye, shorts)
    same_major = (major == row(major, eye)).astype(F32)
    pair_right = same_task * same_major * off_diag
    pair_left = ((at_sub // 4) == (at_lane // 4)).astype(F32) * same_major * off_diag
    minor = split_cycles(pair_left, pair_right, eye, shorts)
    colour = 2.0 * major + minor
    same_owner = ((at_sub // per_owner) == (at_lane // per_owner)).astype(F32)
    same_colour = (colour == row(colour, eye)).astype(F32)
    place = jnp.sum(same_owner * same_colour * earlier, axis=1, keepdims=True)

    sent = iota((shorts, 128), 0)
    lane = iota((shorts, 128), 1)
    sent_f = sent.astype(F32)
    lane_f = lane.astype(F32)
    length_col = col(sl_ref[...].astype(F32), eye)
    own = ((task_col == lane_f) & (colour == mine)).astype(F32)
    owner_col = (iota((shorts, 1), 0) // per_owner).astype(F32)

    def put(r, values):
        tab_ref[r : r + 1, :] = values.astype(jnp.int32)

    def put_away(r, values, low):
        tab_ref[r : r + 1, :] = values.astype(jnp.int32) ^ (here * low)

    def total(values):
        return jnp.sum(values, axis=0, keepdims=True)

    tab_ref[...] = jnp.zeros_like(tab_ref)
    put(0, total(own * sent_f))
    put(1, total(own * length_col))
    put_away(2, total(own * (owner_col * 2.0 + place)), 2)
    natural = (sent == lane + here * per_owner) & (lane < per_owner)
    put_away(6, total(natural.astype(F32) * (colour * 2.0 + place)), 2)

    eye_l = eye_of(longs)
    sub_l, lane_l = iota((longs, longs), 0), iota((longs, longs), 1)
    ltask_row = lt_ref[...].astype(F32)
    ltask_col = col(ltask_row, eye_l)
    right_l = (ltask_col == ltask_row).astype(F32) * (1.0 - eye_l)
    left_l = ((sub_l // 2) == (lane_l // 2)).astype(F32) * (1.0 - eye_l)
    kappa = split_cycles(left_l, right_l, eye_l, longs)
    parity_col = ltask_col - 2.0 * jnp.floor(ltask_col * 0.5)
    parity = jnp.max(parity_col, axis=0, keepdims=True)
    lsent = iota((longs, 128), 0)
    llane = iota((longs, 128), 1)
    unit_task = parity + 2.0 * llane.astype(F32)
    mine_l = (here % 2).astype(F32)
    own_l = ((ltask_col == unit_task) & (kappa == mine_l)).astype(F32)
    llen_col = col(ll_ref[...].astype(F32), eye_l)
    put(3, total(own_l * lsent.astype(F32)))
    put_away(16, total(own_l * (lsent // (longs // 4)).astype(F32)), 1)
    put(4, total(own_l * llen_col))
    row_lane = iota((1, 128), 1)
    row_lane_f = row_lane.astype(F32)
    put(5, parity + 2.0 * row_lane_f)
    natural_l = (lsent == llane + here * (longs // 4)) & (llane < longs // 4)
    put_away(7, total(natural_l.astype(F32) * kappa), 1)
    put_away(15, total(natural_l.astype(F32) * (kappa + 2.0)), 1)

    ids = ids_ref[...].astype(F32)
    eye_t = eye_of(tasks)
    e_first, e_second = col(ids[0:1, :], eye_t), col(ids[1:2, :], eye_t)
    tsub = iota((tasks, 128), 0).astype(F32)
    tlane = iota((tasks, 128), 1).astype(F32)
    diag = (tsub == tlane).astype(F32)
    put(8, total(diag * e_first))
    put(9, total(diag * e_second))
    task_first = total((e_first == tlane).astype(F32) * tsub)
    task_second = total((e_second == tlane).astype(F32) * tsub)
    put(10, task_first)
    put(11, task_second)
    first_parity = task_first - 2.0 * jnp.floor(task_first * 0.5)
    use_second = first_parity != parity
    put(12, use_second.astype(F32))
    unit_of = jnp.where(use_second, task_second, task_first)
    put(13, jnp.floor((unit_of - parity) * 0.5))
    half = here // 2
    tab_ref[14:15, :] = jnp.where(row_lane == 0, half, jnp.where(row_lane == 1, here, group))

    logits = lax.dot_general(
        temb_ref[...],
        gw_ref[...],
        (((1,), (1,)), ((), ())),
        preferred_element_type=F32,
        precision=HIGHEST,
    )
    ecols = iota((tasks, logits.shape[1]), 1).astype(F32)
    first = jnp.sum(jnp.where(ecols == e_first, logits, 0.0), axis=1, keepdims=True)
    second = jnp.sum(jnp.where(ecols == e_second, logits, 0.0), axis=1, keepdims=True)
    top = jnp.maximum(first, second)
    first, second = jnp.exp(first - top), jnp.exp(second - top)
    denominator = first + second
    gate_ref[...] = jnp.where(
        tlane == 0.0, first / denominator, jnp.where(tlane == 1.0, second / denominator, 0.0)
    )


def norm_stats(values):
    centred = values - jnp.mean(values, axis=-1, keepdims=True)
    scale = lax.rsqrt(jnp.mean(centred * centred, axis=-1, keepdims=True) + 1e-05)
    return centred * scale, scale


def prep_kernel(
    tab, gates, cs0, cs1, cl, csb, clb, xs, xl, gain, bias,
    deo, cb_s, cb_l, ns, nl, xb_s, xb_l,
):
    e = pl.program_id(0)
    span = cs0.shape[1]
    for k, ref in ((0, cs0), (1, cs1)):
        t = tab[10 + k, e]
        keep = iota((span, 1), 0) < tab[1, t]
        deo[0, span * k : span * (k + 1), :] = jnp.where(
            keep, gates[t, k] * ref[0].astype(F32), 0.0
        ).astype(BF16)
    half_rows = cl.shape[1]
    u = tab[13, e]
    gate = gates[tab[5, u], tab[12, e]]
    keep = iota((half_rows, 1), 0) + half_rows * tab[14, 0] < tab[4, u]
    deo[0, 2 * span : 2 * span + half_rows, :] = jnp.where(keep, gate * cl[0].astype(F32), 0.0).astype(BF16)
    parity = (tab[5, 0] % 2).astype(F32)
    deo[0, 2 * span + half_rows :, :] = jnp.full((16, deo.shape[2]), parity, F32).astype(BF16)
    cb_s[...] = csb[...]
    cb_l[...] = clb[...]
    xb_s[...] = xs[...]
    xb_l[...] = xl[...]
    ns[0] = (norm_stats(xs[0].astype(F32))[0] * gain[0:1, :] + bias[0:1, :]).astype(BF16)
    nl[0] = (norm_stats(xl[0].astype(F32))[0] * gain[0:1, :] + bias[0:1, :]).astype(BF16)


def unpack_weights(own, other, w, wo, bqv):
    shards = own.shape[0]
    for h in range(shards):
        cols = slice(128 * h, 128 * (h + 1))
        w[0:HALF_PACK, cols] = own[h]
        w[HALF_PACK:QKV_ROWS, cols] = other[h, 0 : QKV_ROWS - HALF_PACK, :]
        for c in range(4):
            at = QKV_ROWS - HALF_PACK + 128 * c
            wo[128 * h : 128 * (h + 1), 128 * c : 128 * (c + 1)] = other[h, at : at + 128, :]
        at = MISC_ROW - HALF_PACK
        lines = other[h, at : at + 16, :].astype(F32)
        bqv[0:2, cols] = lines[0:2] + lines[2:4]


def pair_masks():
    lanes = iota((1, 128), 1)
    first = (lanes < HEAD_DIM).astype(BF16)
    return first, (1.0 - first.astype(F32)).astype(BF16)


def both_heads(block, masks):
    return jnp.concatenate([block * masks[0], block * masks[1]], axis=0)


def fold_heads(stacked, keys):
    lanes = iota((1, 128), 1)
    return jnp.where(lanes < HEAD_DIM, stacked[:keys], stacked[keys:])


def softmax_pair(scores, visible, keys):
    parts = []
    for part in (scores[:, :keys], scores[:, keys:]):
        part = jnp.where(visible, part, -1e30)
        shifted = jnp.exp(part - jnp.max(part, axis=-1, keepdims=True))
        parts.append(shifted * (1.0 / jnp.sum(shifted, axis=-1, keepdims=True)))
    return jnp.concatenate(parts, axis=1).astype(BF16)


def short_visible(tab, i, span):
    rows, lanes = iota((128, 128), 0), iota((128, 128), 1)
    limit = jnp.where(iota((1, 128), 1) < span, tab[1, 2 * i], tab[1, 2 * i + 1] + span)
    return ((rows // span) == (lanes // span)) & (lanes < limit)


def attend_short(
    tab, norm, x, own, other, gain, bias, bo, q_ref, k_ref, v_ref, p_ref, ctx, mid, send, w, wo, bqv
):
    core = tab[14, 2] % 2

    @pl.when(core == 0)
    def _():
        unpack_weights(own, other, w, wo, bqv)

    @pl.when(core != 0)
    def _():
        unpack_weights(other, own, w, wo, bqv)

    feats = norm.shape[1]
    rows = norm[...]
    q_ref[...] = ((mm(rows, w[0:feats, :]) + bqv[0:1, :]).astype(BF16) * HEAD_DIM ** (-0.5)).astype(BF16)
    k_ref[...] = mm(rows, w[feats : 2 * feats, :]).astype(BF16)
    v_ref[...] = (mm(rows, w[2 * feats : 3 * feats, :]) + bqv[1:2, :]).astype(BF16)
    masks = pair_masks()
    span = send.shape[2]
    for i in range(norm.shape[0] // 128):
        visible = short_visible(tab, i, span)
        r = slice(128 * i, 128 * (i + 1))
        for p in range(feats // 128):
            c = slice(128 * p, 128 * (p + 1))
            scores = mm_nt(q_ref[r, c], both_heads(k_ref[r, c], masks))
            probs = softmax_pair(scores, visible, 128)
            p_ref[i * (feats // 128) + p] = probs
            ctx[r, c] = mm(probs, both_heads(v_ref[r, c], masks)).astype(BF16)
    attn = mm(ctx[...], wo[...]) + bo[...]
    for t in range(send.shape[0]):
        r = slice(span * t, span * (t + 1))
        keep = iota((span, 1), 0) < tab[1, t]
        middle = x[r, :].astype(F32) + jnp.where(keep, attn[r, :], 0.0)
        mid[r, :] = middle
        mixin = (norm_stats(middle)[0] * gain[1:2, :] + bias[1:2, :]).astype(BF16)
        send[tab[8, t], 0] = mixin
        send[tab[9, t], 1] = mixin


def attend_long(tab, norm, x, w, wo, bqv, gain, bias, bo, q_ref, k_ref, v_ref, p_ref, ctx, mid, send, nq):
    feats = norm.shape[1]
    half_rows = send.shape[1]
    span = 2 * half_rows
    units = norm.shape[0] // span
    offset = tab[14, 0] * half_rows
    for u in range(units):
        at = pl.multiple_of(span * u + offset, half_rows)
        nq[half_rows * u : half_rows * (u + 1), :] = norm[pl.ds(at, half_rows), :]
    rows = norm[...]
    q_ref[...] = ((mm(nq[...], w[0:feats, :]) + bqv[0:1, :]).astype(BF16) * HEAD_DIM ** (-0.5)).astype(BF16)
    k_ref[...] = mm(rows, w[feats : 2 * feats, :]).astype(BF16)
    v_ref[...] = (mm(rows, w[2 * feats : 3 * feats, :]) + bqv[1:2, :]).astype(BF16)
    masks = pair_masks()
    for u in range(units):
        visible = iota((1, span), 1) < tab[4, u]
        r = slice(half_rows * u, half_rows * (u + 1))
        kr = slice(span * u, span * (u + 1))
        for p in range(feats // 128):
            c = slice(128 * p, 128 * (p + 1))
            scores = mm_nt(q_ref[r, c], both_heads(k_ref[kr, c], masks))
            probs = softmax_pair(scores, visible, span)
            p_ref[u * (feats // 128) + p] = probs
            ctx[r, c] = mm(probs, both_heads(v_ref[kr, c], masks)).astype(BF16)
    attn = mm(ctx[...], wo[...]) + bo[...]
    for u in range(units):
        r = slice(half_rows * u, half_rows * (u + 1))
        keep = iota((half_rows, 1), 0) + offset < tab[4, u]
        at = pl.multiple_of(span * u + offset, half_rows)
        middle = x[pl.ds(at, half_rows), :].astype(F32) + jnp.where(keep, attn[r, :], 0.0)
        mid[r, :] = middle
        mixin = (norm_stats(middle)[0] * gain[1:2, :] + bias[1:2, :]).astype(BF16)
        t = tab[5, u]
        send[tab[8, t]] = mixin
        send[tab[9, t]] = mixin


GELU_A = 0.7978845608028654
GELU_B = 0.044715


def expert_kernel(first, tab, *refs):
    if first:
        x, d, wu, bu, wd, bd, eo, dx, dw, ga, xt, dt, ea, da, hs, ps = refs
        prev = None
    else:
        x, d, wu, bu, wd, bd, par, prev, ga_in, _, eo, dx, dw, ga, xt, dt, ea, da, hs, ps = refs
    j = pl.program_id(0)
    feats = x.shape[2]
    rows = x.shape[0] * x.shape[1]
    step = 4 * x.shape[1]

    @pl.when(j == 0)
    def _():
        for g in range(x.shape[0]):
            cols = slice(x.shape[1] * g, x.shape[1] * (g + 1))
            xt[:, cols] = x[g].T
            dt[:, cols] = d[g].T
        ea[...] = jnp.broadcast_to(bd[...], ea.shape)
        da[...] = jnp.zeros_like(da)

    for i in range(rows // step):
        r = slice(step * i, step * (i + 1))
        xr = x[4 * i : 4 * i + 4].reshape(step, feats)
        dr = d[4 * i : 4 * i + 4].reshape(step, feats)
        pre = (mm(xr, wu[0]) + bu[...]).astype(BF16)
        grad = mm_nt(dr, wd[0]).astype(BF16)
        square = pre * pre
        half = 0.5 + 0.5 * jnp.tanh(pre * (GELU_A + (GELU_A * GELU_B) * square))
        hidden = pre * half
        slope = half + hidden * (1.0 - half) * (2.0 * GELU_A + (6.0 * GELU_A * GELU_B) * square)
        dpre = grad * slope
        hs[r, :] = hidden
        ps[r, :] = dpre
        ea[r, :] += mm(hidden, wd[0])
        da[r, :] += mm_nt(dpre, wu[0])

    wide = wu.shape[2]
    grad_up = mm(xt[...], ps[...])
    grad_down = mm(dt[...], hs[...]).T
    ones = jnp.ones((16, rows), BF16)
    up_bias = mm(ones, ps[...])[0:1, :]
    down_bias = mm_nt(ones, dt[...])[0:1, :]
    if prev is not None:
        grad_up += prev[0, 0:feats, :].astype(F32)
        grad_down += prev[0, feats : feats + wide, :].astype(F32)
        tail = prev[0, feats + wide :, :].astype(F32)
        up_bias += tail[0:1, :]
        down_bias += tail[1:2, :]
    dw[0, 0:feats, :] = grad_up.astype(BF16)
    dw[0, feats : feats + wide, :] = grad_down.astype(BF16)
    which = iota((16, 1), 0)
    dw[0, feats + wide :, :] = jnp.where(
        which == 0, up_bias, jnp.where(which == 1, down_bias, 0.0)
    ).astype(BF16)

    @pl.when(j == pl.num_programs(0) - 1)
    def _():
        own = tab[14, 2]
        t_first, t_second = tab[10, own], tab[11, own]
        lanes = iota((1, 128), 1)
        as_first = (lanes == 2 * t_first).astype(F32)
        as_second = (lanes == 2 * t_second + 1).astype(F32)
        rows_each = x.shape[1]
        gate_sums = jnp.zeros((1, 128), F32)
        for g in range(x.shape[0]):
            r = slice(rows_each * g, rows_each * (g + 1))
            out = ea[r, :].astype(BF16)
            eo[g] = out
            dx[g] = da[r, :].astype(BF16)
            prod = out.astype(F32) * d[g].astype(F32)
            if first:
                half_each = rows_each // 2
                gate_sums += as_first * jnp.sum(prod[:half_each], keepdims=True)
                gate_sums += as_second * jnp.sum(prod[half_each:], keepdims=True)
            else:
                odd = par[g, 0:1, 0:128].astype(F32)
                is_first = odd == (t_first % 2).astype(F32)
                gate_sums += jnp.where(is_first, as_first, as_second) * jnp.sum(prod, keepdims=True)
        if not first:
            gate_sums += ga_in[0:1, :]
        ga[...] = jnp.broadcast_to(gate_sums, ga.shape)


def experts_pass(tab, x, deo, part, w_up, b_up, w_down, b_down, prev, ga, eo):
    experts, rows_each, feats = x.shape
    hidden = w_up.shape[2]
    chunk = hidden // 4
    rows = experts * rows_each
    first = prev is None
    in_specs = [
        SM,
        pl.BlockSpec((experts, rows_each, feats), lambda j: (0, 0, 0)),
        pl.BlockSpec((experts, rows_each, feats), lambda j: (0, part, 0)),
        pl.BlockSpec((1, feats, chunk), lambda j: (0, 0, j)),
        pl.BlockSpec((1, chunk), lambda j: (0, j)),
        pl.BlockSpec((1, chunk, feats), lambda j: (0, j, 0)),
        pl.BlockSpec((1, feats), lambda j: (0, 0)),
    ]
    args = [tab, x, deo, w_up, b_up, w_down, b_down]
    if not first:
        in_specs.append(pl.BlockSpec((experts, 16, feats), lambda j: (0, 2 * rows_each // 16, 0)))
        args.append(deo)
        in_specs.append(pl.BlockSpec((1, GRAD_ROWS, feats), lambda j: (j, 0, 0)))
        args.append(prev)
        in_specs.append(pl.BlockSpec((8, 128), lambda j: (0, 0)))
        args.append(ga)
        in_specs.append(ANY)
        args.append(eo)
    return pl.pallas_call(
        functools.partial(expert_kernel, first),
        grid=(4,),
        in_specs=in_specs,
        out_specs=[
            pl.BlockSpec((experts, rows_each, feats), lambda j: (0, part, 0)),
            pl.BlockSpec((experts, rows_each, feats), lambda j: (0, 0, 0)),
            pl.BlockSpec((1, GRAD_ROWS, feats), lambda j: (j, 0, 0)),
            pl.BlockSpec((8, 128), lambda j: (0, 0)),
        ],
        out_shape=[
            jax.ShapeDtypeStruct((experts, 2 * rows_each, feats), BF16),
            jax.ShapeDtypeStruct(x.shape, BF16),
            jax.ShapeDtypeStruct((4, GRAD_ROWS, feats), BF16),
            jax.ShapeDtypeStruct((8, 128), F32),
        ],
        scratch_shapes=[
            pltpu.VMEM((feats, rows), BF16),
            pltpu.VMEM((feats, rows), BF16),
            pltpu.VMEM((rows, feats), F32),
            pltpu.VMEM((rows, feats), F32),
            pltpu.VMEM((rows, chunk), BF16),
            pltpu.VMEM((rows, chunk), BF16),
        ],
        input_output_aliases={} if first else {len(args) - 1: 0},
        compiler_params=params(),
        cost_estimate=cost(25),
        name="experts_short" if first else "experts_long",
    )(*args)


def norm_back(grad, unit, scale, gain):
    scaled = grad * gain
    return scale * (
        scaled
        - jnp.mean(scaled, axis=-1, keepdims=True)
        - unit * jnp.mean(scaled * unit, axis=-1, keepdims=True)
    )


def head_pair_back(probs, dctx, q, kk, vv, keys):
    dprobs = mm_nt(dctx, vv)
    dvalues = fold_heads(mm_tn(probs, dctx), keys)
    wide = probs.astype(F32)
    prod = wide * dprobs
    parts = []
    for part in (slice(0, keys), slice(keys, 2 * keys)):
        parts.append(prod[:, part] - wide[:, part] * jnp.sum(prod[:, part], axis=-1, keepdims=True))
    dscores = jnp.concatenate(parts, axis=1).astype(BF16)
    dqueries = mm(dscores, kk) * HEAD_DIM ** (-0.5)
    dkeys = fold_heads(mm_tn(dscores, q), keys)
    return dqueries.astype(BF16), dkeys.astype(BF16), dvalues.astype(BF16)


def row_sum(values):
    return jnp.sum(values, axis=0, keepdims=True)


def back_short(
    tab, ret, mid, c, x, norm, q_ref, k_ref, v_ref, p_ref, ctx, w, wo, gain, _,
    zsend, dw, small, _out, dmid, dattn, dctx, dq, dk, dv, dnorm,
):
    feats = norm.shape[1]
    span = zsend.shape[1]
    sums = [jnp.zeros((1, feats), F32) for _ in range(5)]
    for t in range(ret.shape[0]):
        r = slice(span * t, span * (t + 1))
        dmix = ret[tab[8, t], 0].astype(F32) + ret[tab[9, t], 1].astype(F32)
        unit, scale = norm_stats(mid[r, :])
        sums[2] += row_sum(dmix * unit)
        sums[3] += row_sum(dmix)
        middle = c[r, :].astype(F32) + norm_back(dmix, unit, scale, gain[1:2, :])
        dmid[r, :] = middle
        masked = jnp.where(iota((span, 1), 0) < tab[1, t], middle, 0.0)
        sums[4] += row_sum(masked)
        dattn[r, :] = masked.astype(BF16)
    dctx[...] = mm_nt(dattn[...], wo[...]).astype(BF16)
    dw[3 * feats : 4 * feats, :] = mm_tn(ctx[...], dattn[...]).astype(BF16)
    masks = pair_masks()
    for i in range(norm.shape[0] // 128):
        r = slice(128 * i, 128 * (i + 1))
        for p in range(feats // 128):
            c_ = slice(128 * p, 128 * (p + 1))
            a, b, d = head_pair_back(
                p_ref[i * (feats // 128) + p],
                dctx[r, c_],
                q_ref[r, c_],
                both_heads(k_ref[r, c_], masks),
                both_heads(v_ref[r, c_], masks),
                128,
            )
            dq[r, c_] = a
            dk[r, c_] = b
            dv[r, c_] = d
    rows = norm[...]
    for index, ref in enumerate((dq, dk, dv)):
        dw[feats * index : feats * (index + 1), :] = mm_tn(rows, ref[...]).astype(BF16)
    dnorm[...] = (
        mm_nt(dq[...], w[0:feats, :])
        + mm_nt(dk[...], w[feats : 2 * feats, :])
        + mm_nt(dv[...], w[2 * feats : 3 * feats, :])
    )
    for t in range(ret.shape[0]):
        r = slice(span * t, span * (t + 1))
        unit, scale = norm_stats(x[r, :].astype(F32))
        grad = dnorm[r, :]
        sums[0] += row_sum(grad * unit)
        sums[1] += row_sum(grad)
        zsend[tab[2, t]] = (dmid[r, :] + norm_back(grad, unit, scale, gain[0:1, :])).astype(BF16)
    sums.append(row_sum(dq[...].astype(F32)))
    sums.append(row_sum(dv[...].astype(F32)))
    for index, value in enumerate(sums):
        small[index : index + 1, :] = value
    small[7:8, :] = jnp.zeros((1, feats), F32)


def back_long(
    tab, ret, mid, c, x, norm, q_ref, k_ref, v_ref, p_ref, ctx, w, wo, gain, dw_in, small_in, ga, z_short,
    z0, z1, z2, z3, packed, zsend, nq, dmid, dattn, dctx, dq, dk, dv, dnorm, full,
):
    feats = norm.shape[1]
    half_rows = ret.shape[1]
    span = 2 * half_rows
    units = norm.shape[0] // span
    offset = tab[14, 0] * half_rows
    sums = [small_in[index : index + 1, :] for index in range(7)]
    for u in range(units):
        r = slice(half_rows * u, half_rows * (u + 1))
        t = tab[5, u]
        at = pl.multiple_of(span * u + offset, half_rows)
        nq[r, :] = norm[pl.ds(at, half_rows), :]
        dmix = ret[tab[8, t]].astype(F32) + ret[tab[9, t]].astype(F32)
        unit, scale = norm_stats(mid[r, :])
        sums[2] += row_sum(dmix * unit)
        sums[3] += row_sum(dmix)
        middle = c[r, :].astype(F32) + norm_back(dmix, unit, scale, gain[1:2, :])
        dmid[r, :] = middle
        masked = jnp.where(iota((half_rows, 1), 0) + offset < tab[4, u], middle, 0.0)
        sums[4] += row_sum(masked)
        dattn[r, :] = masked.astype(BF16)
    dctx[...] = mm_nt(dattn[...], wo[...]).astype(BF16)
    grad_out = mm_tn(ctx[...], dattn[...]) + dw_in[3 * feats : 4 * feats, :].astype(F32)
    shards = packed.shape[1]
    for h in range(shards):
        for s in range(4):
            full[QKV_ROWS + 128 * s : QKV_ROWS + 128 * (s + 1), 128 * h : 128 * (h + 1)] = grad_out[
                128 * h : 128 * (h + 1), 128 * s : 128 * (s + 1)
            ]
    masks = pair_masks()
    for u in range(units):
        r = slice(half_rows * u, half_rows * (u + 1))
        kr = slice(span * u, span * (u + 1))
        for p in range(feats // 128):
            c_ = slice(128 * p, 128 * (p + 1))
            a, b, d = head_pair_back(
                p_ref[u * (feats // 128) + p],
                dctx[r, c_],
                q_ref[r, c_],
                both_heads(k_ref[kr, c_], masks),
                both_heads(v_ref[kr, c_], masks),
                span,
            )
            dq[r, c_] = a
            dk[kr, c_] = b
            dv[kr, c_] = d
    for index, (left, right) in enumerate(((nq, dq), (norm, dk), (norm, dv))):
        r = slice(feats * index, feats * (index + 1))
        full[r, :] = mm_tn(left[...], right[...]) + dw_in[r, :].astype(F32)
    dnorm[...] = mm_nt(dk[...], w[feats : 2 * feats, :]) + mm_nt(dv[...], w[2 * feats : 3 * feats, :])
    from_q = mm_nt(dq[...], w[0:feats, :])
    for u in range(units):
        at = pl.multiple_of(span * u + offset, half_rows)
        dnorm[pl.ds(at, half_rows), :] += from_q[half_rows * u : half_rows * (u + 1), :]
    for u in range(units):
        owner = tab[16, u]
        for s in range(2):
            r = slice(span * u + half_rows * s, span * u + half_rows * (s + 1))
            unit, scale = norm_stats(x[r, :].astype(F32))
            grad = dnorm[r, :]
            sums[0] += row_sum(grad * unit)
            sums[1] += row_sum(grad)
            own_half = tab[14, 0] == s
            direct = jnp.where(own_half, dmid[half_rows * u : half_rows * (u + 1), :], 0.0)
            zsend[owner, half_rows * s : half_rows * (s + 1), :] = (
                direct + norm_back(grad, unit, scale, gain[0:1, :])
            ).astype(BF16)
    at = z0.shape[1] - span
    for d, ref in enumerate((z0, z1, z2, z3)):
        ref[0, 0:at, :] = z_short[2 * d : 2 * d + 2].reshape(at, feats)
        ref[0, at:, :] = zsend[d]
    sums[5] += row_sum(dq[...].astype(F32))
    sums[6] += row_sum(dv[...].astype(F32))
    full[MISC_ROW:, :] = jnp.zeros((full.shape[0] - MISC_ROW, feats), F32)
    full[MISC_ROW : MISC_ROW + 1, :] = sums[5]
    full[MISC_ROW + 1 : MISC_ROW + 2, :] = sums[6]
    for index in range(5):
        for s in range(4):
            at = MISC_ROW + 2 + 4 * index + s
            piece = sums[index][:, 128 * s : 128 * (s + 1)]
            full[at : at + 1, :] = jnp.concatenate([piece] * shards, axis=1)
    for s in range(shards):
        full[MISC_ROW + 22 : MISC_ROW + 23, 128 * s : 128 * (s + 1)] = ga[0:1, :]
    for g in range(packed.shape[0]):
        for h in range(shards):
            packed[g, tab[14, 1] ^ h] = full[
                SLICE_ROWS * g : SLICE_ROWS * (g + 1), 128 * h : 128 * (h + 1)
            ].astype(BF16)


def mix_kernel(tab, gates, ret, mid_s, mid_l, _, z0, z1, z2, z3, _out, zsend):
    experts = ret.shape[0]
    span = mid_s.shape[0] // experts
    half_rows = ret.shape[1] - 2 * span
    for t in range(experts):
        r = slice(span * t, span * (t + 1))
        keep = iota((span, 1), 0) < tab[1, t]
        e0 = ret[tab[8, t], 0:span, :].astype(F32)
        e1 = ret[tab[9, t], span : 2 * span, :].astype(F32)
        mixed = gates[t, 0] * e0 + gates[t, 1] * e1
        slot = tab[2, t]
        at = pl.multiple_of((slot % 2) * span, span)
        zsend[slot // 2, pl.ds(at, span), :] = (mid_s[r, :] + jnp.where(keep, mixed, 0.0)).astype(BF16)
    for u in range(mid_l.shape[0] // half_rows):
        r = slice(half_rows * u, half_rows * (u + 1))
        t = tab[5, u]
        keep = iota((half_rows, 1), 0) + half_rows * tab[14, 0] < tab[4, u]
        e0 = ret[tab[8, t], 2 * span :, :].astype(F32)
        e1 = ret[tab[9, t], 2 * span :, :].astype(F32)
        mixed = gates[t, 0] * e0 + gates[t, 1] * e1
        zsend[tab[16, u], 2 * span :, :] = (mid_l[r, :] + jnp.where(keep, mixed, 0.0)).astype(BF16)
    for d, ref in enumerate((z0, z1, z2, z3)):
        ref[0] = zsend[d]


def each_distance(index, refs, act):
    for d, ref in enumerate(refs):

        @pl.when(index == d)
        def _(ref=ref):
            act(ref)


def place_out(tab, a0, a1, a2, a3, short_out, long_out):
    parts = (a0, a1, a2, a3)
    span = short_out.shape[1]
    for n in range(short_out.shape[0]):
        slot = tab[6, n]
        at = pl.multiple_of((slot % 2) * span, span)

        def copy_short(ref, n=n, at=at):
            short_out[n] = ref[0, pl.ds(at, span), :]

        each_distance(slot // 2, parts, copy_short)
    half = long_out.shape[1] // 2
    for n in range(long_out.shape[0]):
        for index, row in ((0, 7), (1, 15)):

            def copy_long(ref, n=n, index=index):
                long_out[n, half * index : half * (index + 1), :] = ref[0, 2 * span :, :]

            each_distance(tab[row, n], parts, copy_long)


def place_dx(tab, a0, a1, a2, a3, short_dx, long_dx):
    parts = (a0, a1, a2, a3)
    span = short_dx.shape[1]
    for n in range(short_dx.shape[0]):
        slot = tab[6, n]
        at = pl.multiple_of((slot % 2) * span, span)

        def copy_short(ref, n=n, at=at):
            short_dx[n] = ref[0, pl.ds(at, span), :].astype(F32)

        each_distance(slot // 2, parts, copy_short)
    for n in range(long_dx.shape[0]):

        def first(ref, n=n):
            long_dx[n] = ref[0, 2 * span :, :].astype(F32)

        def second(ref, n=n):
            long_dx[n] += ref[0, 2 * span :, :].astype(F32)

        each_distance(tab[7, n], parts, first)
        each_distance(tab[15, n], parts, second)


def finish_kernel(tab, *refs):
    pieces = refs[:-13]
    ids, gates, temb, gw_t, qkv, qv, wo, gain, shift, bo, grad_temb, grad_gw_t, g = refs[-13:]
    feats = wo.shape[1]
    for d, piece in enumerate(pieces):
        at = pl.multiple_of((tab[14, 2] ^ d) * SLICE_ROWS, 16)
        g[pl.ds(at, SLICE_ROWS), :] = piece[0]
    for j in range(3):
        qkv[j] = g[feats * j : feats * (j + 1), :].astype(F32)
    for c in range(4):
        at = QKV_ROWS + 128 * c
        wo[:, 128 * c : 128 * (c + 1)] = g[at : at + 128, :].astype(F32)
    misc = g[MISC_ROW : MISC_ROW + 32, :].astype(F32)
    qv[...] = misc[0:2, :]

    def line(index):
        at = 2 + 4 * index
        return jnp.concatenate([misc[at + s : at + s + 1, :] for s in range(4)], axis=1)

    gain[0:1, :], gain[1:2, :] = line(0), line(2)
    shift[0:1, :], shift[1:2, :] = line(1), line(3)
    bo[...] = line(4)
    terms = misc[22:23, :]
    tasks = temb.shape[0]
    sub, lane = iota((tasks, 128), 0), iota((tasks, 128), 1)
    first = jnp.sum(jnp.where(lane == 2 * sub, terms, 0.0), axis=1, keepdims=True)
    second = jnp.sum(jnp.where(lane == 2 * sub + 1, terms, 0.0), axis=1, keepdims=True)
    both = first + second
    first = first - gates[:, 0:1] * both
    second = second - gates[:, 1:2] * both
    experts = gw_t.shape[0]
    rows = iota((experts, tasks), 0)
    eye = (iota((tasks, tasks), 0) == iota((tasks, tasks), 1)).astype(F32)
    spread = jnp.zeros((experts, tasks), F32)
    for k, value in ((0, first), (1, second)):
        as_row = jnp.sum(eye * value, axis=0, keepdims=True)
        spread += jnp.where(rows == ids[k : k + 1, :], as_row, 0.0)
    grad_gw_t[...] = lax.dot_general(
        spread, temb[...], (((1,), (0,)), ((), ())), preferred_element_type=F32, precision=HIGHEST
    )
    grad_temb[...] = lax.dot_general(
        spread.T, gw_t[...], (((1,), (0,)), ((), ())), preferred_element_type=F32, precision=HIGHEST
    )


def finish_experts(tab, shard, up, up_b, down, down_b):
    feats = up.shape[1]
    up[0] = shard[0, 0:feats, :].astype(F32)
    down[0] = shard[0, feats : 2 * feats, :].astype(F32)
    tail = shard[0, 2 * feats :, :].astype(F32)
    up_b[...] = tail[0:1, :]
    down_b[...] = jnp.zeros_like(down_b)
    for h in range(feats // 128):

        @pl.when(tab[14, 1] == h)
        def _(h=h):
            down_b[...] = tail[1:2, 128 * h : 128 * (h + 1)]


def shape_of(shape, dtype):
    return jax.ShapeDtypeStruct(shape, dtype)


def balanced(short_x, long_x, expert_ids):
    heads = lax.axis_size("head")
    tasks = expert_ids.shape[0]
    return (
        heads == 4
        and lax.axis_size("expert") == tasks == 8
        and short_x.shape[0] == 4 * tasks
        and long_x.shape[0] == tasks
        and short_x.shape[1:] == (64, 512)
        and long_x.shape[1:] == (256, 512)
    )


def per_device(
    short_x,
    long_x,
    short_cot,
    long_cot,
    short_len,
    long_len,
    short_task,
    long_task,
    expert_ids,
    ln_gain,
    ln_bias,
    w_qkv,
    b_qv,
    w_attn_out,
    b_attn_out,
    w_up,
    b_up,
    w_down,
    b_down,
    task_emb,
    gate_w,
):
    if not balanced(short_x, long_x, expert_ids):
        return per_device_wide(
            short_x, long_x, short_cot, long_cot, short_len, long_len, short_task, long_task,
            expert_ids, ln_gain, ln_bias, w_qkv, b_qv, w_attn_out, b_attn_out, w_up, b_up,
            w_down, b_down, task_emb, gate_w,
        )
    heads = lax.axis_size("head")
    experts = lax.axis_size("expert")
    span, feats = short_x.shape[1:]
    long_span = long_x.shape[1]
    half_rows = long_span // 2
    tasks = expert_ids.shape[0]
    units = long_x.shape[0] // 2
    rows_s = tasks * span
    rows_q = units * half_rows
    rows_l = units * long_span
    pairs = feats // 128

    own_half = pl.pallas_call(
        pack_kernel,
        in_specs=[VM] * 3,
        out_specs=VM,
        out_shape=shape_of((HALF_PACK, 128), BF16),
        compiler_params=params(),
        cost_estimate=cost(2),
        name="pack",
    )(w_qkv, b_qv, w_attn_out)
    raw_own = lax.all_gather(own_half, "head", axis=0)
    raw_other = lax.ppermute(raw_own, "expert", [(i, i ^ 1) for i in range(experts)])

    tab, gates = pl.pallas_call(
        route_kernel,
        in_specs=[VM] * 7,
        out_specs=[VM, VM],
        out_shape=[shape_of((24, 128), jnp.int32), shape_of((tasks, 128), F32)],
        compiler_params=params(),
        cost_estimate=cost(4),
        name="route",
    )(
        short_task.reshape(1, -1),
        short_len.reshape(1, -1),
        long_task.reshape(1, -1),
        long_len.reshape(1, -1),
        expert_ids.T,
        task_emb,
        gate_w.T,
    )

    def blk(n, index):
        return pl.BlockSpec((1, n, feats), index)

    deo, cot_s, cot_l, norm_s, norm_l, own_s, own_l = pl.pallas_call(
        prep_kernel,
        grid_spec=pltpu.PrefetchScalarGridSpec(
            num_scalar_prefetch=1,
            grid=(8,),
            in_specs=[
                SM,
                blk(span, lambda e, tab: (tab[0, tab[10, e]], 0, 0)),
                blk(span, lambda e, tab: (tab[0, tab[11, e]], 0, 0)),
                blk(half_rows, lambda e, tab: (tab[3, tab[13, e]], tab[14, 0], 0)),
                blk(span, lambda e, tab: (tab[0, e], 0, 0)),
                blk(span, lambda e, tab: (tab[3, e // 2], tab[14, 0] * 2 + e % 2, 0)),
                blk(span, lambda e, tab: (tab[0, e], 0, 0)),
                blk(half_rows, lambda e, tab: (tab[3, e // 2], e % 2, 0)),
                pl.BlockSpec((2, feats), lambda e, tab: (0, 0)),
                pl.BlockSpec((2, feats), lambda e, tab: (0, 0)),
            ],
            out_specs=[
                blk(2 * span + half_rows + 16, lambda e, tab: (e, 0, 0)),
                blk(span, lambda e, tab: (e, 0, 0)),
                blk(span, lambda e, tab: (e, 0, 0)),
                blk(span, lambda e, tab: (e, 0, 0)),
                blk(half_rows, lambda e, tab: (e, 0, 0)),
                blk(span, lambda e, tab: (e, 0, 0)),
                blk(half_rows, lambda e, tab: (e, 0, 0)),
            ],
        ),
        out_shape=[
            shape_of((experts, 2 * span + half_rows + 16, feats), BF16),
            shape_of((8, span, feats), BF16),
            shape_of((8, span, feats), BF16),
            shape_of((8, span, feats), BF16),
            shape_of((8, half_rows, feats), BF16),
            shape_of((8, span, feats), BF16),
            shape_of((8, half_rows, feats), BF16),
        ],
        compiler_params=params(),
        cost_estimate=cost(9),
        name="prep",
    )(tab, gates, short_cot, short_cot, long_cot, short_cot, long_cot, short_x, long_x, ln_gain, ln_bias)
    cot_s, norm_s, own_s = (a.reshape(rows_s, feats) for a in (cot_s, norm_s, own_s))
    cot_l = cot_l.reshape(rows_q, feats)
    norm_l, own_l = norm_l.reshape(rows_l, feats), own_l.reshape(rows_l, feats)
    deo = lax.all_to_all(deo, "expert", split_axis=0, concat_axis=0, tiled=True)

    bias_out = b_attn_out.reshape(1, feats)
    w_shapes = [
        shape_of((QKV_ROWS, feats), BF16),
        shape_of((feats, feats), BF16),
        shape_of((8, feats), F32),
    ]

    def attention(kernel, operands, key_rows, query_rows, keys, send_shape, more, scratch, name):
        return pl.pallas_call(
            kernel,
            in_specs=[SM] + [VM] * (len(operands) - 1),
            out_specs=[VM] * (7 + len(more)),
            out_shape=[
                shape_of((query_rows, feats), BF16),
                shape_of((key_rows, feats), BF16),
                shape_of((key_rows, feats), BF16),
                shape_of((4 * pairs, 128, 2 * keys), BF16),
                shape_of((query_rows, feats), BF16),
                shape_of((query_rows, feats), F32),
                shape_of(send_shape, BF16),
            ]
            + more,
            scratch_shapes=scratch,
            compiler_params=params(),
            cost_estimate=cost(12),
            name=name,
        )(*operands)

    q_s, k_s, v_s, p_s, ctx_s, mid_s, send_s, w_all, wo_all, bqv_all = attention(
        attend_short,
        (tab, norm_s, own_s, raw_own, raw_other, ln_gain, ln_bias, bias_out),
        rows_s, rows_s, 128, (experts, 2, span, feats), w_shapes, [], "attend_short",
    )
    send_s = send_s.reshape(experts, 2 * span, feats)
    recv_s = lax.all_to_all(send_s, "expert", split_axis=0, concat_axis=0, tiled=True)
    q_l, k_l, v_l, p_l, ctx_l, mid_l, send_l = attention(
        attend_long,
        (tab, norm_l, own_l, w_all, wo_all, bqv_all, ln_gain, ln_bias, bias_out),
        rows_l, rows_q, long_span, (experts, half_rows, feats), [],
        [pltpu.VMEM((rows_q, feats), BF16)], "attend_long",
    )
    recv_l = lax.all_to_all(send_l, "expert", split_axis=0, concat_axis=0, tiled=True)

    eo, dx_s, dw_s, ga_s = experts_pass(
        tab, recv_s, deo, 0, w_up, b_up, w_down, b_down, None, None, None
    )
    ret_s = lax.all_to_all(dx_s, "expert", split_axis=0, concat_axis=0, tiled=True)
    eo, dx_l, dw_l, ga_l = experts_pass(
        tab, recv_l, deo, 1, w_up, b_up, w_down, b_down, dw_s, ga_s, eo
    )
    ret_l = lax.all_to_all(dx_l, "expert", split_axis=0, concat_axis=0, tiled=True)
    expert_grads = lax.psum_scatter(dw_l, "head", scatter_dimension=0, tiled=True)

    def over_head(blocks):
        return [blocks[0]] + [
            lax.ppermute(blocks[d], "head", [(i, i ^ d) for i in range(heads)]) for d in range(1, heads)
        ]

    zsend_s, dw_attn, small, eo = pl.pallas_call(
        back_short,
        in_specs=[SM] + [VM] * 13 + [ANY],
        out_specs=[VM] * 3 + [ANY],
        out_shape=[
            shape_of((2 * heads, span, feats), BF16),
            shape_of((4 * feats, feats), BF16),
            shape_of((8, feats), F32),
            shape_of(eo.shape, BF16),
        ],
        input_output_aliases={14: 3},
        scratch_shapes=[
            pltpu.VMEM((rows_s, feats), F32),
            pltpu.VMEM((rows_s, feats), BF16),
            pltpu.VMEM((rows_s, feats), BF16),
            pltpu.VMEM((rows_s, feats), BF16),
            pltpu.VMEM((rows_s, feats), BF16),
            pltpu.VMEM((rows_s, feats), BF16),
            pltpu.VMEM((rows_s, feats), F32),
        ],
        compiler_params=params(),
        cost_estimate=cost(36),
        name="back_short",
    )(
        tab, ret_s.reshape(experts, 2, span, feats), mid_s, cot_s, own_s, norm_s,
        q_s, k_s, v_s, p_s, ctx_s, w_all, wo_all, ln_gain, eo,
    )
    out_all = lax.all_to_all(eo, "expert", split_axis=0, concat_axis=0, tiled=True)
    *zsend_x, packed = pl.pallas_call(
        back_long,
        in_specs=[SM] + [VM] * 17,
        out_specs=[VM] * (heads + 1),
        out_shape=[shape_of((1, 2 * span + long_span, feats), BF16)] * heads
        + [shape_of((experts, heads, SLICE_ROWS, 128), BF16)],
        scratch_shapes=[
            pltpu.VMEM((heads, long_span, feats), BF16),
            pltpu.VMEM((rows_q, feats), BF16),
            pltpu.VMEM((rows_q, feats), F32),
            pltpu.VMEM((rows_q, feats), BF16),
            pltpu.VMEM((rows_q, feats), BF16),
            pltpu.VMEM((rows_q, feats), BF16),
            pltpu.VMEM((rows_l, feats), BF16),
            pltpu.VMEM((rows_l, feats), BF16),
            pltpu.VMEM((rows_l, feats), F32),
            pltpu.VMEM((experts * SLICE_ROWS, feats), F32),
        ],
        compiler_params=params(),
        cost_estimate=cost(54),
        name="back_long",
    )(
        tab, ret_l, mid_l, cot_l, own_l, norm_l, q_l, k_l, v_l, p_l, ctx_l, w_all, wo_all, ln_gain,
        dw_attn, small, ga_l, zsend_s,
    )
    back_x = over_head(zsend_x)
    *zsend_o, packed = pl.pallas_call(
        mix_kernel,
        in_specs=[SM, SM] + [VM] * 3 + [ANY],
        out_specs=[VM] * heads + [ANY],
        out_shape=[shape_of((1, 2 * span + half_rows, feats), BF16)] * heads
        + [shape_of(packed.shape, BF16)],
        input_output_aliases={5: heads},
        scratch_shapes=[pltpu.VMEM((heads, 2 * span + half_rows, feats), BF16)],
        compiler_params=params(),
        cost_estimate=cost(12),
        name="mix",
    )(tab, gates, out_all, mid_s, mid_l, packed)
    back_o = over_head(zsend_o)
    terms = lax.all_to_all(packed, "expert", split_axis=0, concat_axis=0, tiled=True)
    terms = jnp.sum(terms.astype(F32), axis=0).astype(BF16)
    terms = sum(
        part.astype(F32) for part in over_head([terms[d : d + 1] for d in range(heads)])
    ).astype(BF16)
    attn_grads = [terms] + [
        lax.ppermute(terms, "expert", [(i, i ^ d) for i in range(experts)]) for d in range(1, experts)
    ]

    short_out, long_out = pl.pallas_call(
        place_out,
        in_specs=[SM] + [VM] * 4,
        out_specs=[VM, VM],
        out_shape=[shape_of((8, span, feats), BF16), shape_of((2, long_span, feats), BF16)],
        compiler_params=params(),
        cost_estimate=cost(3),
        name="place_out",
    )(tab, *back_o)
    short_dx, long_dx = pl.pallas_call(
        place_dx,
        in_specs=[SM] + [VM] * 4,
        out_specs=[VM, VM],
        out_shape=[shape_of((8, span, feats), F32), shape_of((2, long_span, feats), F32)],
        compiler_params=params(),
        cost_estimate=cost(4),
        name="place_dx",
    )(tab, *back_x)

    grad_qkv, grad_qv, grad_wo, grad_gain, grad_shift, grad_bo, grad_task, grad_gate = pl.pallas_call(
        finish_kernel,
        in_specs=[SM] + [VM] * (experts + 4),
        out_specs=[VM] * 8,
        out_shape=[
            shape_of((3, feats, 128), F32),
            shape_of((2, 128), F32),
            shape_of((128, feats), F32),
            shape_of((2, feats), F32),
            shape_of((2, feats), F32),
            shape_of((1, feats), F32),
            shape_of((tasks, feats), F32),
            shape_of((experts, feats), F32),
        ],
        scratch_shapes=[pltpu.VMEM((experts * SLICE_ROWS, 128), BF16)],
        compiler_params=params(),
        cost_estimate=cost(3),
        name="finish",
    )(tab, *attn_grads, expert_ids.T, gates, task_emb, gate_w.T)
    chunk = w_up.shape[2] // 4
    grad_up, grad_up_b, grad_down, grad_down_b = pl.pallas_call(
        finish_experts,
        in_specs=[SM, VM],
        out_specs=[VM] * 4,
        out_shape=[
            shape_of((1, feats, chunk), F32),
            shape_of((1, chunk), F32),
            shape_of((1, chunk, feats), F32),
            shape_of((1, feats // heads), F32),
        ],
        compiler_params=params(),
        cost_estimate=cost(3),
        name="finish_experts",
    )(tab, expert_grads)
    return (
        short_out,
        long_out,
        short_dx,
        long_dx,
        grad_gain,
        grad_shift,
        grad_qkv,
        grad_qv,
        grad_wo,
        grad_bo.reshape(feats),
        grad_up,
        grad_up_b,
        grad_down,
        grad_down_b,
        grad_task,
        grad_gate.T,
    )


def solution(mesh):
    return jax.shard_map(
        per_device,
        mesh=mesh,
        in_specs=(
            P("expert", None, None),
            P("expert", None, None),
            P("expert", None, None),
            P("expert", None, None),
            P("expert"),
            P("expert"),
            P("expert"),
            P("expert"),
            P(),
            P(),
            P(),
            P(None, None, "head"),
            P(None, "head"),
            P("head", None),
            P(),
            P("expert", None, None),
            P("expert", None),
            P("expert", None, None),
            P("expert", None),
            P(),
            P(),
        ),
        out_specs=(
            P(("expert", "head"), None, None),
            P(("expert", "head"), None, None),
            P(("expert", "head"), None, None),
            P(("expert", "head"), None, None),
            P(),
            P(),
            P(None, None, "head"),
            P(None, "head"),
            P("head", None),
            P(),
            P("expert", None, "head"),
            P("expert", "head"),
            P("expert", "head", None),
            P("expert", "head"),
            P(),
            P(),
        ),
        check_vma=False,
    )
```

```python
import functools

import jax
import jax.numpy as jnp
from jax import lax
from jax.experimental import pallas as pl
from jax.experimental.pallas import tpu as pltpu
from jax.sharding import PartitionSpec as P

HEAD_DIM = 64


HIGHEST = lax.Precision.HIGHEST
CONTRACT_ROWS = (((0,), (0,)), ((), ()))
CONTRACT_COLS = (((1,), (1,)), ((), ()))


def layer_norm(values, gain, shift):
    centred = values - jnp.mean(values, axis=-1, keepdims=True)
    spread = jnp.mean(centred * centred, axis=-1, keepdims=True)
    return centred * lax.rsqrt(spread + 1e-05) * gain + shift


def lookup(table, index):
    hits = index[..., None] == jnp.arange(table.shape[0], dtype=jnp.int32)
    return jnp.sum(jnp.where(hits, table, jnp.zeros((), table.dtype)), axis=-1)


def route_slots(tasks, expert_ids, capacity, experts):
    task_hits = tasks[:, None] == jnp.arange(expert_ids.shape[0], dtype=jnp.int32)
    chosen = jnp.sum(jnp.where(task_hits[:, :, None], expert_ids[None, :, :], 0), axis=1).reshape(
        -1
    )
    routes = chosen.shape[0]
    owner_hits = (chosen[:, None] == jnp.arange(experts, dtype=jnp.int32)).astype(jnp.int32)
    earlier = jnp.cumsum(owner_hits, axis=0) - owner_hits
    ranking = jnp.sum(earlier * owner_hits, axis=1)
    slot_key = chosen * capacity + ranking
    slot_hits = slot_key[:, None] == jnp.arange(experts * capacity, dtype=jnp.int32)
    return jnp.sum(jnp.where(slot_hits, jnp.arange(routes, dtype=jnp.int32)[:, None], 0), axis=0)


def masked_scores(queries, key_rows, lengths):
    positions = key_rows.shape[1]
    scores = jnp.einsum(
        "blhd,bmhd->bhlm", queries, key_rows, preferred_element_type=jnp.float32
    ) * HEAD_DIM ** (-0.5)
    visible = (
        jnp.arange(positions, dtype=jnp.int32)[None, None, None, :] < lengths[:, None, None, None]
    )
    return jnp.where(visible, scores, -1e30)


def attend(normed, lengths, weights, biases, head_count):
    sentences, positions, features = normed.shape
    flattened = normed.reshape(-1, features)
    shape_heads = (sentences, positions, head_count, HEAD_DIM)

    def project(index, offset):
        return (
            (jnp.dot(flattened, weights[index], preferred_element_type=jnp.float32) + offset)
            .astype(jnp.bfloat16)
            .reshape(shape_heads)
        )

    queries = project(0, biases[0])
    key_rows = project(1, 0.0)
    values = project(2, biases[1])
    scores = masked_scores(queries, key_rows, lengths)
    highest = jnp.max(scores, axis=-1, keepdims=True)
    shifted = jnp.exp(scores - highest)
    totals = jnp.sum(shifted, axis=-1, keepdims=True)
    attn_probs = (shifted / totals).astype(jnp.bfloat16)
    log_total = highest + jnp.log(totals)
    context = jnp.einsum(
        "bhlm,bmhd->blhd", attn_probs, values, preferred_element_type=jnp.float32
    ).astype(jnp.bfloat16)
    return (queries, key_rows, values, context.reshape(sentences, positions, -1), log_total)


def attend_back(normed, lengths, kept, grad_out, weights, out_weight):
    queries, key_rows, values, context, log_total = kept
    features = normed.shape[-1]
    head_cols = context.shape[-1]
    grad_flat = grad_out.reshape(-1, features)
    context_flat = context.reshape(-1, head_cols)
    grad_context = (
        lax.dot_general(grad_flat, out_weight, CONTRACT_COLS, preferred_element_type=jnp.float32)
        .astype(jnp.bfloat16)
        .reshape(queries.shape)
    )
    grad_out_weight = lax.dot_general(
        context_flat, grad_flat, CONTRACT_ROWS, preferred_element_type=jnp.float32
    )
    probs = jnp.exp(masked_scores(queries, key_rows, lengths) - log_total)
    grad_probs = jnp.einsum(
        "blhd,bmhd->bhlm", grad_context, values, preferred_element_type=jnp.float32
    )
    grad_values = jnp.einsum(
        "bhlm,blhd->bmhd",
        probs.astype(jnp.bfloat16),
        grad_context,
        preferred_element_type=jnp.float32,
    ).astype(jnp.bfloat16)
    grad_scores = (
        probs * (grad_probs - jnp.sum(probs * grad_probs, axis=-1, keepdims=True))
    ).astype(jnp.bfloat16)
    scaling = HEAD_DIM ** (-0.5)
    grad_queries = (
        jnp.einsum("bhlm,bmhd->blhd", grad_scores, key_rows, preferred_element_type=jnp.float32)
        * scaling
    ).astype(jnp.bfloat16)
    grad_keys = (
        jnp.einsum("bhlm,blhd->bmhd", grad_scores, queries, preferred_element_type=jnp.float32)
        * scaling
    ).astype(jnp.bfloat16)
    normed_flat = normed.reshape(-1, features)
    members = [member.reshape(-1, head_cols) for member in (grad_queries, grad_keys, grad_values)]
    grad_weights = jnp.stack(
        [
            lax.dot_general(normed_flat, member, CONTRACT_ROWS, preferred_element_type=jnp.float32)
            for member in members
        ]
    )
    grad_biases = jnp.stack(
        [
            jnp.sum(members[0].astype(jnp.float32), axis=0),
            jnp.sum(members[2].astype(jnp.float32), axis=0),
        ]
    )
    grad_normed = lax.dot_general(
        members[0], weights[0], CONTRACT_COLS, preferred_element_type=jnp.float32
    )
    grad_normed = grad_normed + lax.dot_general(
        members[1], weights[1], CONTRACT_COLS, preferred_element_type=jnp.float32
    )
    grad_normed = grad_normed + lax.dot_general(
        members[2], weights[2], CONTRACT_COLS, preferred_element_type=jnp.float32
    )
    return (grad_normed.reshape(normed.shape), grad_weights, grad_out_weight, grad_biases)


def group_rows(first_rows, second_rows):
    return (
        lax.all_gather(first_rows, "head", axis=0, tiled=True),
        lax.all_gather(second_rows, "head", axis=0, tiled=True),
    )


def per_device_wide(
    short_x,
    long_x,
    short_cot,
    long_cot,
    short_len,
    long_len,
    short_task,
    long_task,
    expert_ids,
    ln_gain,
    ln_bias,
    w_qkv,
    b_qv,
    w_attn_out,
    b_attn_out,
    w_up,
    b_up,
    w_down,
    b_down,
    task_emb,
    gate_w,
):
    heads_here = lax.axis_size("head")
    head_place = lax.axis_index("head")
    experts = lax.axis_size("expert")
    short_group, short_span, features = short_x.shape
    long_group, long_span = (long_x.shape[0], long_x.shape[1])
    short_dev = short_group // heads_here
    long_dev = long_group // heads_here
    hidden_width = w_up.shape[2]
    tasks_total = expert_ids.shape[0]
    cap_short = 2 * short_group // experts
    cap_long = 2 * long_group // experts
    piece_rows = (cap_short * short_span + cap_long * long_span) // heads_here
    short_total = short_group * short_span
    all_rows = short_total + long_group * long_span
    expert_hits = (expert_ids[:, :, None] == jnp.arange(experts, dtype=jnp.int32)).astype(
        jnp.float32
    )
    chosen_cols = jnp.einsum("tke,de->tkd", expert_hits, gate_w, precision=HIGHEST)
    gate_probs = jax.nn.softmax(jnp.sum(task_emb[:, None, :] * chosen_cols, axis=-1), axis=-1)
    short_slots = route_slots(short_task, expert_ids, cap_short, experts)
    long_slots = route_slots(long_task, expert_ids, cap_long, experts)
    offsets = head_place * piece_rows + jnp.arange(piece_rows, dtype=jnp.int32)
    owners = jnp.arange(experts, dtype=jnp.int32)[:, None]
    in_short = jnp.broadcast_to(offsets < cap_short * short_span, (experts, piece_rows))
    short_pos = offsets % short_span
    long_offset = jnp.maximum(offsets - cap_short * short_span, 0)
    long_pos = long_offset % long_span
    short_route = lookup(
        short_slots, owners * cap_short + jnp.minimum(offsets // short_span, cap_short - 1)
    )
    long_route = lookup(
        long_slots, owners * cap_long + jnp.minimum(long_offset // long_span, cap_long - 1)
    )
    short_sent = short_route // 2
    long_sent = long_route // 2
    position = jnp.where(in_short, short_pos, long_pos)
    target = jnp.where(
        in_short,
        short_sent * short_span + short_pos,
        short_total + long_sent * long_span + long_pos,
    )
    task_rows = jnp.where(in_short, lookup(short_task, short_sent), lookup(long_task, long_sent))
    length_rows = jnp.where(in_short, lookup(short_len, short_sent), lookup(long_len, long_sent))
    live_rows = (position < length_rows).astype(jnp.float32)
    gate_index = task_rows * 2 + jnp.where(in_short, short_route % 2, long_route % 2)
    gate_rows = lookup(gate_probs.reshape(-1), gate_index)
    short_mask = (jnp.arange(short_span, dtype=jnp.int32)[None, :] < short_len[:, None]).astype(
        jnp.float32
    )[:, :, None]
    long_mask = (jnp.arange(long_span, dtype=jnp.int32)[None, :] < long_len[:, None]).astype(
        jnp.float32
    )[:, :, None]
    short_start = head_place * short_dev
    long_start = head_place * long_dev
    own_short_mask = lax.dynamic_slice_in_dim(short_mask, short_start, short_dev, 0)
    own_long_mask = lax.dynamic_slice_in_dim(long_mask, long_start, long_dev, 0)
    short_in = short_x.astype(jnp.float32)
    long_in = long_x.astype(jnp.float32)
    own_short_in = lax.dynamic_slice_in_dim(short_in, short_start, short_dev, 0)
    own_long_in = lax.dynamic_slice_in_dim(long_in, long_start, long_dev, 0)
    attn_qkv, attn_qv, attn_out_w = (w_qkv, b_qv, w_attn_out)
    short_src, long_src = (short_in, long_in)
    short_lens, long_lens = (short_len, long_len)
    head_cols = attn_qkv.shape[2]
    head_count = head_cols // HEAD_DIM
    short_normed = layer_norm(short_src, ln_gain[0], ln_bias[0]).astype(jnp.bfloat16)
    long_normed = layer_norm(long_src, ln_gain[0], ln_bias[0]).astype(jnp.bfloat16)
    short_kept = attend(short_normed, short_lens, attn_qkv, attn_qv, head_count)
    long_kept = attend(long_normed, long_lens, attn_qkv, attn_qv, head_count)
    short_part = jnp.dot(
        short_kept[3].reshape(-1, head_cols), attn_out_w, preferred_element_type=jnp.float32
    ).reshape(short_src.shape)
    long_part = jnp.dot(
        long_kept[3].reshape(-1, head_cols), attn_out_w, preferred_element_type=jnp.float32
    ).reshape(long_src.shape)
    short_sum, long_sum = (
        lax.psum(short_part.astype(jnp.bfloat16), "head").astype(jnp.float32),
        lax.psum(long_part.astype(jnp.bfloat16), "head").astype(jnp.float32),
    )
    short_mid = short_in + short_mask * (short_sum + b_attn_out)
    long_mid = long_in + long_mask * (long_sum + b_attn_out)
    short_mixin = layer_norm(short_mid, ln_gain[1], ln_bias[1]).astype(jnp.bfloat16)
    long_mixin = layer_norm(long_mid, ln_gain[1], ln_bias[1]).astype(jnp.bfloat16)
    own_short_mid = lax.dynamic_slice_in_dim(short_mid, short_start, short_dev, 0)
    own_long_mid = lax.dynamic_slice_in_dim(long_mid, long_start, long_dev, 0)
    mixin_rows = jnp.concatenate(
        [short_mixin.reshape(-1, features), long_mixin.reshape(-1, features)], axis=0
    )
    outgoing = mixin_rows[target]
    received = lax.all_to_all(outgoing, "expert", split_axis=0, concat_axis=0, tiled=True)
    inputs = received.reshape(-1, features)
    gelu_in = jnp.dot(inputs, w_up[0], preferred_element_type=jnp.float32) + b_up[0]
    hidden = jax.nn.gelu(gelu_in).astype(jnp.bfloat16)
    output = (jnp.dot(hidden, w_down[0], preferred_element_type=jnp.float32) + b_down[0]).astype(
        jnp.bfloat16
    )
    returned = lax.all_to_all(
        output.reshape(received.shape), "expert", split_axis=0, concat_axis=0, tiled=True
    )
    wide_shape = received.shape[:2] + (hidden_width,)
    packed = (returned, received, hidden.reshape(wide_shape), gelu_in.reshape(wide_shape))
    returned = packed[0]
    received = packed[1]
    contrib = (gate_rows[:, :, None] * returned.astype(jnp.float32)).reshape(-1, features)
    mixed_rows = jnp.zeros((all_rows, features), jnp.float32).at[target.reshape(-1)].add(contrib)
    short_moe, long_moe = (
        lax.psum_scatter(
            mixed_rows[:short_total].reshape(short_in.shape).astype(jnp.bfloat16),
            "head",
            scatter_dimension=0,
            tiled=True,
        ).astype(jnp.float32),
        lax.psum_scatter(
            mixed_rows[short_total:].reshape(long_in.shape).astype(jnp.bfloat16),
            "head",
            scatter_dimension=0,
            tiled=True,
        ).astype(jnp.float32),
    )
    short_out = (own_short_mid + own_short_mask * short_moe).astype(jnp.bfloat16)
    long_out = (own_long_mid + own_long_mask * long_moe).astype(jnp.bfloat16)
    cot_rows = jnp.concatenate(
        [short_cot.reshape(-1, features), long_cot.reshape(-1, features)], axis=0
    )
    cot_picked = cot_rows[target].astype(jnp.float32)
    grad_sent = ((gate_rows * live_rows)[:, :, None] * cot_picked).astype(jnp.bfloat16)
    gate_terms = live_rows * jnp.sum(cot_picked * returned.astype(jnp.float32), axis=-1)
    gate_part = jnp.sum(
        jnp.where(
            gate_index[:, :, None] == jnp.arange(2 * tasks_total, dtype=jnp.int32),
            gate_terms[:, :, None],
            0.0,
        ),
        axis=(0, 1),
    )
    grad_arrived = lax.all_to_all(grad_sent, "expert", split_axis=0, concat_axis=0, tiled=True)
    inputs = received.reshape(-1, features)
    hidden = packed[2].reshape(-1, hidden_width)
    gelu_in = packed[3].reshape(-1, hidden_width)
    grad_output = grad_arrived.reshape(-1, features)
    grad_hidden = lax.dot_general(
        grad_output, w_down[0], CONTRACT_COLS, preferred_element_type=jnp.float32
    )
    grad_gelu = jax.vjp(jax.nn.gelu, gelu_in)[1](grad_hidden)[0].astype(jnp.bfloat16)
    grad_up_w = lax.dot_general(
        inputs, grad_gelu, CONTRACT_ROWS, preferred_element_type=jnp.float32
    )
    grad_up_b = jnp.sum(grad_gelu.astype(jnp.float32), axis=0)
    grad_down_w = lax.dot_general(
        hidden, grad_output, CONTRACT_ROWS, preferred_element_type=jnp.float32
    )
    grad_down_b = jnp.sum(grad_output.astype(jnp.float32), axis=0)
    grad_inputs = (
        lax.dot_general(grad_gelu, w_up[0], CONTRACT_COLS, preferred_element_type=jnp.float32)
        .astype(jnp.bfloat16)
        .reshape(received.shape)
    )
    grad_home = lax.all_to_all(grad_inputs, "expert", split_axis=0, concat_axis=0, tiled=True)
    shard_up_w, shard_up_b, shard_down_w, shard_down_b = (
        lax.psum_scatter(
            grad_up_w[None].astype(jnp.bfloat16), "head", scatter_dimension=2, tiled=True
        ).astype(jnp.float32),
        lax.psum_scatter(
            grad_up_b[None].astype(jnp.bfloat16), "head", scatter_dimension=1, tiled=True
        ).astype(jnp.float32),
        lax.psum_scatter(
            grad_down_w[None].astype(jnp.bfloat16), "head", scatter_dimension=1, tiled=True
        ).astype(jnp.float32),
        lax.psum_scatter(
            grad_down_b[None].astype(jnp.bfloat16), "head", scatter_dimension=1, tiled=True
        ).astype(jnp.float32),
    )
    grad_mixin = (
        jnp.zeros((all_rows, features), jnp.float32)
        .at[target.reshape(-1)]
        .add(grad_home.reshape(-1, features).astype(jnp.float32))
    )
    short_dmix, long_dmix = (
        lax.psum_scatter(
            grad_mixin[:short_total].reshape(short_in.shape).astype(jnp.bfloat16),
            "head",
            scatter_dimension=0,
            tiled=True,
        ).astype(jnp.float32),
        lax.psum_scatter(
            grad_mixin[short_total:].reshape(long_in.shape).astype(jnp.bfloat16),
            "head",
            scatter_dimension=0,
            tiled=True,
        ).astype(jnp.float32),
    )
    short_dmid, short_gain_two, short_shift_two = jax.vjp(
        layer_norm, own_short_mid, ln_gain[1], ln_bias[1]
    )[1](short_dmix)
    long_dmid, long_gain_two, long_shift_two = jax.vjp(
        layer_norm, own_long_mid, ln_gain[1], ln_bias[1]
    )[1](long_dmix)
    short_dmid = short_dmid + lax.dynamic_slice_in_dim(short_cot, short_start, short_dev, 0).astype(
        jnp.float32
    )
    long_dmid = long_dmid + lax.dynamic_slice_in_dim(long_cot, long_start, long_dev, 0).astype(
        jnp.float32
    )
    short_dattn = (own_short_mask * short_dmid).astype(jnp.bfloat16)
    long_dattn = (own_long_mask * long_dmid).astype(jnp.bfloat16)
    bias_out_grad = jnp.sum(short_dattn.astype(jnp.float32), axis=(0, 1)) + jnp.sum(
        long_dattn.astype(jnp.float32), axis=(0, 1)
    )
    attn_short_grad, attn_long_grad = group_rows(short_dattn, long_dattn)
    short_back = attend_back(
        short_normed, short_lens, short_kept, attn_short_grad, attn_qkv, attn_out_w
    )
    long_back = attend_back(long_normed, long_lens, long_kept, attn_long_grad, attn_qkv, attn_out_w)
    short_dnormed, long_dnormed = (
        lax.psum_scatter(
            short_back[0].astype(jnp.bfloat16), "head", scatter_dimension=0, tiled=True
        ).astype(jnp.float32),
        lax.psum_scatter(
            long_back[0].astype(jnp.bfloat16), "head", scatter_dimension=0, tiled=True
        ).astype(jnp.float32),
    )
    short_dln, short_gain_one, short_shift_one = jax.vjp(
        layer_norm, own_short_in, ln_gain[0], ln_bias[0]
    )[1](short_dnormed)
    long_dln, long_gain_one, long_shift_one = jax.vjp(
        layer_norm, own_long_in, ln_gain[0], ln_bias[0]
    )[1](long_dnormed)
    short_dx = short_dmid + short_dln
    long_dx = long_dmid + long_dln
    qkv_terms = short_back[1] + long_back[1]
    out_terms = short_back[2] + long_back[2]
    bias_terms = short_back[3] + long_back[3]
    grad_qkv, grad_attn_weight, grad_qv = (
        lax.psum(qkv_terms.astype(jnp.bfloat16), "expert").astype(jnp.float32),
        lax.psum(out_terms.astype(jnp.bfloat16), "expert").astype(jnp.float32),
        lax.psum(bias_terms.astype(jnp.bfloat16), "expert").astype(jnp.float32),
    )
    gain_grads = jnp.stack([short_gain_one + long_gain_one, short_gain_two + long_gain_two])
    shift_grads = jnp.stack([short_shift_one + long_shift_one, short_shift_two + long_shift_two])
    grad_gain, grad_shift, grad_bias_out, gate_total = lax.psum(
        (gain_grads, shift_grads, bias_out_grad, gate_part), ("expert", "head")
    )
    gate_grad = gate_total.reshape(tasks_total, 2)
    logit_grad = gate_probs * (gate_grad - jnp.sum(gate_probs * gate_grad, axis=-1, keepdims=True))
    grad_task = jnp.sum(logit_grad[:, :, None] * chosen_cols, axis=1)
    grad_gate = jnp.einsum("tke,tk,td->de", expert_hits, logit_grad, task_emb, precision=HIGHEST)
    return (
        short_out,
        long_out,
        short_dx,
        long_dx,
        grad_gain,
        grad_shift,
        grad_qkv,
        grad_qv,
        grad_attn_weight,
        grad_bias_out,
        shard_up_w,
        shard_up_b,
        shard_down_w,
        shard_down_b,
        grad_task,
        grad_gate,
    )


BF16 = jnp.bfloat16
F32 = jnp.float32
SLICE_ROWS = 272
HALF_PACK = 1088
QKV_ROWS = 1536
MISC_ROW = 2048
GRAD_ROWS = 1040


def mm(a, b):
    return lax.dot_general(a, b, (((1,), (0,)), ((), ())), preferred_element_type=F32)


def mm_nt(a, b):
    return lax.dot_general(a, b, (((1,), (1,)), ((), ())), preferred_element_type=F32)


def mm_tn(a, b):
    return lax.dot_general(a, b, (((0,), (0,)), ((), ())), preferred_element_type=F32)


def iota(shape, dim):
    return lax.broadcasted_iota(jnp.int32, shape, dim)


def params(mebibytes):
    return pltpu.CompilerParams(vmem_limit_bytes=mebibytes * 1024 * 1024)


def cost(micros):
    return pl.CostEstimate(flops=0, bytes_accessed=int(micros * 3.7e6), transcendentals=0)


VM = pl.BlockSpec(memory_space=pltpu.VMEM)
SM = pl.BlockSpec(memory_space=pltpu.SMEM)
ANY = pl.BlockSpec(memory_space=pl.ANY)


def pack_kernel(qkv, qv, wo, out):
    core = lax.axis_index("expert") % 2
    feats = qkv.shape[1]
    split = HALF_PACK - 2 * feats

    @pl.when(core == 0)
    def _():
        out[0:feats, :] = qkv[0]
        out[feats : 2 * feats, :] = qkv[1]
        out[2 * feats :, :] = qkv[2, 0:split, :]

    @pl.when(core != 0)
    def _():
        at = feats - split
        out[0:at, :] = qkv[2, split:, :]
        for c in range(4):
            out[at + 128 * c : at + 128 * (c + 1), :] = wo[:, 128 * c : 128 * (c + 1)]
        at += 4 * 128
        out[at:, :] = jnp.zeros((HALF_PACK - at, 128), BF16)
        high = qv[...].astype(BF16)
        low = (qv[...] - high.astype(F32)).astype(BF16)
        out[at : at + 2, :] = high
        out[at + 2 : at + 4, :] = low


def split_cycles(pair_left, pair_right, eye, count):
    step = mm(pair_left.astype(BF16), pair_right.astype(BF16))
    reach = jnp.minimum(eye + step, 1.0)
    hops = 1
    while hops < count // 2:
        wide = reach.astype(BF16)
        reach = jnp.minimum(mm(wide, wide), 1.0)
        hops *= 2
    lanes = iota((count, count), 1).astype(F32)
    lowest = jnp.min(jnp.where(reach > 0.5, lanes, float(count)), axis=1, keepdims=True)
    lowest_row = jnp.sum(eye * lowest, axis=0, keepdims=True)
    other = jnp.sum(pair_left * lowest_row, axis=1, keepdims=True)
    return (lowest > other).astype(F32)


def route_kernel(st_ref, sl_ref, lt_ref, ll_ref, ids_ref, temb_ref, gw_ref, tab_ref, gate_ref):
    here = lax.axis_index("head").astype(jnp.int32)
    group = lax.axis_index("expert").astype(jnp.int32)
    shorts = st_ref.shape[1]
    longs = lt_ref.shape[1]
    tasks = ids_ref.shape[1]
    per_owner = shorts // 4
    mine = here.astype(F32)

    def eye_of(n):
        return (iota((n, n), 0) == iota((n, n), 1)).astype(F32)

    def col(row, eye):
        return jnp.sum(eye * row, axis=1, keepdims=True)

    def row(column, eye):
        return jnp.sum(eye * column, axis=0, keepdims=True)

    eye = eye_of(shorts)
    at_sub, at_lane = iota((shorts, shorts), 0), iota((shorts, shorts), 1)
    off_diag = 1.0 - eye
    task_row = st_ref[...].astype(F32)
    task_col = col(task_row, eye)
    same_task = (task_col == task_row).astype(F32)
    earlier = (at_lane < at_sub).astype(F32)
    later = (at_lane > at_sub).astype(F32)
    rank_col = jnp.sum(same_task * earlier, axis=1, keepdims=True)
    rank_row = jnp.sum(same_task * later, axis=0, keepdims=True)
    first_of_pair = jnp.floor(rank_col * 0.5) == jnp.floor(rank_row * 0.5)
    pair_right = same_task * first_of_pair.astype(F32) * off_diag
    pair_left = ((at_sub // 2) == (at_lane // 2)).astype(F32) * off_diag
    major = split_cycles(pair_left, pair_right, eye, shorts)
    same_major = (major == row(major, eye)).astype(F32)
    pair_right = same_task * same_major * off_diag
    pair_left = ((at_sub // 4) == (at_lane // 4)).astype(F32) * same_major * off_diag
    minor = split_cycles(pair_left, pair_right, eye, shorts)
    colour = 2.0 * major + minor
    same_owner = ((at_sub // per_owner) == (at_lane // per_owner)).astype(F32)
    same_colour = (colour == row(colour, eye)).astype(F32)
    place = jnp.sum(same_owner * same_colour * earlier, axis=1, keepdims=True)

    sent = iota((shorts, 128), 0)
    lane = iota((shorts, 128), 1)
    sent_f = sent.astype(F32)
    lane_f = lane.astype(F32)
    length_col = col(sl_ref[...].astype(F32), eye)
    own = ((task_col == lane_f) & (colour == mine)).astype(F32)
    owner_col = (iota((shorts, 1), 0) // per_owner).astype(F32)

    def put(r, values):
        tab_ref[r : r + 1, :] = values.astype(jnp.int32)

    def put_away(r, values, low):
        tab_ref[r : r + 1, :] = values.astype(jnp.int32) ^ (here * low)

    def total(values):
        return jnp.sum(values, axis=0, keepdims=True)

    tab_ref[...] = jnp.zeros_like(tab_ref)
    put(0, total(own * sent_f))
    put(1, total(own * length_col))
    put_away(2, total(own * (owner_col * 2.0 + place)), 2)
    natural = (sent == lane + here * per_owner) & (lane < per_owner)
    put_away(6, total(natural.astype(F32) * (colour * 2.0 + place)), 2)

    eye_l = eye_of(longs)
    sub_l, lane_l = iota((longs, longs), 0), iota((longs, longs), 1)
    ltask_row = lt_ref[...].astype(F32)
    ltask_col = col(ltask_row, eye_l)
    right_l = (ltask_col == ltask_row).astype(F32) * (1.0 - eye_l)
    left_l = ((sub_l // 2) == (lane_l // 2)).astype(F32) * (1.0 - eye_l)
    kappa = split_cycles(left_l, right_l, eye_l, longs)
    parity_col = ltask_col - 2.0 * jnp.floor(ltask_col * 0.5)
    parity = jnp.max(parity_col, axis=0, keepdims=True)
    lsent = iota((longs, 128), 0)
    llane = iota((longs, 128), 1)
    unit_task = parity + 2.0 * llane.astype(F32)
    mine_l = (here % 2).astype(F32)
    own_l = ((ltask_col == unit_task) & (kappa == mine_l)).astype(F32)
    llen_col = col(ll_ref[...].astype(F32), eye_l)
    put(3, total(own_l * lsent.astype(F32)))
    put_away(16, total(own_l * (lsent // (longs // 4)).astype(F32)), 1)
    put(4, total(own_l * llen_col))
    row_lane = iota((1, 128), 1)
    row_lane_f = row_lane.astype(F32)
    put(5, parity + 2.0 * row_lane_f)
    natural_l = (lsent == llane + here * (longs // 4)) & (llane < longs // 4)
    put_away(7, total(natural_l.astype(F32) * kappa), 1)
    put_away(15, total(natural_l.astype(F32) * (kappa + 2.0)), 1)

    ids = ids_ref[...].astype(F32)
    eye_t = eye_of(tasks)
    e_first, e_second = col(ids[0:1, :], eye_t), col(ids[1:2, :], eye_t)
    tsub = iota((tasks, 128), 0).astype(F32)
    tlane = iota((tasks, 128), 1).astype(F32)
    diag = (tsub == tlane).astype(F32)
    put(8, total(diag * e_first))
    put(9, total(diag * e_second))
    task_first = total((e_first == tlane).astype(F32) * tsub)
    task_second = total((e_second == tlane).astype(F32) * tsub)
    put(10, task_first)
    put(11, task_second)
    first_parity = task_first - 2.0 * jnp.floor(task_first * 0.5)
    use_second = first_parity != parity
    put(12, use_second.astype(F32))
    unit_of = jnp.where(use_second, task_second, task_first)
    put(13, jnp.floor((unit_of - parity) * 0.5))
    half = here // 2
    tab_ref[14:15, :] = jnp.where(row_lane == 0, half, jnp.where(row_lane == 1, here, group))

    logits = lax.dot_general(
        temb_ref[...],
        gw_ref[...],
        (((1,), (1,)), ((), ())),
        preferred_element_type=F32,
        precision=HIGHEST,
    )
    ecols = iota((tasks, logits.shape[1]), 1).astype(F32)
    first = jnp.sum(jnp.where(ecols == e_first, logits, 0.0), axis=1, keepdims=True)
    second = jnp.sum(jnp.where(ecols == e_second, logits, 0.0), axis=1, keepdims=True)
    top = jnp.maximum(first, second)
    first, second = jnp.exp(first - top), jnp.exp(second - top)
    denominator = first + second
    gate_ref[...] = jnp.where(
        tlane == 0.0, first / denominator, jnp.where(tlane == 1.0, second / denominator, 0.0)
    )


def norm_stats(values):
    centred = values - jnp.mean(values, axis=-1, keepdims=True)
    scale = lax.rsqrt(jnp.mean(centred * centred, axis=-1, keepdims=True) + 1e-05)
    return centred * scale, scale


def prep_kernel(
    tab, gates, cs0, cs1, cl, csb, clb, xs, xl, gain, bias,
    deo, cb_s, cb_l, ns, nl, xb_s, xb_l,
):
    e = pl.program_id(0)
    span = cs0.shape[1]
    for k, ref in ((0, cs0), (1, cs1)):
        t = tab[10 + k, e]
        keep = iota((span, 1), 0) < tab[1, t]
        deo[0, span * k : span * (k + 1), :] = jnp.where(
            keep, gates[t, k] * ref[0].astype(F32), 0.0
        ).astype(BF16)
    half_rows = cl.shape[1]
    u = tab[13, e]
    gate = gates[tab[5, u], tab[12, e]]
    keep = iota((half_rows, 1), 0) + half_rows * tab[14, 0] < tab[4, u]
    deo[0, 2 * span : 2 * span + half_rows, :] = jnp.where(keep, gate * cl[0].astype(F32), 0.0).astype(BF16)
    parity = (tab[5, 0] % 2).astype(F32)
    deo[0, 2 * span + half_rows :, :] = jnp.full((16, deo.shape[2]), parity, F32).astype(BF16)
    cb_s[...] = csb[...]
    cb_l[...] = clb[...]
    xb_s[...] = xs[...]
    xb_l[...] = xl[...]
    ns[0] = (norm_stats(xs[0].astype(F32))[0] * gain[0:1, :] + bias[0:1, :]).astype(BF16)
    nl[0] = (norm_stats(xl[0].astype(F32))[0] * gain[0:1, :] + bias[0:1, :]).astype(BF16)


def unpack_weights(low, high, w, wo, bqv):
    for h in range(low.shape[0]):
        cols = slice(128 * h, 128 * (h + 1))
        w[0:HALF_PACK, cols] = low[h]
        w[HALF_PACK:QKV_ROWS, cols] = high[h, 0 : QKV_ROWS - HALF_PACK, :]
        for c in range(4):
            at = QKV_ROWS - HALF_PACK + 128 * c
            wo[128 * h : 128 * (h + 1), 128 * c : 128 * (c + 1)] = high[h, at : at + 128, :]
        at = MISC_ROW - HALF_PACK
        lines = high[h, at : at + 16, :].astype(F32)
        bqv[0:2, cols] = lines[0:2] + lines[2:4]


class Copies:
    def __init__(self, sems):
        self.sems = sems
        self.used = 0
        self.open = []

    def start(self, source, target):
        copy = pltpu.make_async_copy(source, target, self.sems.at[self.used])
        copy.start()
        self.used += 1
        self.open.append(copy)
        return copy

    def finish(self):
        for copy in self.open:
            copy.wait()


def pair_masks():
    lanes = iota((1, 128), 1)
    first = (lanes < HEAD_DIM).astype(BF16)
    return first, (1.0 - first.astype(F32)).astype(BF16)


def both_heads(block, masks):
    return jnp.concatenate([block * masks[0], block * masks[1]], axis=0)


def fold_heads(stacked, keys):
    lanes = iota((1, 128), 1)
    return jnp.where(lanes < HEAD_DIM, stacked[:keys], stacked[keys:])


def softmax_pair(scores, visible, keys):
    parts = []
    for part in (scores[:, :keys], scores[:, keys:]):
        part = jnp.where(visible, part, -1e30)
        shifted = jnp.exp(part - jnp.max(part, axis=-1, keepdims=True))
        parts.append(shifted * (1.0 / jnp.sum(shifted, axis=-1, keepdims=True)))
    return jnp.concatenate(parts, axis=1).astype(BF16)


def short_visible(tab, i, span):
    rows, lanes = iota((128, 128), 0), iota((128, 128), 1)
    limit = jnp.where(iota((1, 128), 1) < span, tab[1, 2 * i], tab[1, 2 * i + 1] + span)
    return ((rows // span) == (lanes // span)) & (lanes < limit)


def attend_short(
    tab, norm_h, x_h, own_h, other_h, gain, bias, bo,
    q_h, k_h, v_h, p_h, ctx_h, mid, send, w_h, wo_h, bqv,
    norm, x, own, other, q_ref, k_ref, v_ref, p_ref, ctx, w, wo, in_sems, out_sems,
):
    core = tab[14, 2] % 2
    fetch, leave = Copies(in_sems), Copies(out_sems)
    pieces = [fetch.start(own_h, own), fetch.start(other_h, other), fetch.start(norm_h, norm)]
    have_x = fetch.start(x_h, x)
    for piece in pieces:
        piece.wait()

    @pl.when(core == 0)
    def _():
        unpack_weights(own, other, w, wo, bqv)

    @pl.when(core != 0)
    def _():
        unpack_weights(other, own, w, wo, bqv)

    leave.start(w, w_h)
    leave.start(wo, wo_h)
    feats = norm.shape[1]
    rows = norm[...]
    q_ref[...] = ((mm(rows, w[0:feats, :]) + bqv[0:1, :]).astype(BF16) * HEAD_DIM ** (-0.5)).astype(BF16)
    leave.start(q_ref, q_h)
    k_ref[...] = mm(rows, w[feats : 2 * feats, :]).astype(BF16)
    leave.start(k_ref, k_h)
    v_ref[...] = (mm(rows, w[2 * feats : 3 * feats, :]) + bqv[1:2, :]).astype(BF16)
    leave.start(v_ref, v_h)
    masks = pair_masks()
    span = send.shape[2]
    pairs = feats // 128
    for i in range(norm.shape[0] // 128):
        visible = short_visible(tab, i, span)
        r = slice(128 * i, 128 * (i + 1))
        for p in range(pairs):
            c = slice(128 * p, 128 * (p + 1))
            scores = mm_nt(q_ref[r, c], both_heads(k_ref[r, c], masks))
            probs = softmax_pair(scores, visible, 128)
            p_ref[i * pairs + p] = probs
            ctx[r, c] = mm(probs, both_heads(v_ref[r, c], masks)).astype(BF16)
        leave.start(p_ref.at[pairs * i : pairs * (i + 1)], p_h.at[pairs * i : pairs * (i + 1)])
    leave.start(ctx, ctx_h)
    attn = mm(ctx[...], wo[...]) + bo[...]
    have_x.wait()
    for t in range(send.shape[0]):
        r = slice(span * t, span * (t + 1))
        keep = iota((span, 1), 0) < tab[1, t]
        middle = x[r, :].astype(F32) + jnp.where(keep, attn[r, :], 0.0)
        mid[r, :] = middle
        mixin = (norm_stats(middle)[0] * gain[1:2, :] + bias[1:2, :]).astype(BF16)
        send[tab[8, t], 0] = mixin
        send[tab[9, t], 1] = mixin
    leave.finish()


def attend_long(
    tab, norm_h, x_h, w_h, wo_h, bqv, gain, bias, bo,
    q_h, k_h, v_h, p_h, ctx_h, mid, send,
    norm, x, w, wo, q_ref, k_ref, v_ref, p_ref, ctx, nq, in_sems, out_sems,
):
    fetch, leave = Copies(in_sems), Copies(out_sems)
    have_norm, have_w = fetch.start(norm_h, norm), fetch.start(w_h, w)
    have_wo, have_x = fetch.start(wo_h, wo), fetch.start(x_h, x)
    feats = norm.shape[1]
    half_rows = send.shape[1]
    span = 2 * half_rows
    units = norm.shape[0] // span
    offset = tab[14, 0] * half_rows
    have_norm.wait()
    for u in range(units):
        at = pl.multiple_of(span * u + offset, half_rows)
        nq[half_rows * u : half_rows * (u + 1), :] = norm[pl.ds(at, half_rows), :]
    rows = norm[...]
    have_w.wait()
    q_ref[...] = ((mm(nq[...], w[0:feats, :]) + bqv[0:1, :]).astype(BF16) * HEAD_DIM ** (-0.5)).astype(BF16)
    leave.start(q_ref, q_h)
    k_ref[...] = mm(rows, w[feats : 2 * feats, :]).astype(BF16)
    leave.start(k_ref, k_h)
    v_ref[...] = (mm(rows, w[2 * feats : 3 * feats, :]) + bqv[1:2, :]).astype(BF16)
    leave.start(v_ref, v_h)
    masks = pair_masks()
    pairs = feats // 128
    for u in range(units):
        visible = iota((1, span), 1) < tab[4, u]
        r = slice(half_rows * u, half_rows * (u + 1))
        kr = slice(span * u, span * (u + 1))
        for p in range(pairs):
            c = slice(128 * p, 128 * (p + 1))
            scores = mm_nt(q_ref[r, c], both_heads(k_ref[kr, c], masks))
            probs = softmax_pair(scores, visible, span)
            p_ref[u * pairs + p] = probs
            ctx[r, c] = mm(probs, both_heads(v_ref[kr, c], masks)).astype(BF16)
        leave.start(p_ref.at[pairs * u : pairs * (u + 1)], p_h.at[pairs * u : pairs * (u + 1)])
    leave.start(ctx, ctx_h)
    have_wo.wait()
    attn = mm(ctx[...], wo[...]) + bo[...]
    have_x.wait()
    for u in range(units):
        r = slice(half_rows * u, half_rows * (u + 1))
        keep = iota((half_rows, 1), 0) + offset < tab[4, u]
        at = pl.multiple_of(span * u + offset, half_rows)
        middle = x[pl.ds(at, half_rows), :].astype(F32) + jnp.where(keep, attn[r, :], 0.0)
        mid[r, :] = middle
        mixin = (norm_stats(middle)[0] * gain[1:2, :] + bias[1:2, :]).astype(BF16)
        t = tab[5, u]
        send[tab[8, t]] = mixin
        send[tab[9, t]] = mixin
    leave.finish()


GELU_A = 0.7978845608028654
GELU_B = 0.044715


def expert_kernel(first, tab, *refs):
    if first:
        x, d, wu, bu, wd, bd, back, dw, ga, xt, dt, ea, da, hs, ps = refs
        prev = None
    else:
        x, d, wu, bu, wd, bd, par, prev, ga_in, back, dw, ga, xt, dt, ea, da, hs, ps = refs
    j = pl.program_id(0)
    feats = x.shape[2]
    rows = x.shape[0] * x.shape[1]
    step = 4 * x.shape[1]

    @pl.when(j == 0)
    def _():
        for g in range(x.shape[0]):
            cols = slice(x.shape[1] * g, x.shape[1] * (g + 1))
            xt[:, cols] = x[g].T
            dt[:, cols] = d[g].T
        ea[...] = jnp.broadcast_to(bd[...], ea.shape)
        da[...] = jnp.zeros_like(da)

    for i in range(rows // step):
        r = slice(step * i, step * (i + 1))
        xr = x[4 * i : 4 * i + 4].reshape(step, feats)
        dr = d[4 * i : 4 * i + 4].reshape(step, feats)
        pre = mm(xr, wu[0]) + bu[...]
        square = pre * pre
        half = 0.5 + 0.5 * jnp.tanh(pre * (GELU_A + (GELU_A * GELU_B) * square))
        hidden = (pre * half).astype(BF16)
        half, square = half.astype(BF16), square.astype(BF16)
        slope = half + hidden * (1.0 - half) * (2.0 * GELU_A + (6.0 * GELU_A * GELU_B) * square)
        dpre = mm_nt(dr, wd[0]).astype(BF16) * slope
        hs[r, :] = hidden
        ps[r, :] = dpre
        ea[r, :] += mm(hidden, wd[0])
        da[r, :] += mm_nt(dpre, wu[0])

    wide = wu.shape[2]
    grad_up = mm(xt[...], ps[...])
    grad_down = mm(dt[...], hs[...]).T
    ones = jnp.ones((16, rows), BF16)
    up_bias = mm(ones, ps[...])[0:1, :]
    down_bias = mm_nt(ones, dt[...])[0:1, :]
    if prev is not None:
        grad_up += prev[0, 0:feats, :].astype(F32)
        grad_down += prev[0, feats : feats + wide, :].astype(F32)
        tail = prev[0, feats + wide :, :].astype(F32)
        up_bias += tail[0:1, :]
        down_bias += tail[1:2, :]
    dw[0, 0:feats, :] = grad_up.astype(BF16)
    dw[0, feats : feats + wide, :] = grad_down.astype(BF16)
    which = iota((16, 1), 0)
    dw[0, feats + wide :, :] = jnp.where(
        which == 0, up_bias, jnp.where(which == 1, down_bias, 0.0)
    ).astype(BF16)

    @pl.when(j == pl.num_programs(0) - 1)
    def _():
        own = tab[14, 2]
        t_first, t_second = tab[10, own], tab[11, own]
        lanes = iota((1, 128), 1)
        as_first = (lanes == 2 * t_first).astype(F32)
        as_second = (lanes == 2 * t_second + 1).astype(F32)
        rows_each = x.shape[1]
        gate_sums = jnp.zeros((1, 128), F32)
        for g in range(x.shape[0]):
            r = slice(rows_each * g, rows_each * (g + 1))
            out = ea[r, :].astype(BF16)
            back[g, 0:rows_each, :] = da[r, :].astype(BF16)
            back[g, rows_each:, :] = out
            prod = out.astype(F32) * d[g].astype(F32)
            if first:
                half_each = rows_each // 2
                gate_sums += as_first * jnp.sum(prod[:half_each], keepdims=True)
                gate_sums += as_second * jnp.sum(prod[half_each:], keepdims=True)
            else:
                odd = par[g, 0:1, 0:128].astype(F32)
                is_first = odd == (t_first % 2).astype(F32)
                gate_sums += jnp.where(is_first, as_first, as_second) * jnp.sum(prod, keepdims=True)
        if not first:
            gate_sums += ga_in[0:1, :]
        ga[...] = jnp.broadcast_to(gate_sums, ga.shape)


def experts_pass(tab, x, deo, part, w_up, b_up, w_down, b_down, prev, ga):
    experts, rows_each, feats = x.shape
    hidden = w_up.shape[2]
    chunk = hidden // 4
    rows = experts * rows_each
    first = prev is None
    in_specs = [
        SM,
        pl.BlockSpec((experts, rows_each, feats), lambda j: (0, 0, 0)),
        pl.BlockSpec((experts, rows_each, feats), lambda j: (0, part, 0)),
        pl.BlockSpec((1, feats, chunk), lambda j: (0, 0, j)),
        pl.BlockSpec((1, chunk), lambda j: (0, j)),
        pl.BlockSpec((1, chunk, feats), lambda j: (0, j, 0)),
        pl.BlockSpec((1, feats), lambda j: (0, 0)),
    ]
    args = [tab, x, deo, w_up, b_up, w_down, b_down]
    if not first:
        in_specs.append(pl.BlockSpec((experts, 16, feats), lambda j: (0, 2 * rows_each // 16, 0)))
        args.append(deo)
        in_specs.append(pl.BlockSpec((1, GRAD_ROWS, feats), lambda j: (j, 0, 0)))
        args.append(prev)
        in_specs.append(pl.BlockSpec((8, 128), lambda j: (0, 0)))
        args.append(ga)
    return pl.pallas_call(
        functools.partial(expert_kernel, first),
        grid=(4,),
        in_specs=in_specs,
        out_specs=[
            pl.BlockSpec((experts, 2 * rows_each, feats), lambda j: (0, 0, 0)),
            pl.BlockSpec((1, GRAD_ROWS, feats), lambda j: (j, 0, 0)),
            pl.BlockSpec((8, 128), lambda j: (0, 0)),
        ],
        out_shape=[
            jax.ShapeDtypeStruct((experts, 2 * rows_each, feats), BF16),
            jax.ShapeDtypeStruct((4, GRAD_ROWS, feats), BF16),
            jax.ShapeDtypeStruct((8, 128), F32),
        ],
        scratch_shapes=[
            pltpu.VMEM((feats, rows), BF16),
            pltpu.VMEM((feats, rows), BF16),
            pltpu.VMEM((rows, feats), F32),
            pltpu.VMEM((rows, feats), F32),
            pltpu.VMEM((rows, chunk), BF16),
            pltpu.VMEM((rows, chunk), BF16),
        ],
        compiler_params=params(56),
        cost_estimate=cost(15),
        name="experts_short" if first else "experts_long",
    )(*args)


def pass_kernel(*refs):
    pass


def after(array, *others):
    return pl.pallas_call(
        pass_kernel,
        in_specs=[ANY] * (1 + len(others)),
        out_specs=ANY,
        out_shape=jax.ShapeDtypeStruct(array.shape, array.dtype),
        input_output_aliases={0: 0},
        compiler_params=params(4),
        cost_estimate=cost(0.1),
        name="after",
    )(array, *others)


def norm_back(grad, unit, scale, gain):
    scaled = grad * gain
    return scale * (
        scaled
        - jnp.mean(scaled, axis=-1, keepdims=True)
        - unit * jnp.mean(scaled * unit, axis=-1, keepdims=True)
    )


def head_pair_back(probs, dctx, q, kk, vv, keys):
    dprobs = mm_nt(dctx, vv)
    dvalues = fold_heads(mm_tn(probs, dctx), keys)
    wide = probs.astype(F32)
    prod = wide * dprobs
    parts = []
    for part in (slice(0, keys), slice(keys, 2 * keys)):
        parts.append(prod[:, part] - wide[:, part] * jnp.sum(prod[:, part], axis=-1, keepdims=True))
    dscores = jnp.concatenate(parts, axis=1).astype(BF16)
    dqueries = mm(dscores, kk) * HEAD_DIM ** (-0.5)
    dkeys = fold_heads(mm_tn(dscores, q), keys)
    return dqueries.astype(BF16), dkeys.astype(BF16), dvalues.astype(BF16)


def row_sum(values):
    return jnp.sum(values, axis=0, keepdims=True)


def back_short(
    tab, gates, gain, *refs
):
    sources, refs = refs[:12], refs[12:]
    zsend, zout, dw_h, small = refs[:4]
    ret, mid, c, wo, ctx, p_ref, q_ref, k_ref, v_ref, norm, w, x = refs[4:16]
    dw, dmid, dattn, dctx, dq, dk, dv, dnorm, in_sems, out_sems = refs[16:]
    fetch, leave = Copies(in_sems), Copies(out_sems)
    have = [fetch.start(a, b) for a, b in zip(sources, refs[4:16])]
    feats = norm.shape[1]
    span = zsend.shape[1]
    sums = [jnp.zeros((1, feats), F32) for _ in range(5)]
    for copy in have[:3]:
        copy.wait()
    for t in range(ret.shape[0]):
        r = slice(span * t, span * (t + 1))
        keep = iota((span, 1), 0) < tab[1, t]
        back_0, back_1 = ret.at[tab[8, t]], ret.at[tab[9, t]]
        mixed = gates[t, 0] * back_0[2 * span : 3 * span, :].astype(F32)
        mixed += gates[t, 1] * back_1[3 * span : 4 * span, :].astype(F32)
        zout[tab[2, t]] = (mid[r, :] + jnp.where(keep, mixed, 0.0)).astype(BF16)
        dmix = back_0[0:span, :].astype(F32) + back_1[span : 2 * span, :].astype(F32)
        unit, scale = norm_stats(mid[r, :])
        sums[2] += row_sum(dmix * unit)
        sums[3] += row_sum(dmix)
        middle = c[r, :].astype(F32) + norm_back(dmix, unit, scale, gain[1:2, :])
        dmid[r, :] = middle
        masked = jnp.where(keep, middle, 0.0)
        sums[4] += row_sum(masked)
        dattn[r, :] = masked.astype(BF16)
    for copy in have[3:5]:
        copy.wait()
    dctx[...] = mm_nt(dattn[...], wo[...]).astype(BF16)
    dw[3 * feats : 4 * feats, :] = mm_tn(ctx[...], dattn[...]).astype(BF16)
    leave.start(dw.at[3 * feats : 4 * feats], dw_h.at[3 * feats : 4 * feats])
    masks = pair_masks()
    for copy in have[5:9]:
        copy.wait()
    for i in range(norm.shape[0] // 128):
        r = slice(128 * i, 128 * (i + 1))
        for p in range(feats // 128):
            c_ = slice(128 * p, 128 * (p + 1))
            a, b, d = head_pair_back(
                p_ref[i * (feats // 128) + p],
                dctx[r, c_],
                q_ref[r, c_],
                both_heads(k_ref[r, c_], masks),
                both_heads(v_ref[r, c_], masks),
                128,
            )
            dq[r, c_] = a
            dk[r, c_] = b
            dv[r, c_] = d
    for copy in have[9:]:
        copy.wait()
    rows = norm[...]
    for index, ref in enumerate((dq, dk, dv)):
        dw[feats * index : feats * (index + 1), :] = mm_tn(rows, ref[...]).astype(BF16)
    leave.start(dw.at[0 : 3 * feats], dw_h.at[0 : 3 * feats])
    dnorm[...] = (
        mm_nt(dq[...], w[0:feats, :])
        + mm_nt(dk[...], w[feats : 2 * feats, :])
        + mm_nt(dv[...], w[2 * feats : 3 * feats, :])
    )
    for t in range(ret.shape[0]):
        r = slice(span * t, span * (t + 1))
        unit, scale = norm_stats(x[r, :].astype(F32))
        grad = dnorm[r, :]
        sums[0] += row_sum(grad * unit)
        sums[1] += row_sum(grad)
        zsend[tab[2, t]] = (dmid[r, :] + norm_back(grad, unit, scale, gain[0:1, :])).astype(BF16)
    sums.append(row_sum(dq[...].astype(F32)))
    sums.append(row_sum(dv[...].astype(F32)))
    for index, value in enumerate(sums):
        small[index : index + 1, :] = value
    small[7:8, :] = jnp.zeros((1, feats), F32)
    leave.finish()


def back_long(
    tab, gates, gain, small_in, ga, *refs
):
    sources, refs = refs[:15], refs[15:]
    z_refs, packed_h = refs[:4], refs[4]
    ret, mid, c, norm, wo, ctx, p_ref, q_ref, k_ref, v_ref, dw_in, w, x, z_short, zout_short = refs[5:20]
    packed, zsend, zout, nq, dmid, dattn, dctx, dq, dk, dv, dnorm, full, in_sems, out_sems = refs[20:]
    fetch, leave = Copies(in_sems), Copies(out_sems)
    have = [fetch.start(a, b) for a, b in zip(sources, refs[5:20])]
    feats = norm.shape[1]
    half_rows = ret.shape[1] // 2
    span = 2 * half_rows
    units = norm.shape[0] // span
    offset = tab[14, 0] * half_rows
    sums = [small_in[index : index + 1, :] for index in range(7)]
    for copy in have[:4]:
        copy.wait()
    for u in range(units):
        r = slice(half_rows * u, half_rows * (u + 1))
        t = tab[5, u]
        at = pl.multiple_of(span * u + offset, half_rows)
        nq[r, :] = norm[pl.ds(at, half_rows), :]
        keep = iota((half_rows, 1), 0) + offset < tab[4, u]
        back_0, back_1 = ret.at[tab[8, t]], ret.at[tab[9, t]]
        mixed = gates[t, 0] * back_0[half_rows:, :].astype(F32) + gates[t, 1] * back_1[half_rows:, :].astype(F32)
        zout[tab[16, u]] = (mid[r, :] + jnp.where(keep, mixed, 0.0)).astype(BF16)
        dmix = back_0[0:half_rows, :].astype(F32) + back_1[0:half_rows, :].astype(F32)
        unit, scale = norm_stats(mid[r, :])
        sums[2] += row_sum(dmix * unit)
        sums[3] += row_sum(dmix)
        middle = c[r, :].astype(F32) + norm_back(dmix, unit, scale, gain[1:2, :])
        dmid[r, :] = middle
        masked = jnp.where(keep, middle, 0.0)
        sums[4] += row_sum(masked)
        dattn[r, :] = masked.astype(BF16)
    for copy in have[4:6]:
        copy.wait()
    dctx[...] = mm_nt(dattn[...], wo[...]).astype(BF16)
    for copy in have[6:11]:
        copy.wait()
    grad_out = mm_tn(ctx[...], dattn[...]) + dw_in[3 * feats : 4 * feats, :].astype(F32)
    shards = packed.shape[1]
    for h in range(shards):
        for s in range(4):
            full[QKV_ROWS + 128 * s : QKV_ROWS + 128 * (s + 1), 128 * h : 128 * (h + 1)] = grad_out[
                128 * h : 128 * (h + 1), 128 * s : 128 * (s + 1)
            ]
    masks = pair_masks()
    for u in range(units):
        r = slice(half_rows * u, half_rows * (u + 1))
        kr = slice(span * u, span * (u + 1))
        for p in range(feats // 128):
            c_ = slice(128 * p, 128 * (p + 1))
            a, b, d = head_pair_back(
                p_ref[u * (feats // 128) + p],
                dctx[r, c_],
                q_ref[r, c_],
                both_heads(k_ref[kr, c_], masks),
                both_heads(v_ref[kr, c_], masks),
                span,
            )
            dq[r, c_] = a
            dk[kr, c_] = b
            dv[kr, c_] = d
    for index, (left, right) in enumerate(((nq, dq), (norm, dk), (norm, dv))):
        r = slice(feats * index, feats * (index + 1))
        full[r, :] = mm_tn(left[...], right[...]) + dw_in[r, :].astype(F32)
    shift = tab[14, 1]
    early = MISC_ROW // SLICE_ROWS
    for g in range(early):
        for h in range(shards):
            packed[g, shift ^ h] = full[
                SLICE_ROWS * g : SLICE_ROWS * (g + 1), 128 * h : 128 * (h + 1)
            ].astype(BF16)
    leave.start(packed.at[0:early], packed_h.at[0:early])
    for copy in have[11:]:
        copy.wait()
    dnorm[...] = mm_nt(dk[...], w[feats : 2 * feats, :]) + mm_nt(dv[...], w[2 * feats : 3 * feats, :])
    from_q = mm_nt(dq[...], w[0:feats, :])
    for u in range(units):
        at = pl.multiple_of(span * u + offset, half_rows)
        dnorm[pl.ds(at, half_rows), :] += from_q[half_rows * u : half_rows * (u + 1), :]
    for u in range(units):
        owner = tab[16, u]
        for s in range(2):
            r = slice(span * u + half_rows * s, span * u + half_rows * (s + 1))
            unit, scale = norm_stats(x[r, :].astype(F32))
            grad = dnorm[r, :]
            sums[0] += row_sum(grad * unit)
            sums[1] += row_sum(grad)
            own_half = tab[14, 0] == s
            direct = jnp.where(own_half, dmid[half_rows * u : half_rows * (u + 1), :], 0.0)
            zsend[owner, half_rows * s : half_rows * (s + 1), :] = (
                direct + norm_back(grad, unit, scale, gain[0:1, :])
            ).astype(BF16)
    shorts = 2 * z_short.shape[1]
    for d, ref in enumerate(z_refs):
        ref[0, 0:shorts, :] = zout_short[2 * d : 2 * d + 2].reshape(shorts, feats)
        at = shorts + half_rows
        ref[0, shorts:at, :] = zout[d]
        ref[0, at : at + shorts, :] = z_short[2 * d : 2 * d + 2].reshape(shorts, feats)
        ref[0, at + shorts :, :] = zsend[d]
    sums[5] += row_sum(dq[...].astype(F32))
    sums[6] += row_sum(dv[...].astype(F32))
    full[MISC_ROW:, :] = jnp.zeros((full.shape[0] - MISC_ROW, feats), F32)
    full[MISC_ROW : MISC_ROW + 1, :] = sums[5]
    full[MISC_ROW + 1 : MISC_ROW + 2, :] = sums[6]
    for index in range(5):
        for s in range(4):
            at = MISC_ROW + 2 + 4 * index + s
            piece = sums[index][:, 128 * s : 128 * (s + 1)]
            full[at : at + 1, :] = jnp.concatenate([piece] * shards, axis=1)
    for s in range(shards):
        full[MISC_ROW + 22 : MISC_ROW + 23, 128 * s : 128 * (s + 1)] = ga[0:1, :]
    for g in range(early, packed.shape[0]):
        for h in range(shards):
            packed[g, shift ^ h] = full[
                SLICE_ROWS * g : SLICE_ROWS * (g + 1), 128 * h : 128 * (h + 1)
            ].astype(BF16)
    leave.start(packed.at[early:], packed_h.at[early:])
    leave.finish()


def each_distance(index, refs, act):
    for d, ref in enumerate(refs):

        @pl.when(index == d)
        def _(ref=ref):
            act(ref)


def place_kernel(tab, a0, a1, a2, a3, _0, _1, short_out, long_out, short_dx, long_dx):
    parts = (a0, a1, a2, a3)
    span = short_out.shape[1]
    half = long_out.shape[1] // 2
    dx_at = 2 * span + half
    for n in range(short_out.shape[0]):
        slot = tab[6, n]
        at = pl.multiple_of((slot % 2) * span, span)

        def copy_short(ref, n=n, at=at):
            short_out[n] = ref[0, pl.ds(at, span), :]
            short_dx[n] = ref[0, pl.ds(pl.multiple_of(dx_at + at, span), span), :].astype(F32)

        each_distance(slot // 2, parts, copy_short)
    dx_at += 2 * span
    for n in range(long_out.shape[0]):

        def first(ref, n=n):
            long_out[n, 0:half, :] = ref[0, 2 * span : 2 * span + half, :]
            long_dx[n] = ref[0, dx_at:, :].astype(F32)

        def second(ref, n=n):
            long_out[n, half:, :] = ref[0, 2 * span : 2 * span + half, :]
            long_dx[n] += ref[0, dx_at:, :].astype(F32)

        each_distance(tab[7, n], parts, first)
        each_distance(tab[15, n], parts, second)


def finish_kernel(
    g, ids, gates, temb, gw_t, qkv, qv, wo, gain, shift, bo, grad_temb, grad_gw_t
):
    feats = wo.shape[1]
    for j in range(3):
        qkv[j] = g[feats * j : feats * (j + 1), :].astype(F32)
    for c in range(4):
        at = QKV_ROWS + 128 * c
        wo[:, 128 * c : 128 * (c + 1)] = g[at : at + 128, :].astype(F32)
    misc = g[MISC_ROW : MISC_ROW + 32, :].astype(F32)
    qv[...] = misc[0:2, :]

    def line(index):
        at = 2 + 4 * index
        return jnp.concatenate([misc[at + s : at + s + 1, :] for s in range(4)], axis=1)

    gain[0:1, :], gain[1:2, :] = line(0), line(2)
    shift[0:1, :], shift[1:2, :] = line(1), line(3)
    bo[...] = line(4)
    terms = misc[22:23, :]
    tasks = temb.shape[0]
    sub, lane = iota((tasks, 128), 0), iota((tasks, 128), 1)
    first = jnp.sum(jnp.where(lane == 2 * sub, terms, 0.0), axis=1, keepdims=True)
    second = jnp.sum(jnp.where(lane == 2 * sub + 1, terms, 0.0), axis=1, keepdims=True)
    both = first + second
    first = first - gates[:, 0:1] * both
    second = second - gates[:, 1:2] * both
    experts = gw_t.shape[0]
    rows = iota((experts, tasks), 0)
    eye = (iota((tasks, tasks), 0) == iota((tasks, tasks), 1)).astype(F32)
    spread = jnp.zeros((experts, tasks), F32)
    for k, value in ((0, first), (1, second)):
        as_row = jnp.sum(eye * value, axis=0, keepdims=True)
        spread += jnp.where(rows == ids[k : k + 1, :], as_row, 0.0)
    grad_gw_t[...] = lax.dot_general(
        spread, temb[...], (((1,), (0,)), ((), ())), preferred_element_type=F32, precision=HIGHEST
    )
    grad_temb[...] = lax.dot_general(
        spread.T, gw_t[...], (((1,), (0,)), ((), ())), preferred_element_type=F32, precision=HIGHEST
    )


def finish_experts(tab, shard, up, up_b, down, down_b):
    feats = up.shape[1]
    up[0] = shard[0, 0:feats, :].astype(F32)
    down[0] = shard[0, feats : 2 * feats, :].astype(F32)
    tail = shard[0, 2 * feats :, :].astype(F32)
    up_b[...] = tail[0:1, :]
    down_b[...] = jnp.zeros_like(down_b)
    for h in range(feats // 128):

        @pl.when(tab[14, 1] == h)
        def _(h=h):
            down_b[...] = tail[1:2, 128 * h : 128 * (h + 1)]


def collect_kernel(arrived, near, far):
    for d in range(arrived.shape[1]):
        terms = arrived[0, d].astype(F32)
        for g in range(1, arrived.shape[0]):
            terms += arrived[g, d].astype(F32)
        if d < 2:
            near[d] = terms.astype(BF16)
        else:
            far[d - 2] = terms.astype(BF16)


def shape_of(shape, dtype):
    return jax.ShapeDtypeStruct(shape, dtype)


def balanced(short_x, long_x, expert_ids):
    heads = lax.axis_size("head")
    tasks = expert_ids.shape[0]
    return (
        heads == 4
        and lax.axis_size("expert") == tasks == 8
        and short_x.shape[0] == 4 * tasks
        and long_x.shape[0] == tasks
        and short_x.shape[1:] == (64, 512)
        and long_x.shape[1:] == (256, 512)
    )


def per_device(
    short_x,
    long_x,
    short_cot,
    long_cot,
    short_len,
    long_len,
    short_task,
    long_task,
    expert_ids,
    ln_gain,
    ln_bias,
    w_qkv,
    b_qv,
    w_attn_out,
    b_attn_out,
    w_up,
    b_up,
    w_down,
    b_down,
    task_emb,
    gate_w,
):
    if not balanced(short_x, long_x, expert_ids):
        return per_device_wide(
            short_x, long_x, short_cot, long_cot, short_len, long_len, short_task, long_task,
            expert_ids, ln_gain, ln_bias, w_qkv, b_qv, w_attn_out, b_attn_out, w_up, b_up,
            w_down, b_down, task_emb, gate_w,
        )
    heads = lax.axis_size("head")
    experts = lax.axis_size("expert")
    span, feats = short_x.shape[1:]
    long_span = long_x.shape[1]
    half_rows = long_span // 2
    tasks = expert_ids.shape[0]
    units = long_x.shape[0] // 2
    rows_s = tasks * span
    rows_q = units * half_rows
    rows_l = units * long_span
    pairs = feats // 128

    own_half = pl.pallas_call(
        pack_kernel,
        in_specs=[VM] * 3,
        out_specs=VM,
        out_shape=shape_of((HALF_PACK, 128), BF16),
        compiler_params=params(56),
        cost_estimate=cost(2),
        name="pack",
    )(w_qkv, b_qv, w_attn_out)
    raw_own = lax.all_gather(own_half, "head", axis=0)
    raw_other = lax.ppermute(raw_own, "expert", [(i, i ^ 1) for i in range(experts)])

    tab, gates = pl.pallas_call(
        route_kernel,
        in_specs=[VM] * 7,
        out_specs=[VM, VM],
        out_shape=[shape_of((24, 128), jnp.int32), shape_of((tasks, 128), F32)],
        compiler_params=params(56),
        cost_estimate=cost(4),
        name="route",
    )(
        short_task.reshape(1, -1),
        short_len.reshape(1, -1),
        long_task.reshape(1, -1),
        long_len.reshape(1, -1),
        expert_ids.T,
        task_emb,
        gate_w.T,
    )

    def blk(n, index):
        return pl.BlockSpec((1, n, feats), index)

    deo, cot_s, cot_l, norm_s, norm_l, own_s, own_l = pl.pallas_call(
        prep_kernel,
        grid_spec=pltpu.PrefetchScalarGridSpec(
            num_scalar_prefetch=1,
            grid=(8,),
            in_specs=[
                SM,
                blk(span, lambda e, tab: (tab[0, tab[10, e]], 0, 0)),
                blk(span, lambda e, tab: (tab[0, tab[11, e]], 0, 0)),
                blk(half_rows, lambda e, tab: (tab[3, tab[13, e]], tab[14, 0], 0)),
                blk(span, lambda e, tab: (tab[0, e], 0, 0)),
                blk(span, lambda e, tab: (tab[3, e // 2], tab[14, 0] * 2 + e % 2, 0)),
                blk(span, lambda e, tab: (tab[0, e], 0, 0)),
                blk(half_rows, lambda e, tab: (tab[3, e // 2], e % 2, 0)),
                pl.BlockSpec((2, feats), lambda e, tab: (0, 0)),
                pl.BlockSpec((2, feats), lambda e, tab: (0, 0)),
            ],
            out_specs=[
                blk(2 * span + half_rows + 16, lambda e, tab: (e, 0, 0)),
                blk(span, lambda e, tab: (e, 0, 0)),
                blk(span, lambda e, tab: (e, 0, 0)),
                blk(span, lambda e, tab: (e, 0, 0)),
                blk(half_rows, lambda e, tab: (e, 0, 0)),
                blk(span, lambda e, tab: (e, 0, 0)),
                blk(half_rows, lambda e, tab: (e, 0, 0)),
            ],
        ),
        out_shape=[
            shape_of((experts, 2 * span + half_rows + 16, feats), BF16),
            shape_of((8, span, feats), BF16),
            shape_of((8, span, feats), BF16),
            shape_of((8, span, feats), BF16),
            shape_of((8, half_rows, feats), BF16),
            shape_of((8, span, feats), BF16),
            shape_of((8, half_rows, feats), BF16),
        ],
        compiler_params=params(56),
        cost_estimate=cost(9),
        name="prep",
    )(tab, gates, short_cot, short_cot, long_cot, short_cot, long_cot, short_x, long_x, ln_gain, ln_bias)
    cot_s, norm_s, own_s = (a.reshape(rows_s, feats) for a in (cot_s, norm_s, own_s))
    cot_l = cot_l.reshape(rows_q, feats)
    norm_l, own_l = norm_l.reshape(rows_l, feats), own_l.reshape(rows_l, feats)
    deo = lax.all_to_all(deo, "expert", split_axis=0, concat_axis=0, tiled=True)

    bias_out = b_attn_out.reshape(1, feats)
    w_shapes = [
        shape_of((QKV_ROWS, feats), BF16),
        shape_of((feats, feats), BF16),
        shape_of((8, feats), F32),
    ]

    def vmem(shape, dtype=BF16):
        return pltpu.VMEM(shape, dtype)

    def sems(count):
        return pltpu.SemaphoreType.DMA((count,))

    def attention(kernel, operands, far, key_rows, query_rows, keys, send_shape, more, scratch, counts, name):
        kept = [
            shape_of((query_rows, feats), BF16),
            shape_of((key_rows, feats), BF16),
            shape_of((key_rows, feats), BF16),
            shape_of((4 * pairs, 128, 2 * keys), BF16),
            shape_of((query_rows, feats), BF16),
        ]
        return pl.pallas_call(
            kernel,
            in_specs=[SM] + [ANY] * far + [VM] * (len(operands) - far - 1),
            out_specs=[ANY] * 5 + [VM] * 2 + ([ANY] * 2 + [VM] if more else []),
            out_shape=kept + [shape_of((query_rows, feats), F32), shape_of(send_shape, BF16)] + more,
            scratch_shapes=[vmem(a.shape) for a in operands[1 : far + 1]]
            + [vmem(a.shape) for a in kept]
            + scratch
            + [sems(count) for count in counts],
            compiler_params=params(56),
            cost_estimate=cost(10),
            name=name,
        )(*operands)

    q_s, k_s, v_s, p_s, ctx_s, mid_s, send_s, w_all, wo_all, bqv_all = attention(
        attend_short,
        (tab, norm_s, own_s, raw_own, raw_other, ln_gain, ln_bias, bias_out),
        4, rows_s, rows_s, 128, (experts, 2, span, feats), w_shapes,
        [vmem((QKV_ROWS, feats)), vmem((feats, feats))], (4, 10), "attend_short",
    )
    send_s = send_s.reshape(experts, 2 * span, feats)
    recv_s = lax.all_to_all(send_s, "expert", split_axis=0, concat_axis=0, tiled=True)
    q_l, k_l, v_l, p_l, ctx_l, mid_l, send_l = attention(
        attend_long,
        (tab, norm_l, own_l, w_all, wo_all, bqv_all, ln_gain, ln_bias, bias_out),
        4, rows_l, rows_q, long_span, (experts, half_rows, feats), [],
        [vmem((rows_q, feats))], (4, 8), "attend_long",
    )
    recv_l = lax.all_to_all(send_l, "expert", split_axis=0, concat_axis=0, tiled=True)

    ret_s, dw_s, ga_s = experts_pass(tab, recv_s, deo, 0, w_up, b_up, w_down, b_down, None, None)
    ret_s = lax.all_to_all(ret_s, "expert", split_axis=0, concat_axis=0, tiled=True)
    ret_l, dw_l, ga_l = experts_pass(tab, recv_l, deo, 1, w_up, b_up, w_down, b_down, dw_s, ga_s)
    ret_l = lax.all_to_all(ret_l, "expert", split_axis=0, concat_axis=0, tiled=True)
    dw_l = after(dw_l, ret_s)
    expert_grads = lax.psum_scatter(dw_l, "head", scatter_dimension=0, tiled=True)

    def over_head(blocks):
        return [blocks[0]] + [
            lax.ppermute(blocks[d], "head", [(i, i ^ d) for i in range(heads)]) for d in range(1, heads)
        ]

    far = (ret_s, mid_s, cot_s, wo_all, ctx_s, p_s, q_s, k_s, v_s, norm_s, w_all, own_s)
    zsend_s, zout_s, dw_attn, small = pl.pallas_call(
        back_short,
        in_specs=[SM, SM, VM] + [ANY] * len(far),
        out_specs=[VM, VM, ANY, VM],
        out_shape=[
            shape_of((2 * heads, span, feats), BF16),
            shape_of((2 * heads, span, feats), BF16),
            shape_of((4 * feats, feats), BF16),
            shape_of((8, feats), F32),
        ],
        scratch_shapes=[vmem(a.shape, a.dtype) for a in far]
        + [vmem((4 * feats, feats)), vmem((rows_s, feats), F32)]
        + [vmem((rows_s, feats))] * 5
        + [vmem((rows_s, feats), F32), sems(len(far)), sems(2)],
        compiler_params=params(56),
        cost_estimate=cost(12),
        name="back_short",
    )(tab, gates, ln_gain, *far)
    far = (
        ret_l, mid_l, cot_l, norm_l, wo_all, ctx_l, p_l, q_l, k_l, v_l, dw_attn, w_all, own_l, zsend_s,
        zout_s,
    )
    rows_z = 4 * span + half_rows + long_span
    *zsend, packed = pl.pallas_call(
        back_long,
        in_specs=[SM, SM, VM, VM, VM] + [ANY] * len(far),
        out_specs=[VM] * heads + [ANY],
        out_shape=[shape_of((1, rows_z, feats), BF16)] * heads
        + [shape_of((experts, heads, SLICE_ROWS, 128), BF16)],
        scratch_shapes=[vmem(a.shape, a.dtype) for a in far]
        + [
            vmem((experts, heads, SLICE_ROWS, 128)),
            vmem((heads, long_span, feats)),
            vmem((heads, half_rows, feats)),
            vmem((rows_q, feats)),
            vmem((rows_q, feats), F32),
            vmem((rows_q, feats)),
            vmem((rows_q, feats)),
            vmem((rows_q, feats)),
            vmem((rows_l, feats)),
            vmem((rows_l, feats)),
            vmem((rows_l, feats), F32),
            vmem((experts * SLICE_ROWS, feats), F32),
            sems(len(far)),
            sems(2),
        ],
        compiler_params=params(56),
        cost_estimate=cost(17),
        name="back_long",
    )(tab, gates, ln_gain, small, ga_l, *far)
    home = over_head(zsend)
    arrived = lax.all_to_all(packed, "expert", split_axis=0, concat_axis=0, tiled=True)
    near, far = pl.pallas_call(
        collect_kernel,
        in_specs=[VM],
        out_specs=[VM] * 2,
        out_shape=[shape_of((2, SLICE_ROWS, 128), BF16)] * 2,
        compiler_params=params(56),
        cost_estimate=cost(0.1),
        name="collect",
    )(arrived)
    near = near.astype(F32) + lax.ppermute(far, "head", [(i, i ^ 2) for i in range(heads)]).astype(F32)
    other = lax.ppermute(near[1].astype(BF16), "head", [(i, i ^ 1) for i in range(heads)])
    terms = (near[0] + other.astype(F32)).astype(BF16)
    attn_grads = lax.all_gather(terms, "expert", axis=0, tiled=True)
    chunk = w_up.shape[2] // 4
    grad_up, grad_up_b, grad_down, grad_down_b = pl.pallas_call(
        finish_experts,
        in_specs=[SM, VM],
        out_specs=[VM] * 4,
        out_shape=[
            shape_of((1, feats, chunk), F32),
            shape_of((1, chunk), F32),
            shape_of((1, chunk, feats), F32),
            shape_of((1, feats // heads), F32),
        ],
        compiler_params=params(56),
        cost_estimate=cost(0.1),
        name="finish_experts",
    )(tab, expert_grads)
    grad_qkv, grad_qv, grad_wo, grad_gain, grad_shift, grad_bo, grad_task, grad_gate = pl.pallas_call(
        finish_kernel,
        in_specs=[VM] * 5,
        out_specs=[VM] * 8,
        out_shape=[
            shape_of((3, feats, 128), F32),
            shape_of((2, 128), F32),
            shape_of((128, feats), F32),
            shape_of((2, feats), F32),
            shape_of((2, feats), F32),
            shape_of((1, feats), F32),
            shape_of((tasks, feats), F32),
            shape_of((experts, feats), F32),
        ],
        compiler_params=params(56),
        cost_estimate=cost(0.1),
        name="finish",
    )(attn_grads, expert_ids.T, gates, task_emb, gate_w.T)
    short_out, long_out, short_dx, long_dx = pl.pallas_call(
        place_kernel,
        in_specs=[SM] + [VM] * heads + [ANY] * 2,
        out_specs=[VM] * 4,
        out_shape=[
            shape_of((8, span, feats), BF16),
            shape_of((2, long_span, feats), BF16),
            shape_of((8, span, feats), F32),
            shape_of((2, long_span, feats), F32),
        ],
        compiler_params=params(56),
        cost_estimate=cost(0.1),
        name="place",
    )(tab, *home, grad_bo, grad_down_b)

    return (
        short_out,
        long_out,
        short_dx,
        long_dx,
        grad_gain,
        grad_shift,
        grad_qkv,
        grad_qv,
        grad_wo,
        grad_bo.reshape(feats),
        grad_up,
        grad_up_b,
        grad_down,
        grad_down_b,
        grad_task,
        grad_gate.T,
    )


def solution(mesh):
    return jax.shard_map(
        per_device,
        mesh=mesh,
        in_specs=(
            P("expert", None, None),
            P("expert", None, None),
            P("expert", None, None),
            P("expert", None, None),
            P("expert"),
            P("expert"),
            P("expert"),
            P("expert"),
            P(),
            P(),
            P(),
            P(None, None, "head"),
            P(None, "head"),
            P("head", None),
            P(),
            P("expert", None, None),
            P("expert", None),
            P("expert", None, None),
            P("expert", None),
            P(),
            P(),
        ),
        out_specs=(
            P(("expert", "head"), None, None),
            P(("expert", "head"), None, None),
            P(("expert", "head"), None, None),
            P(("expert", "head"), None, None),
            P(),
            P(),
            P(None, None, "head"),
            P(None, "head"),
            P("head", None),
            P(),
            P("expert", None, "head"),
            P("expert", "head"),
            P("expert", "head", None),
            P("expert", "head"),
            P(),
            P(),
        ),
        check_vma=False,
    )
```

```python
import functools

import jax
import jax.numpy as jnp
from jax import lax
from jax.experimental import pallas as pl
from jax.experimental.pallas import tpu as pltpu
from jax.sharding import PartitionSpec as P

HEAD_DIM = 64


HIGHEST = lax.Precision.HIGHEST
CONTRACT_ROWS = (((0,), (0,)), ((), ()))
CONTRACT_COLS = (((1,), (1,)), ((), ()))


def layer_norm(values, gain, shift):
    centred = values - jnp.mean(values, axis=-1, keepdims=True)
    spread = jnp.mean(centred * centred, axis=-1, keepdims=True)
    return centred * lax.rsqrt(spread + 1e-05) * gain + shift


def lookup(table, index):
    hits = index[..., None] == jnp.arange(table.shape[0], dtype=jnp.int32)
    return jnp.sum(jnp.where(hits, table, jnp.zeros((), table.dtype)), axis=-1)


def route_slots(tasks, expert_ids, capacity, experts):
    task_hits = tasks[:, None] == jnp.arange(expert_ids.shape[0], dtype=jnp.int32)
    chosen = jnp.sum(jnp.where(task_hits[:, :, None], expert_ids[None, :, :], 0), axis=1).reshape(
        -1
    )
    routes = chosen.shape[0]
    owner_hits = (chosen[:, None] == jnp.arange(experts, dtype=jnp.int32)).astype(jnp.int32)
    earlier = jnp.cumsum(owner_hits, axis=0) - owner_hits
    ranking = jnp.sum(earlier * owner_hits, axis=1)
    slot_key = chosen * capacity + ranking
    slot_hits = slot_key[:, None] == jnp.arange(experts * capacity, dtype=jnp.int32)
    return jnp.sum(jnp.where(slot_hits, jnp.arange(routes, dtype=jnp.int32)[:, None], 0), axis=0)


def masked_scores(queries, key_rows, lengths):
    positions = key_rows.shape[1]
    scores = jnp.einsum(
        "blhd,bmhd->bhlm", queries, key_rows, preferred_element_type=jnp.float32
    ) * HEAD_DIM ** (-0.5)
    visible = (
        jnp.arange(positions, dtype=jnp.int32)[None, None, None, :] < lengths[:, None, None, None]
    )
    return jnp.where(visible, scores, -1e30)


def attend(normed, lengths, weights, biases, head_count):
    sentences, positions, features = normed.shape
    flattened = normed.reshape(-1, features)
    shape_heads = (sentences, positions, head_count, HEAD_DIM)

    def project(index, offset):
        return (
            (jnp.dot(flattened, weights[index], preferred_element_type=jnp.float32) + offset)
            .astype(jnp.bfloat16)
            .reshape(shape_heads)
        )

    queries = project(0, biases[0])
    key_rows = project(1, 0.0)
    values = project(2, biases[1])
    scores = masked_scores(queries, key_rows, lengths)
    highest = jnp.max(scores, axis=-1, keepdims=True)
    shifted = jnp.exp(scores - highest)
    totals = jnp.sum(shifted, axis=-1, keepdims=True)
    attn_probs = (shifted / totals).astype(jnp.bfloat16)
    log_total = highest + jnp.log(totals)
    context = jnp.einsum(
        "bhlm,bmhd->blhd", attn_probs, values, preferred_element_type=jnp.float32
    ).astype(jnp.bfloat16)
    return (queries, key_rows, values, context.reshape(sentences, positions, -1), log_total)


def attend_back(normed, lengths, kept, grad_out, weights, out_weight):
    queries, key_rows, values, context, log_total = kept
    features = normed.shape[-1]
    head_cols = context.shape[-1]
    grad_flat = grad_out.reshape(-1, features)
    context_flat = context.reshape(-1, head_cols)
    grad_context = (
        lax.dot_general(grad_flat, out_weight, CONTRACT_COLS, preferred_element_type=jnp.float32)
        .astype(jnp.bfloat16)
        .reshape(queries.shape)
    )
    grad_out_weight = lax.dot_general(
        context_flat, grad_flat, CONTRACT_ROWS, preferred_element_type=jnp.float32
    )
    probs = jnp.exp(masked_scores(queries, key_rows, lengths) - log_total)
    grad_probs = jnp.einsum(
        "blhd,bmhd->bhlm", grad_context, values, preferred_element_type=jnp.float32
    )
    grad_values = jnp.einsum(
        "bhlm,blhd->bmhd",
        probs.astype(jnp.bfloat16),
        grad_context,
        preferred_element_type=jnp.float32,
    ).astype(jnp.bfloat16)
    grad_scores = (
        probs * (grad_probs - jnp.sum(probs * grad_probs, axis=-1, keepdims=True))
    ).astype(jnp.bfloat16)
    scaling = HEAD_DIM ** (-0.5)
    grad_queries = (
        jnp.einsum("bhlm,bmhd->blhd", grad_scores, key_rows, preferred_element_type=jnp.float32)
        * scaling
    ).astype(jnp.bfloat16)
    grad_keys = (
        jnp.einsum("bhlm,blhd->bmhd", grad_scores, queries, preferred_element_type=jnp.float32)
        * scaling
    ).astype(jnp.bfloat16)
    normed_flat = normed.reshape(-1, features)
    members = [member.reshape(-1, head_cols) for member in (grad_queries, grad_keys, grad_values)]
    grad_weights = jnp.stack(
        [
            lax.dot_general(normed_flat, member, CONTRACT_ROWS, preferred_element_type=jnp.float32)
            for member in members
        ]
    )
    grad_biases = jnp.stack(
        [
            jnp.sum(members[0].astype(jnp.float32), axis=0),
            jnp.sum(members[2].astype(jnp.float32), axis=0),
        ]
    )
    grad_normed = lax.dot_general(
        members[0], weights[0], CONTRACT_COLS, preferred_element_type=jnp.float32
    )
    grad_normed = grad_normed + lax.dot_general(
        members[1], weights[1], CONTRACT_COLS, preferred_element_type=jnp.float32
    )
    grad_normed = grad_normed + lax.dot_general(
        members[2], weights[2], CONTRACT_COLS, preferred_element_type=jnp.float32
    )
    return (grad_normed.reshape(normed.shape), grad_weights, grad_out_weight, grad_biases)


def group_rows(first_rows, second_rows):
    return (
        lax.all_gather(first_rows, "head", axis=0, tiled=True),
        lax.all_gather(second_rows, "head", axis=0, tiled=True),
    )


def per_device_wide(
    short_x,
    long_x,
    short_cot,
    long_cot,
    short_len,
    long_len,
    short_task,
    long_task,
    expert_ids,
    ln_gain,
    ln_bias,
    w_qkv,
    b_qv,
    w_attn_out,
    b_attn_out,
    w_up,
    b_up,
    w_down,
    b_down,
    task_emb,
    gate_w,
):
    heads_here = lax.axis_size("head")
    head_place = lax.axis_index("head")
    experts = lax.axis_size("expert")
    short_group, short_span, features = short_x.shape
    long_group, long_span = (long_x.shape[0], long_x.shape[1])
    short_dev = short_group // heads_here
    long_dev = long_group // heads_here
    hidden_width = w_up.shape[2]
    tasks_total = expert_ids.shape[0]
    cap_short = 2 * short_group // experts
    cap_long = 2 * long_group // experts
    piece_rows = (cap_short * short_span + cap_long * long_span) // heads_here
    short_total = short_group * short_span
    all_rows = short_total + long_group * long_span
    expert_hits = (expert_ids[:, :, None] == jnp.arange(experts, dtype=jnp.int32)).astype(
        jnp.float32
    )
    chosen_cols = jnp.einsum("tke,de->tkd", expert_hits, gate_w, precision=HIGHEST)
    gate_probs = jax.nn.softmax(jnp.sum(task_emb[:, None, :] * chosen_cols, axis=-1), axis=-1)
    short_slots = route_slots(short_task, expert_ids, cap_short, experts)
    long_slots = route_slots(long_task, expert_ids, cap_long, experts)
    offsets = head_place * piece_rows + jnp.arange(piece_rows, dtype=jnp.int32)
    owners = jnp.arange(experts, dtype=jnp.int32)[:, None]
    in_short = jnp.broadcast_to(offsets < cap_short * short_span, (experts, piece_rows))
    short_pos = offsets % short_span
    long_offset = jnp.maximum(offsets - cap_short * short_span, 0)
    long_pos = long_offset % long_span
    short_route = lookup(
        short_slots, owners * cap_short + jnp.minimum(offsets // short_span, cap_short - 1)
    )
    long_route = lookup(
        long_slots, owners * cap_long + jnp.minimum(long_offset // long_span, cap_long - 1)
    )
    short_sent = short_route // 2
    long_sent = long_route // 2
    position = jnp.where(in_short, short_pos, long_pos)
    target = jnp.where(
        in_short,
        short_sent * short_span + short_pos,
        short_total + long_sent * long_span + long_pos,
    )
    task_rows = jnp.where(in_short, lookup(short_task, short_sent), lookup(long_task, long_sent))
    length_rows = jnp.where(in_short, lookup(short_len, short_sent), lookup(long_len, long_sent))
    live_rows = (position < length_rows).astype(jnp.float32)
    gate_index = task_rows * 2 + jnp.where(in_short, short_route % 2, long_route % 2)
    gate_rows = lookup(gate_probs.reshape(-1), gate_index)
    short_mask = (jnp.arange(short_span, dtype=jnp.int32)[None, :] < short_len[:, None]).astype(
        jnp.float32
    )[:, :, None]
    long_mask = (jnp.arange(long_span, dtype=jnp.int32)[None, :] < long_len[:, None]).astype(
        jnp.float32
    )[:, :, None]
    short_start = head_place * short_dev
    long_start = head_place * long_dev
    own_short_mask = lax.dynamic_slice_in_dim(short_mask, short_start, short_dev, 0)
    own_long_mask = lax.dynamic_slice_in_dim(long_mask, long_start, long_dev, 0)
    short_in = short_x.astype(jnp.float32)
    long_in = long_x.astype(jnp.float32)
    own_short_in = lax.dynamic_slice_in_dim(short_in, short_start, short_dev, 0)
    own_long_in = lax.dynamic_slice_in_dim(long_in, long_start, long_dev, 0)
    attn_qkv, attn_qv, attn_out_w = (w_qkv, b_qv, w_attn_out)
    short_src, long_src = (short_in, long_in)
    short_lens, long_lens = (short_len, long_len)
    head_cols = attn_qkv.shape[2]
    head_count = head_cols // HEAD_DIM
    short_normed = layer_norm(short_src, ln_gain[0], ln_bias[0]).astype(jnp.bfloat16)
    long_normed = layer_norm(long_src, ln_gain[0], ln_bias[0]).astype(jnp.bfloat16)
    short_kept = attend(short_normed, short_lens, attn_qkv, attn_qv, head_count)
    long_kept = attend(long_normed, long_lens, attn_qkv, attn_qv, head_count)
    short_part = jnp.dot(
        short_kept[3].reshape(-1, head_cols), attn_out_w, preferred_element_type=jnp.float32
    ).reshape(short_src.shape)
    long_part = jnp.dot(
        long_kept[3].reshape(-1, head_cols), attn_out_w, preferred_element_type=jnp.float32
    ).reshape(long_src.shape)
    short_sum, long_sum = (
        lax.psum(short_part.astype(jnp.bfloat16), "head").astype(jnp.float32),
        lax.psum(long_part.astype(jnp.bfloat16), "head").astype(jnp.float32),
    )
    short_mid = short_in + short_mask * (short_sum + b_attn_out)
    long_mid = long_in + long_mask * (long_sum + b_attn_out)
    short_mixin = layer_norm(short_mid, ln_gain[1], ln_bias[1]).astype(jnp.bfloat16)
    long_mixin = layer_norm(long_mid, ln_gain[1], ln_bias[1]).astype(jnp.bfloat16)
    own_short_mid = lax.dynamic_slice_in_dim(short_mid, short_start, short_dev, 0)
    own_long_mid = lax.dynamic_slice_in_dim(long_mid, long_start, long_dev, 0)
    mixin_rows = jnp.concatenate(
        [short_mixin.reshape(-1, features), long_mixin.reshape(-1, features)], axis=0
    )
    outgoing = mixin_rows[target]
    received = lax.all_to_all(outgoing, "expert", split_axis=0, concat_axis=0, tiled=True)
    inputs = received.reshape(-1, features)
    gelu_in = jnp.dot(inputs, w_up[0], preferred_element_type=jnp.float32) + b_up[0]
    hidden = jax.nn.gelu(gelu_in).astype(jnp.bfloat16)
    output = (jnp.dot(hidden, w_down[0], preferred_element_type=jnp.float32) + b_down[0]).astype(
        jnp.bfloat16
    )
    returned = lax.all_to_all(
        output.reshape(received.shape), "expert", split_axis=0, concat_axis=0, tiled=True
    )
    wide_shape = received.shape[:2] + (hidden_width,)
    packed = (returned, received, hidden.reshape(wide_shape), gelu_in.reshape(wide_shape))
    returned = packed[0]
    received = packed[1]
    contrib = (gate_rows[:, :, None] * returned.astype(jnp.float32)).reshape(-1, features)
    mixed_rows = jnp.zeros((all_rows, features), jnp.float32).at[target.reshape(-1)].add(contrib)
    short_moe, long_moe = (
        lax.psum_scatter(
            mixed_rows[:short_total].reshape(short_in.shape).astype(jnp.bfloat16),
            "head",
            scatter_dimension=0,
            tiled=True,
        ).astype(jnp.float32),
        lax.psum_scatter(
            mixed_rows[short_total:].reshape(long_in.shape).astype(jnp.bfloat16),
            "head",
            scatter_dimension=0,
            tiled=True,
        ).astype(jnp.float32),
    )
    short_out = (own_short_mid + own_short_mask * short_moe).astype(jnp.bfloat16)
    long_out = (own_long_mid + own_long_mask * long_moe).astype(jnp.bfloat16)
    cot_rows = jnp.concatenate(
        [short_cot.reshape(-1, features), long_cot.reshape(-1, features)], axis=0
    )
    cot_picked = cot_rows[target].astype(jnp.float32)
    grad_sent = ((gate_rows * live_rows)[:, :, None] * cot_picked).astype(jnp.bfloat16)
    gate_terms = live_rows * jnp.sum(cot_picked * returned.astype(jnp.float32), axis=-1)
    gate_part = jnp.sum(
        jnp.where(
            gate_index[:, :, None] == jnp.arange(2 * tasks_total, dtype=jnp.int32),
            gate_terms[:, :, None],
            0.0,
        ),
        axis=(0, 1),
    )
    grad_arrived = lax.all_to_all(grad_sent, "expert", split_axis=0, concat_axis=0, tiled=True)
    inputs = received.reshape(-1, features)
    hidden = packed[2].reshape(-1, hidden_width)
    gelu_in = packed[3].reshape(-1, hidden_width)
    grad_output = grad_arrived.reshape(-1, features)
    grad_hidden = lax.dot_general(
        grad_output, w_down[0], CONTRACT_COLS, preferred_element_type=jnp.float32
    )
    grad_gelu = jax.vjp(jax.nn.gelu, gelu_in)[1](grad_hidden)[0].astype(jnp.bfloat16)
    grad_up_w = lax.dot_general(
        inputs, grad_gelu, CONTRACT_ROWS, preferred_element_type=jnp.float32
    )
    grad_up_b = jnp.sum(grad_gelu.astype(jnp.float32), axis=0)
    grad_down_w = lax.dot_general(
        hidden, grad_output, CONTRACT_ROWS, preferred_element_type=jnp.float32
    )
    grad_down_b = jnp.sum(grad_output.astype(jnp.float32), axis=0)
    grad_inputs = (
        lax.dot_general(grad_gelu, w_up[0], CONTRACT_COLS, preferred_element_type=jnp.float32)
        .astype(jnp.bfloat16)
        .reshape(received.shape)
    )
    grad_home = lax.all_to_all(grad_inputs, "expert", split_axis=0, concat_axis=0, tiled=True)
    shard_up_w, shard_up_b, shard_down_w, shard_down_b = (
        lax.psum_scatter(
            grad_up_w[None].astype(jnp.bfloat16), "head", scatter_dimension=2, tiled=True
        ).astype(jnp.float32),
        lax.psum_scatter(
            grad_up_b[None].astype(jnp.bfloat16), "head", scatter_dimension=1, tiled=True
        ).astype(jnp.float32),
        lax.psum_scatter(
            grad_down_w[None].astype(jnp.bfloat16), "head", scatter_dimension=1, tiled=True
        ).astype(jnp.float32),
        lax.psum_scatter(
            grad_down_b[None].astype(jnp.bfloat16), "head", scatter_dimension=1, tiled=True
        ).astype(jnp.float32),
    )
    grad_mixin = (
        jnp.zeros((all_rows, features), jnp.float32)
        .at[target.reshape(-1)]
        .add(grad_home.reshape(-1, features).astype(jnp.float32))
    )
    short_dmix, long_dmix = (
        lax.psum_scatter(
            grad_mixin[:short_total].reshape(short_in.shape).astype(jnp.bfloat16),
            "head",
            scatter_dimension=0,
            tiled=True,
        ).astype(jnp.float32),
        lax.psum_scatter(
            grad_mixin[short_total:].reshape(long_in.shape).astype(jnp.bfloat16),
            "head",
            scatter_dimension=0,
            tiled=True,
        ).astype(jnp.float32),
    )
    short_dmid, short_gain_two, short_shift_two = jax.vjp(
        layer_norm, own_short_mid, ln_gain[1], ln_bias[1]
    )[1](short_dmix)
    long_dmid, long_gain_two, long_shift_two = jax.vjp(
        layer_norm, own_long_mid, ln_gain[1], ln_bias[1]
    )[1](long_dmix)
    short_dmid = short_dmid + lax.dynamic_slice_in_dim(short_cot, short_start, short_dev, 0).astype(
        jnp.float32
    )
    long_dmid = long_dmid + lax.dynamic_slice_in_dim(long_cot, long_start, long_dev, 0).astype(
        jnp.float32
    )
    short_dattn = (own_short_mask * short_dmid).astype(jnp.bfloat16)
    long_dattn = (own_long_mask * long_dmid).astype(jnp.bfloat16)
    bias_out_grad = jnp.sum(short_dattn.astype(jnp.float32), axis=(0, 1)) + jnp.sum(
        long_dattn.astype(jnp.float32), axis=(0, 1)
    )
    attn_short_grad, attn_long_grad = group_rows(short_dattn, long_dattn)
    short_back = attend_back(
        short_normed, short_lens, short_kept, attn_short_grad, attn_qkv, attn_out_w
    )
    long_back = attend_back(long_normed, long_lens, long_kept, attn_long_grad, attn_qkv, attn_out_w)
    short_dnormed, long_dnormed = (
        lax.psum_scatter(
            short_back[0].astype(jnp.bfloat16), "head", scatter_dimension=0, tiled=True
        ).astype(jnp.float32),
        lax.psum_scatter(
            long_back[0].astype(jnp.bfloat16), "head", scatter_dimension=0, tiled=True
        ).astype(jnp.float32),
    )
    short_dln, short_gain_one, short_shift_one = jax.vjp(
        layer_norm, own_short_in, ln_gain[0], ln_bias[0]
    )[1](short_dnormed)
    long_dln, long_gain_one, long_shift_one = jax.vjp(
        layer_norm, own_long_in, ln_gain[0], ln_bias[0]
    )[1](long_dnormed)
    short_dx = short_dmid + short_dln
    long_dx = long_dmid + long_dln
    qkv_terms = short_back[1] + long_back[1]
    out_terms = short_back[2] + long_back[2]
    bias_terms = short_back[3] + long_back[3]
    grad_qkv, grad_attn_weight, grad_qv = (
        lax.psum(qkv_terms.astype(jnp.bfloat16), "expert").astype(jnp.float32),
        lax.psum(out_terms.astype(jnp.bfloat16), "expert").astype(jnp.float32),
        lax.psum(bias_terms.astype(jnp.bfloat16), "expert").astype(jnp.float32),
    )
    gain_grads = jnp.stack([short_gain_one + long_gain_one, short_gain_two + long_gain_two])
    shift_grads = jnp.stack([short_shift_one + long_shift_one, short_shift_two + long_shift_two])
    grad_gain, grad_shift, grad_bias_out, gate_total = lax.psum(
        (gain_grads, shift_grads, bias_out_grad, gate_part), ("expert", "head")
    )
    gate_grad = gate_total.reshape(tasks_total, 2)
    logit_grad = gate_probs * (gate_grad - jnp.sum(gate_probs * gate_grad, axis=-1, keepdims=True))
    grad_task = jnp.sum(logit_grad[:, :, None] * chosen_cols, axis=1)
    grad_gate = jnp.einsum("tke,tk,td->de", expert_hits, logit_grad, task_emb, precision=HIGHEST)
    return (
        short_out,
        long_out,
        short_dx,
        long_dx,
        grad_gain,
        grad_shift,
        grad_qkv,
        grad_qv,
        grad_attn_weight,
        grad_bias_out,
        shard_up_w,
        shard_up_b,
        shard_down_w,
        shard_down_b,
        grad_task,
        grad_gate,
    )


BF16 = jnp.bfloat16
F32 = jnp.float32
SLICE_ROWS = 272
HALF_PACK = 1088
QKV_ROWS = 1536
MISC_ROW = 2048
GRAD_ROWS = 1040


def mm(a, b):
    return lax.dot_general(a, b, (((1,), (0,)), ((), ())), preferred_element_type=F32)


def mm_nt(a, b):
    return lax.dot_general(a, b, (((1,), (1,)), ((), ())), preferred_element_type=F32)


def mm_tn(a, b):
    return lax.dot_general(a, b, (((0,), (0,)), ((), ())), preferred_element_type=F32)


def iota(shape, dim):
    return lax.broadcasted_iota(jnp.int32, shape, dim)


def params(mebibytes):
    return pltpu.CompilerParams(vmem_limit_bytes=mebibytes * 1024 * 1024)


def cost(micros):
    return pl.CostEstimate(flops=0, bytes_accessed=int(micros * 3.7e6), transcendentals=0)


VM = pl.BlockSpec(memory_space=pltpu.VMEM)
SM = pl.BlockSpec(memory_space=pltpu.SMEM)
ANY = pl.BlockSpec(memory_space=pl.ANY)


def pack_kernel(qkv, qv, wo, out):
    core = lax.axis_index("expert") % 2
    feats = qkv.shape[1]
    split = HALF_PACK - 2 * feats

    @pl.when(core == 0)
    def _():
        out[0:feats, :] = qkv[0]
        out[feats : 2 * feats, :] = qkv[1]
        out[2 * feats :, :] = qkv[2, 0:split, :]

    @pl.when(core != 0)
    def _():
        at = feats - split
        out[0:at, :] = qkv[2, split:, :]
        for c in range(4):
            out[at + 128 * c : at + 128 * (c + 1), :] = wo[:, 128 * c : 128 * (c + 1)]
        at += 4 * 128
        out[at:, :] = jnp.zeros((HALF_PACK - at, 128), BF16)
        high = qv[...].astype(BF16)
        low = (qv[...] - high.astype(F32)).astype(BF16)
        out[at : at + 2, :] = high
        out[at + 2 : at + 4, :] = low


def split_cycles(pair_left, pair_right, eye, count):
    step = mm(pair_left.astype(BF16), pair_right.astype(BF16))
    reach = jnp.minimum(eye + step, 1.0)
    hops = 1
    while hops < count // 2:
        wide = reach.astype(BF16)
        reach = jnp.minimum(mm(wide, wide), 1.0)
        hops *= 2
    lanes = iota((count, count), 1).astype(F32)
    lowest = jnp.min(jnp.where(reach > 0.5, lanes, float(count)), axis=1, keepdims=True)
    lowest_row = jnp.sum(eye * lowest, axis=0, keepdims=True)
    other = jnp.sum(pair_left * lowest_row, axis=1, keepdims=True)
    return (lowest > other).astype(F32)


def route_kernel(st_ref, sl_ref, lt_ref, ll_ref, ids_ref, temb_ref, gw_ref, tab_ref, gate_ref):
    here = lax.axis_index("head").astype(jnp.int32)
    group = lax.axis_index("expert").astype(jnp.int32)
    shorts = st_ref.shape[1]
    longs = lt_ref.shape[1]
    tasks = ids_ref.shape[1]
    per_owner = shorts // 4
    mine = here.astype(F32)

    def eye_of(n):
        return (iota((n, n), 0) == iota((n, n), 1)).astype(F32)

    def col(row, eye):
        return jnp.sum(eye * row, axis=1, keepdims=True)

    def row(column, eye):
        return jnp.sum(eye * column, axis=0, keepdims=True)

    eye = eye_of(shorts)
    at_sub, at_lane = iota((shorts, shorts), 0), iota((shorts, shorts), 1)
    off_diag = 1.0 - eye
    task_row = st_ref[...].astype(F32)
    task_col = col(task_row, eye)
    same_task = (task_col == task_row).astype(F32)
    earlier = (at_lane < at_sub).astype(F32)
    later = (at_lane > at_sub).astype(F32)
    rank_col = jnp.sum(same_task * earlier, axis=1, keepdims=True)
    rank_row = jnp.sum(same_task * later, axis=0, keepdims=True)
    first_of_pair = jnp.floor(rank_col * 0.5) == jnp.floor(rank_row * 0.5)
    pair_right = same_task * first_of_pair.astype(F32) * off_diag
    pair_left = ((at_sub // 2) == (at_lane // 2)).astype(F32) * off_diag
    major = split_cycles(pair_left, pair_right, eye, shorts)
    same_major = (major == row(major, eye)).astype(F32)
    pair_right = same_task * same_major * off_diag
    pair_left = ((at_sub // 4) == (at_lane // 4)).astype(F32) * same_major * off_diag
    minor = split_cycles(pair_left, pair_right, eye, shorts)
    colour = 2.0 * major + minor
    same_owner = ((at_sub // per_owner) == (at_lane // per_owner)).astype(F32)
    same_colour = (colour == row(colour, eye)).astype(F32)
    place = jnp.sum(same_owner * same_colour * earlier, axis=1, keepdims=True)

    sent = iota((shorts, 128), 0)
    lane = iota((shorts, 128), 1)
    sent_f = sent.astype(F32)
    lane_f = lane.astype(F32)
    length_col = col(sl_ref[...].astype(F32), eye)
    own = ((task_col == lane_f) & (colour == mine)).astype(F32)
    owner_col = (iota((shorts, 1), 0) // per_owner).astype(F32)

    def put(r, values):
        tab_ref[r : r + 1, :] = values.astype(jnp.int32)

    def put_away(r, values, low):
        tab_ref[r : r + 1, :] = values.astype(jnp.int32) ^ (here * low)

    def total(values):
        return jnp.sum(values, axis=0, keepdims=True)

    tab_ref[...] = jnp.zeros_like(tab_ref)
    put(0, total(own * sent_f))
    put(1, total(own * length_col))
    put_away(2, total(own * (owner_col * 2.0 + place)), 2)
    natural = (sent == lane + here * per_owner) & (lane < per_owner)
    put_away(6, total(natural.astype(F32) * (colour * 2.0 + place)), 2)

    eye_l = eye_of(longs)
    sub_l, lane_l = iota((longs, longs), 0), iota((longs, longs), 1)
    ltask_row = lt_ref[...].astype(F32)
    ltask_col = col(ltask_row, eye_l)
    right_l = (ltask_col == ltask_row).astype(F32) * (1.0 - eye_l)
    left_l = ((sub_l // 2) == (lane_l // 2)).astype(F32) * (1.0 - eye_l)
    kappa = split_cycles(left_l, right_l, eye_l, longs)
    parity_col = ltask_col - 2.0 * jnp.floor(ltask_col * 0.5)
    parity = jnp.max(parity_col, axis=0, keepdims=True)
    lsent = iota((longs, 128), 0)
    llane = iota((longs, 128), 1)
    unit_task = parity + 2.0 * llane.astype(F32)
    mine_l = (here % 2).astype(F32)
    own_l = ((ltask_col == unit_task) & (kappa == mine_l)).astype(F32)
    llen_col = col(ll_ref[...].astype(F32), eye_l)
    put(3, total(own_l * lsent.astype(F32)))
    put_away(16, total(own_l * (lsent // (longs // 4)).astype(F32)), 1)
    put(4, total(own_l * llen_col))
    row_lane = iota((1, 128), 1)
    row_lane_f = row_lane.astype(F32)
    put(5, parity + 2.0 * row_lane_f)
    natural_l = (lsent == llane + here * (longs // 4)) & (llane < longs // 4)
    put_away(7, total(natural_l.astype(F32) * kappa), 1)
    put_away(15, total(natural_l.astype(F32) * (kappa + 2.0)), 1)

    ids = ids_ref[...].astype(F32)
    eye_t = eye_of(tasks)
    e_first, e_second = col(ids[0:1, :], eye_t), col(ids[1:2, :], eye_t)
    tsub = iota((tasks, 128), 0).astype(F32)
    tlane = iota((tasks, 128), 1).astype(F32)
    diag = (tsub == tlane).astype(F32)
    put(8, total(diag * e_first))
    put(9, total(diag * e_second))
    task_first = total((e_first == tlane).astype(F32) * tsub)
    task_second = total((e_second == tlane).astype(F32) * tsub)
    put(10, task_first)
    put(11, task_second)
    first_parity = task_first - 2.0 * jnp.floor(task_first * 0.5)
    use_second = first_parity != parity
    put(12, use_second.astype(F32))
    unit_of = jnp.where(use_second, task_second, task_first)
    put(13, jnp.floor((unit_of - parity) * 0.5))
    half = here // 2
    tab_ref[14:15, :] = jnp.where(row_lane == 0, half, jnp.where(row_lane == 1, here, group))

    logits = lax.dot_general(
        temb_ref[...],
        gw_ref[...],
        (((1,), (1,)), ((), ())),
        preferred_element_type=F32,
        precision=HIGHEST,
    )
    ecols = iota((tasks, logits.shape[1]), 1).astype(F32)
    first = jnp.sum(jnp.where(ecols == e_first, logits, 0.0), axis=1, keepdims=True)
    second = jnp.sum(jnp.where(ecols == e_second, logits, 0.0), axis=1, keepdims=True)
    top = jnp.maximum(first, second)
    first, second = jnp.exp(first - top), jnp.exp(second - top)
    denominator = first + second
    gate_ref[...] = jnp.where(
        tlane == 0.0, first / denominator, jnp.where(tlane == 1.0, second / denominator, 0.0)
    )


def norm_stats(values):
    centred = values - jnp.mean(values, axis=-1, keepdims=True)
    scale = lax.rsqrt(jnp.mean(centred * centred, axis=-1, keepdims=True) + 1e-05)
    return centred * scale, scale


def prep_kernel(
    tab, gates, cs0, cs1, cl, csb, clb, xs, xl, gain, bias,
    deo, cb_s, cb_l, ns, nl, xb_s, xb_l,
):
    e = pl.program_id(0)
    span = cs0.shape[1]
    for k, ref in ((0, cs0), (1, cs1)):
        t = tab[10 + k, e]
        keep = iota((span, 1), 0) < tab[1, t]
        deo[0, span * k : span * (k + 1), :] = jnp.where(
            keep, gates[t, k] * ref[0].astype(F32), 0.0
        ).astype(BF16)
    half_rows = cl.shape[1]
    u = tab[13, e]
    gate = gates[tab[5, u], tab[12, e]]
    keep = iota((half_rows, 1), 0) + half_rows * tab[14, 0] < tab[4, u]
    deo[0, 2 * span : 2 * span + half_rows, :] = jnp.where(keep, gate * cl[0].astype(F32), 0.0).astype(BF16)
    parity = (tab[5, 0] % 2).astype(F32)
    deo[0, 2 * span + half_rows :, :] = jnp.full((16, deo.shape[2]), parity, F32).astype(BF16)
    cb_s[...] = csb[...]
    cb_l[...] = clb[...]
    xb_s[...] = xs[...]
    xb_l[...] = xl[...]
    ns[0] = (norm_stats(xs[0].astype(F32))[0] * gain[0:1, :] + bias[0:1, :]).astype(BF16)
    nl[0] = (norm_stats(xl[0].astype(F32))[0] * gain[0:1, :] + bias[0:1, :]).astype(BF16)


def unpack_weights(low, high, w, wo, bqv):
    for h in range(low.shape[0]):
        cols = slice(128 * h, 128 * (h + 1))
        w[0:HALF_PACK, cols] = low[h]
        w[HALF_PACK:QKV_ROWS, cols] = high[h, 0 : QKV_ROWS - HALF_PACK, :]
        for c in range(4):
            at = QKV_ROWS - HALF_PACK + 128 * c
            wo[128 * h : 128 * (h + 1), 128 * c : 128 * (c + 1)] = high[h, at : at + 128, :]
        at = MISC_ROW - HALF_PACK
        lines = high[h, at : at + 16, :].astype(F32)
        bqv[0:2, cols] = lines[0:2] + lines[2:4]


class Copies:
    def __init__(self, sems):
        self.sems = sems
        self.used = 0
        self.open = []

    def start(self, source, target):
        copy = pltpu.make_async_copy(source, target, self.sems.at[self.used])
        copy.start()
        self.used += 1
        self.open.append(copy)
        return copy

    def finish(self):
        for copy in self.open:
            copy.wait()


def pair_masks():
    lanes = iota((1, 128), 1)
    first = (lanes < HEAD_DIM).astype(BF16)
    return first, (1.0 - first.astype(F32)).astype(BF16)


def both_heads(block, masks):
    return jnp.concatenate([block * masks[0], block * masks[1]], axis=0)


def fold_heads(stacked, keys):
    lanes = iota((1, 128), 1)
    return jnp.where(lanes < HEAD_DIM, stacked[:keys], stacked[keys:])


def softmax_pair(scores, visible, keys):
    parts = []
    for part in (scores[:, :keys], scores[:, keys:]):
        part = jnp.where(visible, part, -1e30)
        shifted = jnp.exp(part - jnp.max(part, axis=-1, keepdims=True))
        parts.append(shifted * (1.0 / jnp.sum(shifted, axis=-1, keepdims=True)))
    return jnp.concatenate(parts, axis=1).astype(BF16)


def short_visible(tab, i, span):
    rows, lanes = iota((128, 128), 0), iota((128, 128), 1)
    limit = jnp.where(iota((1, 128), 1) < span, tab[1, 2 * i], tab[1, 2 * i + 1] + span)
    return ((rows // span) == (lanes // span)) & (lanes < limit)


def attend_short(
    tab, norm_h, x_h, own_h, other_h, gain, bias, bo,
    q_h, k_h, v_h, p_h, ctx_h, mid, send, w_h, wo_h, bqv,
    norm, x, own, other, q_ref, k_ref, v_ref, p_ref, ctx, w, wo, in_sems, out_sems,
):
    core = tab[14, 2] % 2
    fetch, leave = Copies(in_sems), Copies(out_sems)
    pieces = [fetch.start(own_h, own), fetch.start(other_h, other), fetch.start(norm_h, norm)]
    have_x = fetch.start(x_h, x)
    for piece in pieces:
        piece.wait()

    @pl.when(core == 0)
    def _():
        unpack_weights(own, other, w, wo, bqv)

    @pl.when(core != 0)
    def _():
        unpack_weights(other, own, w, wo, bqv)

    leave.start(w, w_h)
    leave.start(wo, wo_h)
    feats = norm.shape[1]
    rows = norm[...]
    q_ref[...] = ((mm(rows, w[0:feats, :]) + bqv[0:1, :]).astype(BF16) * HEAD_DIM ** (-0.5)).astype(BF16)
    leave.start(q_ref, q_h)
    k_ref[...] = mm(rows, w[feats : 2 * feats, :]).astype(BF16)
    leave.start(k_ref, k_h)
    v_ref[...] = (mm(rows, w[2 * feats : 3 * feats, :]) + bqv[1:2, :]).astype(BF16)
    leave.start(v_ref, v_h)
    masks = pair_masks()
    span = send.shape[2]
    pairs = feats // 128
    for i in range(norm.shape[0] // 128):
        visible = short_visible(tab, i, span)
        r = slice(128 * i, 128 * (i + 1))
        for p in range(pairs):
            c = slice(128 * p, 128 * (p + 1))
            scores = mm_nt(q_ref[r, c], both_heads(k_ref[r, c], masks))
            probs = softmax_pair(scores, visible, 128)
            p_ref[i * pairs + p] = probs
            ctx[r, c] = mm(probs, both_heads(v_ref[r, c], masks)).astype(BF16)
        leave.start(p_ref.at[pairs * i : pairs * (i + 1)], p_h.at[pairs * i : pairs * (i + 1)])
    leave.start(ctx, ctx_h)
    attn = mm(ctx[...], wo[...]) + bo[...]
    have_x.wait()
    for t in range(send.shape[0]):
        r = slice(span * t, span * (t + 1))
        keep = iota((span, 1), 0) < tab[1, t]
        middle = x[r, :].astype(F32) + jnp.where(keep, attn[r, :], 0.0)
        mid[r, :] = middle
        mixin = (norm_stats(middle)[0] * gain[1:2, :] + bias[1:2, :]).astype(BF16)
        send[tab[8, t], 0] = mixin
        send[tab[9, t], 1] = mixin
    leave.finish()


def attend_long(
    tab, norm_h, x_h, w_h, wo_h, bqv, gain, bias, bo,
    q_h, k_h, v_h, p_h, ctx_h, mid, send,
    norm, x, w, wo, q_ref, k_ref, v_ref, p_ref, ctx, nq, in_sems, out_sems,
):
    fetch, leave = Copies(in_sems), Copies(out_sems)
    have_norm, have_w = fetch.start(norm_h, norm), fetch.start(w_h, w)
    have_wo, have_x = fetch.start(wo_h, wo), fetch.start(x_h, x)
    feats = norm.shape[1]
    half_rows = send.shape[1]
    span = 2 * half_rows
    units = norm.shape[0] // span
    offset = tab[14, 0] * half_rows
    have_norm.wait()
    for u in range(units):
        at = pl.multiple_of(span * u + offset, half_rows)
        nq[half_rows * u : half_rows * (u + 1), :] = norm[pl.ds(at, half_rows), :]
    rows = norm[...]
    have_w.wait()
    q_ref[...] = ((mm(nq[...], w[0:feats, :]) + bqv[0:1, :]).astype(BF16) * HEAD_DIM ** (-0.5)).astype(BF16)
    leave.start(q_ref, q_h)
    k_ref[...] = mm(rows, w[feats : 2 * feats, :]).astype(BF16)
    leave.start(k_ref, k_h)
    v_ref[...] = (mm(rows, w[2 * feats : 3 * feats, :]) + bqv[1:2, :]).astype(BF16)
    leave.start(v_ref, v_h)
    masks = pair_masks()
    pairs = feats // 128
    for u in range(units):
        visible = iota((1, span), 1) < tab[4, u]
        r = slice(half_rows * u, half_rows * (u + 1))
        kr = slice(span * u, span * (u + 1))
        for p in range(pairs):
            c = slice(128 * p, 128 * (p + 1))
            scores = mm_nt(q_ref[r, c], both_heads(k_ref[kr, c], masks))
            probs = softmax_pair(scores, visible, span)
            p_ref[u * pairs + p] = probs
            ctx[r, c] = mm(probs, both_heads(v_ref[kr, c], masks)).astype(BF16)
        leave.start(p_ref.at[pairs * u : pairs * (u + 1)], p_h.at[pairs * u : pairs * (u + 1)])
    leave.start(ctx, ctx_h)
    have_wo.wait()
    attn = mm(ctx[...], wo[...]) + bo[...]
    have_x.wait()
    for u in range(units):
        r = slice(half_rows * u, half_rows * (u + 1))
        keep = iota((half_rows, 1), 0) + offset < tab[4, u]
        at = pl.multiple_of(span * u + offset, half_rows)
        middle = x[pl.ds(at, half_rows), :].astype(F32) + jnp.where(keep, attn[r, :], 0.0)
        mid[r, :] = middle
        mixin = (norm_stats(middle)[0] * gain[1:2, :] + bias[1:2, :]).astype(BF16)
        t = tab[5, u]
        send[tab[8, t]] = mixin
        send[tab[9, t]] = mixin
    leave.finish()


GELU_A = 0.7978845608028654
GELU_B = 0.044715


def expert_kernel(first, tab, *refs):
    if first:
        x, d, wu, bu, wd, bd, back, dw, ga, xt, dt, ea, da, hs, ps = refs
        prev = None
    else:
        x, d, wu, bu, wd, bd, par, prev, ga_in, back, eo, dw, ga, xt, dt, ea, da, hs, ps = refs
    j = pl.program_id(0)
    feats = x.shape[2]
    rows = x.shape[0] * x.shape[1]
    step = 4 * x.shape[1]

    @pl.when(j == 0)
    def _():
        for g in range(x.shape[0]):
            cols = slice(x.shape[1] * g, x.shape[1] * (g + 1))
            xt[:, cols] = x[g].T
            dt[:, cols] = d[g].T
        ea[...] = jnp.broadcast_to(bd[...], ea.shape)
        da[...] = jnp.zeros_like(da)

    for i in range(rows // step):
        r = slice(step * i, step * (i + 1))
        xr = x[4 * i : 4 * i + 4].reshape(step, feats)
        dr = d[4 * i : 4 * i + 4].reshape(step, feats)
        pre = mm(xr, wu[0]) + bu[...]
        square = pre * pre
        half = 0.5 + 0.5 * jnp.tanh(pre * (GELU_A + (GELU_A * GELU_B) * square))
        hidden = (pre * half).astype(BF16)
        half, square = half.astype(BF16), square.astype(BF16)
        slope = half + hidden * (1.0 - half) * (2.0 * GELU_A + (6.0 * GELU_A * GELU_B) * square)
        dpre = mm_nt(dr, wd[0]).astype(BF16) * slope
        hs[r, :] = hidden
        ps[r, :] = dpre
        ea[r, :] += mm(hidden, wd[0])
        da[r, :] += mm_nt(dpre, wu[0])

    wide = wu.shape[2]
    grad_up = mm(xt[...], ps[...])
    grad_down = mm(dt[...], hs[...]).T
    ones = jnp.ones((16, rows), BF16)
    up_bias = mm(ones, ps[...])[0:1, :]
    down_bias = mm_nt(ones, dt[...])[0:1, :]
    if prev is not None:
        grad_up += prev[0, 0:feats, :].astype(F32)
        grad_down += prev[0, feats : feats + wide, :].astype(F32)
        tail = prev[0, feats + wide :, :].astype(F32)
        up_bias += tail[0:1, :]
        down_bias += tail[1:2, :]
    dw[0, 0:feats, :] = grad_up.astype(BF16)
    dw[0, feats : feats + wide, :] = grad_down.astype(BF16)
    which = iota((16, 1), 0)
    dw[0, feats + wide :, :] = jnp.where(
        which == 0, up_bias, jnp.where(which == 1, down_bias, 0.0)
    ).astype(BF16)

    @pl.when(j == pl.num_programs(0) - 1)
    def _():
        own = tab[14, 2]
        t_first, t_second = tab[10, own], tab[11, own]
        lanes = iota((1, 128), 1)
        as_first = (lanes == 2 * t_first).astype(F32)
        as_second = (lanes == 2 * t_second + 1).astype(F32)
        rows_each = x.shape[1]
        gate_sums = jnp.zeros((1, 128), F32)
        for g in range(x.shape[0]):
            r = slice(rows_each * g, rows_each * (g + 1))
            out = ea[r, :].astype(BF16)
            back[g, 0:rows_each, :] = da[r, :].astype(BF16)
            if first:
                back[g, rows_each:, :] = out
            else:
                eo[g] = out
            prod = out.astype(F32) * d[g].astype(F32)
            if first:
                half_each = rows_each // 2
                gate_sums += as_first * jnp.sum(prod[:half_each], keepdims=True)
                gate_sums += as_second * jnp.sum(prod[half_each:], keepdims=True)
            else:
                odd = par[g, 0:1, 0:128].astype(F32)
                is_first = odd == (t_first % 2).astype(F32)
                gate_sums += jnp.where(is_first, as_first, as_second) * jnp.sum(prod, keepdims=True)
        if not first:
            gate_sums += ga_in[0:1, :]
        ga[...] = jnp.broadcast_to(gate_sums, ga.shape)


def experts_pass(tab, x, deo, part, w_up, b_up, w_down, b_down, prev, ga):
    experts, rows_each, feats = x.shape
    hidden = w_up.shape[2]
    chunk = hidden // 4
    rows = experts * rows_each
    first = prev is None
    in_specs = [
        SM,
        pl.BlockSpec((experts, rows_each, feats), lambda j: (0, 0, 0)),
        pl.BlockSpec((experts, rows_each, feats), lambda j: (0, part, 0)),
        pl.BlockSpec((1, feats, chunk), lambda j: (0, 0, j)),
        pl.BlockSpec((1, chunk), lambda j: (0, j)),
        pl.BlockSpec((1, chunk, feats), lambda j: (0, j, 0)),
        pl.BlockSpec((1, feats), lambda j: (0, 0)),
    ]
    args = [tab, x, deo, w_up, b_up, w_down, b_down]
    if not first:
        in_specs.append(pl.BlockSpec((experts, 16, feats), lambda j: (0, 2 * rows_each // 16, 0)))
        args.append(deo)
        in_specs.append(pl.BlockSpec((1, GRAD_ROWS, feats), lambda j: (j, 0, 0)))
        args.append(prev)
        in_specs.append(pl.BlockSpec((8, 128), lambda j: (0, 0)))
        args.append(ga)
    back = (
        [jax.ShapeDtypeStruct((experts, 2 * rows_each, feats), BF16)]
        if first
        else [jax.ShapeDtypeStruct(x.shape, BF16)] * 2
    )
    return pl.pallas_call(
        functools.partial(expert_kernel, first),
        grid=(4,),
        in_specs=in_specs,
        out_specs=[pl.BlockSpec(a.shape, lambda j: (0, 0, 0)) for a in back]
        + [
            pl.BlockSpec((1, GRAD_ROWS, feats), lambda j: (j, 0, 0)),
            pl.BlockSpec((8, 128), lambda j: (0, 0)),
        ],
        out_shape=back
        + [
            jax.ShapeDtypeStruct((4, GRAD_ROWS, feats), BF16),
            jax.ShapeDtypeStruct((8, 128), F32),
        ],
        scratch_shapes=[
            pltpu.VMEM((feats, rows), BF16),
            pltpu.VMEM((feats, rows), BF16),
            pltpu.VMEM((rows, feats), F32),
            pltpu.VMEM((rows, feats), F32),
            pltpu.VMEM((rows, chunk), BF16),
            pltpu.VMEM((rows, chunk), BF16),
        ],
        compiler_params=params(56),
        cost_estimate=cost(15),
        name="experts_short" if first else "experts_long",
    )(*args)


def pass_kernel(*refs):
    pass


def after(array, *others):
    return pl.pallas_call(
        pass_kernel,
        in_specs=[ANY] * (1 + len(others)),
        out_specs=ANY,
        out_shape=jax.ShapeDtypeStruct(array.shape, array.dtype),
        input_output_aliases={0: 0},
        compiler_params=params(56),
        cost_estimate=cost(0.1),
        name="after",
    )(array, *others)


def norm_back(grad, unit, scale, gain):
    scaled = grad * gain
    return scale * (
        scaled
        - jnp.mean(scaled, axis=-1, keepdims=True)
        - unit * jnp.mean(scaled * unit, axis=-1, keepdims=True)
    )


def head_pair_back(probs, dctx, q, kk, vv, keys):
    dprobs = mm_nt(dctx, vv)
    dvalues = fold_heads(mm_tn(probs, dctx), keys)
    wide = probs.astype(F32)
    prod = wide * dprobs
    parts = []
    for part in (slice(0, keys), slice(keys, 2 * keys)):
        parts.append(prod[:, part] - wide[:, part] * jnp.sum(prod[:, part], axis=-1, keepdims=True))
    dscores = jnp.concatenate(parts, axis=1).astype(BF16)
    dqueries = mm(dscores, kk) * HEAD_DIM ** (-0.5)
    dkeys = fold_heads(mm_tn(dscores, q), keys)
    return dqueries.astype(BF16), dkeys.astype(BF16), dvalues.astype(BF16)


def row_sum(values):
    return jnp.sum(values, axis=0, keepdims=True)


def back_short(
    tab, gates, gain, *refs
):
    sources, refs = refs[1:13], refs[13:]
    z_refs, dw_h, small, _out = refs[:4], refs[4], refs[5], refs[6]
    ret, mid, c, wo, ctx, p_ref, q_ref, k_ref, v_ref, norm, w, x = refs[7:19]
    zsend, zout, dw, dmid, dattn, dctx, dq, dk, dv, dnorm, in_sems, out_sems = refs[19:]
    fetch, leave = Copies(in_sems), Copies(out_sems)
    have = [fetch.start(a, b) for a, b in zip(sources, refs[7:19])]
    feats = norm.shape[1]
    span = zsend.shape[1]
    sums = [jnp.zeros((1, feats), F32) for _ in range(5)]
    for copy in have[:3]:
        copy.wait()
    for t in range(ret.shape[0]):
        r = slice(span * t, span * (t + 1))
        keep = iota((span, 1), 0) < tab[1, t]
        back_0, back_1 = ret.at[tab[8, t]], ret.at[tab[9, t]]
        mixed = gates[t, 0] * back_0[2 * span : 3 * span, :].astype(F32)
        mixed += gates[t, 1] * back_1[3 * span : 4 * span, :].astype(F32)
        zout[tab[2, t]] = (mid[r, :] + jnp.where(keep, mixed, 0.0)).astype(BF16)
        dmix = back_0[0:span, :].astype(F32) + back_1[span : 2 * span, :].astype(F32)
        unit, scale = norm_stats(mid[r, :])
        sums[2] += row_sum(dmix * unit)
        sums[3] += row_sum(dmix)
        middle = c[r, :].astype(F32) + norm_back(dmix, unit, scale, gain[1:2, :])
        dmid[r, :] = middle
        masked = jnp.where(keep, middle, 0.0)
        sums[4] += row_sum(masked)
        dattn[r, :] = masked.astype(BF16)
    for copy in have[3:5]:
        copy.wait()
    dctx[...] = mm_nt(dattn[...], wo[...]).astype(BF16)
    dw[3 * feats : 4 * feats, :] = mm_tn(ctx[...], dattn[...]).astype(BF16)
    leave.start(dw.at[3 * feats : 4 * feats], dw_h.at[3 * feats : 4 * feats])
    masks = pair_masks()
    for copy in have[5:9]:
        copy.wait()
    for i in range(norm.shape[0] // 128):
        r = slice(128 * i, 128 * (i + 1))
        for p in range(feats // 128):
            c_ = slice(128 * p, 128 * (p + 1))
            a, b, d = head_pair_back(
                p_ref[i * (feats // 128) + p],
                dctx[r, c_],
                q_ref[r, c_],
                both_heads(k_ref[r, c_], masks),
                both_heads(v_ref[r, c_], masks),
                128,
            )
            dq[r, c_] = a
            dk[r, c_] = b
            dv[r, c_] = d
    for copy in have[9:]:
        copy.wait()
    rows = norm[...]
    for index, ref in enumerate((dq, dk, dv)):
        dw[feats * index : feats * (index + 1), :] = mm_tn(rows, ref[...]).astype(BF16)
    leave.start(dw.at[0 : 3 * feats], dw_h.at[0 : 3 * feats])
    dnorm[...] = (
        mm_nt(dq[...], w[0:feats, :])
        + mm_nt(dk[...], w[feats : 2 * feats, :])
        + mm_nt(dv[...], w[2 * feats : 3 * feats, :])
    )
    for t in range(ret.shape[0]):
        r = slice(span * t, span * (t + 1))
        unit, scale = norm_stats(x[r, :].astype(F32))
        grad = dnorm[r, :]
        sums[0] += row_sum(grad * unit)
        sums[1] += row_sum(grad)
        zsend[tab[2, t]] = (dmid[r, :] + norm_back(grad, unit, scale, gain[0:1, :])).astype(BF16)
    sums.append(row_sum(dq[...].astype(F32)))
    sums.append(row_sum(dv[...].astype(F32)))
    for index, value in enumerate(sums):
        small[index : index + 1, :] = value
    small[7:8, :] = jnp.zeros((1, feats), F32)
    for d, ref in enumerate(z_refs):
        ref[0, 0 : 2 * span, :] = zout[2 * d : 2 * d + 2].reshape(2 * span, feats)
        ref[0, 2 * span :, :] = zsend[2 * d : 2 * d + 2].reshape(2 * span, feats)
    leave.finish()


def back_long(
    tab, gain, small_in, ga, *refs
):
    sources, refs = refs[:13], refs[13:]
    zsend, packed_h = refs[:2]
    ret, mid, c, norm, wo, ctx, p_ref, q_ref, k_ref, v_ref, dw_in, w, x = refs[2:15]
    packed, nq, dmid, dattn, dctx, dq, dk, dv, dnorm, full, in_sems, out_sems = refs[15:]
    fetch, leave = Copies(in_sems), Copies(out_sems)
    have = [fetch.start(a, b) for a, b in zip(sources, refs[2:15])]
    feats = norm.shape[1]
    half_rows = ret.shape[1]
    span = 2 * half_rows
    units = norm.shape[0] // span
    offset = tab[14, 0] * half_rows
    sums = [small_in[index : index + 1, :] for index in range(7)]
    for copy in have[:4]:
        copy.wait()
    for u in range(units):
        r = slice(half_rows * u, half_rows * (u + 1))
        t = tab[5, u]
        at = pl.multiple_of(span * u + offset, half_rows)
        nq[r, :] = norm[pl.ds(at, half_rows), :]
        keep = iota((half_rows, 1), 0) + offset < tab[4, u]
        dmix = ret[tab[8, t]].astype(F32) + ret[tab[9, t]].astype(F32)
        unit, scale = norm_stats(mid[r, :])
        sums[2] += row_sum(dmix * unit)
        sums[3] += row_sum(dmix)
        middle = c[r, :].astype(F32) + norm_back(dmix, unit, scale, gain[1:2, :])
        dmid[r, :] = middle
        masked = jnp.where(keep, middle, 0.0)
        sums[4] += row_sum(masked)
        dattn[r, :] = masked.astype(BF16)
    for copy in have[4:6]:
        copy.wait()
    dctx[...] = mm_nt(dattn[...], wo[...]).astype(BF16)
    for copy in have[6:11]:
        copy.wait()
    grad_out = mm_tn(ctx[...], dattn[...]) + dw_in[3 * feats : 4 * feats, :].astype(F32)
    shards = packed.shape[1]
    for h in range(shards):
        for s in range(4):
            full[QKV_ROWS + 128 * s : QKV_ROWS + 128 * (s + 1), 128 * h : 128 * (h + 1)] = grad_out[
                128 * h : 128 * (h + 1), 128 * s : 128 * (s + 1)
            ]
    masks = pair_masks()
    for u in range(units):
        r = slice(half_rows * u, half_rows * (u + 1))
        kr = slice(span * u, span * (u + 1))
        for p in range(feats // 128):
            c_ = slice(128 * p, 128 * (p + 1))
            a, b, d = head_pair_back(
                p_ref[u * (feats // 128) + p],
                dctx[r, c_],
                q_ref[r, c_],
                both_heads(k_ref[kr, c_], masks),
                both_heads(v_ref[kr, c_], masks),
                span,
            )
            dq[r, c_] = a
            dk[kr, c_] = b
            dv[kr, c_] = d
    for index, (left, right) in enumerate(((nq, dq), (norm, dk), (norm, dv))):
        r = slice(feats * index, feats * (index + 1))
        full[r, :] = mm_tn(left[...], right[...]) + dw_in[r, :].astype(F32)
    shift = tab[14, 1]
    early = MISC_ROW // SLICE_ROWS
    for g in range(early):
        for h in range(shards):
            packed[g, shift ^ h] = full[
                SLICE_ROWS * g : SLICE_ROWS * (g + 1), 128 * h : 128 * (h + 1)
            ].astype(BF16)
    leave.start(packed.at[0:early], packed_h.at[0:early])
    for copy in have[11:]:
        copy.wait()
    dnorm[...] = mm_nt(dk[...], w[feats : 2 * feats, :]) + mm_nt(dv[...], w[2 * feats : 3 * feats, :])
    from_q = mm_nt(dq[...], w[0:feats, :])
    for u in range(units):
        at = pl.multiple_of(span * u + offset, half_rows)
        dnorm[pl.ds(at, half_rows), :] += from_q[half_rows * u : half_rows * (u + 1), :]
    for u in range(units):
        owner = tab[16, u]
        for s in range(2):
            r = slice(span * u + half_rows * s, span * u + half_rows * (s + 1))
            unit, scale = norm_stats(x[r, :].astype(F32))
            grad = dnorm[r, :]
            sums[0] += row_sum(grad * unit)
            sums[1] += row_sum(grad)
            own_half = tab[14, 0] == s
            direct = jnp.where(own_half, dmid[half_rows * u : half_rows * (u + 1), :], 0.0)
            zsend[owner, half_rows * s : half_rows * (s + 1), :] = (
                direct + norm_back(grad, unit, scale, gain[0:1, :])
            ).astype(BF16)
    sums[5] += row_sum(dq[...].astype(F32))
    sums[6] += row_sum(dv[...].astype(F32))
    full[MISC_ROW:, :] = jnp.zeros((full.shape[0] - MISC_ROW, feats), F32)
    full[MISC_ROW : MISC_ROW + 1, :] = sums[5]
    full[MISC_ROW + 1 : MISC_ROW + 2, :] = sums[6]
    for index in range(5):
        for s in range(4):
            at = MISC_ROW + 2 + 4 * index + s
            piece = sums[index][:, 128 * s : 128 * (s + 1)]
            full[at : at + 1, :] = jnp.concatenate([piece] * shards, axis=1)
    for s in range(shards):
        full[MISC_ROW + 22 : MISC_ROW + 23, 128 * s : 128 * (s + 1)] = ga[0:1, :]
    for g in range(early, packed.shape[0]):
        for h in range(shards):
            packed[g, shift ^ h] = full[
                SLICE_ROWS * g : SLICE_ROWS * (g + 1), 128 * h : 128 * (h + 1)
            ].astype(BF16)
    leave.start(packed.at[early:], packed_h.at[early:])
    leave.finish()


def mix_long(tab, gates, ret, mid, dx, z0, z1, z2, z3, zout):
    half_rows = ret.shape[1]
    for u in range(mid.shape[0] // half_rows):
        r = slice(half_rows * u, half_rows * (u + 1))
        t = tab[5, u]
        keep = iota((half_rows, 1), 0) + half_rows * tab[14, 0] < tab[4, u]
        mixed = gates[t, 0] * ret[tab[8, t]].astype(F32) + gates[t, 1] * ret[tab[9, t]].astype(F32)
        zout[tab[16, u]] = (mid[r, :] + jnp.where(keep, mixed, 0.0)).astype(BF16)
    for d, ref in enumerate((z0, z1, z2, z3)):
        ref[0, 0:half_rows, :] = zout[d]
        ref[0, half_rows:, :] = dx[d]


def each_distance(index, refs, act):
    for d, ref in enumerate(refs):

        @pl.when(index == d)
        def _(ref=ref):
            act(ref)


def place_kernel(tab, s0, s1, s2, s3, l0, l1, l2, l3, _0, _1, short_out, long_out, short_dx, long_dx):
    span = short_out.shape[1]
    half = long_out.shape[1] // 2
    for n in range(short_out.shape[0]):
        slot = tab[6, n]
        at = pl.multiple_of((slot % 2) * span, span)

        def copy_short(ref, n=n, at=at):
            short_out[n] = ref[0, pl.ds(at, span), :]
            short_dx[n] = ref[0, pl.ds(pl.multiple_of(2 * span + at, span), span), :].astype(F32)

        each_distance(slot // 2, (s0, s1, s2, s3), copy_short)
    for n in range(long_out.shape[0]):

        def first(ref, n=n):
            long_out[n, 0:half, :] = ref[0, 0:half, :]
            long_dx[n] = ref[0, half:, :].astype(F32)

        def second(ref, n=n):
            long_out[n, half:, :] = ref[0, 0:half, :]
            long_dx[n] += ref[0, half:, :].astype(F32)

        each_distance(tab[7, n], (l0, l1, l2, l3), first)
        each_distance(tab[15, n], (l0, l1, l2, l3), second)


def finish_kernel(
    g, ids, gates, temb, gw_t, qkv, qv, wo, gain, shift, bo, grad_temb, grad_gw_t
):
    feats = wo.shape[1]
    for j in range(3):
        qkv[j] = g[feats * j : feats * (j + 1), :].astype(F32)
    for c in range(4):
        at = QKV_ROWS + 128 * c
        wo[:, 128 * c : 128 * (c + 1)] = g[at : at + 128, :].astype(F32)
    misc = g[MISC_ROW : MISC_ROW + 32, :].astype(F32)
    qv[...] = misc[0:2, :]

    def line(index):
        at = 2 + 4 * index
        return jnp.concatenate([misc[at + s : at + s + 1, :] for s in range(4)], axis=1)

    gain[0:1, :], gain[1:2, :] = line(0), line(2)
    shift[0:1, :], shift[1:2, :] = line(1), line(3)
    bo[...] = line(4)
    terms = misc[22:23, :]
    tasks = temb.shape[0]
    sub, lane = iota((tasks, 128), 0), iota((tasks, 128), 1)
    first = jnp.sum(jnp.where(lane == 2 * sub, terms, 0.0), axis=1, keepdims=True)
    second = jnp.sum(jnp.where(lane == 2 * sub + 1, terms, 0.0), axis=1, keepdims=True)
    both = first + second
    first = first - gates[:, 0:1] * both
    second = second - gates[:, 1:2] * both
    experts = gw_t.shape[0]
    rows = iota((experts, tasks), 0)
    eye = (iota((tasks, tasks), 0) == iota((tasks, tasks), 1)).astype(F32)
    spread = jnp.zeros((experts, tasks), F32)
    for k, value in ((0, first), (1, second)):
        as_row = jnp.sum(eye * value, axis=0, keepdims=True)
        spread += jnp.where(rows == ids[k : k + 1, :], as_row, 0.0)
    grad_gw_t[...] = lax.dot_general(
        spread, temb[...], (((1,), (0,)), ((), ())), preferred_element_type=F32, precision=HIGHEST
    )
    grad_temb[...] = lax.dot_general(
        spread.T, gw_t[...], (((1,), (0,)), ((), ())), preferred_element_type=F32, precision=HIGHEST
    )


def finish_experts(tab, shard, up, up_b, down, down_b):
    feats = up.shape[1]
    up[0] = shard[0, 0:feats, :].astype(F32)
    down[0] = shard[0, feats : 2 * feats, :].astype(F32)
    tail = shard[0, 2 * feats :, :].astype(F32)
    up_b[...] = tail[0:1, :]
    down_b[...] = jnp.zeros_like(down_b)
    for h in range(feats // 128):

        @pl.when(tab[14, 1] == h)
        def _(h=h):
            down_b[...] = tail[1:2, 128 * h : 128 * (h + 1)]


def collect_kernel(arrived, *refs):
    for d, ref in enumerate(refs[8:12]):
        terms = arrived[0, d].astype(F32)
        for g in range(1, arrived.shape[0]):
            terms += arrived[g, d].astype(F32)
        ref[0] = terms.astype(BF16)


def shape_of(shape, dtype):
    return jax.ShapeDtypeStruct(shape, dtype)


def balanced(short_x, long_x, expert_ids):
    heads = lax.axis_size("head")
    tasks = expert_ids.shape[0]
    return (
        heads == 4
        and lax.axis_size("expert") == tasks == 8
        and short_x.shape[0] == 4 * tasks
        and long_x.shape[0] == tasks
        and short_x.shape[1:] == (64, 512)
        and long_x.shape[1:] == (256, 512)
    )


def per_device(
    short_x,
    long_x,
    short_cot,
    long_cot,
    short_len,
    long_len,
    short_task,
    long_task,
    expert_ids,
    ln_gain,
    ln_bias,
    w_qkv,
    b_qv,
    w_attn_out,
    b_attn_out,
    w_up,
    b_up,
    w_down,
    b_down,
    task_emb,
    gate_w,
):
    if not balanced(short_x, long_x, expert_ids):
        return per_device_wide(
            short_x, long_x, short_cot, long_cot, short_len, long_len, short_task, long_task,
            expert_ids, ln_gain, ln_bias, w_qkv, b_qv, w_attn_out, b_attn_out, w_up, b_up,
            w_down, b_down, task_emb, gate_w,
        )
    heads = lax.axis_size("head")
    experts = lax.axis_size("expert")
    span, feats = short_x.shape[1:]
    long_span = long_x.shape[1]
    half_rows = long_span // 2
    tasks = expert_ids.shape[0]
    units = long_x.shape[0] // 2
    rows_s = tasks * span
    rows_q = units * half_rows
    rows_l = units * long_span
    pairs = feats // 128

    own_half = pl.pallas_call(
        pack_kernel,
        in_specs=[VM] * 3,
        out_specs=VM,
        out_shape=shape_of((HALF_PACK, 128), BF16),
        compiler_params=params(56),
        cost_estimate=cost(2),
        name="pack",
    )(w_qkv, b_qv, w_attn_out)
    raw_own = lax.all_gather(own_half, "head", axis=0)
    raw_other = lax.ppermute(raw_own, "expert", [(i, i ^ 1) for i in range(experts)])

    tab, gates = pl.pallas_call(
        route_kernel,
        in_specs=[VM] * 7,
        out_specs=[VM, VM],
        out_shape=[shape_of((24, 128), jnp.int32), shape_of((tasks, 128), F32)],
        compiler_params=params(56),
        cost_estimate=cost(4),
        name="route",
    )(
        short_task.reshape(1, -1),
        short_len.reshape(1, -1),
        long_task.reshape(1, -1),
        long_len.reshape(1, -1),
        expert_ids.T,
        task_emb,
        gate_w.T,
    )

    def blk(n, index):
        return pl.BlockSpec((1, n, feats), index)

    deo, cot_s, cot_l, norm_s, norm_l, own_s, own_l = pl.pallas_call(
        prep_kernel,
        grid_spec=pltpu.PrefetchScalarGridSpec(
            num_scalar_prefetch=1,
            grid=(8,),
            in_specs=[
                SM,
                blk(span, lambda e, tab: (tab[0, tab[10, e]], 0, 0)),
                blk(span, lambda e, tab: (tab[0, tab[11, e]], 0, 0)),
                blk(half_rows, lambda e, tab: (tab[3, tab[13, e]], tab[14, 0], 0)),
                blk(span, lambda e, tab: (tab[0, e], 0, 0)),
                blk(span, lambda e, tab: (tab[3, e // 2], tab[14, 0] * 2 + e % 2, 0)),
                blk(span, lambda e, tab: (tab[0, e], 0, 0)),
                blk(half_rows, lambda e, tab: (tab[3, e // 2], e % 2, 0)),
                pl.BlockSpec((2, feats), lambda e, tab: (0, 0)),
                pl.BlockSpec((2, feats), lambda e, tab: (0, 0)),
            ],
            out_specs=[
                blk(2 * span + half_rows + 16, lambda e, tab: (e, 0, 0)),
                blk(span, lambda e, tab: (e, 0, 0)),
                blk(span, lambda e, tab: (e, 0, 0)),
                blk(span, lambda e, tab: (e, 0, 0)),
                blk(half_rows, lambda e, tab: (e, 0, 0)),
                blk(span, lambda e, tab: (e, 0, 0)),
                blk(half_rows, lambda e, tab: (e, 0, 0)),
            ],
        ),
        out_shape=[
            shape_of((experts, 2 * span + half_rows + 16, feats), BF16),
            shape_of((8, span, feats), BF16),
            shape_of((8, span, feats), BF16),
            shape_of((8, span, feats), BF16),
            shape_of((8, half_rows, feats), BF16),
            shape_of((8, span, feats), BF16),
            shape_of((8, half_rows, feats), BF16),
        ],
        compiler_params=params(56),
        cost_estimate=cost(9),
        name="prep",
    )(tab, gates, short_cot, short_cot, long_cot, short_cot, long_cot, short_x, long_x, ln_gain, ln_bias)
    cot_s, norm_s, own_s = (a.reshape(rows_s, feats) for a in (cot_s, norm_s, own_s))
    cot_l = cot_l.reshape(rows_q, feats)
    norm_l, own_l = norm_l.reshape(rows_l, feats), own_l.reshape(rows_l, feats)
    deo = lax.all_to_all(deo, "expert", split_axis=0, concat_axis=0, tiled=True)

    bias_out = b_attn_out.reshape(1, feats)
    w_shapes = [
        shape_of((QKV_ROWS, feats), BF16),
        shape_of((feats, feats), BF16),
        shape_of((8, feats), F32),
    ]

    def vmem(shape, dtype=BF16):
        return pltpu.VMEM(shape, dtype)

    def sems(count):
        return pltpu.SemaphoreType.DMA((count,))

    def attention(kernel, operands, far, key_rows, query_rows, keys, send_shape, more, scratch, counts, name):
        kept = [
            shape_of((query_rows, feats), BF16),
            shape_of((key_rows, feats), BF16),
            shape_of((key_rows, feats), BF16),
            shape_of((4 * pairs, 128, 2 * keys), BF16),
            shape_of((query_rows, feats), BF16),
        ]
        return pl.pallas_call(
            kernel,
            in_specs=[SM] + [ANY] * far + [VM] * (len(operands) - far - 1),
            out_specs=[ANY] * 5 + [VM] * 2 + ([ANY] * 2 + [VM] if more else []),
            out_shape=kept + [shape_of((query_rows, feats), F32), shape_of(send_shape, BF16)] + more,
            scratch_shapes=[vmem(a.shape) for a in operands[1 : far + 1]]
            + [vmem(a.shape) for a in kept]
            + scratch
            + [sems(count) for count in counts],
            compiler_params=params(56),
            cost_estimate=cost(10),
            name=name,
        )(*operands)

    q_s, k_s, v_s, p_s, ctx_s, mid_s, send_s, w_all, wo_all, bqv_all = attention(
        attend_short,
        (tab, norm_s, own_s, raw_own, raw_other, ln_gain, ln_bias, bias_out),
        4, rows_s, rows_s, 128, (experts, 2, span, feats), w_shapes,
        [vmem((QKV_ROWS, feats)), vmem((feats, feats))], (4, 10), "attend_short",
    )
    send_s = send_s.reshape(experts, 2 * span, feats)
    recv_s = lax.all_to_all(send_s, "expert", split_axis=0, concat_axis=0, tiled=True)
    q_l, k_l, v_l, p_l, ctx_l, mid_l, send_l = attention(
        attend_long,
        (tab, norm_l, own_l, w_all, wo_all, bqv_all, ln_gain, ln_bias, bias_out),
        4, rows_l, rows_q, long_span, (experts, half_rows, feats), [],
        [vmem((rows_q, feats))], (4, 8), "attend_long",
    )
    recv_l = lax.all_to_all(send_l, "expert", split_axis=0, concat_axis=0, tiled=True)

    ret_s, dw_s, ga_s = experts_pass(tab, recv_s, deo, 0, w_up, b_up, w_down, b_down, None, None)
    ret_s = lax.all_to_all(ret_s, "expert", split_axis=0, concat_axis=0, tiled=True)
    ret_l, eo_l, dw_l, ga_l = experts_pass(tab, recv_l, deo, 1, w_up, b_up, w_down, b_down, dw_s, ga_s)
    ret_l = lax.all_to_all(ret_l, "expert", split_axis=0, concat_axis=0, tiled=True)
    dw_l = after(dw_l, ret_s)
    expert_grads = lax.psum_scatter(dw_l, "head", scatter_dimension=0, tiled=True)

    def over_head(blocks):
        return [blocks[0]] + [
            lax.ppermute(blocks[d], "head", [(i, i ^ d) for i in range(heads)]) for d in range(1, heads)
        ]

    far = (ret_s, mid_s, cot_s, wo_all, ctx_s, p_s, q_s, k_s, v_s, norm_s, w_all, own_s)
    *zsend_s, dw_attn, small, eo_l = pl.pallas_call(
        back_short,
        in_specs=[SM, SM, VM, ANY] + [ANY] * len(far),
        out_specs=[VM] * heads + [ANY, VM, ANY],
        out_shape=[shape_of((1, 4 * span, feats), BF16)] * heads
        + [
            shape_of((4 * feats, feats), BF16),
            shape_of((8, feats), F32),
            shape_of(eo_l.shape, BF16),
        ],
        input_output_aliases={3: heads + 2},
        scratch_shapes=[vmem(a.shape, a.dtype) for a in far]
        + [vmem((2 * heads, span, feats))] * 2
        + [vmem((4 * feats, feats)), vmem((rows_s, feats), F32)]
        + [vmem((rows_s, feats))] * 5
        + [vmem((rows_s, feats), F32), sems(len(far)), sems(2)],
        compiler_params=params(56),
        cost_estimate=cost(12),
        name="back_short",
    )(tab, gates, ln_gain, eo_l, *far)
    out_l = lax.all_to_all(eo_l, "expert", split_axis=0, concat_axis=0, tiled=True)
    home_s = over_head(zsend_s)
    far = (ret_l, mid_l, cot_l, norm_l, wo_all, ctx_l, p_l, q_l, k_l, v_l, dw_attn, w_all, own_l)
    zsend_l, packed = pl.pallas_call(
        back_long,
        in_specs=[SM, VM, VM, VM] + [ANY] * len(far),
        out_specs=[VM, ANY],
        out_shape=[
            shape_of((heads, long_span, feats), BF16),
            shape_of((experts, heads, SLICE_ROWS, 128), BF16),
        ],
        scratch_shapes=[vmem(a.shape, a.dtype) for a in far]
        + [
            vmem((experts, heads, SLICE_ROWS, 128)),
            vmem((rows_q, feats)),
            vmem((rows_q, feats), F32),
            vmem((rows_q, feats)),
            vmem((rows_q, feats)),
            vmem((rows_q, feats)),
            vmem((rows_l, feats)),
            vmem((rows_l, feats)),
            vmem((rows_l, feats), F32),
            vmem((experts * SLICE_ROWS, feats), F32),
            sems(len(far)),
            sems(2),
        ],
        compiler_params=params(56),
        cost_estimate=cost(17),
        name="back_long",
    )(tab, ln_gain, small, ga_l, *far)
    arrived = lax.all_to_all(packed, "expert", split_axis=0, concat_axis=0, tiled=True)
    zsend_l = pl.pallas_call(
        mix_long,
        in_specs=[SM, SM] + [VM] * 3,
        out_specs=[VM] * heads,
        out_shape=[shape_of((1, half_rows + long_span, feats), BF16)] * heads,
        scratch_shapes=[vmem((heads, half_rows, feats))],
        compiler_params=params(56),
        cost_estimate=cost(3),
        name="mix_long",
    )(tab, gates, out_l, mid_l, zsend_l)
    through = (*home_s, *zsend_l)
    terms = pl.pallas_call(
        collect_kernel,
        in_specs=[VM] + [ANY] * len(through),
        out_specs=[VM] * heads + [ANY] * len(through),
        out_shape=[shape_of((1, SLICE_ROWS, 128), BF16)] * heads
        + [shape_of(a.shape, a.dtype) for a in through],
        input_output_aliases={1 + i: heads + i for i in range(len(through))},
        compiler_params=params(56),
        cost_estimate=cost(0.1),
        name="collect",
    )(arrived, *through)
    home_s, zsend_l = terms[heads : 2 * heads], terms[2 * heads :]
    terms = sum(part.astype(F32) for part in over_head(terms[:heads])).astype(BF16)
    home_l = over_head(zsend_l)
    attn_grads = lax.all_gather(terms[0], "expert", axis=0, tiled=True)
    chunk = w_up.shape[2] // 4
    grad_up, grad_up_b, grad_down, grad_down_b = pl.pallas_call(
        finish_experts,
        in_specs=[SM, VM],
        out_specs=[VM] * 4,
        out_shape=[
            shape_of((1, feats, chunk), F32),
            shape_of((1, chunk), F32),
            shape_of((1, chunk, feats), F32),
            shape_of((1, feats // heads), F32),
        ],
        compiler_params=params(56),
        cost_estimate=cost(0.1),
        name="finish_experts",
    )(tab, expert_grads)
    grad_qkv, grad_qv, grad_wo, grad_gain, grad_shift, grad_bo, grad_task, grad_gate = pl.pallas_call(
        finish_kernel,
        in_specs=[VM] * 5,
        out_specs=[VM] * 8,
        out_shape=[
            shape_of((3, feats, 128), F32),
            shape_of((2, 128), F32),
            shape_of((128, feats), F32),
            shape_of((2, feats), F32),
            shape_of((2, feats), F32),
            shape_of((1, feats), F32),
            shape_of((tasks, feats), F32),
            shape_of((experts, feats), F32),
        ],
        compiler_params=params(56),
        cost_estimate=cost(0.1),
        name="finish",
    )(attn_grads, expert_ids.T, gates, task_emb, gate_w.T)
    short_out, long_out, short_dx, long_dx = pl.pallas_call(
        place_kernel,
        in_specs=[SM] + [VM] * (2 * heads) + [ANY] * 2,
        out_specs=[VM] * 4,
        out_shape=[
            shape_of((8, span, feats), BF16),
            shape_of((2, long_span, feats), BF16),
            shape_of((8, span, feats), F32),
            shape_of((2, long_span, feats), F32),
        ],
        compiler_params=params(56),
        cost_estimate=cost(0.1),
        name="place",
    )(tab, *home_s, *home_l, grad_bo, grad_down_b)

    return (
        short_out,
        long_out,
        short_dx,
        long_dx,
        grad_gain,
        grad_shift,
        grad_qkv,
        grad_qv,
        grad_wo,
        grad_bo.reshape(feats),
        grad_up,
        grad_up_b,
        grad_down,
        grad_down_b,
        grad_task,
        grad_gate.T,
    )


def solution(mesh):
    return jax.shard_map(
        per_device,
        mesh=mesh,
        in_specs=(
            P("expert", None, None),
            P("expert", None, None),
            P("expert", None, None),
            P("expert", None, None),
            P("expert"),
            P("expert"),
            P("expert"),
            P("expert"),
            P(),
            P(),
            P(),
            P(None, None, "head"),
            P(None, "head"),
            P("head", None),
            P(),
            P("expert", None, None),
            P("expert", None),
            P("expert", None, None),
            P("expert", None),
            P(),
            P(),
        ),
        out_specs=(
            P(("expert", "head"), None, None),
            P(("expert", "head"), None, None),
            P(("expert", "head"), None, None),
            P(("expert", "head"), None, None),
            P(),
            P(),
            P(None, None, "head"),
            P(None, "head"),
            P("head", None),
            P(),
            P("expert", None, "head"),
            P("expert", "head"),
            P("expert", "head", None),
            P("expert", "head"),
            P(),
            P(),
        ),
        check_vma=False,
    )
```

```python
import functools

import jax
import jax.numpy as jnp
from jax import lax
from jax.experimental import pallas as pl
from jax.experimental.pallas import tpu as pltpu
from jax.sharding import PartitionSpec as P

HEAD_DIM = 64


HIGHEST = lax.Precision.HIGHEST
CONTRACT_ROWS = (((0,), (0,)), ((), ()))
CONTRACT_COLS = (((1,), (1,)), ((), ()))


def layer_norm(values, gain, shift):
    centred = values - jnp.mean(values, axis=-1, keepdims=True)
    spread = jnp.mean(centred * centred, axis=-1, keepdims=True)
    return centred * lax.rsqrt(spread + 1e-05) * gain + shift


def lookup(table, index):
    hits = index[..., None] == jnp.arange(table.shape[0], dtype=jnp.int32)
    return jnp.sum(jnp.where(hits, table, jnp.zeros((), table.dtype)), axis=-1)


def route_slots(tasks, expert_ids, capacity, experts):
    task_hits = tasks[:, None] == jnp.arange(expert_ids.shape[0], dtype=jnp.int32)
    chosen = jnp.sum(jnp.where(task_hits[:, :, None], expert_ids[None, :, :], 0), axis=1).reshape(
        -1
    )
    routes = chosen.shape[0]
    owner_hits = (chosen[:, None] == jnp.arange(experts, dtype=jnp.int32)).astype(jnp.int32)
    earlier = jnp.cumsum(owner_hits, axis=0) - owner_hits
    ranking = jnp.sum(earlier * owner_hits, axis=1)
    slot_key = chosen * capacity + ranking
    slot_hits = slot_key[:, None] == jnp.arange(experts * capacity, dtype=jnp.int32)
    return jnp.sum(jnp.where(slot_hits, jnp.arange(routes, dtype=jnp.int32)[:, None], 0), axis=0)


def masked_scores(queries, key_rows, lengths):
    positions = key_rows.shape[1]
    scores = jnp.einsum(
        "blhd,bmhd->bhlm", queries, key_rows, preferred_element_type=jnp.float32
    ) * HEAD_DIM ** (-0.5)
    visible = (
        jnp.arange(positions, dtype=jnp.int32)[None, None, None, :] < lengths[:, None, None, None]
    )
    return jnp.where(visible, scores, -1e30)


def attend(normed, lengths, weights, biases, head_count):
    sentences, positions, features = normed.shape
    flattened = normed.reshape(-1, features)
    shape_heads = (sentences, positions, head_count, HEAD_DIM)

    def project(index, offset):
        return (
            (jnp.dot(flattened, weights[index], preferred_element_type=jnp.float32) + offset)
            .astype(jnp.bfloat16)
            .reshape(shape_heads)
        )

    queries = project(0, biases[0])
    key_rows = project(1, 0.0)
    values = project(2, biases[1])
    scores = masked_scores(queries, key_rows, lengths)
    highest = jnp.max(scores, axis=-1, keepdims=True)
    shifted = jnp.exp(scores - highest)
    totals = jnp.sum(shifted, axis=-1, keepdims=True)
    attn_probs = (shifted / totals).astype(jnp.bfloat16)
    log_total = highest + jnp.log(totals)
    context = jnp.einsum(
        "bhlm,bmhd->blhd", attn_probs, values, preferred_element_type=jnp.float32
    ).astype(jnp.bfloat16)
    return (queries, key_rows, values, context.reshape(sentences, positions, -1), log_total)


def attend_back(normed, lengths, kept, grad_out, weights, out_weight):
    queries, key_rows, values, context, log_total = kept
    features = normed.shape[-1]
    head_cols = context.shape[-1]
    grad_flat = grad_out.reshape(-1, features)
    context_flat = context.reshape(-1, head_cols)
    grad_context = (
        lax.dot_general(grad_flat, out_weight, CONTRACT_COLS, preferred_element_type=jnp.float32)
        .astype(jnp.bfloat16)
        .reshape(queries.shape)
    )
    grad_out_weight = lax.dot_general(
        context_flat, grad_flat, CONTRACT_ROWS, preferred_element_type=jnp.float32
    )
    probs = jnp.exp(masked_scores(queries, key_rows, lengths) - log_total)
    grad_probs = jnp.einsum(
        "blhd,bmhd->bhlm", grad_context, values, preferred_element_type=jnp.float32
    )
    grad_values = jnp.einsum(
        "bhlm,blhd->bmhd",
        probs.astype(jnp.bfloat16),
        grad_context,
        preferred_element_type=jnp.float32,
    ).astype(jnp.bfloat16)
    grad_scores = (
        probs * (grad_probs - jnp.sum(probs * grad_probs, axis=-1, keepdims=True))
    ).astype(jnp.bfloat16)
    scaling = HEAD_DIM ** (-0.5)
    grad_queries = (
        jnp.einsum("bhlm,bmhd->blhd", grad_scores, key_rows, preferred_element_type=jnp.float32)
        * scaling
    ).astype(jnp.bfloat16)
    grad_keys = (
        jnp.einsum("bhlm,blhd->bmhd", grad_scores, queries, preferred_element_type=jnp.float32)
        * scaling
    ).astype(jnp.bfloat16)
    normed_flat = normed.reshape(-1, features)
    members = [member.reshape(-1, head_cols) for member in (grad_queries, grad_keys, grad_values)]
    grad_weights = jnp.stack(
        [
            lax.dot_general(normed_flat, member, CONTRACT_ROWS, preferred_element_type=jnp.float32)
            for member in members
        ]
    )
    grad_biases = jnp.stack(
        [
            jnp.sum(members[0].astype(jnp.float32), axis=0),
            jnp.sum(members[2].astype(jnp.float32), axis=0),
        ]
    )
    grad_normed = lax.dot_general(
        members[0], weights[0], CONTRACT_COLS, preferred_element_type=jnp.float32
    )
    grad_normed = grad_normed + lax.dot_general(
        members[1], weights[1], CONTRACT_COLS, preferred_element_type=jnp.float32
    )
    grad_normed = grad_normed + lax.dot_general(
        members[2], weights[2], CONTRACT_COLS, preferred_element_type=jnp.float32
    )
    return (grad_normed.reshape(normed.shape), grad_weights, grad_out_weight, grad_biases)


def group_rows(first_rows, second_rows):
    return (
        lax.all_gather(first_rows, "head", axis=0, tiled=True),
        lax.all_gather(second_rows, "head", axis=0, tiled=True),
    )


def per_device_wide(
    short_x,
    long_x,
    short_cot,
    long_cot,
    short_len,
    long_len,
    short_task,
    long_task,
    expert_ids,
    ln_gain,
    ln_bias,
    w_qkv,
    b_qv,
    w_attn_out,
    b_attn_out,
    w_up,
    b_up,
    w_down,
    b_down,
    task_emb,
    gate_w,
):
    heads_here = lax.axis_size("head")
    head_place = lax.axis_index("head")
    experts = lax.axis_size("expert")
    short_group, short_span, features = short_x.shape
    long_group, long_span = (long_x.shape[0], long_x.shape[1])
    short_dev = short_group // heads_here
    long_dev = long_group // heads_here
    hidden_width = w_up.shape[2]
    tasks_total = expert_ids.shape[0]
    cap_short = 2 * short_group // experts
    cap_long = 2 * long_group // experts
    piece_rows = (cap_short * short_span + cap_long * long_span) // heads_here
    short_total = short_group * short_span
    all_rows = short_total + long_group * long_span
    expert_hits = (expert_ids[:, :, None] == jnp.arange(experts, dtype=jnp.int32)).astype(
        jnp.float32
    )
    chosen_cols = jnp.einsum("tke,de->tkd", expert_hits, gate_w, precision=HIGHEST)
    gate_probs = jax.nn.softmax(jnp.sum(task_emb[:, None, :] * chosen_cols, axis=-1), axis=-1)
    short_slots = route_slots(short_task, expert_ids, cap_short, experts)
    long_slots = route_slots(long_task, expert_ids, cap_long, experts)
    offsets = head_place * piece_rows + jnp.arange(piece_rows, dtype=jnp.int32)
    owners = jnp.arange(experts, dtype=jnp.int32)[:, None]
    in_short = jnp.broadcast_to(offsets < cap_short * short_span, (experts, piece_rows))
    short_pos = offsets % short_span
    long_offset = jnp.maximum(offsets - cap_short * short_span, 0)
    long_pos = long_offset % long_span
    short_route = lookup(
        short_slots, owners * cap_short + jnp.minimum(offsets // short_span, cap_short - 1)
    )
    long_route = lookup(
        long_slots, owners * cap_long + jnp.minimum(long_offset // long_span, cap_long - 1)
    )
    short_sent = short_route // 2
    long_sent = long_route // 2
    position = jnp.where(in_short, short_pos, long_pos)
    target = jnp.where(
        in_short,
        short_sent * short_span + short_pos,
        short_total + long_sent * long_span + long_pos,
    )
    task_rows = jnp.where(in_short, lookup(short_task, short_sent), lookup(long_task, long_sent))
    length_rows = jnp.where(in_short, lookup(short_len, short_sent), lookup(long_len, long_sent))
    live_rows = (position < length_rows).astype(jnp.float32)
    gate_index = task_rows * 2 + jnp.where(in_short, short_route % 2, long_route % 2)
    gate_rows = lookup(gate_probs.reshape(-1), gate_index)
    short_mask = (jnp.arange(short_span, dtype=jnp.int32)[None, :] < short_len[:, None]).astype(
        jnp.float32
    )[:, :, None]
    long_mask = (jnp.arange(long_span, dtype=jnp.int32)[None, :] < long_len[:, None]).astype(
        jnp.float32
    )[:, :, None]
    short_start = head_place * short_dev
    long_start = head_place * long_dev
    own_short_mask = lax.dynamic_slice_in_dim(short_mask, short_start, short_dev, 0)
    own_long_mask = lax.dynamic_slice_in_dim(long_mask, long_start, long_dev, 0)
    short_in = short_x.astype(jnp.float32)
    long_in = long_x.astype(jnp.float32)
    own_short_in = lax.dynamic_slice_in_dim(short_in, short_start, short_dev, 0)
    own_long_in = lax.dynamic_slice_in_dim(long_in, long_start, long_dev, 0)
    attn_qkv, attn_qv, attn_out_w = (w_qkv, b_qv, w_attn_out)
    short_src, long_src = (short_in, long_in)
    short_lens, long_lens = (short_len, long_len)
    head_cols = attn_qkv.shape[2]
    head_count = head_cols // HEAD_DIM
    short_normed = layer_norm(short_src, ln_gain[0], ln_bias[0]).astype(jnp.bfloat16)
    long_normed = layer_norm(long_src, ln_gain[0], ln_bias[0]).astype(jnp.bfloat16)
    short_kept = attend(short_normed, short_lens, attn_qkv, attn_qv, head_count)
    long_kept = attend(long_normed, long_lens, attn_qkv, attn_qv, head_count)
    short_part = jnp.dot(
        short_kept[3].reshape(-1, head_cols), attn_out_w, preferred_element_type=jnp.float32
    ).reshape(short_src.shape)
    long_part = jnp.dot(
        long_kept[3].reshape(-1, head_cols), attn_out_w, preferred_element_type=jnp.float32
    ).reshape(long_src.shape)
    short_sum, long_sum = (
        lax.psum(short_part.astype(jnp.bfloat16), "head").astype(jnp.float32),
        lax.psum(long_part.astype(jnp.bfloat16), "head").astype(jnp.float32),
    )
    short_mid = short_in + short_mask * (short_sum + b_attn_out)
    long_mid = long_in + long_mask * (long_sum + b_attn_out)
    short_mixin = layer_norm(short_mid, ln_gain[1], ln_bias[1]).astype(jnp.bfloat16)
    long_mixin = layer_norm(long_mid, ln_gain[1], ln_bias[1]).astype(jnp.bfloat16)
    own_short_mid = lax.dynamic_slice_in_dim(short_mid, short_start, short_dev, 0)
    own_long_mid = lax.dynamic_slice_in_dim(long_mid, long_start, long_dev, 0)
    mixin_rows = jnp.concatenate(
        [short_mixin.reshape(-1, features), long_mixin.reshape(-1, features)], axis=0
    )
    outgoing = mixin_rows[target]
    received = lax.all_to_all(outgoing, "expert", split_axis=0, concat_axis=0, tiled=True)
    inputs = received.reshape(-1, features)
    gelu_in = jnp.dot(inputs, w_up[0], preferred_element_type=jnp.float32) + b_up[0]
    hidden = jax.nn.gelu(gelu_in).astype(jnp.bfloat16)
    output = (jnp.dot(hidden, w_down[0], preferred_element_type=jnp.float32) + b_down[0]).astype(
        jnp.bfloat16
    )
    returned = lax.all_to_all(
        output.reshape(received.shape), "expert", split_axis=0, concat_axis=0, tiled=True
    )
    wide_shape = received.shape[:2] + (hidden_width,)
    packed = (returned, received, hidden.reshape(wide_shape), gelu_in.reshape(wide_shape))
    returned = packed[0]
    received = packed[1]
    contrib = (gate_rows[:, :, None] * returned.astype(jnp.float32)).reshape(-1, features)
    mixed_rows = jnp.zeros((all_rows, features), jnp.float32).at[target.reshape(-1)].add(contrib)
    short_moe, long_moe = (
        lax.psum_scatter(
            mixed_rows[:short_total].reshape(short_in.shape).astype(jnp.bfloat16),
            "head",
            scatter_dimension=0,
            tiled=True,
        ).astype(jnp.float32),
        lax.psum_scatter(
            mixed_rows[short_total:].reshape(long_in.shape).astype(jnp.bfloat16),
            "head",
            scatter_dimension=0,
            tiled=True,
        ).astype(jnp.float32),
    )
    short_out = (own_short_mid + own_short_mask * short_moe).astype(jnp.bfloat16)
    long_out = (own_long_mid + own_long_mask * long_moe).astype(jnp.bfloat16)
    cot_rows = jnp.concatenate(
        [short_cot.reshape(-1, features), long_cot.reshape(-1, features)], axis=0
    )
    cot_picked = cot_rows[target].astype(jnp.float32)
    grad_sent = ((gate_rows * live_rows)[:, :, None] * cot_picked).astype(jnp.bfloat16)
    gate_terms = live_rows * jnp.sum(cot_picked * returned.astype(jnp.float32), axis=-1)
    gate_part = jnp.sum(
        jnp.where(
            gate_index[:, :, None] == jnp.arange(2 * tasks_total, dtype=jnp.int32),
            gate_terms[:, :, None],
            0.0,
        ),
        axis=(0, 1),
    )
    grad_arrived = lax.all_to_all(grad_sent, "expert", split_axis=0, concat_axis=0, tiled=True)
    inputs = received.reshape(-1, features)
    hidden = packed[2].reshape(-1, hidden_width)
    gelu_in = packed[3].reshape(-1, hidden_width)
    grad_output = grad_arrived.reshape(-1, features)
    grad_hidden = lax.dot_general(
        grad_output, w_down[0], CONTRACT_COLS, preferred_element_type=jnp.float32
    )
    grad_gelu = jax.vjp(jax.nn.gelu, gelu_in)[1](grad_hidden)[0].astype(jnp.bfloat16)
    grad_up_w = lax.dot_general(
        inputs, grad_gelu, CONTRACT_ROWS, preferred_element_type=jnp.float32
    )
    grad_up_b = jnp.sum(grad_gelu.astype(jnp.float32), axis=0)
    grad_down_w = lax.dot_general(
        hidden, grad_output, CONTRACT_ROWS, preferred_element_type=jnp.float32
    )
    grad_down_b = jnp.sum(grad_output.astype(jnp.float32), axis=0)
    grad_inputs = (
        lax.dot_general(grad_gelu, w_up[0], CONTRACT_COLS, preferred_element_type=jnp.float32)
        .astype(jnp.bfloat16)
        .reshape(received.shape)
    )
    grad_home = lax.all_to_all(grad_inputs, "expert", split_axis=0, concat_axis=0, tiled=True)
    shard_up_w, shard_up_b, shard_down_w, shard_down_b = (
        lax.psum_scatter(
            grad_up_w[None].astype(jnp.bfloat16), "head", scatter_dimension=2, tiled=True
        ).astype(jnp.float32),
        lax.psum_scatter(
            grad_up_b[None].astype(jnp.bfloat16), "head", scatter_dimension=1, tiled=True
        ).astype(jnp.float32),
        lax.psum_scatter(
            grad_down_w[None].astype(jnp.bfloat16), "head", scatter_dimension=1, tiled=True
        ).astype(jnp.float32),
        lax.psum_scatter(
            grad_down_b[None].astype(jnp.bfloat16), "head", scatter_dimension=1, tiled=True
        ).astype(jnp.float32),
    )
    grad_mixin = (
        jnp.zeros((all_rows, features), jnp.float32)
        .at[target.reshape(-1)]
        .add(grad_home.reshape(-1, features).astype(jnp.float32))
    )
    short_dmix, long_dmix = (
        lax.psum_scatter(
            grad_mixin[:short_total].reshape(short_in.shape).astype(jnp.bfloat16),
            "head",
            scatter_dimension=0,
            tiled=True,
        ).astype(jnp.float32),
        lax.psum_scatter(
            grad_mixin[short_total:].reshape(long_in.shape).astype(jnp.bfloat16),
            "head",
            scatter_dimension=0,
            tiled=True,
        ).astype(jnp.float32),
    )
    short_dmid, short_gain_two, short_shift_two = jax.vjp(
        layer_norm, own_short_mid, ln_gain[1], ln_bias[1]
    )[1](short_dmix)
    long_dmid, long_gain_two, long_shift_two = jax.vjp(
        layer_norm, own_long_mid, ln_gain[1], ln_bias[1]
    )[1](long_dmix)
    short_dmid = short_dmid + lax.dynamic_slice_in_dim(short_cot, short_start, short_dev, 0).astype(
        jnp.float32
    )
    long_dmid = long_dmid + lax.dynamic_slice_in_dim(long_cot, long_start, long_dev, 0).astype(
        jnp.float32
    )
    short_dattn = (own_short_mask * short_dmid).astype(jnp.bfloat16)
    long_dattn = (own_long_mask * long_dmid).astype(jnp.bfloat16)
    bias_out_grad = jnp.sum(short_dattn.astype(jnp.float32), axis=(0, 1)) + jnp.sum(
        long_dattn.astype(jnp.float32), axis=(0, 1)
    )
    attn_short_grad, attn_long_grad = group_rows(short_dattn, long_dattn)
    short_back = attend_back(
        short_normed, short_lens, short_kept, attn_short_grad, attn_qkv, attn_out_w
    )
    long_back = attend_back(long_normed, long_lens, long_kept, attn_long_grad, attn_qkv, attn_out_w)
    short_dnormed, long_dnormed = (
        lax.psum_scatter(
            short_back[0].astype(jnp.bfloat16), "head", scatter_dimension=0, tiled=True
        ).astype(jnp.float32),
        lax.psum_scatter(
            long_back[0].astype(jnp.bfloat16), "head", scatter_dimension=0, tiled=True
        ).astype(jnp.float32),
    )
    short_dln, short_gain_one, short_shift_one = jax.vjp(
        layer_norm, own_short_in, ln_gain[0], ln_bias[0]
    )[1](short_dnormed)
    long_dln, long_gain_one, long_shift_one = jax.vjp(
        layer_norm, own_long_in, ln_gain[0], ln_bias[0]
    )[1](long_dnormed)
    short_dx = short_dmid + short_dln
    long_dx = long_dmid + long_dln
    qkv_terms = short_back[1] + long_back[1]
    out_terms = short_back[2] + long_back[2]
    bias_terms = short_back[3] + long_back[3]
    grad_qkv, grad_attn_weight, grad_qv = (
        lax.psum(qkv_terms.astype(jnp.bfloat16), "expert").astype(jnp.float32),
        lax.psum(out_terms.astype(jnp.bfloat16), "expert").astype(jnp.float32),
        lax.psum(bias_terms.astype(jnp.bfloat16), "expert").astype(jnp.float32),
    )
    gain_grads = jnp.stack([short_gain_one + long_gain_one, short_gain_two + long_gain_two])
    shift_grads = jnp.stack([short_shift_one + long_shift_one, short_shift_two + long_shift_two])
    grad_gain, grad_shift, grad_bias_out, gate_total = lax.psum(
        (gain_grads, shift_grads, bias_out_grad, gate_part), ("expert", "head")
    )
    gate_grad = gate_total.reshape(tasks_total, 2)
    logit_grad = gate_probs * (gate_grad - jnp.sum(gate_probs * gate_grad, axis=-1, keepdims=True))
    grad_task = jnp.sum(logit_grad[:, :, None] * chosen_cols, axis=1)
    grad_gate = jnp.einsum("tke,tk,td->de", expert_hits, logit_grad, task_emb, precision=HIGHEST)
    return (
        short_out,
        long_out,
        short_dx,
        long_dx,
        grad_gain,
        grad_shift,
        grad_qkv,
        grad_qv,
        grad_attn_weight,
        grad_bias_out,
        shard_up_w,
        shard_up_b,
        shard_down_w,
        shard_down_b,
        grad_task,
        grad_gate,
    )


BF16 = jnp.bfloat16
F32 = jnp.float32
SLICE_ROWS = 272
HALF_PACK = 1088
QKV_ROWS = 1536
MISC_ROW = 2048
GRAD_ROWS = 1040


def mm(a, b):
    return lax.dot_general(a, b, (((1,), (0,)), ((), ())), preferred_element_type=F32)


def mm_nt(a, b):
    return lax.dot_general(a, b, (((1,), (1,)), ((), ())), preferred_element_type=F32)


def mm_tn(a, b):
    return lax.dot_general(a, b, (((0,), (0,)), ((), ())), preferred_element_type=F32)


def iota(shape, dim):
    return lax.broadcasted_iota(jnp.int32, shape, dim)


def params(mebibytes):
    return pltpu.CompilerParams(vmem_limit_bytes=mebibytes * 1024 * 1024)


def cost(micros):
    return pl.CostEstimate(flops=0, bytes_accessed=int(micros * 3.7e6), transcendentals=0)


VM = pl.BlockSpec(memory_space=pltpu.VMEM)
SM = pl.BlockSpec(memory_space=pltpu.SMEM)
ANY = pl.BlockSpec(memory_space=pl.ANY)


def pack_kernel(qkv, qv, wo, out):
    core = lax.axis_index("expert") % 2
    feats = qkv.shape[1]
    split = HALF_PACK - 2 * feats

    @pl.when(core == 0)
    def _():
        out[0:feats, :] = qkv[0]
        out[feats : 2 * feats, :] = qkv[1]
        out[2 * feats :, :] = qkv[2, 0:split, :]

    @pl.when(core != 0)
    def _():
        at = feats - split
        out[0:at, :] = qkv[2, split:, :]
        for c in range(4):
            out[at + 128 * c : at + 128 * (c + 1), :] = wo[:, 128 * c : 128 * (c + 1)]
        at += 4 * 128
        out[at:, :] = jnp.zeros((HALF_PACK - at, 128), BF16)
        high = qv[...].astype(BF16)
        low = (qv[...] - high.astype(F32)).astype(BF16)
        out[at : at + 2, :] = high
        out[at + 2 : at + 4, :] = low


def split_cycles(pair_left, pair_right, eye, count):
    step = mm(pair_left.astype(BF16), pair_right.astype(BF16))
    reach = jnp.minimum(eye + step, 1.0)
    hops = 1
    while hops < count // 2:
        wide = reach.astype(BF16)
        reach = jnp.minimum(mm(wide, wide), 1.0)
        hops *= 2
    lanes = iota((count, count), 1).astype(F32)
    lowest = jnp.min(jnp.where(reach > 0.5, lanes, float(count)), axis=1, keepdims=True)
    lowest_row = jnp.sum(eye * lowest, axis=0, keepdims=True)
    other = jnp.sum(pair_left * lowest_row, axis=1, keepdims=True)
    return (lowest > other).astype(F32)


def route_kernel(st_ref, sl_ref, lt_ref, ll_ref, ids_ref, temb_ref, gw_ref, tab_ref, gate_ref):
    here = lax.axis_index("head").astype(jnp.int32)
    group = lax.axis_index("expert").astype(jnp.int32)
    shorts = st_ref.shape[1]
    longs = lt_ref.shape[1]
    tasks = ids_ref.shape[1]
    per_owner = shorts // 4
    mine = here.astype(F32)

    def eye_of(n):
        return (iota((n, n), 0) == iota((n, n), 1)).astype(F32)

    def col(row, eye):
        return jnp.sum(eye * row, axis=1, keepdims=True)

    def row(column, eye):
        return jnp.sum(eye * column, axis=0, keepdims=True)

    eye = eye_of(shorts)
    at_sub, at_lane = iota((shorts, shorts), 0), iota((shorts, shorts), 1)
    off_diag = 1.0 - eye
    task_row = st_ref[...].astype(F32)
    task_col = col(task_row, eye)
    same_task = (task_col == task_row).astype(F32)
    earlier = (at_lane < at_sub).astype(F32)
    later = (at_lane > at_sub).astype(F32)
    rank_col = jnp.sum(same_task * earlier, axis=1, keepdims=True)
    rank_row = jnp.sum(same_task * later, axis=0, keepdims=True)
    first_of_pair = jnp.floor(rank_col * 0.5) == jnp.floor(rank_row * 0.5)
    pair_right = same_task * first_of_pair.astype(F32) * off_diag
    pair_left = ((at_sub // 2) == (at_lane // 2)).astype(F32) * off_diag
    major = split_cycles(pair_left, pair_right, eye, shorts)
    same_major = (major == row(major, eye)).astype(F32)
    pair_right = same_task * same_major * off_diag
    pair_left = ((at_sub // 4) == (at_lane // 4)).astype(F32) * same_major * off_diag
    minor = split_cycles(pair_left, pair_right, eye, shorts)
    colour = 2.0 * major + minor
    same_owner = ((at_sub // per_owner) == (at_lane // per_owner)).astype(F32)
    same_colour = (colour == row(colour, eye)).astype(F32)
    place = jnp.sum(same_owner * same_colour * earlier, axis=1, keepdims=True)

    sent = iota((shorts, 128), 0)
    lane = iota((shorts, 128), 1)
    sent_f = sent.astype(F32)
    lane_f = lane.astype(F32)
    length_col = col(sl_ref[...].astype(F32), eye)
    own = ((task_col == lane_f) & (colour == mine)).astype(F32)
    owner_col = (iota((shorts, 1), 0) // per_owner).astype(F32)

    def put(r, values):
        tab_ref[r : r + 1, :] = values.astype(jnp.int32)

    def put_away(r, values, low):
        tab_ref[r : r + 1, :] = values.astype(jnp.int32) ^ (here * low)

    def total(values):
        return jnp.sum(values, axis=0, keepdims=True)

    tab_ref[...] = jnp.zeros_like(tab_ref)
    put(0, total(own * sent_f))
    put(1, total(own * length_col))
    put_away(2, total(own * (owner_col * 2.0 + place)), 2)
    natural = (sent == lane + here * per_owner) & (lane < per_owner)
    put_away(6, total(natural.astype(F32) * (colour * 2.0 + place)), 2)

    eye_l = eye_of(longs)
    sub_l, lane_l = iota((longs, longs), 0), iota((longs, longs), 1)
    ltask_row = lt_ref[...].astype(F32)
    ltask_col = col(ltask_row, eye_l)
    right_l = (ltask_col == ltask_row).astype(F32) * (1.0 - eye_l)
    left_l = ((sub_l // 2) == (lane_l // 2)).astype(F32) * (1.0 - eye_l)
    kappa = split_cycles(left_l, right_l, eye_l, longs)
    parity_col = ltask_col - 2.0 * jnp.floor(ltask_col * 0.5)
    parity = jnp.max(parity_col, axis=0, keepdims=True)
    lsent = iota((longs, 128), 0)
    llane = iota((longs, 128), 1)
    unit_task = parity + 2.0 * llane.astype(F32)
    mine_l = (here % 2).astype(F32)
    own_l = ((ltask_col == unit_task) & (kappa == mine_l)).astype(F32)
    llen_col = col(ll_ref[...].astype(F32), eye_l)
    put(3, total(own_l * lsent.astype(F32)))
    put_away(16, total(own_l * (lsent // (longs // 4)).astype(F32)), 1)
    put(4, total(own_l * llen_col))
    row_lane = iota((1, 128), 1)
    row_lane_f = row_lane.astype(F32)
    put(5, parity + 2.0 * row_lane_f)
    natural_l = (lsent == llane + here * (longs // 4)) & (llane < longs // 4)
    put_away(7, total(natural_l.astype(F32) * kappa), 1)
    put_away(15, total(natural_l.astype(F32) * (kappa + 2.0)), 1)

    ids = ids_ref[...].astype(F32)
    eye_t = eye_of(tasks)
    e_first, e_second = col(ids[0:1, :], eye_t), col(ids[1:2, :], eye_t)
    tsub = iota((tasks, 128), 0).astype(F32)
    tlane = iota((tasks, 128), 1).astype(F32)
    diag = (tsub == tlane).astype(F32)
    put(8, total(diag * e_first))
    put(9, total(diag * e_second))
    task_first = total((e_first == tlane).astype(F32) * tsub)
    task_second = total((e_second == tlane).astype(F32) * tsub)
    put(10, task_first)
    put(11, task_second)
    first_parity = task_first - 2.0 * jnp.floor(task_first * 0.5)
    use_second = first_parity != parity
    put(12, use_second.astype(F32))
    unit_of = jnp.where(use_second, task_second, task_first)
    put(13, jnp.floor((unit_of - parity) * 0.5))
    half = here // 2
    tab_ref[14:15, :] = jnp.where(row_lane == 0, half, jnp.where(row_lane == 1, here, group))

    logits = lax.dot_general(
        temb_ref[...],
        gw_ref[...],
        (((1,), (1,)), ((), ())),
        preferred_element_type=F32,
        precision=HIGHEST,
    )
    ecols = iota((tasks, logits.shape[1]), 1).astype(F32)
    first = jnp.sum(jnp.where(ecols == e_first, logits, 0.0), axis=1, keepdims=True)
    second = jnp.sum(jnp.where(ecols == e_second, logits, 0.0), axis=1, keepdims=True)
    top = jnp.maximum(first, second)
    first, second = jnp.exp(first - top), jnp.exp(second - top)
    denominator = first + second
    gate_ref[...] = jnp.where(
        tlane == 0.0, first / denominator, jnp.where(tlane == 1.0, second / denominator, 0.0)
    )


def norm_stats(values):
    centred = values - jnp.mean(values, axis=-1, keepdims=True)
    scale = lax.rsqrt(jnp.mean(centred * centred, axis=-1, keepdims=True) + 1e-05)
    return centred * scale, scale


def prep_kernel(
    tab, gates, cs0, cs1, cl, csb, clb, xs, xl, gain, bias,
    deo, cb_s, cb_l, ns, nl, xb_s, xb_l,
):
    e = pl.program_id(0)
    span = cs0.shape[1]
    for k, ref in ((0, cs0), (1, cs1)):
        t = tab[10 + k, e]
        keep = iota((span, 1), 0) < tab[1, t]
        deo[0, span * k : span * (k + 1), :] = jnp.where(
            keep, gates[t, k] * ref[0].astype(F32), 0.0
        ).astype(BF16)
    half_rows = cl.shape[1]
    u = tab[13, e]
    gate = gates[tab[5, u], tab[12, e]]
    keep = iota((half_rows, 1), 0) + half_rows * tab[14, 0] < tab[4, u]
    deo[0, 2 * span : 2 * span + half_rows, :] = jnp.where(keep, gate * cl[0].astype(F32), 0.0).astype(BF16)
    parity = (tab[5, 0] % 2).astype(F32)
    deo[0, 2 * span + half_rows :, :] = jnp.full((16, deo.shape[2]), parity, F32).astype(BF16)
    cb_s[...] = csb[...]
    cb_l[...] = clb[...]
    xb_s[...] = xs[...]
    xb_l[...] = xl[...]
    ns[0] = (norm_stats(xs[0].astype(F32))[0] * gain[0:1, :] + bias[0:1, :]).astype(BF16)
    nl[0] = (norm_stats(xl[0].astype(F32))[0] * gain[0:1, :] + bias[0:1, :]).astype(BF16)


def unpack_weights(low, high, w, wo, bqv):
    for h in range(low.shape[0]):
        cols = slice(128 * h, 128 * (h + 1))
        w[0:HALF_PACK, cols] = low[h]
        w[HALF_PACK:QKV_ROWS, cols] = high[h, 0 : QKV_ROWS - HALF_PACK, :]
        for c in range(4):
            at = QKV_ROWS - HALF_PACK + 128 * c
            wo[128 * h : 128 * (h + 1), 128 * c : 128 * (c + 1)] = high[h, at : at + 128, :]
        at = MISC_ROW - HALF_PACK
        lines = high[h, at : at + 16, :].astype(F32)
        bqv[0:2, cols] = lines[0:2] + lines[2:4]


class Copies:
    def __init__(self, sems):
        self.sems = sems
        self.used = 0
        self.open = []

    def start(self, source, target):
        copy = pltpu.make_async_copy(source, target, self.sems.at[self.used])
        copy.start()
        self.used += 1
        self.open.append(copy)
        return copy

    def finish(self):
        for copy in self.open:
            copy.wait()


def pair_masks():
    lanes = iota((1, 128), 1)
    first = (lanes < HEAD_DIM).astype(BF16)
    return first, (1.0 - first.astype(F32)).astype(BF16)


def both_heads(block, masks):
    return jnp.concatenate([block * masks[0], block * masks[1]], axis=0)


def fold_heads(stacked, keys):
    lanes = iota((1, 128), 1)
    return jnp.where(lanes < HEAD_DIM, stacked[:keys], stacked[keys:])


def softmax_pair(scores, visible, keys):
    parts = []
    for part in (scores[:, :keys], scores[:, keys:]):
        part = jnp.where(visible, part, -1e30)
        shifted = jnp.exp(part - jnp.max(part, axis=-1, keepdims=True))
        parts.append(shifted * (1.0 / jnp.sum(shifted, axis=-1, keepdims=True)))
    return jnp.concatenate(parts, axis=1).astype(BF16)


def short_visible(tab, i, span):
    rows, lanes = iota((128, 128), 0), iota((128, 128), 1)
    limit = jnp.where(iota((1, 128), 1) < span, tab[1, 2 * i], tab[1, 2 * i + 1] + span)
    return ((rows // span) == (lanes // span)) & (lanes < limit)


def attend_short(
    tab, norm_h, x_h, own_h, other_h, gain, bias, bo,
    q_h, k_h, v_h, p_h, ctx_h, mid, send, w_h, wo_h, bqv,
    norm, x, own, other, q_ref, k_ref, v_ref, p_ref, ctx, w, wo, in_sems, out_sems,
):
    core = tab[14, 2] % 2
    fetch, leave = Copies(in_sems), Copies(out_sems)
    pieces = [fetch.start(own_h, own), fetch.start(other_h, other), fetch.start(norm_h, norm)]
    have_x = fetch.start(x_h, x)
    for piece in pieces:
        piece.wait()

    @pl.when(core == 0)
    def _():
        unpack_weights(own, other, w, wo, bqv)

    @pl.when(core != 0)
    def _():
        unpack_weights(other, own, w, wo, bqv)

    leave.start(w, w_h)
    leave.start(wo, wo_h)
    feats = norm.shape[1]
    rows = norm[...]
    q_ref[...] = ((mm(rows, w[0:feats, :]) + bqv[0:1, :]).astype(BF16) * HEAD_DIM ** (-0.5)).astype(BF16)
    leave.start(q_ref, q_h)
    k_ref[...] = mm(rows, w[feats : 2 * feats, :]).astype(BF16)
    leave.start(k_ref, k_h)
    v_ref[...] = (mm(rows, w[2 * feats : 3 * feats, :]) + bqv[1:2, :]).astype(BF16)
    leave.start(v_ref, v_h)
    masks = pair_masks()
    span = send.shape[2]
    pairs = feats // 128
    for i in range(norm.shape[0] // 128):
        visible = short_visible(tab, i, span)
        r = slice(128 * i, 128 * (i + 1))
        for p in range(pairs):
            c = slice(128 * p, 128 * (p + 1))
            scores = mm_nt(q_ref[r, c], both_heads(k_ref[r, c], masks))
            probs = softmax_pair(scores, visible, 128)
            p_ref[i * pairs + p] = probs
            ctx[r, c] = mm(probs, both_heads(v_ref[r, c], masks)).astype(BF16)
        leave.start(p_ref.at[pairs * i : pairs * (i + 1)], p_h.at[pairs * i : pairs * (i + 1)])
    leave.start(ctx, ctx_h)
    attn = mm(ctx[...], wo[...]) + bo[...]
    have_x.wait()
    for t in range(send.shape[0]):
        r = slice(span * t, span * (t + 1))
        keep = iota((span, 1), 0) < tab[1, t]
        middle = x[r, :].astype(F32) + jnp.where(keep, attn[r, :], 0.0)
        mid[r, :] = middle
        mixin = (norm_stats(middle)[0] * gain[1:2, :] + bias[1:2, :]).astype(BF16)
        send[tab[8, t], 0] = mixin
        send[tab[9, t], 1] = mixin
    leave.finish()


def attend_long(
    tab, norm_h, x_h, w_h, wo_h, bqv, gain, bias, bo,
    q_h, k_h, v_h, p_h, ctx_h, mid, send,
    norm, x, w, wo, q_ref, k_ref, v_ref, p_ref, ctx, nq, in_sems, out_sems,
):
    fetch, leave = Copies(in_sems), Copies(out_sems)
    have_norm, have_w = fetch.start(norm_h, norm), fetch.start(w_h, w)
    have_wo, have_x = fetch.start(wo_h, wo), fetch.start(x_h, x)
    feats = norm.shape[1]
    half_rows = send.shape[1]
    span = 2 * half_rows
    units = norm.shape[0] // span
    offset = tab[14, 0] * half_rows
    have_norm.wait()
    for u in range(units):
        at = pl.multiple_of(span * u + offset, half_rows)
        nq[half_rows * u : half_rows * (u + 1), :] = norm[pl.ds(at, half_rows), :]
    rows = norm[...]
    have_w.wait()
    q_ref[...] = ((mm(nq[...], w[0:feats, :]) + bqv[0:1, :]).astype(BF16) * HEAD_DIM ** (-0.5)).astype(BF16)
    leave.start(q_ref, q_h)
    k_ref[...] = mm(rows, w[feats : 2 * feats, :]).astype(BF16)
    leave.start(k_ref, k_h)
    v_ref[...] = (mm(rows, w[2 * feats : 3 * feats, :]) + bqv[1:2, :]).astype(BF16)
    leave.start(v_ref, v_h)
    masks = pair_masks()
    pairs = feats // 128
    for u in range(units):
        visible = iota((1, span), 1) < tab[4, u]
        r = slice(half_rows * u, half_rows * (u + 1))
        kr = slice(span * u, span * (u + 1))
        for p in range(pairs):
            c = slice(128 * p, 128 * (p + 1))
            scores = mm_nt(q_ref[r, c], both_heads(k_ref[kr, c], masks))
            probs = softmax_pair(scores, visible, span)
            p_ref[u * pairs + p] = probs
            ctx[r, c] = mm(probs, both_heads(v_ref[kr, c], masks)).astype(BF16)
        leave.start(p_ref.at[pairs * u : pairs * (u + 1)], p_h.at[pairs * u : pairs * (u + 1)])
    leave.start(ctx, ctx_h)
    have_wo.wait()
    attn = mm(ctx[...], wo[...]) + bo[...]
    have_x.wait()
    for u in range(units):
        r = slice(half_rows * u, half_rows * (u + 1))
        keep = iota((half_rows, 1), 0) + offset < tab[4, u]
        at = pl.multiple_of(span * u + offset, half_rows)
        middle = x[pl.ds(at, half_rows), :].astype(F32) + jnp.where(keep, attn[r, :], 0.0)
        mid[r, :] = middle
        mixin = (norm_stats(middle)[0] * gain[1:2, :] + bias[1:2, :]).astype(BF16)
        t = tab[5, u]
        send[tab[8, t]] = mixin
        send[tab[9, t]] = mixin
    leave.finish()


def turn_kernel(up, down, up_t, down_t):
    up_t[...] = up[0].T
    down_t[...] = down[0].T


def turn_weights(w_up, w_down):
    feats, hidden = w_up.shape[1:]
    return pl.pallas_call(
        turn_kernel,
        grid=(4,),
        in_specs=[
            pl.BlockSpec((1, feats, hidden // 4), lambda j: (0, 0, j)),
            pl.BlockSpec((1, hidden // 4, feats), lambda j: (0, j, 0)),
        ],
        out_specs=[
            pl.BlockSpec((hidden // 4, feats), lambda j: (j, 0)),
            pl.BlockSpec((feats, hidden // 4), lambda j: (0, j)),
        ],
        out_shape=[
            jax.ShapeDtypeStruct((hidden, feats), BF16),
            jax.ShapeDtypeStruct((feats, hidden), BF16),
        ],
        compiler_params=params(56),
        cost_estimate=cost(6),
        name="turn",
    )(w_up, w_down)


GELU_A = 0.7978845608028654
GELU_B = 0.044715


def expert_kernel(first, tab, *refs):
    if first:
        x, d, wu, bu, wd, bd, wut, wdt, back, dw, ga, xt, dt, ea, da, hs, ps = refs
        prev = None
    else:
        x, d, wu, bu, wd, bd, wut, wdt, par, prev, ga_in, back, eo, dw, ga, xt, dt, ea, da, hs, ps = refs
    j = pl.program_id(0)
    feats = x.shape[2]
    rows = x.shape[0] * x.shape[1]
    step = 4 * x.shape[1]

    @pl.when(j == 0)
    def _():
        for g in range(x.shape[0]):
            cols = slice(x.shape[1] * g, x.shape[1] * (g + 1))
            xt[:, cols] = x[g].T
            dt[:, cols] = d[g].T
        ea[...] = jnp.broadcast_to(bd[...], ea.shape)
        da[...] = jnp.zeros_like(da)

    for i in range(rows // step):
        r = slice(step * i, step * (i + 1))
        xr = x[4 * i : 4 * i + 4].reshape(step, feats)
        dr = d[4 * i : 4 * i + 4].reshape(step, feats)
        pre = mm(xr, wu[0]) + bu[...]
        square = pre * pre
        half = 0.5 + 0.5 * jnp.tanh(pre * (GELU_A + (GELU_A * GELU_B) * square))
        hidden = (pre * half).astype(BF16)
        half, square = half.astype(BF16), square.astype(BF16)
        slope = half + hidden * (1.0 - half) * (2.0 * GELU_A + (6.0 * GELU_A * GELU_B) * square)
        dpre = mm(dr, wdt[...]).astype(BF16) * slope
        hs[r, :] = hidden
        ps[r, :] = dpre
        ea[r, :] += mm(hidden, wd[0])
        da[r, :] += mm(dpre, wut[...])

    ones = jnp.ones((16, rows), BF16)
    down_bias = mm_nt(ones, dt[...])[0:1, :]
    which = iota((16, 1), 0)
    for c in range(dw.shape[0]):
        cols = slice(feats * c, feats * (c + 1))
        grad_up = mm(xt[...], ps[:, cols])
        grad_down_t = mm(dt[...], hs[:, cols])
        tail = jnp.where(which == 0, mm(ones, ps[:, cols]), jnp.where(which == 1, down_bias, 0.0))
        if prev is not None:
            grad_up += prev[c, 0:feats, :].astype(F32)
            grad_down_t += prev[c, feats : 2 * feats, :].astype(F32)
            tail += prev[c, 2 * feats :, :].astype(F32)
        dw[c, 0:feats, :] = grad_up.astype(BF16)
        dw[c, feats : 2 * feats, :] = grad_down_t.astype(BF16)
        dw[c, 2 * feats :, :] = tail.astype(BF16)

    @pl.when(j == pl.num_programs(0) - 1)
    def _():
        own = tab[14, 2]
        t_first, t_second = tab[10, own], tab[11, own]
        lanes = iota((1, 128), 1)
        as_first = (lanes == 2 * t_first).astype(F32)
        as_second = (lanes == 2 * t_second + 1).astype(F32)
        rows_each = x.shape[1]
        gate_sums = jnp.zeros((1, 128), F32)
        for g in range(x.shape[0]):
            r = slice(rows_each * g, rows_each * (g + 1))
            out = ea[r, :].astype(BF16)
            back[g, 0:rows_each, :] = da[r, :].astype(BF16)
            if first:
                back[g, rows_each:, :] = out
            else:
                eo[g] = out
            prod = out.astype(F32) * d[g].astype(F32)
            if first:
                half_each = rows_each // 2
                gate_sums += as_first * jnp.sum(prod[:half_each], keepdims=True)
                gate_sums += as_second * jnp.sum(prod[half_each:], keepdims=True)
            else:
                odd = par[g, 0:1, 0:128].astype(F32)
                is_first = odd == (t_first % 2).astype(F32)
                gate_sums += jnp.where(is_first, as_first, as_second) * jnp.sum(prod, keepdims=True)
        if not first:
            gate_sums += ga_in[0:1, :]
        ga[...] = jnp.broadcast_to(gate_sums, ga.shape)


def experts_pass(tab, x, deo, part, w_up, b_up, w_down, b_down, turned, prev, ga):
    experts, rows_each, feats = x.shape
    hidden = w_up.shape[2]
    steps = 2
    chunk = hidden // steps
    shards = 4 // steps
    rows = experts * rows_each
    first = prev is None
    in_specs = [
        SM,
        pl.BlockSpec((experts, rows_each, feats), lambda j: (0, 0, 0)),
        pl.BlockSpec((experts, rows_each, feats), lambda j: (0, part, 0)),
        pl.BlockSpec((1, feats, chunk), lambda j: (0, 0, j)),
        pl.BlockSpec((1, chunk), lambda j: (0, j)),
        pl.BlockSpec((1, chunk, feats), lambda j: (0, j, 0)),
        pl.BlockSpec((1, feats), lambda j: (0, 0)),
        pl.BlockSpec((chunk, feats), lambda j: (j, 0)),
        pl.BlockSpec((feats, chunk), lambda j: (0, j)),
    ]
    args = [tab, x, deo, w_up, b_up, w_down, b_down, *turned]
    if not first:
        in_specs.append(pl.BlockSpec((experts, 16, feats), lambda j: (0, 2 * rows_each // 16, 0)))
        args.append(deo)
        in_specs.append(pl.BlockSpec((shards, GRAD_ROWS, feats), lambda j: (j, 0, 0)))
        args.append(prev)
        in_specs.append(pl.BlockSpec((8, 128), lambda j: (0, 0)))
        args.append(ga)
    back = (
        [jax.ShapeDtypeStruct((experts, 2 * rows_each, feats), BF16)]
        if first
        else [jax.ShapeDtypeStruct(x.shape, BF16)] * 2
    )
    return pl.pallas_call(
        functools.partial(expert_kernel, first),
        grid=(steps,),
        in_specs=in_specs,
        out_specs=[pl.BlockSpec(a.shape, lambda j: (0, 0, 0)) for a in back]
        + [
            pl.BlockSpec((shards, GRAD_ROWS, feats), lambda j: (j, 0, 0)),
            pl.BlockSpec((8, 128), lambda j: (0, 0)),
        ],
        out_shape=back
        + [
            jax.ShapeDtypeStruct((4, GRAD_ROWS, feats), BF16),
            jax.ShapeDtypeStruct((8, 128), F32),
        ],
        scratch_shapes=[
            pltpu.VMEM((feats, rows), BF16),
            pltpu.VMEM((feats, rows), BF16),
            pltpu.VMEM((rows, feats), F32),
            pltpu.VMEM((rows, feats), F32),
            pltpu.VMEM((rows, chunk), BF16),
            pltpu.VMEM((rows, chunk), BF16),
        ],
        compiler_params=params(56),
        cost_estimate=cost(15),
        name="experts_short" if first else "experts_long",
    )(*args)


def pass_kernel(*refs):
    pass


def after(array, *others):
    return pl.pallas_call(
        pass_kernel,
        in_specs=[ANY] * (1 + len(others)),
        out_specs=ANY,
        out_shape=jax.ShapeDtypeStruct(array.shape, array.dtype),
        input_output_aliases={0: 0},
        compiler_params=params(56),
        cost_estimate=cost(0.1),
        name="after",
    )(array, *others)


def norm_back(grad, unit, scale, gain):
    scaled = grad * gain
    return scale * (
        scaled
        - jnp.mean(scaled, axis=-1, keepdims=True)
        - unit * jnp.mean(scaled * unit, axis=-1, keepdims=True)
    )


def head_pair_back(probs, dctx, q, kk, vv, keys):
    dprobs = mm_nt(dctx, vv)
    dvalues = fold_heads(mm_tn(probs, dctx), keys)
    wide = probs.astype(F32)
    prod = wide * dprobs
    parts = []
    for part in (slice(0, keys), slice(keys, 2 * keys)):
        parts.append(prod[:, part] - wide[:, part] * jnp.sum(prod[:, part], axis=-1, keepdims=True))
    dscores = jnp.concatenate(parts, axis=1).astype(BF16)
    dqueries = mm(dscores, kk) * HEAD_DIM ** (-0.5)
    dkeys = fold_heads(mm_tn(dscores, q), keys)
    return dqueries.astype(BF16), dkeys.astype(BF16), dvalues.astype(BF16)


def row_sum(values):
    return jnp.sum(values, axis=0, keepdims=True)


def back_short(
    tab, gates, gain, *refs
):
    sources, refs = refs[:12], refs[13:]
    z_refs, dw_h, small, _out = refs[:4], refs[4], refs[5], refs[6]
    ret, mid, c, wo, ctx, p_ref, q_ref, k_ref, v_ref, norm, w, x = refs[7:19]
    zsend, zout, dw, dmid, dattn, dctx, dq, dk, dv, dnorm, in_sems, out_sems = refs[19:]
    fetch, leave = Copies(in_sems), Copies(out_sems)
    have = [fetch.start(a, b) for a, b in zip(sources, refs[7:19])]
    feats = norm.shape[1]
    span = zsend.shape[1]
    sums = [jnp.zeros((1, feats), F32) for _ in range(5)]
    for copy in have[:3]:
        copy.wait()
    for t in range(ret.shape[0]):
        r = slice(span * t, span * (t + 1))
        keep = iota((span, 1), 0) < tab[1, t]
        back_0, back_1 = ret.at[tab[8, t]], ret.at[tab[9, t]]
        mixed = gates[t, 0] * back_0[2 * span : 3 * span, :].astype(F32)
        mixed += gates[t, 1] * back_1[3 * span : 4 * span, :].astype(F32)
        zout[tab[2, t]] = (mid[r, :] + jnp.where(keep, mixed, 0.0)).astype(BF16)
        dmix = back_0[0:span, :].astype(F32) + back_1[span : 2 * span, :].astype(F32)
        unit, scale = norm_stats(mid[r, :])
        sums[2] += row_sum(dmix * unit)
        sums[3] += row_sum(dmix)
        middle = c[r, :].astype(F32) + norm_back(dmix, unit, scale, gain[1:2, :])
        dmid[r, :] = middle
        masked = jnp.where(keep, middle, 0.0)
        sums[4] += row_sum(masked)
        dattn[r, :] = masked.astype(BF16)
    for copy in have[3:5]:
        copy.wait()
    dctx[...] = mm_nt(dattn[...], wo[...]).astype(BF16)
    dw[3 * feats : 4 * feats, :] = mm_tn(ctx[...], dattn[...]).astype(BF16)
    leave.start(dw.at[3 * feats : 4 * feats], dw_h.at[3 * feats : 4 * feats])
    masks = pair_masks()
    for copy in have[5:9]:
        copy.wait()
    for i in range(norm.shape[0] // 128):
        r = slice(128 * i, 128 * (i + 1))
        for p in range(feats // 128):
            c_ = slice(128 * p, 128 * (p + 1))
            a, b, d = head_pair_back(
                p_ref[i * (feats // 128) + p],
                dctx[r, c_],
                q_ref[r, c_],
                both_heads(k_ref[r, c_], masks),
                both_heads(v_ref[r, c_], masks),
                128,
            )
            dq[r, c_] = a
            dk[r, c_] = b
            dv[r, c_] = d
    for copy in have[9:]:
        copy.wait()
    rows = norm[...]
    for index, ref in enumerate((dq, dk, dv)):
        dw[feats * index : feats * (index + 1), :] = mm_tn(rows, ref[...]).astype(BF16)
    leave.start(dw.at[0 : 3 * feats], dw_h.at[0 : 3 * feats])
    dnorm[...] = (
        mm_nt(dq[...], w[0:feats, :])
        + mm_nt(dk[...], w[feats : 2 * feats, :])
        + mm_nt(dv[...], w[2 * feats : 3 * feats, :])
    )
    for t in range(ret.shape[0]):
        r = slice(span * t, span * (t + 1))
        unit, scale = norm_stats(x[r, :].astype(F32))
        grad = dnorm[r, :]
        sums[0] += row_sum(grad * unit)
        sums[1] += row_sum(grad)
        zsend[tab[2, t]] = (dmid[r, :] + norm_back(grad, unit, scale, gain[0:1, :])).astype(BF16)
    sums.append(row_sum(dq[...].astype(F32)))
    sums.append(row_sum(dv[...].astype(F32)))
    for index, value in enumerate(sums):
        small[index : index + 1, :] = value
    small[7:8, :] = jnp.zeros((1, feats), F32)
    for d, ref in enumerate(z_refs):
        ref[0, 0 : 2 * span, :] = zout[2 * d : 2 * d + 2].reshape(2 * span, feats)
        ref[0, 2 * span :, :] = zsend[2 * d : 2 * d + 2].reshape(2 * span, feats)
    leave.finish()


def back_long(
    tab, gain, small_in, ga, *refs
):
    sources, refs = refs[:13], refs[13:]
    zsend, packed_h = refs[:2]
    ret, mid, c, norm, wo, ctx, p_ref, q_ref, k_ref, v_ref, dw_in, w, x = refs[2:15]
    packed, nq, dmid, dattn, dctx, dq, dk, dv, dnorm, full, in_sems, out_sems = refs[15:]
    fetch, leave = Copies(in_sems), Copies(out_sems)
    have = [fetch.start(a, b) for a, b in zip(sources, refs[2:15])]
    feats = norm.shape[1]
    half_rows = ret.shape[1]
    span = 2 * half_rows
    units = norm.shape[0] // span
    offset = tab[14, 0] * half_rows
    sums = [small_in[index : index + 1, :] for index in range(7)]
    for copy in have[:4]:
        copy.wait()
    for u in range(units):
        r = slice(half_rows * u, half_rows * (u + 1))
        t = tab[5, u]
        at = pl.multiple_of(span * u + offset, half_rows)
        nq[r, :] = norm[pl.ds(at, half_rows), :]
        keep = iota((half_rows, 1), 0) + offset < tab[4, u]
        dmix = ret[tab[8, t]].astype(F32) + ret[tab[9, t]].astype(F32)
        unit, scale = norm_stats(mid[r, :])
        sums[2] += row_sum(dmix * unit)
        sums[3] += row_sum(dmix)
        middle = c[r, :].astype(F32) + norm_back(dmix, unit, scale, gain[1:2, :])
        dmid[r, :] = middle
        masked = jnp.where(keep, middle, 0.0)
        sums[4] += row_sum(masked)
        dattn[r, :] = masked.astype(BF16)
    for copy in have[4:6]:
        copy.wait()
    dctx[...] = mm_nt(dattn[...], wo[...]).astype(BF16)
    for copy in have[6:11]:
        copy.wait()
    grad_out = mm_tn(ctx[...], dattn[...]) + dw_in[3 * feats : 4 * feats, :].astype(F32)
    shards = packed.shape[1]
    for h in range(shards):
        for s in range(4):
            full[QKV_ROWS + 128 * s : QKV_ROWS + 128 * (s + 1), 128 * h : 128 * (h + 1)] = grad_out[
                128 * h : 128 * (h + 1), 128 * s : 128 * (s + 1)
            ]
    masks = pair_masks()
    for u in range(units):
        r = slice(half_rows * u, half_rows * (u + 1))
        kr = slice(span * u, span * (u + 1))
        for p in range(feats // 128):
            c_ = slice(128 * p, 128 * (p + 1))
            a, b, d = head_pair_back(
                p_ref[u * (feats // 128) + p],
                dctx[r, c_],
                q_ref[r, c_],
                both_heads(k_ref[kr, c_], masks),
                both_heads(v_ref[kr, c_], masks),
                span,
            )
            dq[r, c_] = a
            dk[kr, c_] = b
            dv[kr, c_] = d
    for index, (left, right) in enumerate(((nq, dq), (norm, dk), (norm, dv))):
        r = slice(feats * index, feats * (index + 1))
        full[r, :] = mm_tn(left[...], right[...]) + dw_in[r, :].astype(F32)
    shift = tab[14, 1]
    early = MISC_ROW // SLICE_ROWS
    for g in range(early):
        for h in range(shards):
            packed[g, shift ^ h] = full[
                SLICE_ROWS * g : SLICE_ROWS * (g + 1), 128 * h : 128 * (h + 1)
            ].astype(BF16)
    leave.start(packed.at[0:early], packed_h.at[0:early])
    for copy in have[11:]:
        copy.wait()
    dnorm[...] = mm_nt(dk[...], w[feats : 2 * feats, :]) + mm_nt(dv[...], w[2 * feats : 3 * feats, :])
    from_q = mm_nt(dq[...], w[0:feats, :])
    for u in range(units):
        at = pl.multiple_of(span * u + offset, half_rows)
        dnorm[pl.ds(at, half_rows), :] += from_q[half_rows * u : half_rows * (u + 1), :]
    for u in range(units):
        owner = tab[16, u]
        for s in range(2):
            r = slice(span * u + half_rows * s, span * u + half_rows * (s + 1))
            unit, scale = norm_stats(x[r, :].astype(F32))
            grad = dnorm[r, :]
            sums[0] += row_sum(grad * unit)
            sums[1] += row_sum(grad)
            own_half = tab[14, 0] == s
            direct = jnp.where(own_half, dmid[half_rows * u : half_rows * (u + 1), :], 0.0)
            zsend[owner, half_rows * s : half_rows * (s + 1), :] = (
                direct + norm_back(grad, unit, scale, gain[0:1, :])
            ).astype(BF16)
    sums[5] += row_sum(dq[...].astype(F32))
    sums[6] += row_sum(dv[...].astype(F32))
    full[MISC_ROW:, :] = jnp.zeros((full.shape[0] - MISC_ROW, feats), F32)
    full[MISC_ROW : MISC_ROW + 1, :] = sums[5]
    full[MISC_ROW + 1 : MISC_ROW + 2, :] = sums[6]
    for index in range(5):
        for s in range(4):
            at = MISC_ROW + 2 + 4 * index + s
            piece = sums[index][:, 128 * s : 128 * (s + 1)]
            full[at : at + 1, :] = jnp.concatenate([piece] * shards, axis=1)
    for s in range(shards):
        full[MISC_ROW + 22 : MISC_ROW + 23, 128 * s : 128 * (s + 1)] = ga[0:1, :]
    for g in range(early, packed.shape[0]):
        for h in range(shards):
            packed[g, shift ^ h] = full[
                SLICE_ROWS * g : SLICE_ROWS * (g + 1), 128 * h : 128 * (h + 1)
            ].astype(BF16)
    leave.start(packed.at[early:], packed_h.at[early:])
    leave.finish()


def mix_long(tab, gates, ret, mid, dx, z0, z1, z2, z3, zout):
    half_rows = ret.shape[1]
    for u in range(mid.shape[0] // half_rows):
        r = slice(half_rows * u, half_rows * (u + 1))
        t = tab[5, u]
        keep = iota((half_rows, 1), 0) + half_rows * tab[14, 0] < tab[4, u]
        mixed = gates[t, 0] * ret[tab[8, t]].astype(F32) + gates[t, 1] * ret[tab[9, t]].astype(F32)
        zout[tab[16, u]] = (mid[r, :] + jnp.where(keep, mixed, 0.0)).astype(BF16)
    for d, ref in enumerate((z0, z1, z2, z3)):
        ref[0, 0:half_rows, :] = zout[d]
        ref[0, half_rows:, :] = dx[d]


def each_distance(index, refs, act):
    for d, ref in enumerate(refs):

        @pl.when(index == d)
        def _(ref=ref):
            act(ref)


def place_kernel(tab, s0, s1, s2, s3, l0, l1, l2, l3, _0, _1, short_out, long_out, short_dx, long_dx):
    span = short_out.shape[1]
    half = long_out.shape[1] // 2
    for n in range(short_out.shape[0]):
        slot = tab[6, n]
        at = pl.multiple_of((slot % 2) * span, span)

        def copy_short(ref, n=n, at=at):
            short_out[n] = ref[0, pl.ds(at, span), :]
            short_dx[n] = ref[0, pl.ds(pl.multiple_of(2 * span + at, span), span), :].astype(F32)

        each_distance(slot // 2, (s0, s1, s2, s3), copy_short)
    for n in range(long_out.shape[0]):

        def first(ref, n=n):
            long_out[n, 0:half, :] = ref[0, 0:half, :]
            long_dx[n] = ref[0, half:, :].astype(F32)

        def second(ref, n=n):
            long_out[n, half:, :] = ref[0, 0:half, :]
            long_dx[n] += ref[0, half:, :].astype(F32)

        each_distance(tab[7, n], (l0, l1, l2, l3), first)
        each_distance(tab[15, n], (l0, l1, l2, l3), second)


def finish_kernel(
    g, ids, gates, temb, gw_t, qkv, qv, wo, gain, shift, bo, grad_temb, grad_gw_t
):
    feats = wo.shape[1]
    for j in range(3):
        qkv[j] = g[feats * j : feats * (j + 1), :].astype(F32)
    for c in range(4):
        at = QKV_ROWS + 128 * c
        wo[:, 128 * c : 128 * (c + 1)] = g[at : at + 128, :].astype(F32)
    misc = g[MISC_ROW : MISC_ROW + 32, :].astype(F32)
    qv[...] = misc[0:2, :]

    def line(index):
        at = 2 + 4 * index
        return jnp.concatenate([misc[at + s : at + s + 1, :] for s in range(4)], axis=1)

    gain[0:1, :], gain[1:2, :] = line(0), line(2)
    shift[0:1, :], shift[1:2, :] = line(1), line(3)
    bo[...] = line(4)
    terms = misc[22:23, :]
    tasks = temb.shape[0]
    sub, lane = iota((tasks, 128), 0), iota((tasks, 128), 1)
    first = jnp.sum(jnp.where(lane == 2 * sub, terms, 0.0), axis=1, keepdims=True)
    second = jnp.sum(jnp.where(lane == 2 * sub + 1, terms, 0.0), axis=1, keepdims=True)
    both = first + second
    first = first - gates[:, 0:1] * both
    second = second - gates[:, 1:2] * both
    experts = gw_t.shape[0]
    rows = iota((experts, tasks), 0)
    eye = (iota((tasks, tasks), 0) == iota((tasks, tasks), 1)).astype(F32)
    spread = jnp.zeros((experts, tasks), F32)
    for k, value in ((0, first), (1, second)):
        as_row = jnp.sum(eye * value, axis=0, keepdims=True)
        spread += jnp.where(rows == ids[k : k + 1, :], as_row, 0.0)
    grad_gw_t[...] = lax.dot_general(
        spread, temb[...], (((1,), (0,)), ((), ())), preferred_element_type=F32, precision=HIGHEST
    )
    grad_temb[...] = lax.dot_general(
        spread.T, gw_t[...], (((1,), (0,)), ((), ())), preferred_element_type=F32, precision=HIGHEST
    )


def finish_experts(tab, shard, up, up_b, down, down_b):
    feats = up.shape[1]
    up[0] = shard[0, 0:feats, :].astype(F32)
    down[0] = shard[0, feats : 2 * feats, :].astype(F32).T
    tail = shard[0, 2 * feats :, :].astype(F32)
    up_b[...] = tail[0:1, :]
    down_b[...] = jnp.zeros_like(down_b)
    for h in range(feats // 128):

        @pl.when(tab[14, 1] == h)
        def _(h=h):
            down_b[...] = tail[1:2, 128 * h : 128 * (h + 1)]


def collect_kernel(arrived, *refs):
    for d, ref in enumerate(refs[8:12]):
        terms = arrived[0, d].astype(F32)
        for g in range(1, arrived.shape[0]):
            terms += arrived[g, d].astype(F32)
        ref[0] = terms.astype(BF16)


def shape_of(shape, dtype):
    return jax.ShapeDtypeStruct(shape, dtype)


def balanced(short_x, long_x, expert_ids):
    heads = lax.axis_size("head")
    tasks = expert_ids.shape[0]
    return (
        heads == 4
        and lax.axis_size("expert") == tasks == 8
        and short_x.shape[0] == 4 * tasks
        and long_x.shape[0] == tasks
        and short_x.shape[1:] == (64, 512)
        and long_x.shape[1:] == (256, 512)
    )


def per_device(
    short_x,
    long_x,
    short_cot,
    long_cot,
    short_len,
    long_len,
    short_task,
    long_task,
    expert_ids,
    ln_gain,
    ln_bias,
    w_qkv,
    b_qv,
    w_attn_out,
    b_attn_out,
    w_up,
    b_up,
    w_down,
    b_down,
    task_emb,
    gate_w,
):
    if not balanced(short_x, long_x, expert_ids):
        return per_device_wide(
            short_x, long_x, short_cot, long_cot, short_len, long_len, short_task, long_task,
            expert_ids, ln_gain, ln_bias, w_qkv, b_qv, w_attn_out, b_attn_out, w_up, b_up,
            w_down, b_down, task_emb, gate_w,
        )
    heads = lax.axis_size("head")
    experts = lax.axis_size("expert")
    span, feats = short_x.shape[1:]
    long_span = long_x.shape[1]
    half_rows = long_span // 2
    tasks = expert_ids.shape[0]
    units = long_x.shape[0] // 2
    rows_s = tasks * span
    rows_q = units * half_rows
    rows_l = units * long_span
    pairs = feats // 128

    own_half = pl.pallas_call(
        pack_kernel,
        in_specs=[VM] * 3,
        out_specs=VM,
        out_shape=shape_of((HALF_PACK, 128), BF16),
        compiler_params=params(56),
        cost_estimate=cost(2),
        name="pack",
    )(w_qkv, b_qv, w_attn_out)
    raw_own = lax.all_gather(own_half, "head", axis=0)
    raw_other = lax.ppermute(raw_own, "expert", [(i, i ^ 1) for i in range(experts)])

    tab, gates = pl.pallas_call(
        route_kernel,
        in_specs=[VM] * 7,
        out_specs=[VM, VM],
        out_shape=[shape_of((24, 128), jnp.int32), shape_of((tasks, 128), F32)],
        compiler_params=params(56),
        cost_estimate=cost(4),
        name="route",
    )(
        short_task.reshape(1, -1),
        short_len.reshape(1, -1),
        long_task.reshape(1, -1),
        long_len.reshape(1, -1),
        expert_ids.T,
        task_emb,
        gate_w.T,
    )

    def blk(n, index):
        return pl.BlockSpec((1, n, feats), index)

    deo, cot_s, cot_l, norm_s, norm_l, own_s, own_l = pl.pallas_call(
        prep_kernel,
        grid_spec=pltpu.PrefetchScalarGridSpec(
            num_scalar_prefetch=1,
            grid=(8,),
            in_specs=[
                SM,
                blk(span, lambda e, tab: (tab[0, tab[10, e]], 0, 0)),
                blk(span, lambda e, tab: (tab[0, tab[11, e]], 0, 0)),
                blk(half_rows, lambda e, tab: (tab[3, tab[13, e]], tab[14, 0], 0)),
                blk(span, lambda e, tab: (tab[0, e], 0, 0)),
                blk(span, lambda e, tab: (tab[3, e // 2], tab[14, 0] * 2 + e % 2, 0)),
                blk(span, lambda e, tab: (tab[0, e], 0, 0)),
                blk(half_rows, lambda e, tab: (tab[3, e // 2], e % 2, 0)),
                pl.BlockSpec((2, feats), lambda e, tab: (0, 0)),
                pl.BlockSpec((2, feats), lambda e, tab: (0, 0)),
            ],
            out_specs=[
                blk(2 * span + half_rows + 16, lambda e, tab: (e, 0, 0)),
                blk(span, lambda e, tab: (e, 0, 0)),
                blk(span, lambda e, tab: (e, 0, 0)),
                blk(span, lambda e, tab: (e, 0, 0)),
                blk(half_rows, lambda e, tab: (e, 0, 0)),
                blk(span, lambda e, tab: (e, 0, 0)),
                blk(half_rows, lambda e, tab: (e, 0, 0)),
            ],
        ),
        out_shape=[
            shape_of((experts, 2 * span + half_rows + 16, feats), BF16),
            shape_of((8, span, feats), BF16),
            shape_of((8, span, feats), BF16),
            shape_of((8, span, feats), BF16),
            shape_of((8, half_rows, feats), BF16),
            shape_of((8, span, feats), BF16),
            shape_of((8, half_rows, feats), BF16),
        ],
        compiler_params=params(56),
        cost_estimate=cost(9),
        name="prep",
    )(tab, gates, short_cot, short_cot, long_cot, short_cot, long_cot, short_x, long_x, ln_gain, ln_bias)
    cot_s, norm_s, own_s = (a.reshape(rows_s, feats) for a in (cot_s, norm_s, own_s))
    cot_l = cot_l.reshape(rows_q, feats)
    norm_l, own_l = norm_l.reshape(rows_l, feats), own_l.reshape(rows_l, feats)
    deo = lax.all_to_all(deo, "expert", split_axis=0, concat_axis=0, tiled=True)

    turned = turn_weights(w_up, w_down)

    bias_out = b_attn_out.reshape(1, feats)
    w_shapes = [
        shape_of((QKV_ROWS, feats), BF16),
        shape_of((feats, feats), BF16),
        shape_of((8, feats), F32),
    ]

    def vmem(shape, dtype=BF16):
        return pltpu.VMEM(shape, dtype)

    def sems(count):
        return pltpu.SemaphoreType.DMA((count,))

    def attention(kernel, operands, far, key_rows, query_rows, keys, send_shape, more, scratch, counts, name):
        kept = [
            shape_of((query_rows, feats), BF16),
            shape_of((key_rows, feats), BF16),
            shape_of((key_rows, feats), BF16),
            shape_of((4 * pairs, 128, 2 * keys), BF16),
            shape_of((query_rows, feats), BF16),
        ]
        return pl.pallas_call(
            kernel,
            in_specs=[SM] + [ANY] * far + [VM] * (len(operands) - far - 1),
            out_specs=[ANY] * 5 + [VM] * 2 + ([ANY] * 2 + [VM] if more else []),
            out_shape=kept + [shape_of((query_rows, feats), F32), shape_of(send_shape, BF16)] + more,
            scratch_shapes=[vmem(a.shape) for a in operands[1 : far + 1]]
            + [vmem(a.shape) for a in kept]
            + scratch
            + [sems(count) for count in counts],
            compiler_params=params(56),
            cost_estimate=cost(10),
            name=name,
        )(*operands)

    q_s, k_s, v_s, p_s, ctx_s, mid_s, send_s, w_all, wo_all, bqv_all = attention(
        attend_short,
        (tab, norm_s, own_s, raw_own, raw_other, ln_gain, ln_bias, bias_out),
        4, rows_s, rows_s, 128, (experts, 2, span, feats), w_shapes,
        [vmem((QKV_ROWS, feats)), vmem((feats, feats))], (4, 10), "attend_short",
    )
    send_s = send_s.reshape(experts, 2 * span, feats)
    recv_s = lax.all_to_all(send_s, "expert", split_axis=0, concat_axis=0, tiled=True)
    q_l, k_l, v_l, p_l, ctx_l, mid_l, send_l = attention(
        attend_long,
        (tab, norm_l, own_l, w_all, wo_all, bqv_all, ln_gain, ln_bias, bias_out),
        4, rows_l, rows_q, long_span, (experts, half_rows, feats), [],
        [vmem((rows_q, feats))], (4, 8), "attend_long",
    )
    recv_l = lax.all_to_all(send_l, "expert", split_axis=0, concat_axis=0, tiled=True)

    ret_s, dw_s, ga_s = experts_pass(tab, recv_s, deo, 0, w_up, b_up, w_down, b_down, turned, None, None)
    ret_s = lax.all_to_all(ret_s, "expert", split_axis=0, concat_axis=0, tiled=True)
    ret_l, eo_l, dw_l, ga_l = experts_pass(tab, recv_l, deo, 1, w_up, b_up, w_down, b_down, turned, dw_s, ga_s)
    ret_l = lax.all_to_all(ret_l, "expert", split_axis=0, concat_axis=0, tiled=True)
    dw_l = after(dw_l, ret_s)
    expert_grads = lax.psum_scatter(dw_l, "head", scatter_dimension=0, tiled=True)

    def over_head(blocks):
        return [blocks[0]] + [
            lax.ppermute(blocks[d], "head", [(i, i ^ d) for i in range(heads)]) for d in range(1, heads)
        ]

    far = (ret_s, mid_s, cot_s, wo_all, ctx_s, p_s, q_s, k_s, v_s, norm_s, w_all, own_s)
    *zsend_s, dw_attn, small, eo_l = pl.pallas_call(
        back_short,
        in_specs=[SM, SM, VM] + [ANY] * (len(far) + 1),
        out_specs=[VM] * heads + [ANY, VM, ANY],
        out_shape=[shape_of((1, 4 * span, feats), BF16)] * heads
        + [
            shape_of((4 * feats, feats), BF16),
            shape_of((8, feats), F32),
            shape_of(eo_l.shape, BF16),
        ],
        input_output_aliases={3 + len(far): heads + 2},
        scratch_shapes=[vmem(a.shape, a.dtype) for a in far]
        + [vmem((2 * heads, span, feats))] * 2
        + [vmem((4 * feats, feats)), vmem((rows_s, feats), F32)]
        + [vmem((rows_s, feats))] * 5
        + [vmem((rows_s, feats), F32), sems(len(far)), sems(2)],
        compiler_params=params(56),
        cost_estimate=cost(12),
        name="back_short",
    )(tab, gates, ln_gain, *far, eo_l)
    out_l = lax.all_to_all(eo_l, "expert", split_axis=0, concat_axis=0, tiled=True)
    home_s = over_head(zsend_s)
    far = (ret_l, mid_l, cot_l, norm_l, wo_all, ctx_l, p_l, q_l, k_l, v_l, dw_attn, w_all, own_l)
    zsend_l, packed = pl.pallas_call(
        back_long,
        in_specs=[SM, VM, VM, VM] + [ANY] * len(far),
        out_specs=[VM, ANY],
        out_shape=[
            shape_of((heads, long_span, feats), BF16),
            shape_of((experts, heads, SLICE_ROWS, 128), BF16),
        ],
        scratch_shapes=[vmem(a.shape, a.dtype) for a in far]
        + [
            vmem((experts, heads, SLICE_ROWS, 128)),
            vmem((rows_q, feats)),
            vmem((rows_q, feats), F32),
            vmem((rows_q, feats)),
            vmem((rows_q, feats)),
            vmem((rows_q, feats)),
            vmem((rows_l, feats)),
            vmem((rows_l, feats)),
            vmem((rows_l, feats), F32),
            vmem((experts * SLICE_ROWS, feats), F32),
            sems(len(far)),
            sems(2),
        ],
        compiler_params=params(56),
        cost_estimate=cost(17),
        name="back_long",
    )(tab, ln_gain, small, ga_l, *far)
    arrived = lax.all_to_all(packed, "expert", split_axis=0, concat_axis=0, tiled=True)
    zsend_l = pl.pallas_call(
        mix_long,
        in_specs=[SM, SM] + [VM] * 3,
        out_specs=[VM] * heads,
        out_shape=[shape_of((1, half_rows + long_span, feats), BF16)] * heads,
        scratch_shapes=[vmem((heads, half_rows, feats))],
        compiler_params=params(56),
        cost_estimate=cost(3),
        name="mix_long",
    )(tab, gates, out_l, mid_l, zsend_l)
    through = (*home_s, *zsend_l)
    terms = pl.pallas_call(
        collect_kernel,
        in_specs=[VM] + [ANY] * len(through),
        out_specs=[VM] * heads + [ANY] * len(through),
        out_shape=[shape_of((1, SLICE_ROWS, 128), BF16)] * heads
        + [shape_of(a.shape, a.dtype) for a in through],
        input_output_aliases={1 + i: heads + i for i in range(len(through))},
        compiler_params=params(56),
        cost_estimate=cost(0.1),
        name="collect",
    )(arrived, *through)
    home_s, zsend_l = terms[heads : 2 * heads], terms[2 * heads :]
    terms = sum(part.astype(F32) for part in over_head(terms[:heads])).astype(BF16)
    home_l = over_head(zsend_l)
    attn_grads = lax.all_gather(terms[0], "expert", axis=0, tiled=True)
    chunk = w_up.shape[2] // 4
    grad_up, grad_up_b, grad_down, grad_down_b = pl.pallas_call(
        finish_experts,
        in_specs=[SM, VM],
        out_specs=[VM] * 4,
        out_shape=[
            shape_of((1, feats, chunk), F32),
            shape_of((1, chunk), F32),
            shape_of((1, chunk, feats), F32),
            shape_of((1, feats // heads), F32),
        ],
        compiler_params=params(56),
        cost_estimate=cost(0.1),
        name="finish_experts",
    )(tab, expert_grads)
    grad_qkv, grad_qv, grad_wo, grad_gain, grad_shift, grad_bo, grad_task, grad_gate = pl.pallas_call(
        finish_kernel,
        in_specs=[VM] * 5,
        out_specs=[VM] * 8,
        out_shape=[
            shape_of((3, feats, 128), F32),
            shape_of((2, 128), F32),
            shape_of((128, feats), F32),
            shape_of((2, feats), F32),
            shape_of((2, feats), F32),
            shape_of((1, feats), F32),
            shape_of((tasks, feats), F32),
            shape_of((experts, feats), F32),
        ],
        compiler_params=params(56),
        cost_estimate=cost(0.1),
        name="finish",
    )(attn_grads, expert_ids.T, gates, task_emb, gate_w.T)
    short_out, long_out, short_dx, long_dx = pl.pallas_call(
        place_kernel,
        in_specs=[SM] + [VM] * (2 * heads) + [ANY] * 2,
        out_specs=[VM] * 4,
        out_shape=[
            shape_of((8, span, feats), BF16),
            shape_of((2, long_span, feats), BF16),
            shape_of((8, span, feats), F32),
            shape_of((2, long_span, feats), F32),
        ],
        compiler_params=params(56),
        cost_estimate=cost(0.1),
        name="place",
    )(tab, *home_s, *home_l, grad_bo, grad_down_b)

    return (
        short_out,
        long_out,
        short_dx,
        long_dx,
        grad_gain,
        grad_shift,
        grad_qkv,
        grad_qv,
        grad_wo,
        grad_bo.reshape(feats),
        grad_up,
        grad_up_b,
        grad_down,
        grad_down_b,
        grad_task,
        grad_gate.T,
    )


def solution(mesh):
    return jax.shard_map(
        per_device,
        mesh=mesh,
        in_specs=(
            P("expert", None, None),
            P("expert", None, None),
            P("expert", None, None),
            P("expert", None, None),
            P("expert"),
            P("expert"),
            P("expert"),
            P("expert"),
            P(),
            P(),
            P(),
            P(None, None, "head"),
            P(None, "head"),
            P("head", None),
            P(),
            P("expert", None, None),
            P("expert", None),
            P("expert", None, None),
            P("expert", None),
            P(),
            P(),
        ),
        out_specs=(
            P(("expert", "head"), None, None),
            P(("expert", "head"), None, None),
            P(("expert", "head"), None, None),
            P(("expert", "head"), None, None),
            P(),
            P(),
            P(None, None, "head"),
            P(None, "head"),
            P("head", None),
            P(),
            P("expert", None, "head"),
            P("expert", "head"),
            P("expert", "head", None),
            P("expert", "head"),
            P(),
            P(),
        ),
        check_vma=False,
    )
```

```python
import functools

import jax
import jax.numpy as jnp
from jax import lax
from jax.experimental import pallas as pl
from jax.experimental.pallas import tpu as pltpu
from jax.sharding import PartitionSpec as P

HEAD_DIM = 64


HIGHEST = lax.Precision.HIGHEST
CONTRACT_ROWS = (((0,), (0,)), ((), ()))
CONTRACT_COLS = (((1,), (1,)), ((), ()))


def layer_norm(values, gain, shift):
    centred = values - jnp.mean(values, axis=-1, keepdims=True)
    spread = jnp.mean(centred * centred, axis=-1, keepdims=True)
    return centred * lax.rsqrt(spread + 1e-05) * gain + shift


def lookup(table, index):
    hits = index[..., None] == jnp.arange(table.shape[0], dtype=jnp.int32)
    return jnp.sum(jnp.where(hits, table, jnp.zeros((), table.dtype)), axis=-1)


def route_slots(tasks, expert_ids, capacity, experts):
    task_hits = tasks[:, None] == jnp.arange(expert_ids.shape[0], dtype=jnp.int32)
    chosen = jnp.sum(jnp.where(task_hits[:, :, None], expert_ids[None, :, :], 0), axis=1).reshape(
        -1
    )
    routes = chosen.shape[0]
    owner_hits = (chosen[:, None] == jnp.arange(experts, dtype=jnp.int32)).astype(jnp.int32)
    earlier = jnp.cumsum(owner_hits, axis=0) - owner_hits
    ranking = jnp.sum(earlier * owner_hits, axis=1)
    slot_key = chosen * capacity + ranking
    slot_hits = slot_key[:, None] == jnp.arange(experts * capacity, dtype=jnp.int32)
    return jnp.sum(jnp.where(slot_hits, jnp.arange(routes, dtype=jnp.int32)[:, None], 0), axis=0)


def masked_scores(queries, key_rows, lengths):
    positions = key_rows.shape[1]
    scores = jnp.einsum(
        "blhd,bmhd->bhlm", queries, key_rows, preferred_element_type=jnp.float32
    ) * HEAD_DIM ** (-0.5)
    visible = (
        jnp.arange(positions, dtype=jnp.int32)[None, None, None, :] < lengths[:, None, None, None]
    )
    return jnp.where(visible, scores, -1e30)


def attend(normed, lengths, weights, biases, head_count):
    sentences, positions, features = normed.shape
    flattened = normed.reshape(-1, features)
    shape_heads = (sentences, positions, head_count, HEAD_DIM)

    def project(index, offset):
        return (
            (jnp.dot(flattened, weights[index], preferred_element_type=jnp.float32) + offset)
            .astype(jnp.bfloat16)
            .reshape(shape_heads)
        )

    queries = project(0, biases[0])
    key_rows = project(1, 0.0)
    values = project(2, biases[1])
    scores = masked_scores(queries, key_rows, lengths)
    highest = jnp.max(scores, axis=-1, keepdims=True)
    shifted = jnp.exp(scores - highest)
    totals = jnp.sum(shifted, axis=-1, keepdims=True)
    attn_probs = (shifted / totals).astype(jnp.bfloat16)
    log_total = highest + jnp.log(totals)
    context = jnp.einsum(
        "bhlm,bmhd->blhd", attn_probs, values, preferred_element_type=jnp.float32
    ).astype(jnp.bfloat16)
    return (queries, key_rows, values, context.reshape(sentences, positions, -1), log_total)


def attend_back(normed, lengths, kept, grad_out, weights, out_weight):
    queries, key_rows, values, context, log_total = kept
    features = normed.shape[-1]
    head_cols = context.shape[-1]
    grad_flat = grad_out.reshape(-1, features)
    context_flat = context.reshape(-1, head_cols)
    grad_context = (
        lax.dot_general(grad_flat, out_weight, CONTRACT_COLS, preferred_element_type=jnp.float32)
        .astype(jnp.bfloat16)
        .reshape(queries.shape)
    )
    grad_out_weight = lax.dot_general(
        context_flat, grad_flat, CONTRACT_ROWS, preferred_element_type=jnp.float32
    )
    probs = jnp.exp(masked_scores(queries, key_rows, lengths) - log_total)
    grad_probs = jnp.einsum(
        "blhd,bmhd->bhlm", grad_context, values, preferred_element_type=jnp.float32
    )
    grad_values = jnp.einsum(
        "bhlm,blhd->bmhd",
        probs.astype(jnp.bfloat16),
        grad_context,
        preferred_element_type=jnp.float32,
    ).astype(jnp.bfloat16)
    grad_scores = (
        probs * (grad_probs - jnp.sum(probs * grad_probs, axis=-1, keepdims=True))
    ).astype(jnp.bfloat16)
    scaling = HEAD_DIM ** (-0.5)
    grad_queries = (
        jnp.einsum("bhlm,bmhd->blhd", grad_scores, key_rows, preferred_element_type=jnp.float32)
        * scaling
    ).astype(jnp.bfloat16)
    grad_keys = (
        jnp.einsum("bhlm,blhd->bmhd", grad_scores, queries, preferred_element_type=jnp.float32)
        * scaling
    ).astype(jnp.bfloat16)
    normed_flat = normed.reshape(-1, features)
    members = [member.reshape(-1, head_cols) for member in (grad_queries, grad_keys, grad_values)]
    grad_weights = jnp.stack(
        [
            lax.dot_general(normed_flat, member, CONTRACT_ROWS, preferred_element_type=jnp.float32)
            for member in members
        ]
    )
    grad_biases = jnp.stack(
        [
            jnp.sum(members[0].astype(jnp.float32), axis=0),
            jnp.sum(members[2].astype(jnp.float32), axis=0),
        ]
    )
    grad_normed = lax.dot_general(
        members[0], weights[0], CONTRACT_COLS, preferred_element_type=jnp.float32
    )
    grad_normed = grad_normed + lax.dot_general(
        members[1], weights[1], CONTRACT_COLS, preferred_element_type=jnp.float32
    )
    grad_normed = grad_normed + lax.dot_general(
        members[2], weights[2], CONTRACT_COLS, preferred_element_type=jnp.float32
    )
    return (grad_normed.reshape(normed.shape), grad_weights, grad_out_weight, grad_biases)


def group_rows(first_rows, second_rows):
    return (
        lax.all_gather(first_rows, "head", axis=0, tiled=True),
        lax.all_gather(second_rows, "head", axis=0, tiled=True),
    )


def per_device_wide(
    short_x,
    long_x,
    short_cot,
    long_cot,
    short_len,
    long_len,
    short_task,
    long_task,
    expert_ids,
    ln_gain,
    ln_bias,
    w_qkv,
    b_qv,
    w_attn_out,
    b_attn_out,
    w_up,
    b_up,
    w_down,
    b_down,
    task_emb,
    gate_w,
):
    heads_here = lax.axis_size("head")
    head_place = lax.axis_index("head")
    experts = lax.axis_size("expert")
    short_group, short_span, features = short_x.shape
    long_group, long_span = (long_x.shape[0], long_x.shape[1])
    short_dev = short_group // heads_here
    long_dev = long_group // heads_here
    hidden_width = w_up.shape[2]
    tasks_total = expert_ids.shape[0]
    cap_short = 2 * short_group // experts
    cap_long = 2 * long_group // experts
    piece_rows = (cap_short * short_span + cap_long * long_span) // heads_here
    short_total = short_group * short_span
    all_rows = short_total + long_group * long_span
    expert_hits = (expert_ids[:, :, None] == jnp.arange(experts, dtype=jnp.int32)).astype(
        jnp.float32
    )
    chosen_cols = jnp.einsum("tke,de->tkd", expert_hits, gate_w, precision=HIGHEST)
    gate_probs = jax.nn.softmax(jnp.sum(task_emb[:, None, :] * chosen_cols, axis=-1), axis=-1)
    short_slots = route_slots(short_task, expert_ids, cap_short, experts)
    long_slots = route_slots(long_task, expert_ids, cap_long, experts)
    offsets = head_place * piece_rows + jnp.arange(piece_rows, dtype=jnp.int32)
    owners = jnp.arange(experts, dtype=jnp.int32)[:, None]
    in_short = jnp.broadcast_to(offsets < cap_short * short_span, (experts, piece_rows))
    short_pos = offsets % short_span
    long_offset = jnp.maximum(offsets - cap_short * short_span, 0)
    long_pos = long_offset % long_span
    short_route = lookup(
        short_slots, owners * cap_short + jnp.minimum(offsets // short_span, cap_short - 1)
    )
    long_route = lookup(
        long_slots, owners * cap_long + jnp.minimum(long_offset // long_span, cap_long - 1)
    )
    short_sent = short_route // 2
    long_sent = long_route // 2
    position = jnp.where(in_short, short_pos, long_pos)
    target = jnp.where(
        in_short,
        short_sent * short_span + short_pos,
        short_total + long_sent * long_span + long_pos,
    )
    task_rows = jnp.where(in_short, lookup(short_task, short_sent), lookup(long_task, long_sent))
    length_rows = jnp.where(in_short, lookup(short_len, short_sent), lookup(long_len, long_sent))
    live_rows = (position < length_rows).astype(jnp.float32)
    gate_index = task_rows * 2 + jnp.where(in_short, short_route % 2, long_route % 2)
    gate_rows = lookup(gate_probs.reshape(-1), gate_index)
    short_mask = (jnp.arange(short_span, dtype=jnp.int32)[None, :] < short_len[:, None]).astype(
        jnp.float32
    )[:, :, None]
    long_mask = (jnp.arange(long_span, dtype=jnp.int32)[None, :] < long_len[:, None]).astype(
        jnp.float32
    )[:, :, None]
    short_start = head_place * short_dev
    long_start = head_place * long_dev
    own_short_mask = lax.dynamic_slice_in_dim(short_mask, short_start, short_dev, 0)
    own_long_mask = lax.dynamic_slice_in_dim(long_mask, long_start, long_dev, 0)
    short_in = short_x.astype(jnp.float32)
    long_in = long_x.astype(jnp.float32)
    own_short_in = lax.dynamic_slice_in_dim(short_in, short_start, short_dev, 0)
    own_long_in = lax.dynamic_slice_in_dim(long_in, long_start, long_dev, 0)
    attn_qkv, attn_qv, attn_out_w = (w_qkv, b_qv, w_attn_out)
    short_src, long_src = (short_in, long_in)
    short_lens, long_lens = (short_len, long_len)
    head_cols = attn_qkv.shape[2]
    head_count = head_cols // HEAD_DIM
    short_normed = layer_norm(short_src, ln_gain[0], ln_bias[0]).astype(jnp.bfloat16)
    long_normed = layer_norm(long_src, ln_gain[0], ln_bias[0]).astype(jnp.bfloat16)
    short_kept = attend(short_normed, short_lens, attn_qkv, attn_qv, head_count)
    long_kept = attend(long_normed, long_lens, attn_qkv, attn_qv, head_count)
    short_part = jnp.dot(
        short_kept[3].reshape(-1, head_cols), attn_out_w, preferred_element_type=jnp.float32
    ).reshape(short_src.shape)
    long_part = jnp.dot(
        long_kept[3].reshape(-1, head_cols), attn_out_w, preferred_element_type=jnp.float32
    ).reshape(long_src.shape)
    short_sum, long_sum = (
        lax.psum(short_part.astype(jnp.bfloat16), "head").astype(jnp.float32),
        lax.psum(long_part.astype(jnp.bfloat16), "head").astype(jnp.float32),
    )
    short_mid = short_in + short_mask * (short_sum + b_attn_out)
    long_mid = long_in + long_mask * (long_sum + b_attn_out)
    short_mixin = layer_norm(short_mid, ln_gain[1], ln_bias[1]).astype(jnp.bfloat16)
    long_mixin = layer_norm(long_mid, ln_gain[1], ln_bias[1]).astype(jnp.bfloat16)
    own_short_mid = lax.dynamic_slice_in_dim(short_mid, short_start, short_dev, 0)
    own_long_mid = lax.dynamic_slice_in_dim(long_mid, long_start, long_dev, 0)
    mixin_rows = jnp.concatenate(
        [short_mixin.reshape(-1, features), long_mixin.reshape(-1, features)], axis=0
    )
    outgoing = mixin_rows[target]
    received = lax.all_to_all(outgoing, "expert", split_axis=0, concat_axis=0, tiled=True)
    inputs = received.reshape(-1, features)
    gelu_in = jnp.dot(inputs, w_up[0], preferred_element_type=jnp.float32) + b_up[0]
    hidden = jax.nn.gelu(gelu_in).astype(jnp.bfloat16)
    output = (jnp.dot(hidden, w_down[0], preferred_element_type=jnp.float32) + b_down[0]).astype(
        jnp.bfloat16
    )
    returned = lax.all_to_all(
        output.reshape(received.shape), "expert", split_axis=0, concat_axis=0, tiled=True
    )
    wide_shape = received.shape[:2] + (hidden_width,)
    packed = (returned, received, hidden.reshape(wide_shape), gelu_in.reshape(wide_shape))
    returned = packed[0]
    received = packed[1]
    contrib = (gate_rows[:, :, None] * returned.astype(jnp.float32)).reshape(-1, features)
    mixed_rows = jnp.zeros((all_rows, features), jnp.float32).at[target.reshape(-1)].add(contrib)
    short_moe, long_moe = (
        lax.psum_scatter(
            mixed_rows[:short_total].reshape(short_in.shape).astype(jnp.bfloat16),
            "head",
            scatter_dimension=0,
            tiled=True,
        ).astype(jnp.float32),
        lax.psum_scatter(
            mixed_rows[short_total:].reshape(long_in.shape).astype(jnp.bfloat16),
            "head",
            scatter_dimension=0,
            tiled=True,
        ).astype(jnp.float32),
    )
    short_out = (own_short_mid + own_short_mask * short_moe).astype(jnp.bfloat16)
    long_out = (own_long_mid + own_long_mask * long_moe).astype(jnp.bfloat16)
    cot_rows = jnp.concatenate(
        [short_cot.reshape(-1, features), long_cot.reshape(-1, features)], axis=0
    )
    cot_picked = cot_rows[target].astype(jnp.float32)
    grad_sent = ((gate_rows * live_rows)[:, :, None] * cot_picked).astype(jnp.bfloat16)
    gate_terms = live_rows * jnp.sum(cot_picked * returned.astype(jnp.float32), axis=-1)
    gate_part = jnp.sum(
        jnp.where(
            gate_index[:, :, None] == jnp.arange(2 * tasks_total, dtype=jnp.int32),
            gate_terms[:, :, None],
            0.0,
        ),
        axis=(0, 1),
    )
    grad_arrived = lax.all_to_all(grad_sent, "expert", split_axis=0, concat_axis=0, tiled=True)
    inputs = received.reshape(-1, features)
    hidden = packed[2].reshape(-1, hidden_width)
    gelu_in = packed[3].reshape(-1, hidden_width)
    grad_output = grad_arrived.reshape(-1, features)
    grad_hidden = lax.dot_general(
        grad_output, w_down[0], CONTRACT_COLS, preferred_element_type=jnp.float32
    )
    grad_gelu = jax.vjp(jax.nn.gelu, gelu_in)[1](grad_hidden)[0].astype(jnp.bfloat16)
    grad_up_w = lax.dot_general(
        inputs, grad_gelu, CONTRACT_ROWS, preferred_element_type=jnp.float32
    )
    grad_up_b = jnp.sum(grad_gelu.astype(jnp.float32), axis=0)
    grad_down_w = lax.dot_general(
        hidden, grad_output, CONTRACT_ROWS, preferred_element_type=jnp.float32
    )
    grad_down_b = jnp.sum(grad_output.astype(jnp.float32), axis=0)
    grad_inputs = (
        lax.dot_general(grad_gelu, w_up[0], CONTRACT_COLS, preferred_element_type=jnp.float32)
        .astype(jnp.bfloat16)
        .reshape(received.shape)
    )
    grad_home = lax.all_to_all(grad_inputs, "expert", split_axis=0, concat_axis=0, tiled=True)
    shard_up_w, shard_up_b, shard_down_w, shard_down_b = (
        lax.psum_scatter(
            grad_up_w[None].astype(jnp.bfloat16), "head", scatter_dimension=2, tiled=True
        ).astype(jnp.float32),
        lax.psum_scatter(
            grad_up_b[None].astype(jnp.bfloat16), "head", scatter_dimension=1, tiled=True
        ).astype(jnp.float32),
        lax.psum_scatter(
            grad_down_w[None].astype(jnp.bfloat16), "head", scatter_dimension=1, tiled=True
        ).astype(jnp.float32),
        lax.psum_scatter(
            grad_down_b[None].astype(jnp.bfloat16), "head", scatter_dimension=1, tiled=True
        ).astype(jnp.float32),
    )
    grad_mixin = (
        jnp.zeros((all_rows, features), jnp.float32)
        .at[target.reshape(-1)]
        .add(grad_home.reshape(-1, features).astype(jnp.float32))
    )
    short_dmix, long_dmix = (
        lax.psum_scatter(
            grad_mixin[:short_total].reshape(short_in.shape).astype(jnp.bfloat16),
            "head",
            scatter_dimension=0,
            tiled=True,
        ).astype(jnp.float32),
        lax.psum_scatter(
            grad_mixin[short_total:].reshape(long_in.shape).astype(jnp.bfloat16),
            "head",
            scatter_dimension=0,
            tiled=True,
        ).astype(jnp.float32),
    )
    short_dmid, short_gain_two, short_shift_two = jax.vjp(
        layer_norm, own_short_mid, ln_gain[1], ln_bias[1]
    )[1](short_dmix)
    long_dmid, long_gain_two, long_shift_two = jax.vjp(
        layer_norm, own_long_mid, ln_gain[1], ln_bias[1]
    )[1](long_dmix)
    short_dmid = short_dmid + lax.dynamic_slice_in_dim(short_cot, short_start, short_dev, 0).astype(
        jnp.float32
    )
    long_dmid = long_dmid + lax.dynamic_slice_in_dim(long_cot, long_start, long_dev, 0).astype(
        jnp.float32
    )
    short_dattn = (own_short_mask * short_dmid).astype(jnp.bfloat16)
    long_dattn = (own_long_mask * long_dmid).astype(jnp.bfloat16)
    bias_out_grad = jnp.sum(short_dattn.astype(jnp.float32), axis=(0, 1)) + jnp.sum(
        long_dattn.astype(jnp.float32), axis=(0, 1)
    )
    attn_short_grad, attn_long_grad = group_rows(short_dattn, long_dattn)
    short_back = attend_back(
        short_normed, short_lens, short_kept, attn_short_grad, attn_qkv, attn_out_w
    )
    long_back = attend_back(long_normed, long_lens, long_kept, attn_long_grad, attn_qkv, attn_out_w)
    short_dnormed, long_dnormed = (
        lax.psum_scatter(
            short_back[0].astype(jnp.bfloat16), "head", scatter_dimension=0, tiled=True
        ).astype(jnp.float32),
        lax.psum_scatter(
            long_back[0].astype(jnp.bfloat16), "head", scatter_dimension=0, tiled=True
        ).astype(jnp.float32),
    )
    short_dln, short_gain_one, short_shift_one = jax.vjp(
        layer_norm, own_short_in, ln_gain[0], ln_bias[0]
    )[1](short_dnormed)
    long_dln, long_gain_one, long_shift_one = jax.vjp(
        layer_norm, own_long_in, ln_gain[0], ln_bias[0]
    )[1](long_dnormed)
    short_dx = short_dmid + short_dln
    long_dx = long_dmid + long_dln
    qkv_terms = short_back[1] + long_back[1]
    out_terms = short_back[2] + long_back[2]
    bias_terms = short_back[3] + long_back[3]
    grad_qkv, grad_attn_weight, grad_qv = (
        lax.psum(qkv_terms.astype(jnp.bfloat16), "expert").astype(jnp.float32),
        lax.psum(out_terms.astype(jnp.bfloat16), "expert").astype(jnp.float32),
        lax.psum(bias_terms.astype(jnp.bfloat16), "expert").astype(jnp.float32),
    )
    gain_grads = jnp.stack([short_gain_one + long_gain_one, short_gain_two + long_gain_two])
    shift_grads = jnp.stack([short_shift_one + long_shift_one, short_shift_two + long_shift_two])
    grad_gain, grad_shift, grad_bias_out, gate_total = lax.psum(
        (gain_grads, shift_grads, bias_out_grad, gate_part), ("expert", "head")
    )
    gate_grad = gate_total.reshape(tasks_total, 2)
    logit_grad = gate_probs * (gate_grad - jnp.sum(gate_probs * gate_grad, axis=-1, keepdims=True))
    grad_task = jnp.sum(logit_grad[:, :, None] * chosen_cols, axis=1)
    grad_gate = jnp.einsum("tke,tk,td->de", expert_hits, logit_grad, task_emb, precision=HIGHEST)
    return (
        short_out,
        long_out,
        short_dx,
        long_dx,
        grad_gain,
        grad_shift,
        grad_qkv,
        grad_qv,
        grad_attn_weight,
        grad_bias_out,
        shard_up_w,
        shard_up_b,
        shard_down_w,
        shard_down_b,
        grad_task,
        grad_gate,
    )


BF16 = jnp.bfloat16
F32 = jnp.float32
VMEM_LIMIT = 56 * 1024 * 1024
SLICE_ROWS = 272
HALF_PACK = 1088
QKV_ROWS = 1536
MISC_ROW = 2048
GRAD_ROWS = 1040


def mm(a, b):
    return lax.dot_general(a, b, (((1,), (0,)), ((), ())), preferred_element_type=F32)


def mm_nt(a, b):
    return lax.dot_general(a, b, (((1,), (1,)), ((), ())), preferred_element_type=F32)


def mm_tn(a, b):
    return lax.dot_general(a, b, (((0,), (0,)), ((), ())), preferred_element_type=F32)


def iota(shape, dim):
    return lax.broadcasted_iota(jnp.int32, shape, dim)


def params(**kw):
    return pltpu.CompilerParams(vmem_limit_bytes=VMEM_LIMIT, **kw)


def cost(micros):
    return pl.CostEstimate(flops=0, bytes_accessed=int(micros * 3.7e6), transcendentals=0)


VM = pl.BlockSpec(memory_space=pltpu.VMEM)
SM = pl.BlockSpec(memory_space=pltpu.SMEM)
ANY = pl.BlockSpec(memory_space=pl.ANY)


def pack_kernel(qkv, qv, wo, out):
    core = lax.axis_index("expert") % 2
    feats = qkv.shape[1]
    split = HALF_PACK - 2 * feats

    @pl.when(core == 0)
    def _():
        out[0:feats, :] = qkv[0]
        out[feats : 2 * feats, :] = qkv[1]
        out[2 * feats :, :] = qkv[2, 0:split, :]

    @pl.when(core != 0)
    def _():
        at = feats - split
        out[0:at, :] = qkv[2, split:, :]
        for c in range(4):
            out[at + 128 * c : at + 128 * (c + 1), :] = wo[:, 128 * c : 128 * (c + 1)]
        at += 4 * 128
        out[at:, :] = jnp.zeros((HALF_PACK - at, 128), BF16)
        high = qv[...].astype(BF16)
        low = (qv[...] - high.astype(F32)).astype(BF16)
        out[at : at + 2, :] = high
        out[at + 2 : at + 4, :] = low


def split_cycles(pair_left, pair_right, eye, count):
    step = mm(pair_left.astype(BF16), pair_right.astype(BF16))
    reach = jnp.minimum(eye + step, 1.0)
    hops = 1
    while hops < count // 2:
        wide = reach.astype(BF16)
        reach = jnp.minimum(mm(wide, wide), 1.0)
        hops *= 2
    lanes = iota((count, count), 1).astype(F32)
    lowest = jnp.min(jnp.where(reach > 0.5, lanes, float(count)), axis=1, keepdims=True)
    lowest_row = jnp.sum(eye * lowest, axis=0, keepdims=True)
    other = jnp.sum(pair_left * lowest_row, axis=1, keepdims=True)
    return (lowest > other).astype(F32)


def route_kernel(st_ref, sl_ref, lt_ref, ll_ref, ids_ref, temb_ref, gw_ref, tab_ref, gate_ref):
    here = lax.axis_index("head").astype(jnp.int32)
    group = lax.axis_index("expert").astype(jnp.int32)
    shorts = st_ref.shape[1]
    longs = lt_ref.shape[1]
    tasks = ids_ref.shape[1]
    per_owner = shorts // 4
    mine = here.astype(F32)

    def eye_of(n):
        return (iota((n, n), 0) == iota((n, n), 1)).astype(F32)

    def col(row, eye):
        return jnp.sum(eye * row, axis=1, keepdims=True)

    def row(column, eye):
        return jnp.sum(eye * column, axis=0, keepdims=True)

    eye = eye_of(shorts)
    at_sub, at_lane = iota((shorts, shorts), 0), iota((shorts, shorts), 1)
    off_diag = 1.0 - eye
    task_row = st_ref[...].astype(F32)
    task_col = col(task_row, eye)
    same_task = (task_col == task_row).astype(F32)
    earlier = (at_lane < at_sub).astype(F32)
    later = (at_lane > at_sub).astype(F32)
    rank_col = jnp.sum(same_task * earlier, axis=1, keepdims=True)
    rank_row = jnp.sum(same_task * later, axis=0, keepdims=True)
    first_of_pair = jnp.floor(rank_col * 0.5) == jnp.floor(rank_row * 0.5)
    pair_right = same_task * first_of_pair.astype(F32) * off_diag
    pair_left = ((at_sub // 2) == (at_lane // 2)).astype(F32) * off_diag
    major = split_cycles(pair_left, pair_right, eye, shorts)
    same_major = (major == row(major, eye)).astype(F32)
    pair_right = same_task * same_major * off_diag
    pair_left = ((at_sub // 4) == (at_lane // 4)).astype(F32) * same_major * off_diag
    minor = split_cycles(pair_left, pair_right, eye, shorts)
    colour = 2.0 * major + minor
    same_owner = ((at_sub // per_owner) == (at_lane // per_owner)).astype(F32)
    same_colour = (colour == row(colour, eye)).astype(F32)
    place = jnp.sum(same_owner * same_colour * earlier, axis=1, keepdims=True)

    sent = iota((shorts, 128), 0)
    lane = iota((shorts, 128), 1)
    sent_f = sent.astype(F32)
    lane_f = lane.astype(F32)
    length_col = col(sl_ref[...].astype(F32), eye)
    own = ((task_col == lane_f) & (colour == mine)).astype(F32)
    owner_col = (iota((shorts, 1), 0) // per_owner).astype(F32)

    def put(r, values):
        tab_ref[r : r + 1, :] = values.astype(jnp.int32)

    def put_away(r, values, low):
        tab_ref[r : r + 1, :] = values.astype(jnp.int32) ^ (here * low)

    def total(values):
        return jnp.sum(values, axis=0, keepdims=True)

    tab_ref[...] = jnp.zeros_like(tab_ref)
    put(0, total(own * sent_f))
    put(1, total(own * length_col))
    put_away(2, total(own * (owner_col * 2.0 + place)), 2)
    natural = (sent == lane + here * per_owner) & (lane < per_owner)
    put_away(6, total(natural.astype(F32) * (colour * 2.0 + place)), 2)

    eye_l = eye_of(longs)
    sub_l, lane_l = iota((longs, longs), 0), iota((longs, longs), 1)
    ltask_row = lt_ref[...].astype(F32)
    ltask_col = col(ltask_row, eye_l)
    right_l = (ltask_col == ltask_row).astype(F32) * (1.0 - eye_l)
    left_l = ((sub_l // 2) == (lane_l // 2)).astype(F32) * (1.0 - eye_l)
    kappa = split_cycles(left_l, right_l, eye_l, longs)
    parity_col = ltask_col - 2.0 * jnp.floor(ltask_col * 0.5)
    parity = jnp.max(parity_col, axis=0, keepdims=True)
    lsent = iota((longs, 128), 0)
    llane = iota((longs, 128), 1)
    unit_task = parity + 2.0 * llane.astype(F32)
    mine_l = (here % 2).astype(F32)
    own_l = ((ltask_col == unit_task) & (kappa == mine_l)).astype(F32)
    llen_col = col(ll_ref[...].astype(F32), eye_l)
    put(3, total(own_l * lsent.astype(F32)))
    put_away(16, total(own_l * (lsent // (longs // 4)).astype(F32)), 1)
    put(4, total(own_l * llen_col))
    row_lane = iota((1, 128), 1)
    row_lane_f = row_lane.astype(F32)
    put(5, parity + 2.0 * row_lane_f)
    natural_l = (lsent == llane + here * (longs // 4)) & (llane < longs // 4)
    put_away(7, total(natural_l.astype(F32) * kappa), 1)
    put_away(15, total(natural_l.astype(F32) * (kappa + 2.0)), 1)

    ids = ids_ref[...].astype(F32)
    eye_t = eye_of(tasks)
    e_first, e_second = col(ids[0:1, :], eye_t), col(ids[1:2, :], eye_t)
    tsub = iota((tasks, 128), 0).astype(F32)
    tlane = iota((tasks, 128), 1).astype(F32)
    diag = (tsub == tlane).astype(F32)
    put(8, total(diag * e_first))
    put(9, total(diag * e_second))
    task_first = total((e_first == tlane).astype(F32) * tsub)
    task_second = total((e_second == tlane).astype(F32) * tsub)
    put(10, task_first)
    put(11, task_second)
    first_parity = task_first - 2.0 * jnp.floor(task_first * 0.5)
    use_second = first_parity != parity
    put(12, use_second.astype(F32))
    unit_of = jnp.where(use_second, task_second, task_first)
    put(13, jnp.floor((unit_of - parity) * 0.5))
    half = here // 2
    tab_ref[14:15, :] = jnp.where(row_lane == 0, half, jnp.where(row_lane == 1, here, group))

    logits = lax.dot_general(
        temb_ref[...],
        gw_ref[...],
        (((1,), (1,)), ((), ())),
        preferred_element_type=F32,
        precision=HIGHEST,
    )
    ecols = iota((tasks, logits.shape[1]), 1).astype(F32)
    first = jnp.sum(jnp.where(ecols == e_first, logits, 0.0), axis=1, keepdims=True)
    second = jnp.sum(jnp.where(ecols == e_second, logits, 0.0), axis=1, keepdims=True)
    top = jnp.maximum(first, second)
    first, second = jnp.exp(first - top), jnp.exp(second - top)
    denominator = first + second
    gate_ref[...] = jnp.where(
        tlane == 0.0, first / denominator, jnp.where(tlane == 1.0, second / denominator, 0.0)
    )


def norm_stats(values):
    centred = values - jnp.mean(values, axis=-1, keepdims=True)
    scale = lax.rsqrt(jnp.mean(centred * centred, axis=-1, keepdims=True) + 1e-05)
    return centred * scale, scale


def prep_kernel(
    tab, gates, cs0, cs1, cl, csb, clb, xs, xl, gain, bias,
    deo, cb_s, cb_l, ns, nl, xb_s, xb_l,
):
    e = pl.program_id(0)
    span = cs0.shape[1]
    for k, ref in ((0, cs0), (1, cs1)):
        t = tab[10 + k, e]
        keep = iota((span, 1), 0) < tab[1, t]
        deo[0, span * k : span * (k + 1), :] = jnp.where(
            keep, gates[t, k] * ref[0].astype(F32), 0.0
        ).astype(BF16)
    half_rows = cl.shape[1]
    u = tab[13, e]
    gate = gates[tab[5, u], tab[12, e]]
    keep = iota((half_rows, 1), 0) + half_rows * tab[14, 0] < tab[4, u]
    deo[0, 2 * span : 2 * span + half_rows, :] = jnp.where(keep, gate * cl[0].astype(F32), 0.0).astype(BF16)
    parity = (tab[5, 0] % 2).astype(F32)
    deo[0, 2 * span + half_rows :, :] = jnp.full((16, deo.shape[2]), parity, F32).astype(BF16)
    cb_s[...] = csb[...]
    cb_l[...] = clb[...]
    xb_s[...] = xs[...]
    xb_l[...] = xl[...]
    ns[0] = (norm_stats(xs[0].astype(F32))[0] * gain[0:1, :] + bias[0:1, :]).astype(BF16)
    nl[0] = (norm_stats(xl[0].astype(F32))[0] * gain[0:1, :] + bias[0:1, :]).astype(BF16)


def unpack_weights(own, other, w, wo, bqv):
    shards = own.shape[0]
    for h in range(shards):
        cols = slice(128 * h, 128 * (h + 1))
        w[0:HALF_PACK, cols] = own[h]
        w[HALF_PACK:QKV_ROWS, cols] = other[h, 0 : QKV_ROWS - HALF_PACK, :]
        for c in range(4):
            at = QKV_ROWS - HALF_PACK + 128 * c
            wo[128 * h : 128 * (h + 1), 128 * c : 128 * (c + 1)] = other[h, at : at + 128, :]
        at = MISC_ROW - HALF_PACK
        lines = other[h, at : at + 16, :].astype(F32)
        bqv[0:2, cols] = lines[0:2] + lines[2:4]


def pair_masks():
    lanes = iota((1, 128), 1)
    first = (lanes < HEAD_DIM).astype(BF16)
    return first, (1.0 - first.astype(F32)).astype(BF16)


def both_heads(block, masks):
    return jnp.concatenate([block * masks[0], block * masks[1]], axis=0)


def fold_heads(stacked, keys):
    lanes = iota((1, 128), 1)
    return jnp.where(lanes < HEAD_DIM, stacked[:keys], stacked[keys:])


def softmax_pair(scores, visible, keys):
    parts = []
    for part in (scores[:, :keys], scores[:, keys:]):
        part = jnp.where(visible, part, -1e30)
        shifted = jnp.exp(part - jnp.max(part, axis=-1, keepdims=True))
        parts.append(shifted * (1.0 / jnp.sum(shifted, axis=-1, keepdims=True)))
    return jnp.concatenate(parts, axis=1).astype(BF16)


def short_visible(tab, i, span):
    rows, lanes = iota((128, 128), 0), iota((128, 128), 1)
    limit = jnp.where(iota((1, 128), 1) < span, tab[1, 2 * i], tab[1, 2 * i + 1] + span)
    return ((rows // span) == (lanes // span)) & (lanes < limit)


def attend_short(
    tab, norm, x, own, other, gain, bias, bo, q_ref, k_ref, v_ref, p_ref, ctx, mid, send, w, wo, bqv
):
    core = tab[14, 2] % 2

    @pl.when(core == 0)
    def _():
        unpack_weights(own, other, w, wo, bqv)

    @pl.when(core != 0)
    def _():
        unpack_weights(other, own, w, wo, bqv)

    feats = norm.shape[1]
    rows = norm[...]
    q_ref[...] = ((mm(rows, w[0:feats, :]) + bqv[0:1, :]).astype(BF16) * HEAD_DIM ** (-0.5)).astype(BF16)
    k_ref[...] = mm(rows, w[feats : 2 * feats, :]).astype(BF16)
    v_ref[...] = (mm(rows, w[2 * feats : 3 * feats, :]) + bqv[1:2, :]).astype(BF16)
    masks = pair_masks()
    span = send.shape[2]
    for i in range(norm.shape[0] // 128):
        visible = short_visible(tab, i, span)
        r = slice(128 * i, 128 * (i + 1))
        for p in range(feats // 128):
            c = slice(128 * p, 128 * (p + 1))
            scores = mm_nt(q_ref[r, c], both_heads(k_ref[r, c], masks))
            probs = softmax_pair(scores, visible, 128)
            p_ref[i * (feats // 128) + p] = probs
            ctx[r, c] = mm(probs, both_heads(v_ref[r, c], masks)).astype(BF16)
    attn = mm(ctx[...], wo[...]) + bo[...]
    for t in range(send.shape[0]):
        r = slice(span * t, span * (t + 1))
        keep = iota((span, 1), 0) < tab[1, t]
        middle = x[r, :].astype(F32) + jnp.where(keep, attn[r, :], 0.0)
        mid[r, :] = middle
        mixin = (norm_stats(middle)[0] * gain[1:2, :] + bias[1:2, :]).astype(BF16)
        send[tab[8, t], 0] = mixin
        send[tab[9, t], 1] = mixin


def attend_long(tab, norm, x, w, wo, bqv, gain, bias, bo, q_ref, k_ref, v_ref, p_ref, ctx, mid, send, nq):
    feats = norm.shape[1]
    half_rows = send.shape[1]
    span = 2 * half_rows
    units = norm.shape[0] // span
    offset = tab[14, 0] * half_rows
    for u in range(units):
        at = pl.multiple_of(span * u + offset, half_rows)
        nq[half_rows * u : half_rows * (u + 1), :] = norm[pl.ds(at, half_rows), :]
    rows = norm[...]
    q_ref[...] = ((mm(nq[...], w[0:feats, :]) + bqv[0:1, :]).astype(BF16) * HEAD_DIM ** (-0.5)).astype(BF16)
    k_ref[...] = mm(rows, w[feats : 2 * feats, :]).astype(BF16)
    v_ref[...] = (mm(rows, w[2 * feats : 3 * feats, :]) + bqv[1:2, :]).astype(BF16)
    masks = pair_masks()
    for u in range(units):
        visible = iota((1, span), 1) < tab[4, u]
        r = slice(half_rows * u, half_rows * (u + 1))
        kr = slice(span * u, span * (u + 1))
        for p in range(feats // 128):
            c = slice(128 * p, 128 * (p + 1))
            scores = mm_nt(q_ref[r, c], both_heads(k_ref[kr, c], masks))
            probs = softmax_pair(scores, visible, span)
            p_ref[u * (feats // 128) + p] = probs
            ctx[r, c] = mm(probs, both_heads(v_ref[kr, c], masks)).astype(BF16)
    attn = mm(ctx[...], wo[...]) + bo[...]
    for u in range(units):
        r = slice(half_rows * u, half_rows * (u + 1))
        keep = iota((half_rows, 1), 0) + offset < tab[4, u]
        at = pl.multiple_of(span * u + offset, half_rows)
        middle = x[pl.ds(at, half_rows), :].astype(F32) + jnp.where(keep, attn[r, :], 0.0)
        mid[r, :] = middle
        mixin = (norm_stats(middle)[0] * gain[1:2, :] + bias[1:2, :]).astype(BF16)
        t = tab[5, u]
        send[tab[8, t]] = mixin
        send[tab[9, t]] = mixin


GELU_A = 0.7978845608028654
GELU_B = 0.044715


def expert_kernel(first, tab, *refs):
    if first:
        x, d, wu, bu, wd, bd, eo, dx, dw, ga, xt, dt, ea, da, hs, ps = refs
        prev = None
    else:
        x, d, wu, bu, wd, bd, par, prev, ga_in, _, eo, dx, dw, ga, xt, dt, ea, da, hs, ps = refs
    j = pl.program_id(0)
    feats = x.shape[2]
    rows = x.shape[0] * x.shape[1]
    step = 8 * x.shape[1]

    @pl.when(j == 0)
    def _():
        for g in range(x.shape[0]):
            cols = slice(x.shape[1] * g, x.shape[1] * (g + 1))
            xt[:, cols] = x[g].T
            dt[:, cols] = d[g].T
        ea[...] = jnp.broadcast_to(bd[...], ea.shape)
        da[...] = jnp.zeros_like(da)

    for i in range(rows // step):
        r = slice(step * i, step * (i + 1))
        xr = x[8 * i : 8 * i + 8].reshape(step, feats)
        dr = d[8 * i : 8 * i + 8].reshape(step, feats)
        pre = mm(xr, wu[0]) + bu[...]
        square = pre * pre
        half = 0.5 + 0.5 * jnp.tanh(pre * (GELU_A + (GELU_A * GELU_B) * square))
        hidden = (pre * half).astype(BF16)
        half, square = half.astype(BF16), square.astype(BF16)
        slope = half + hidden * (1.0 - half) * (2.0 * GELU_A + (6.0 * GELU_A * GELU_B) * square)
        dpre = mm_nt(dr, wd[0]).astype(BF16) * slope
        hs[r, :] = hidden
        ps[r, :] = dpre
        ea[r, :] += mm(hidden, wd[0])
        da[r, :] += mm_nt(dpre, wu[0])

    wide = wu.shape[2]
    grad_up = mm(xt[...], ps[...])
    grad_down = mm(dt[...], hs[...]).T
    ones = jnp.ones((16, rows), BF16)
    up_bias = mm(ones, ps[...])[0:1, :]
    down_bias = mm_nt(ones, dt[...])[0:1, :]
    if prev is not None:
        grad_up += prev[0, 0:feats, :].astype(F32)
        grad_down += prev[0, feats : feats + wide, :].astype(F32)
        tail = prev[0, feats + wide :, :].astype(F32)
        up_bias += tail[0:1, :]
        down_bias += tail[1:2, :]
    dw[0, 0:feats, :] = grad_up.astype(BF16)
    dw[0, feats : feats + wide, :] = grad_down.astype(BF16)
    which = iota((16, 1), 0)
    dw[0, feats + wide :, :] = jnp.where(
        which == 0, up_bias, jnp.where(which == 1, down_bias, 0.0)
    ).astype(BF16)

    @pl.when(j == pl.num_programs(0) - 1)
    def _():
        own = tab[14, 2]
        t_first, t_second = tab[10, own], tab[11, own]
        lanes = iota((1, 128), 1)
        as_first = (lanes == 2 * t_first).astype(F32)
        as_second = (lanes == 2 * t_second + 1).astype(F32)
        rows_each = x.shape[1]
        gate_sums = jnp.zeros((1, 128), F32)
        for g in range(x.shape[0]):
            r = slice(rows_each * g, rows_each * (g + 1))
            out = ea[r, :].astype(BF16)
            eo[g] = out
            dx[g] = da[r, :].astype(BF16)
            prod = out.astype(F32) * d[g].astype(F32)
            if first:
                half_each = rows_each // 2
                gate_sums += as_first * jnp.sum(prod[:half_each], keepdims=True)
                gate_sums += as_second * jnp.sum(prod[half_each:], keepdims=True)
            else:
                odd = par[g, 0:1, 0:128].astype(F32)
                is_first = odd == (t_first % 2).astype(F32)
                gate_sums += jnp.where(is_first, as_first, as_second) * jnp.sum(prod, keepdims=True)
        if not first:
            gate_sums += ga_in[0:1, :]
        ga[...] = jnp.broadcast_to(gate_sums, ga.shape)


def experts_pass(tab, x, deo, part, w_up, b_up, w_down, b_down, prev, ga, eo):
    experts, rows_each, feats = x.shape
    hidden = w_up.shape[2]
    chunk = hidden // 4
    rows = experts * rows_each
    first = prev is None
    in_specs = [
        SM,
        pl.BlockSpec((experts, rows_each, feats), lambda j: (0, 0, 0)),
        pl.BlockSpec((experts, rows_each, feats), lambda j: (0, part, 0)),
        pl.BlockSpec((1, feats, chunk), lambda j: (0, 0, j)),
        pl.BlockSpec((1, chunk), lambda j: (0, j)),
        pl.BlockSpec((1, chunk, feats), lambda j: (0, j, 0)),
        pl.BlockSpec((1, feats), lambda j: (0, 0)),
    ]
    args = [tab, x, deo, w_up, b_up, w_down, b_down]
    if not first:
        in_specs.append(pl.BlockSpec((experts, 16, feats), lambda j: (0, 2 * rows_each // 16, 0)))
        args.append(deo)
        in_specs.append(pl.BlockSpec((1, GRAD_ROWS, feats), lambda j: (j, 0, 0)))
        args.append(prev)
        in_specs.append(pl.BlockSpec((8, 128), lambda j: (0, 0)))
        args.append(ga)
        in_specs.append(ANY)
        args.append(eo)
    return pl.pallas_call(
        functools.partial(expert_kernel, first),
        grid=(4,),
        in_specs=in_specs,
        out_specs=[
            pl.BlockSpec((experts, rows_each, feats), lambda j: (0, part, 0)),
            pl.BlockSpec((experts, rows_each, feats), lambda j: (0, 0, 0)),
            pl.BlockSpec((1, GRAD_ROWS, feats), lambda j: (j, 0, 0)),
            pl.BlockSpec((8, 128), lambda j: (0, 0)),
        ],
        out_shape=[
            jax.ShapeDtypeStruct((experts, 2 * rows_each, feats), BF16),
            jax.ShapeDtypeStruct(x.shape, BF16),
            jax.ShapeDtypeStruct((4, GRAD_ROWS, feats), BF16),
            jax.ShapeDtypeStruct((8, 128), F32),
        ],
        scratch_shapes=[
            pltpu.VMEM((feats, rows), BF16),
            pltpu.VMEM((feats, rows), BF16),
            pltpu.VMEM((rows, feats), F32),
            pltpu.VMEM((rows, feats), F32),
            pltpu.VMEM((rows, chunk), BF16),
            pltpu.VMEM((rows, chunk), BF16),
        ],
        input_output_aliases={} if first else {len(args) - 1: 0},
        compiler_params=params(),
        cost_estimate=cost(25),
        name="experts_short" if first else "experts_long",
    )(*args)


def norm_back(grad, unit, scale, gain):
    scaled = grad * gain
    return scale * (
        scaled
        - jnp.mean(scaled, axis=-1, keepdims=True)
        - unit * jnp.mean(scaled * unit, axis=-1, keepdims=True)
    )


def head_pair_back(probs, dctx, q, kk, vv, keys):
    dprobs = mm_nt(dctx, vv)
    dvalues = fold_heads(mm_tn(probs, dctx), keys)
    wide = probs.astype(F32)
    prod = wide * dprobs
    parts = []
    for part in (slice(0, keys), slice(keys, 2 * keys)):
        parts.append(prod[:, part] - wide[:, part] * jnp.sum(prod[:, part], axis=-1, keepdims=True))
    dscores = jnp.concatenate(parts, axis=1).astype(BF16)
    dqueries = mm(dscores, kk) * HEAD_DIM ** (-0.5)
    dkeys = fold_heads(mm_tn(dscores, q), keys)
    return dqueries.astype(BF16), dkeys.astype(BF16), dvalues.astype(BF16)


def row_sum(values):
    return jnp.sum(values, axis=0, keepdims=True)


def back_short(
    tab, ret, mid, c, x, norm, q_ref, k_ref, v_ref, p_ref, ctx, w, wo, gain, _,
    zsend, dw, small, _out, dmid, dattn, dctx, dq, dk, dv, dnorm,
):
    feats = norm.shape[1]
    span = zsend.shape[1]
    sums = [jnp.zeros((1, feats), F32) for _ in range(5)]
    for t in range(ret.shape[0]):
        r = slice(span * t, span * (t + 1))
        dmix = ret[tab[8, t], 0].astype(F32) + ret[tab[9, t], 1].astype(F32)
        unit, scale = norm_stats(mid[r, :])
        sums[2] += row_sum(dmix * unit)
        sums[3] += row_sum(dmix)
        middle = c[r, :].astype(F32) + norm_back(dmix, unit, scale, gain[1:2, :])
        dmid[r, :] = middle
        masked = jnp.where(iota((span, 1), 0) < tab[1, t], middle, 0.0)
        sums[4] += row_sum(masked)
        dattn[r, :] = masked.astype(BF16)
    dctx[...] = mm_nt(dattn[...], wo[...]).astype(BF16)
    dw[3 * feats : 4 * feats, :] = mm_tn(ctx[...], dattn[...]).astype(BF16)
    masks = pair_masks()
    for i in range(norm.shape[0] // 128):
        r = slice(128 * i, 128 * (i + 1))
        for p in range(feats // 128):
            c_ = slice(128 * p, 128 * (p + 1))
            a, b, d = head_pair_back(
                p_ref[i * (feats // 128) + p],
                dctx[r, c_],
                q_ref[r, c_],
                both_heads(k_ref[r, c_], masks),
                both_heads(v_ref[r, c_], masks),
                128,
            )
            dq[r, c_] = a
            dk[r, c_] = b
            dv[r, c_] = d
    rows = norm[...]
    for index, ref in enumerate((dq, dk, dv)):
        dw[feats * index : feats * (index + 1), :] = mm_tn(rows, ref[...]).astype(BF16)
    dnorm[...] = (
        mm_nt(dq[...], w[0:feats, :])
        + mm_nt(dk[...], w[feats : 2 * feats, :])
        + mm_nt(dv[...], w[2 * feats : 3 * feats, :])
    )
    for t in range(ret.shape[0]):
        r = slice(span * t, span * (t + 1))
        unit, scale = norm_stats(x[r, :].astype(F32))
        grad = dnorm[r, :]
        sums[0] += row_sum(grad * unit)
        sums[1] += row_sum(grad)
        zsend[tab[2, t]] = (dmid[r, :] + norm_back(grad, unit, scale, gain[0:1, :])).astype(BF16)
    sums.append(row_sum(dq[...].astype(F32)))
    sums.append(row_sum(dv[...].astype(F32)))
    for index, value in enumerate(sums):
        small[index : index + 1, :] = value
    small[7:8, :] = jnp.zeros((1, feats), F32)


def back_long(
    tab, ret, mid, c, x, norm, q_ref, k_ref, v_ref, p_ref, ctx, w, wo, gain, dw_in, small_in, ga, z_short,
    z0, z1, z2, z3, packed, zsend, nq, dmid, dattn, dctx, dq, dk, dv, dnorm, full,
):
    feats = norm.shape[1]
    half_rows = ret.shape[1]
    span = 2 * half_rows
    units = norm.shape[0] // span
    offset = tab[14, 0] * half_rows
    sums = [small_in[index : index + 1, :] for index in range(7)]
    for u in range(units):
        r = slice(half_rows * u, half_rows * (u + 1))
        t = tab[5, u]
        at = pl.multiple_of(span * u + offset, half_rows)
        nq[r, :] = norm[pl.ds(at, half_rows), :]
        dmix = ret[tab[8, t]].astype(F32) + ret[tab[9, t]].astype(F32)
        unit, scale = norm_stats(mid[r, :])
        sums[2] += row_sum(dmix * unit)
        sums[3] += row_sum(dmix)
        middle = c[r, :].astype(F32) + norm_back(dmix, unit, scale, gain[1:2, :])
        dmid[r, :] = middle
        masked = jnp.where(iota((half_rows, 1), 0) + offset < tab[4, u], middle, 0.0)
        sums[4] += row_sum(masked)
        dattn[r, :] = masked.astype(BF16)
    dctx[...] = mm_nt(dattn[...], wo[...]).astype(BF16)
    grad_out = mm_tn(ctx[...], dattn[...]) + dw_in[3 * feats : 4 * feats, :].astype(F32)
    shards = packed.shape[1]
    for h in range(shards):
        for s in range(4):
            full[QKV_ROWS + 128 * s : QKV_ROWS + 128 * (s + 1), 128 * h : 128 * (h + 1)] = grad_out[
                128 * h : 128 * (h + 1), 128 * s : 128 * (s + 1)
            ]
    masks = pair_masks()
    for u in range(units):
        r = slice(half_rows * u, half_rows * (u + 1))
        kr = slice(span * u, span * (u + 1))
        for p in range(feats // 128):
            c_ = slice(128 * p, 128 * (p + 1))
            a, b, d = head_pair_back(
                p_ref[u * (feats // 128) + p],
                dctx[r, c_],
                q_ref[r, c_],
                both_heads(k_ref[kr, c_], masks),
                both_heads(v_ref[kr, c_], masks),
                span,
            )
            dq[r, c_] = a
            dk[kr, c_] = b
            dv[kr, c_] = d
    for index, (left, right) in enumerate(((nq, dq), (norm, dk), (norm, dv))):
        r = slice(feats * index, feats * (index + 1))
        full[r, :] = mm_tn(left[...], right[...]) + dw_in[r, :].astype(F32)
    dnorm[...] = mm_nt(dk[...], w[feats : 2 * feats, :]) + mm_nt(dv[...], w[2 * feats : 3 * feats, :])
    from_q = mm_nt(dq[...], w[0:feats, :])
    for u in range(units):
        at = pl.multiple_of(span * u + offset, half_rows)
        dnorm[pl.ds(at, half_rows), :] += from_q[half_rows * u : half_rows * (u + 1), :]
    for u in range(units):
        owner = tab[16, u]
        for s in range(2):
            r = slice(span * u + half_rows * s, span * u + half_rows * (s + 1))
            unit, scale = norm_stats(x[r, :].astype(F32))
            grad = dnorm[r, :]
            sums[0] += row_sum(grad * unit)
            sums[1] += row_sum(grad)
            own_half = tab[14, 0] == s
            direct = jnp.where(own_half, dmid[half_rows * u : half_rows * (u + 1), :], 0.0)
            zsend[owner, half_rows * s : half_rows * (s + 1), :] = (
                direct + norm_back(grad, unit, scale, gain[0:1, :])
            ).astype(BF16)
    at = z0.shape[1] - span
    for d, ref in enumerate((z0, z1, z2, z3)):
        ref[0, 0:at, :] = z_short[2 * d : 2 * d + 2].reshape(at, feats)
        ref[0, at:, :] = zsend[d]
    sums[5] += row_sum(dq[...].astype(F32))
    sums[6] += row_sum(dv[...].astype(F32))
    full[MISC_ROW:, :] = jnp.zeros((full.shape[0] - MISC_ROW, feats), F32)
    full[MISC_ROW : MISC_ROW + 1, :] = sums[5]
    full[MISC_ROW + 1 : MISC_ROW + 2, :] = sums[6]
    for index in range(5):
        for s in range(4):
            at = MISC_ROW + 2 + 4 * index + s
            piece = sums[index][:, 128 * s : 128 * (s + 1)]
            full[at : at + 1, :] = jnp.concatenate([piece] * shards, axis=1)
    for s in range(shards):
        full[MISC_ROW + 22 : MISC_ROW + 23, 128 * s : 128 * (s + 1)] = ga[0:1, :]
    for g in range(packed.shape[0]):
        for h in range(shards):
            packed[g, tab[14, 1] ^ h] = full[
                SLICE_ROWS * g : SLICE_ROWS * (g + 1), 128 * h : 128 * (h + 1)
            ].astype(BF16)


def mix_kernel(tab, gates, ret, mid_s, mid_l, _, z0, z1, z2, z3, _out, zsend):
    experts = ret.shape[0]
    span = mid_s.shape[0] // experts
    half_rows = ret.shape[1] - 2 * span
    for t in range(experts):
        r = slice(span * t, span * (t + 1))
        keep = iota((span, 1), 0) < tab[1, t]
        e0 = ret[tab[8, t], 0:span, :].astype(F32)
        e1 = ret[tab[9, t], span : 2 * span, :].astype(F32)
        mixed = gates[t, 0] * e0 + gates[t, 1] * e1
        slot = tab[2, t]
        at = pl.multiple_of((slot % 2) * span, span)
        zsend[slot // 2, pl.ds(at, span), :] = (mid_s[r, :] + jnp.where(keep, mixed, 0.0)).astype(BF16)
    for u in range(mid_l.shape[0] // half_rows):
        r = slice(half_rows * u, half_rows * (u + 1))
        t = tab[5, u]
        keep = iota((half_rows, 1), 0) + half_rows * tab[14, 0] < tab[4, u]
        e0 = ret[tab[8, t], 2 * span :, :].astype(F32)
        e1 = ret[tab[9, t], 2 * span :, :].astype(F32)
        mixed = gates[t, 0] * e0 + gates[t, 1] * e1
        zsend[tab[16, u], 2 * span :, :] = (mid_l[r, :] + jnp.where(keep, mixed, 0.0)).astype(BF16)
    for d, ref in enumerate((z0, z1, z2, z3)):
        ref[0] = zsend[d]


def each_distance(index, refs, act):
    for d, ref in enumerate(refs):

        @pl.when(index == d)
        def _(ref=ref):
            act(ref)


def place_out(tab, a0, a1, a2, a3, _0, _1, _2, short_out, long_out):
    parts = (a0, a1, a2, a3)
    span = short_out.shape[1]
    for n in range(short_out.shape[0]):
        slot = tab[6, n]
        at = pl.multiple_of((slot % 2) * span, span)

        def copy_short(ref, n=n, at=at):
            short_out[n] = ref[0, pl.ds(at, span), :]

        each_distance(slot // 2, parts, copy_short)
    half = long_out.shape[1] // 2
    for n in range(long_out.shape[0]):
        for index, row in ((0, 7), (1, 15)):

            def copy_long(ref, n=n, index=index):
                long_out[n, half * index : half * (index + 1), :] = ref[0, 2 * span :, :]

            each_distance(tab[row, n], parts, copy_long)


def place_dx(tab, a0, a1, a2, a3, short_dx, long_dx):
    parts = (a0, a1, a2, a3)
    span = short_dx.shape[1]
    for n in range(short_dx.shape[0]):
        slot = tab[6, n]
        at = pl.multiple_of((slot % 2) * span, span)

        def copy_short(ref, n=n, at=at):
            short_dx[n] = ref[0, pl.ds(at, span), :].astype(F32)

        each_distance(slot // 2, parts, copy_short)
    for n in range(long_dx.shape[0]):

        def first(ref, n=n):
            long_dx[n] = ref[0, 2 * span :, :].astype(F32)

        def second(ref, n=n):
            long_dx[n] += ref[0, 2 * span :, :].astype(F32)

        each_distance(tab[7, n], parts, first)
        each_distance(tab[15, n], parts, second)


def finish_kernel(
    g, ids, gates, temb, gw_t, qkv, qv, wo, gain, shift, bo, grad_temb, grad_gw_t
):
    feats = wo.shape[1]
    for j in range(3):
        qkv[j] = g[feats * j : feats * (j + 1), :].astype(F32)
    for c in range(4):
        at = QKV_ROWS + 128 * c
        wo[:, 128 * c : 128 * (c + 1)] = g[at : at + 128, :].astype(F32)
    misc = g[MISC_ROW : MISC_ROW + 32, :].astype(F32)
    qv[...] = misc[0:2, :]

    def line(index):
        at = 2 + 4 * index
        return jnp.concatenate([misc[at + s : at + s + 1, :] for s in range(4)], axis=1)

    gain[0:1, :], gain[1:2, :] = line(0), line(2)
    shift[0:1, :], shift[1:2, :] = line(1), line(3)
    bo[...] = line(4)
    terms = misc[22:23, :]
    tasks = temb.shape[0]
    sub, lane = iota((tasks, 128), 0), iota((tasks, 128), 1)
    first = jnp.sum(jnp.where(lane == 2 * sub, terms, 0.0), axis=1, keepdims=True)
    second = jnp.sum(jnp.where(lane == 2 * sub + 1, terms, 0.0), axis=1, keepdims=True)
    both = first + second
    first = first - gates[:, 0:1] * both
    second = second - gates[:, 1:2] * both
    experts = gw_t.shape[0]
    rows = iota((experts, tasks), 0)
    eye = (iota((tasks, tasks), 0) == iota((tasks, tasks), 1)).astype(F32)
    spread = jnp.zeros((experts, tasks), F32)
    for k, value in ((0, first), (1, second)):
        as_row = jnp.sum(eye * value, axis=0, keepdims=True)
        spread += jnp.where(rows == ids[k : k + 1, :], as_row, 0.0)
    grad_gw_t[...] = lax.dot_general(
        spread, temb[...], (((1,), (0,)), ((), ())), preferred_element_type=F32, precision=HIGHEST
    )
    grad_temb[...] = lax.dot_general(
        spread.T, gw_t[...], (((1,), (0,)), ((), ())), preferred_element_type=F32, precision=HIGHEST
    )


def finish_experts(tab, shard, up, up_b, down, down_b):
    feats = up.shape[1]
    up[0] = shard[0, 0:feats, :].astype(F32)
    down[0] = shard[0, feats : 2 * feats, :].astype(F32)
    tail = shard[0, 2 * feats :, :].astype(F32)
    up_b[...] = tail[0:1, :]
    down_b[...] = jnp.zeros_like(down_b)
    for h in range(feats // 128):

        @pl.when(tab[14, 1] == h)
        def _(h=h):
            down_b[...] = tail[1:2, 128 * h : 128 * (h + 1)]


def collect_kernel(arrived, *refs):
    for d, ref in enumerate(refs[8:12]):
        terms = arrived[0, d].astype(F32)
        for g in range(1, arrived.shape[0]):
            terms += arrived[g, d].astype(F32)
        ref[0] = terms.astype(BF16)


def shape_of(shape, dtype):
    return jax.ShapeDtypeStruct(shape, dtype)


def balanced(short_x, long_x, expert_ids):
    heads = lax.axis_size("head")
    tasks = expert_ids.shape[0]
    return (
        heads == 4
        and lax.axis_size("expert") == tasks == 8
        and short_x.shape[0] == 4 * tasks
        and long_x.shape[0] == tasks
        and short_x.shape[1:] == (64, 512)
        and long_x.shape[1:] == (256, 512)
    )


def per_device(
    short_x,
    long_x,
    short_cot,
    long_cot,
    short_len,
    long_len,
    short_task,
    long_task,
    expert_ids,
    ln_gain,
    ln_bias,
    w_qkv,
    b_qv,
    w_attn_out,
    b_attn_out,
    w_up,
    b_up,
    w_down,
    b_down,
    task_emb,
    gate_w,
):
    if not balanced(short_x, long_x, expert_ids):
        return per_device_wide(
            short_x, long_x, short_cot, long_cot, short_len, long_len, short_task, long_task,
            expert_ids, ln_gain, ln_bias, w_qkv, b_qv, w_attn_out, b_attn_out, w_up, b_up,
            w_down, b_down, task_emb, gate_w,
        )
    heads = lax.axis_size("head")
    experts = lax.axis_size("expert")
    span, feats = short_x.shape[1:]
    long_span = long_x.shape[1]
    half_rows = long_span // 2
    tasks = expert_ids.shape[0]
    units = long_x.shape[0] // 2
    rows_s = tasks * span
    rows_q = units * half_rows
    rows_l = units * long_span
    pairs = feats // 128

    own_half = pl.pallas_call(
        pack_kernel,
        in_specs=[VM] * 3,
        out_specs=VM,
        out_shape=shape_of((HALF_PACK, 128), BF16),
        compiler_params=params(),
        cost_estimate=cost(2),
        name="pack",
    )(w_qkv, b_qv, w_attn_out)
    raw_own = lax.all_gather(own_half, "head", axis=0)
    raw_other = lax.ppermute(raw_own, "expert", [(i, i ^ 1) for i in range(experts)])

    tab, gates = pl.pallas_call(
        route_kernel,
        in_specs=[VM] * 7,
        out_specs=[VM, VM],
        out_shape=[shape_of((24, 128), jnp.int32), shape_of((tasks, 128), F32)],
        compiler_params=params(),
        cost_estimate=cost(4),
        name="route",
    )(
        short_task.reshape(1, -1),
        short_len.reshape(1, -1),
        long_task.reshape(1, -1),
        long_len.reshape(1, -1),
        expert_ids.T,
        task_emb,
        gate_w.T,
    )

    def blk(n, index):
        return pl.BlockSpec((1, n, feats), index)

    deo, cot_s, cot_l, norm_s, norm_l, own_s, own_l = pl.pallas_call(
        prep_kernel,
        grid_spec=pltpu.PrefetchScalarGridSpec(
            num_scalar_prefetch=1,
            grid=(8,),
            in_specs=[
                SM,
                blk(span, lambda e, tab: (tab[0, tab[10, e]], 0, 0)),
                blk(span, lambda e, tab: (tab[0, tab[11, e]], 0, 0)),
                blk(half_rows, lambda e, tab: (tab[3, tab[13, e]], tab[14, 0], 0)),
                blk(span, lambda e, tab: (tab[0, e], 0, 0)),
                blk(span, lambda e, tab: (tab[3, e // 2], tab[14, 0] * 2 + e % 2, 0)),
                blk(span, lambda e, tab: (tab[0, e], 0, 0)),
                blk(half_rows, lambda e, tab: (tab[3, e // 2], e % 2, 0)),
                pl.BlockSpec((2, feats), lambda e, tab: (0, 0)),
                pl.BlockSpec((2, feats), lambda e, tab: (0, 0)),
            ],
            out_specs=[
                blk(2 * span + half_rows + 16, lambda e, tab: (e, 0, 0)),
                blk(span, lambda e, tab: (e, 0, 0)),
                blk(span, lambda e, tab: (e, 0, 0)),
                blk(span, lambda e, tab: (e, 0, 0)),
                blk(half_rows, lambda e, tab: (e, 0, 0)),
                blk(span, lambda e, tab: (e, 0, 0)),
                blk(half_rows, lambda e, tab: (e, 0, 0)),
            ],
        ),
        out_shape=[
            shape_of((experts, 2 * span + half_rows + 16, feats), BF16),
            shape_of((8, span, feats), BF16),
            shape_of((8, span, feats), BF16),
            shape_of((8, span, feats), BF16),
            shape_of((8, half_rows, feats), BF16),
            shape_of((8, span, feats), BF16),
            shape_of((8, half_rows, feats), BF16),
        ],
        compiler_params=params(),
        cost_estimate=cost(9),
        name="prep",
    )(tab, gates, short_cot, short_cot, long_cot, short_cot, long_cot, short_x, long_x, ln_gain, ln_bias)
    cot_s, norm_s, own_s = (a.reshape(rows_s, feats) for a in (cot_s, norm_s, own_s))
    cot_l = cot_l.reshape(rows_q, feats)
    norm_l, own_l = norm_l.reshape(rows_l, feats), own_l.reshape(rows_l, feats)
    deo = lax.all_to_all(deo, "expert", split_axis=0, concat_axis=0, tiled=True)

    bias_out = b_attn_out.reshape(1, feats)
    w_shapes = [
        shape_of((QKV_ROWS, feats), BF16),
        shape_of((feats, feats), BF16),
        shape_of((8, feats), F32),
    ]

    def attention(kernel, operands, key_rows, query_rows, keys, send_shape, more, scratch, name):
        return pl.pallas_call(
            kernel,
            in_specs=[SM] + [VM] * (len(operands) - 1),
            out_specs=[VM] * (7 + len(more)),
            out_shape=[
                shape_of((query_rows, feats), BF16),
                shape_of((key_rows, feats), BF16),
                shape_of((key_rows, feats), BF16),
                shape_of((4 * pairs, 128, 2 * keys), BF16),
                shape_of((query_rows, feats), BF16),
                shape_of((query_rows, feats), F32),
                shape_of(send_shape, BF16),
            ]
            + more,
            scratch_shapes=scratch,
            compiler_params=params(),
            cost_estimate=cost(12),
            name=name,
        )(*operands)

    q_s, k_s, v_s, p_s, ctx_s, mid_s, send_s, w_all, wo_all, bqv_all = attention(
        attend_short,
        (tab, norm_s, own_s, raw_own, raw_other, ln_gain, ln_bias, bias_out),
        rows_s, rows_s, 128, (experts, 2, span, feats), w_shapes, [], "attend_short",
    )
    send_s = send_s.reshape(experts, 2 * span, feats)
    recv_s = lax.all_to_all(send_s, "expert", split_axis=0, concat_axis=0, tiled=True)
    q_l, k_l, v_l, p_l, ctx_l, mid_l, send_l = attention(
        attend_long,
        (tab, norm_l, own_l, w_all, wo_all, bqv_all, ln_gain, ln_bias, bias_out),
        rows_l, rows_q, long_span, (experts, half_rows, feats), [],
        [pltpu.VMEM((rows_q, feats), BF16)], "attend_long",
    )
    recv_l = lax.all_to_all(send_l, "expert", split_axis=0, concat_axis=0, tiled=True)

    eo, dx_s, dw_s, ga_s = experts_pass(
        tab, recv_s, deo, 0, w_up, b_up, w_down, b_down, None, None, None
    )
    ret_s = lax.all_to_all(dx_s, "expert", split_axis=0, concat_axis=0, tiled=True)
    eo, dx_l, dw_l, ga_l = experts_pass(
        tab, recv_l, deo, 1, w_up, b_up, w_down, b_down, dw_s, ga_s, eo
    )
    ret_l = lax.all_to_all(dx_l, "expert", split_axis=0, concat_axis=0, tiled=True)
    expert_grads = lax.psum_scatter(dw_l, "head", scatter_dimension=0, tiled=True)

    def over_head(blocks):
        return [blocks[0]] + [
            lax.ppermute(blocks[d], "head", [(i, i ^ d) for i in range(heads)]) for d in range(1, heads)
        ]

    zsend_s, dw_attn, small, eo = pl.pallas_call(
        back_short,
        in_specs=[SM] + [VM] * 13 + [ANY],
        out_specs=[VM] * 3 + [ANY],
        out_shape=[
            shape_of((2 * heads, span, feats), BF16),
            shape_of((4 * feats, feats), BF16),
            shape_of((8, feats), F32),
            shape_of(eo.shape, BF16),
        ],
        input_output_aliases={14: 3},
        scratch_shapes=[
            pltpu.VMEM((rows_s, feats), F32),
            pltpu.VMEM((rows_s, feats), BF16),
            pltpu.VMEM((rows_s, feats), BF16),
            pltpu.VMEM((rows_s, feats), BF16),
            pltpu.VMEM((rows_s, feats), BF16),
            pltpu.VMEM((rows_s, feats), BF16),
            pltpu.VMEM((rows_s, feats), F32),
        ],
        compiler_params=params(),
        cost_estimate=cost(36),
        name="back_short",
    )(
        tab, ret_s.reshape(experts, 2, span, feats), mid_s, cot_s, own_s, norm_s,
        q_s, k_s, v_s, p_s, ctx_s, w_all, wo_all, ln_gain, eo,
    )
    out_all = lax.all_to_all(eo, "expert", split_axis=0, concat_axis=0, tiled=True)
    *zsend_x, packed = pl.pallas_call(
        back_long,
        in_specs=[SM] + [VM] * 17,
        out_specs=[VM] * (heads + 1),
        out_shape=[shape_of((1, 2 * span + long_span, feats), BF16)] * heads
        + [shape_of((experts, heads, SLICE_ROWS, 128), BF16)],
        scratch_shapes=[
            pltpu.VMEM((heads, long_span, feats), BF16),
            pltpu.VMEM((rows_q, feats), BF16),
            pltpu.VMEM((rows_q, feats), F32),
            pltpu.VMEM((rows_q, feats), BF16),
            pltpu.VMEM((rows_q, feats), BF16),
            pltpu.VMEM((rows_q, feats), BF16),
            pltpu.VMEM((rows_l, feats), BF16),
            pltpu.VMEM((rows_l, feats), BF16),
            pltpu.VMEM((rows_l, feats), F32),
            pltpu.VMEM((experts * SLICE_ROWS, feats), F32),
        ],
        compiler_params=params(),
        cost_estimate=cost(54),
        name="back_long",
    )(
        tab, ret_l, mid_l, cot_l, own_l, norm_l, q_l, k_l, v_l, p_l, ctx_l, w_all, wo_all, ln_gain,
        dw_attn, small, ga_l, zsend_s,
    )
    back_x = over_head(zsend_x)
    *zsend_o, packed = pl.pallas_call(
        mix_kernel,
        in_specs=[SM, SM] + [VM] * 3 + [ANY],
        out_specs=[VM] * heads + [ANY],
        out_shape=[shape_of((1, 2 * span + half_rows, feats), BF16)] * heads
        + [shape_of(packed.shape, BF16)],
        input_output_aliases={5: heads},
        scratch_shapes=[pltpu.VMEM((heads, 2 * span + half_rows, feats), BF16)],
        compiler_params=params(),
        cost_estimate=cost(12),
        name="mix",
    )(tab, gates, out_all, mid_s, mid_l, packed)
    arrived = lax.all_to_all(packed, "expert", split_axis=0, concat_axis=0, tiled=True)
    through = (*back_x, *zsend_o)
    passed = pl.pallas_call(
        collect_kernel,
        in_specs=[VM] + [ANY] * len(through),
        out_specs=[VM] * heads + [ANY] * len(through),
        out_shape=[shape_of((1, SLICE_ROWS, 128), BF16)] * heads
        + [shape_of(a.shape, a.dtype) for a in through],
        input_output_aliases={1 + i: heads + i for i in range(len(through))},
        compiler_params=params(),
        cost_estimate=cost(3),
        name="collect",
    )(arrived, *through)
    terms, back_x, zsend_o = passed[:heads], passed[heads : 2 * heads], passed[2 * heads :]
    terms = sum(part.astype(F32) for part in over_head(terms)).astype(BF16)
    back_o = over_head(zsend_o)
    attn_grads = lax.all_gather(terms[0], "expert", axis=0, tiled=True)

    short_dx, long_dx = pl.pallas_call(
        place_dx,
        in_specs=[SM] + [VM] * 4,
        out_specs=[VM, VM],
        out_shape=[shape_of((8, span, feats), F32), shape_of((2, long_span, feats), F32)],
        compiler_params=params(),
        cost_estimate=cost(4),
        name="place_dx",
    )(tab, *back_x)

    grad_qkv, grad_qv, grad_wo, grad_gain, grad_shift, grad_bo, grad_task, grad_gate = pl.pallas_call(
        finish_kernel,
        in_specs=[VM] * 5,
        out_specs=[VM] * 8,
        out_shape=[
            shape_of((3, feats, 128), F32),
            shape_of((2, 128), F32),
            shape_of((128, feats), F32),
            shape_of((2, feats), F32),
            shape_of((2, feats), F32),
            shape_of((1, feats), F32),
            shape_of((tasks, feats), F32),
            shape_of((experts, feats), F32),
        ],
        compiler_params=params(),
        cost_estimate=cost(3),
        name="finish",
    )(attn_grads, expert_ids.T, gates, task_emb, gate_w.T)
    chunk = w_up.shape[2] // 4
    grad_up, grad_up_b, grad_down, grad_down_b = pl.pallas_call(
        finish_experts,
        in_specs=[SM, VM],
        out_specs=[VM] * 4,
        out_shape=[
            shape_of((1, feats, chunk), F32),
            shape_of((1, chunk), F32),
            shape_of((1, chunk, feats), F32),
            shape_of((1, feats // heads), F32),
        ],
        compiler_params=params(),
        cost_estimate=cost(3),
        name="finish_experts",
    )(tab, expert_grads)
    short_out, long_out = pl.pallas_call(
        place_out,
        in_specs=[SM] + [VM] * 4 + [ANY] * 3,
        out_specs=[VM, VM],
        out_shape=[shape_of((8, span, feats), BF16), shape_of((2, long_span, feats), BF16)],
        compiler_params=params(),
        cost_estimate=cost(3),
        name="place_out",
    )(tab, *back_o, grad_bo, grad_down_b, short_dx)

    return (
        short_out,
        long_out,
        short_dx,
        long_dx,
        grad_gain,
        grad_shift,
        grad_qkv,
        grad_qv,
        grad_wo,
        grad_bo.reshape(feats),
        grad_up,
        grad_up_b,
        grad_down,
        grad_down_b,
        grad_task,
        grad_gate.T,
    )


def solution(mesh):
    return jax.shard_map(
        per_device,
        mesh=mesh,
        in_specs=(
            P("expert", None, None),
            P("expert", None, None),
            P("expert", None, None),
            P("expert", None, None),
            P("expert"),
            P("expert"),
            P("expert"),
            P("expert"),
            P(),
            P(),
            P(),
            P(None, None, "head"),
            P(None, "head"),
            P("head", None),
            P(),
            P("expert", None, None),
            P("expert", None),
            P("expert", None, None),
            P("expert", None),
            P(),
            P(),
        ),
        out_specs=(
            P(("expert", "head"), None, None),
            P(("expert", "head"), None, None),
            P(("expert", "head"), None, None),
            P(("expert", "head"), None, None),
            P(),
            P(),
            P(None, None, "head"),
            P(None, "head"),
            P("head", None),
            P(),
            P("expert", None, "head"),
            P("expert", "head"),
            P("expert", "head", None),
            P("expert", "head"),
            P(),
            P(),
        ),
        check_vma=False,
    )
```

```python
import functools

import jax
import jax.numpy as jnp
from jax import lax
from jax.experimental import pallas as pl
from jax.experimental.pallas import tpu as pltpu
from jax.sharding import PartitionSpec as P

HEAD_DIM = 64


HIGHEST = lax.Precision.HIGHEST
CONTRACT_ROWS = (((0,), (0,)), ((), ()))
CONTRACT_COLS = (((1,), (1,)), ((), ()))


def layer_norm(values, gain, shift):
    centred = values - jnp.mean(values, axis=-1, keepdims=True)
    spread = jnp.mean(centred * centred, axis=-1, keepdims=True)
    return centred * lax.rsqrt(spread + 1e-05) * gain + shift


def lookup(table, index):
    hits = index[..., None] == jnp.arange(table.shape[0], dtype=jnp.int32)
    return jnp.sum(jnp.where(hits, table, jnp.zeros((), table.dtype)), axis=-1)


def route_slots(tasks, expert_ids, capacity, experts):
    task_hits = tasks[:, None] == jnp.arange(expert_ids.shape[0], dtype=jnp.int32)
    chosen = jnp.sum(jnp.where(task_hits[:, :, None], expert_ids[None, :, :], 0), axis=1).reshape(
        -1
    )
    routes = chosen.shape[0]
    owner_hits = (chosen[:, None] == jnp.arange(experts, dtype=jnp.int32)).astype(jnp.int32)
    earlier = jnp.cumsum(owner_hits, axis=0) - owner_hits
    ranking = jnp.sum(earlier * owner_hits, axis=1)
    slot_key = chosen * capacity + ranking
    slot_hits = slot_key[:, None] == jnp.arange(experts * capacity, dtype=jnp.int32)
    return jnp.sum(jnp.where(slot_hits, jnp.arange(routes, dtype=jnp.int32)[:, None], 0), axis=0)


def masked_scores(queries, key_rows, lengths):
    positions = key_rows.shape[1]
    scores = jnp.einsum(
        "blhd,bmhd->bhlm", queries, key_rows, preferred_element_type=jnp.float32
    ) * HEAD_DIM ** (-0.5)
    visible = (
        jnp.arange(positions, dtype=jnp.int32)[None, None, None, :] < lengths[:, None, None, None]
    )
    return jnp.where(visible, scores, -1e30)


def attend(normed, lengths, weights, biases, head_count):
    sentences, positions, features = normed.shape
    flattened = normed.reshape(-1, features)
    shape_heads = (sentences, positions, head_count, HEAD_DIM)

    def project(index, offset):
        return (
            (jnp.dot(flattened, weights[index], preferred_element_type=jnp.float32) + offset)
            .astype(jnp.bfloat16)
            .reshape(shape_heads)
        )

    queries = project(0, biases[0])
    key_rows = project(1, 0.0)
    values = project(2, biases[1])
    scores = masked_scores(queries, key_rows, lengths)
    highest = jnp.max(scores, axis=-1, keepdims=True)
    shifted = jnp.exp(scores - highest)
    totals = jnp.sum(shifted, axis=-1, keepdims=True)
    attn_probs = (shifted / totals).astype(jnp.bfloat16)
    log_total = highest + jnp.log(totals)
    context = jnp.einsum(
        "bhlm,bmhd->blhd", attn_probs, values, preferred_element_type=jnp.float32
    ).astype(jnp.bfloat16)
    return (queries, key_rows, values, context.reshape(sentences, positions, -1), log_total)


def attend_back(normed, lengths, kept, grad_out, weights, out_weight):
    queries, key_rows, values, context, log_total = kept
    features = normed.shape[-1]
    head_cols = context.shape[-1]
    grad_flat = grad_out.reshape(-1, features)
    context_flat = context.reshape(-1, head_cols)
    grad_context = (
        lax.dot_general(grad_flat, out_weight, CONTRACT_COLS, preferred_element_type=jnp.float32)
        .astype(jnp.bfloat16)
        .reshape(queries.shape)
    )
    grad_out_weight = lax.dot_general(
        context_flat, grad_flat, CONTRACT_ROWS, preferred_element_type=jnp.float32
    )
    probs = jnp.exp(masked_scores(queries, key_rows, lengths) - log_total)
    grad_probs = jnp.einsum(
        "blhd,bmhd->bhlm", grad_context, values, preferred_element_type=jnp.float32
    )
    grad_values = jnp.einsum(
        "bhlm,blhd->bmhd",
        probs.astype(jnp.bfloat16),
        grad_context,
        preferred_element_type=jnp.float32,
    ).astype(jnp.bfloat16)
    grad_scores = (
        probs * (grad_probs - jnp.sum(probs * grad_probs, axis=-1, keepdims=True))
    ).astype(jnp.bfloat16)
    scaling = HEAD_DIM ** (-0.5)
    grad_queries = (
        jnp.einsum("bhlm,bmhd->blhd", grad_scores, key_rows, preferred_element_type=jnp.float32)
        * scaling
    ).astype(jnp.bfloat16)
    grad_keys = (
        jnp.einsum("bhlm,blhd->bmhd", grad_scores, queries, preferred_element_type=jnp.float32)
        * scaling
    ).astype(jnp.bfloat16)
    normed_flat = normed.reshape(-1, features)
    members = [member.reshape(-1, head_cols) for member in (grad_queries, grad_keys, grad_values)]
    grad_weights = jnp.stack(
        [
            lax.dot_general(normed_flat, member, CONTRACT_ROWS, preferred_element_type=jnp.float32)
            for member in members
        ]
    )
    grad_biases = jnp.stack(
        [
            jnp.sum(members[0].astype(jnp.float32), axis=0),
            jnp.sum(members[2].astype(jnp.float32), axis=0),
        ]
    )
    grad_normed = lax.dot_general(
        members[0], weights[0], CONTRACT_COLS, preferred_element_type=jnp.float32
    )
    grad_normed = grad_normed + lax.dot_general(
        members[1], weights[1], CONTRACT_COLS, preferred_element_type=jnp.float32
    )
    grad_normed = grad_normed + lax.dot_general(
        members[2], weights[2], CONTRACT_COLS, preferred_element_type=jnp.float32
    )
    return (grad_normed.reshape(normed.shape), grad_weights, grad_out_weight, grad_biases)


def group_rows(first_rows, second_rows):
    return (
        lax.all_gather(first_rows, "head", axis=0, tiled=True),
        lax.all_gather(second_rows, "head", axis=0, tiled=True),
    )


def per_device_wide(
    short_x,
    long_x,
    short_cot,
    long_cot,
    short_len,
    long_len,
    short_task,
    long_task,
    expert_ids,
    ln_gain,
    ln_bias,
    w_qkv,
    b_qv,
    w_attn_out,
    b_attn_out,
    w_up,
    b_up,
    w_down,
    b_down,
    task_emb,
    gate_w,
):
    heads_here = lax.axis_size("head")
    head_place = lax.axis_index("head")
    experts = lax.axis_size("expert")
    short_group, short_span, features = short_x.shape
    long_group, long_span = (long_x.shape[0], long_x.shape[1])
    short_dev = short_group // heads_here
    long_dev = long_group // heads_here
    hidden_width = w_up.shape[2]
    tasks_total = expert_ids.shape[0]
    cap_short = 2 * short_group // experts
    cap_long = 2 * long_group // experts
    piece_rows = (cap_short * short_span + cap_long * long_span) // heads_here
    short_total = short_group * short_span
    all_rows = short_total + long_group * long_span
    expert_hits = (expert_ids[:, :, None] == jnp.arange(experts, dtype=jnp.int32)).astype(
        jnp.float32
    )
    chosen_cols = jnp.einsum("tke,de->tkd", expert_hits, gate_w, precision=HIGHEST)
    gate_probs = jax.nn.softmax(jnp.sum(task_emb[:, None, :] * chosen_cols, axis=-1), axis=-1)
    short_slots = route_slots(short_task, expert_ids, cap_short, experts)
    long_slots = route_slots(long_task, expert_ids, cap_long, experts)
    offsets = head_place * piece_rows + jnp.arange(piece_rows, dtype=jnp.int32)
    owners = jnp.arange(experts, dtype=jnp.int32)[:, None]
    in_short = jnp.broadcast_to(offsets < cap_short * short_span, (experts, piece_rows))
    short_pos = offsets % short_span
    long_offset = jnp.maximum(offsets - cap_short * short_span, 0)
    long_pos = long_offset % long_span
    short_route = lookup(
        short_slots, owners * cap_short + jnp.minimum(offsets // short_span, cap_short - 1)
    )
    long_route = lookup(
        long_slots, owners * cap_long + jnp.minimum(long_offset // long_span, cap_long - 1)
    )
    short_sent = short_route // 2
    long_sent = long_route // 2
    position = jnp.where(in_short, short_pos, long_pos)
    target = jnp.where(
        in_short,
        short_sent * short_span + short_pos,
        short_total + long_sent * long_span + long_pos,
    )
    task_rows = jnp.where(in_short, lookup(short_task, short_sent), lookup(long_task, long_sent))
    length_rows = jnp.where(in_short, lookup(short_len, short_sent), lookup(long_len, long_sent))
    live_rows = (position < length_rows).astype(jnp.float32)
    gate_index = task_rows * 2 + jnp.where(in_short, short_route % 2, long_route % 2)
    gate_rows = lookup(gate_probs.reshape(-1), gate_index)
    short_mask = (jnp.arange(short_span, dtype=jnp.int32)[None, :] < short_len[:, None]).astype(
        jnp.float32
    )[:, :, None]
    long_mask = (jnp.arange(long_span, dtype=jnp.int32)[None, :] < long_len[:, None]).astype(
        jnp.float32
    )[:, :, None]
    short_start = head_place * short_dev
    long_start = head_place * long_dev
    own_short_mask = lax.dynamic_slice_in_dim(short_mask, short_start, short_dev, 0)
    own_long_mask = lax.dynamic_slice_in_dim(long_mask, long_start, long_dev, 0)
    short_in = short_x.astype(jnp.float32)
    long_in = long_x.astype(jnp.float32)
    own_short_in = lax.dynamic_slice_in_dim(short_in, short_start, short_dev, 0)
    own_long_in = lax.dynamic_slice_in_dim(long_in, long_start, long_dev, 0)
    attn_qkv, attn_qv, attn_out_w = (w_qkv, b_qv, w_attn_out)
    short_src, long_src = (short_in, long_in)
    short_lens, long_lens = (short_len, long_len)
    head_cols = attn_qkv.shape[2]
    head_count = head_cols // HEAD_DIM
    short_normed = layer_norm(short_src, ln_gain[0], ln_bias[0]).astype(jnp.bfloat16)
    long_normed = layer_norm(long_src, ln_gain[0], ln_bias[0]).astype(jnp.bfloat16)
    short_kept = attend(short_normed, short_lens, attn_qkv, attn_qv, head_count)
    long_kept = attend(long_normed, long_lens, attn_qkv, attn_qv, head_count)
    short_part = jnp.dot(
        short_kept[3].reshape(-1, head_cols), attn_out_w, preferred_element_type=jnp.float32
    ).reshape(short_src.shape)
    long_part = jnp.dot(
        long_kept[3].reshape(-1, head_cols), attn_out_w, preferred_element_type=jnp.float32
    ).reshape(long_src.shape)
    short_sum, long_sum = (
        lax.psum(short_part.astype(jnp.bfloat16), "head").astype(jnp.float32),
        lax.psum(long_part.astype(jnp.bfloat16), "head").astype(jnp.float32),
    )
    short_mid = short_in + short_mask * (short_sum + b_attn_out)
    long_mid = long_in + long_mask * (long_sum + b_attn_out)
    short_mixin = layer_norm(short_mid, ln_gain[1], ln_bias[1]).astype(jnp.bfloat16)
    long_mixin = layer_norm(long_mid, ln_gain[1], ln_bias[1]).astype(jnp.bfloat16)
    own_short_mid = lax.dynamic_slice_in_dim(short_mid, short_start, short_dev, 0)
    own_long_mid = lax.dynamic_slice_in_dim(long_mid, long_start, long_dev, 0)
    mixin_rows = jnp.concatenate(
        [short_mixin.reshape(-1, features), long_mixin.reshape(-1, features)], axis=0
    )
    outgoing = mixin_rows[target]
    received = lax.all_to_all(outgoing, "expert", split_axis=0, concat_axis=0, tiled=True)
    inputs = received.reshape(-1, features)
    gelu_in = jnp.dot(inputs, w_up[0], preferred_element_type=jnp.float32) + b_up[0]
    hidden = jax.nn.gelu(gelu_in).astype(jnp.bfloat16)
    output = (jnp.dot(hidden, w_down[0], preferred_element_type=jnp.float32) + b_down[0]).astype(
        jnp.bfloat16
    )
    returned = lax.all_to_all(
        output.reshape(received.shape), "expert", split_axis=0, concat_axis=0, tiled=True
    )
    wide_shape = received.shape[:2] + (hidden_width,)
    packed = (returned, received, hidden.reshape(wide_shape), gelu_in.reshape(wide_shape))
    returned = packed[0]
    received = packed[1]
    contrib = (gate_rows[:, :, None] * returned.astype(jnp.float32)).reshape(-1, features)
    mixed_rows = jnp.zeros((all_rows, features), jnp.float32).at[target.reshape(-1)].add(contrib)
    short_moe, long_moe = (
        lax.psum_scatter(
            mixed_rows[:short_total].reshape(short_in.shape).astype(jnp.bfloat16),
            "head",
            scatter_dimension=0,
            tiled=True,
        ).astype(jnp.float32),
        lax.psum_scatter(
            mixed_rows[short_total:].reshape(long_in.shape).astype(jnp.bfloat16),
            "head",
            scatter_dimension=0,
            tiled=True,
        ).astype(jnp.float32),
    )
    short_out = (own_short_mid + own_short_mask * short_moe).astype(jnp.bfloat16)
    long_out = (own_long_mid + own_long_mask * long_moe).astype(jnp.bfloat16)
    cot_rows = jnp.concatenate(
        [short_cot.reshape(-1, features), long_cot.reshape(-1, features)], axis=0
    )
    cot_picked = cot_rows[target].astype(jnp.float32)
    grad_sent = ((gate_rows * live_rows)[:, :, None] * cot_picked).astype(jnp.bfloat16)
    gate_terms = live_rows * jnp.sum(cot_picked * returned.astype(jnp.float32), axis=-1)
    gate_part = jnp.sum(
        jnp.where(
            gate_index[:, :, None] == jnp.arange(2 * tasks_total, dtype=jnp.int32),
            gate_terms[:, :, None],
            0.0,
        ),
        axis=(0, 1),
    )
    grad_arrived = lax.all_to_all(grad_sent, "expert", split_axis=0, concat_axis=0, tiled=True)
    inputs = received.reshape(-1, features)
    hidden = packed[2].reshape(-1, hidden_width)
    gelu_in = packed[3].reshape(-1, hidden_width)
    grad_output = grad_arrived.reshape(-1, features)
    grad_hidden = lax.dot_general(
        grad_output, w_down[0], CONTRACT_COLS, preferred_element_type=jnp.float32
    )
    grad_gelu = jax.vjp(jax.nn.gelu, gelu_in)[1](grad_hidden)[0].astype(jnp.bfloat16)
    grad_up_w = lax.dot_general(
        inputs, grad_gelu, CONTRACT_ROWS, preferred_element_type=jnp.float32
    )
    grad_up_b = jnp.sum(grad_gelu.astype(jnp.float32), axis=0)
    grad_down_w = lax.dot_general(
        hidden, grad_output, CONTRACT_ROWS, preferred_element_type=jnp.float32
    )
    grad_down_b = jnp.sum(grad_output.astype(jnp.float32), axis=0)
    grad_inputs = (
        lax.dot_general(grad_gelu, w_up[0], CONTRACT_COLS, preferred_element_type=jnp.float32)
        .astype(jnp.bfloat16)
        .reshape(received.shape)
    )
    grad_home = lax.all_to_all(grad_inputs, "expert", split_axis=0, concat_axis=0, tiled=True)
    shard_up_w, shard_up_b, shard_down_w, shard_down_b = (
        lax.psum_scatter(
            grad_up_w[None].astype(jnp.bfloat16), "head", scatter_dimension=2, tiled=True
        ).astype(jnp.float32),
        lax.psum_scatter(
            grad_up_b[None].astype(jnp.bfloat16), "head", scatter_dimension=1, tiled=True
        ).astype(jnp.float32),
        lax.psum_scatter(
            grad_down_w[None].astype(jnp.bfloat16), "head", scatter_dimension=1, tiled=True
        ).astype(jnp.float32),
        lax.psum_scatter(
            grad_down_b[None].astype(jnp.bfloat16), "head", scatter_dimension=1, tiled=True
        ).astype(jnp.float32),
    )
    grad_mixin = (
        jnp.zeros((all_rows, features), jnp.float32)
        .at[target.reshape(-1)]
        .add(grad_home.reshape(-1, features).astype(jnp.float32))
    )
    short_dmix, long_dmix = (
        lax.psum_scatter(
            grad_mixin[:short_total].reshape(short_in.shape).astype(jnp.bfloat16),
            "head",
            scatter_dimension=0,
            tiled=True,
        ).astype(jnp.float32),
        lax.psum_scatter(
            grad_mixin[short_total:].reshape(long_in.shape).astype(jnp.bfloat16),
            "head",
            scatter_dimension=0,
            tiled=True,
        ).astype(jnp.float32),
    )
    short_dmid, short_gain_two, short_shift_two = jax.vjp(
        layer_norm, own_short_mid, ln_gain[1], ln_bias[1]
    )[1](short_dmix)
    long_dmid, long_gain_two, long_shift_two = jax.vjp(
        layer_norm, own_long_mid, ln_gain[1], ln_bias[1]
    )[1](long_dmix)
    short_dmid = short_dmid + lax.dynamic_slice_in_dim(short_cot, short_start, short_dev, 0).astype(
        jnp.float32
    )
    long_dmid = long_dmid + lax.dynamic_slice_in_dim(long_cot, long_start, long_dev, 0).astype(
        jnp.float32
    )
    short_dattn = (own_short_mask * short_dmid).astype(jnp.bfloat16)
    long_dattn = (own_long_mask * long_dmid).astype(jnp.bfloat16)
    bias_out_grad = jnp.sum(short_dattn.astype(jnp.float32), axis=(0, 1)) + jnp.sum(
        long_dattn.astype(jnp.float32), axis=(0, 1)
    )
    attn_short_grad, attn_long_grad = group_rows(short_dattn, long_dattn)
    short_back = attend_back(
        short_normed, short_lens, short_kept, attn_short_grad, attn_qkv, attn_out_w
    )
    long_back = attend_back(long_normed, long_lens, long_kept, attn_long_grad, attn_qkv, attn_out_w)
    short_dnormed, long_dnormed = (
        lax.psum_scatter(
            short_back[0].astype(jnp.bfloat16), "head", scatter_dimension=0, tiled=True
        ).astype(jnp.float32),
        lax.psum_scatter(
            long_back[0].astype(jnp.bfloat16), "head", scatter_dimension=0, tiled=True
        ).astype(jnp.float32),
    )
    short_dln, short_gain_one, short_shift_one = jax.vjp(
        layer_norm, own_short_in, ln_gain[0], ln_bias[0]
    )[1](short_dnormed)
    long_dln, long_gain_one, long_shift_one = jax.vjp(
        layer_norm, own_long_in, ln_gain[0], ln_bias[0]
    )[1](long_dnormed)
    short_dx = short_dmid + short_dln
    long_dx = long_dmid + long_dln
    qkv_terms = short_back[1] + long_back[1]
    out_terms = short_back[2] + long_back[2]
    bias_terms = short_back[3] + long_back[3]
    grad_qkv, grad_attn_weight, grad_qv = (
        lax.psum(qkv_terms.astype(jnp.bfloat16), "expert").astype(jnp.float32),
        lax.psum(out_terms.astype(jnp.bfloat16), "expert").astype(jnp.float32),
        lax.psum(bias_terms.astype(jnp.bfloat16), "expert").astype(jnp.float32),
    )
    gain_grads = jnp.stack([short_gain_one + long_gain_one, short_gain_two + long_gain_two])
    shift_grads = jnp.stack([short_shift_one + long_shift_one, short_shift_two + long_shift_two])
    grad_gain, grad_shift, grad_bias_out, gate_total = lax.psum(
        (gain_grads, shift_grads, bias_out_grad, gate_part), ("expert", "head")
    )
    gate_grad = gate_total.reshape(tasks_total, 2)
    logit_grad = gate_probs * (gate_grad - jnp.sum(gate_probs * gate_grad, axis=-1, keepdims=True))
    grad_task = jnp.sum(logit_grad[:, :, None] * chosen_cols, axis=1)
    grad_gate = jnp.einsum("tke,tk,td->de", expert_hits, logit_grad, task_emb, precision=HIGHEST)
    return (
        short_out,
        long_out,
        short_dx,
        long_dx,
        grad_gain,
        grad_shift,
        grad_qkv,
        grad_qv,
        grad_attn_weight,
        grad_bias_out,
        shard_up_w,
        shard_up_b,
        shard_down_w,
        shard_down_b,
        grad_task,
        grad_gate,
    )


BF16 = jnp.bfloat16
F32 = jnp.float32
VMEM_LIMIT = 56 * 1024 * 1024
SLICE_ROWS = 272
HALF_PACK = 1088
QKV_ROWS = 1536
MISC_ROW = 2048
GRAD_ROWS = 1040


def mm(a, b):
    return lax.dot_general(a, b, (((1,), (0,)), ((), ())), preferred_element_type=F32)


def mm_nt(a, b):
    return lax.dot_general(a, b, (((1,), (1,)), ((), ())), preferred_element_type=F32)


def mm_tn(a, b):
    return lax.dot_general(a, b, (((0,), (0,)), ((), ())), preferred_element_type=F32)


def iota(shape, dim):
    return lax.broadcasted_iota(jnp.int32, shape, dim)


def params(**kw):
    return pltpu.CompilerParams(vmem_limit_bytes=VMEM_LIMIT, **kw)


def cost(micros):
    return pl.CostEstimate(flops=0, bytes_accessed=int(micros * 3.7e6), transcendentals=0)


VM = pl.BlockSpec(memory_space=pltpu.VMEM)
SM = pl.BlockSpec(memory_space=pltpu.SMEM)
ANY = pl.BlockSpec(memory_space=pl.ANY)


def pack_kernel(qkv, qv, wo, out):
    core = lax.axis_index("expert") % 2
    feats = qkv.shape[1]
    split = HALF_PACK - 2 * feats

    @pl.when(core == 0)
    def _():
        out[0:feats, :] = qkv[0]
        out[feats : 2 * feats, :] = qkv[1]
        out[2 * feats :, :] = qkv[2, 0:split, :]

    @pl.when(core != 0)
    def _():
        at = feats - split
        out[0:at, :] = qkv[2, split:, :]
        for c in range(4):
            out[at + 128 * c : at + 128 * (c + 1), :] = wo[:, 128 * c : 128 * (c + 1)]
        at += 4 * 128
        out[at:, :] = jnp.zeros((HALF_PACK - at, 128), BF16)
        high = qv[...].astype(BF16)
        low = (qv[...] - high.astype(F32)).astype(BF16)
        out[at : at + 2, :] = high
        out[at + 2 : at + 4, :] = low


def split_cycles(pair_left, pair_right, eye, count):
    step = mm(pair_left.astype(BF16), pair_right.astype(BF16))
    reach = jnp.minimum(eye + step, 1.0)
    hops = 1
    while hops < count // 2:
        wide = reach.astype(BF16)
        reach = jnp.minimum(mm(wide, wide), 1.0)
        hops *= 2
    lanes = iota((count, count), 1).astype(F32)
    lowest = jnp.min(jnp.where(reach > 0.5, lanes, float(count)), axis=1, keepdims=True)
    lowest_row = jnp.sum(eye * lowest, axis=0, keepdims=True)
    other = jnp.sum(pair_left * lowest_row, axis=1, keepdims=True)
    return (lowest > other).astype(F32)


def route_kernel(st_ref, sl_ref, lt_ref, ll_ref, ids_ref, temb_ref, gw_ref, tab_ref, gate_ref):
    here = lax.axis_index("head").astype(jnp.int32)
    group = lax.axis_index("expert").astype(jnp.int32)
    shorts = st_ref.shape[1]
    longs = lt_ref.shape[1]
    tasks = ids_ref.shape[1]
    per_owner = shorts // 4
    mine = here.astype(F32)

    def eye_of(n):
        return (iota((n, n), 0) == iota((n, n), 1)).astype(F32)

    def col(row, eye):
        return jnp.sum(eye * row, axis=1, keepdims=True)

    def row(column, eye):
        return jnp.sum(eye * column, axis=0, keepdims=True)

    eye = eye_of(shorts)
    at_sub, at_lane = iota((shorts, shorts), 0), iota((shorts, shorts), 1)
    off_diag = 1.0 - eye
    task_row = st_ref[...].astype(F32)
    task_col = col(task_row, eye)
    same_task = (task_col == task_row).astype(F32)
    earlier = (at_lane < at_sub).astype(F32)
    later = (at_lane > at_sub).astype(F32)
    rank_col = jnp.sum(same_task * earlier, axis=1, keepdims=True)
    rank_row = jnp.sum(same_task * later, axis=0, keepdims=True)
    first_of_pair = jnp.floor(rank_col * 0.5) == jnp.floor(rank_row * 0.5)
    pair_right = same_task * first_of_pair.astype(F32) * off_diag
    pair_left = ((at_sub // 2) == (at_lane // 2)).astype(F32) * off_diag
    major = split_cycles(pair_left, pair_right, eye, shorts)
    same_major = (major == row(major, eye)).astype(F32)
    pair_right = same_task * same_major * off_diag
    pair_left = ((at_sub // 4) == (at_lane // 4)).astype(F32) * same_major * off_diag
    minor = split_cycles(pair_left, pair_right, eye, shorts)
    colour = 2.0 * major + minor
    same_owner = ((at_sub // per_owner) == (at_lane // per_owner)).astype(F32)
    same_colour = (colour == row(colour, eye)).astype(F32)
    place = jnp.sum(same_owner * same_colour * earlier, axis=1, keepdims=True)

    sent = iota((shorts, 128), 0)
    lane = iota((shorts, 128), 1)
    sent_f = sent.astype(F32)
    lane_f = lane.astype(F32)
    length_col = col(sl_ref[...].astype(F32), eye)
    own = ((task_col == lane_f) & (colour == mine)).astype(F32)
    owner_col = (iota((shorts, 1), 0) // per_owner).astype(F32)

    def put(r, values):
        tab_ref[r : r + 1, :] = values.astype(jnp.int32)

    def put_away(r, values, low):
        tab_ref[r : r + 1, :] = values.astype(jnp.int32) ^ (here * low)

    def total(values):
        return jnp.sum(values, axis=0, keepdims=True)

    tab_ref[...] = jnp.zeros_like(tab_ref)
    put(0, total(own * sent_f))
    put(1, total(own * length_col))
    put_away(2, total(own * (owner_col * 2.0 + place)), 2)
    natural = (sent == lane + here * per_owner) & (lane < per_owner)
    put_away(6, total(natural.astype(F32) * (colour * 2.0 + place)), 2)

    eye_l = eye_of(longs)
    sub_l, lane_l = iota((longs, longs), 0), iota((longs, longs), 1)
    ltask_row = lt_ref[...].astype(F32)
    ltask_col = col(ltask_row, eye_l)
    right_l = (ltask_col == ltask_row).astype(F32) * (1.0 - eye_l)
    left_l = ((sub_l // 2) == (lane_l // 2)).astype(F32) * (1.0 - eye_l)
    kappa = split_cycles(left_l, right_l, eye_l, longs)
    parity_col = ltask_col - 2.0 * jnp.floor(ltask_col * 0.5)
    parity = jnp.max(parity_col, axis=0, keepdims=True)
    lsent = iota((longs, 128), 0)
    llane = iota((longs, 128), 1)
    unit_task = parity + 2.0 * llane.astype(F32)
    mine_l = (here % 2).astype(F32)
    own_l = ((ltask_col == unit_task) & (kappa == mine_l)).astype(F32)
    llen_col = col(ll_ref[...].astype(F32), eye_l)
    put(3, total(own_l * lsent.astype(F32)))
    put_away(16, total(own_l * (lsent // (longs // 4)).astype(F32)), 1)
    put(4, total(own_l * llen_col))
    row_lane = iota((1, 128), 1)
    row_lane_f = row_lane.astype(F32)
    put(5, parity + 2.0 * row_lane_f)
    natural_l = (lsent == llane + here * (longs // 4)) & (llane < longs // 4)
    put_away(7, total(natural_l.astype(F32) * kappa), 1)
    put_away(15, total(natural_l.astype(F32) * (kappa + 2.0)), 1)

    ids = ids_ref[...].astype(F32)
    eye_t = eye_of(tasks)
    e_first, e_second = col(ids[0:1, :], eye_t), col(ids[1:2, :], eye_t)
    tsub = iota((tasks, 128), 0).astype(F32)
    tlane = iota((tasks, 128), 1).astype(F32)
    diag = (tsub == tlane).astype(F32)
    put(8, total(diag * e_first))
    put(9, total(diag * e_second))
    task_first = total((e_first == tlane).astype(F32) * tsub)
    task_second = total((e_second == tlane).astype(F32) * tsub)
    put(10, task_first)
    put(11, task_second)
    first_parity = task_first - 2.0 * jnp.floor(task_first * 0.5)
    use_second = first_parity != parity
    put(12, use_second.astype(F32))
    unit_of = jnp.where(use_second, task_second, task_first)
    put(13, jnp.floor((unit_of - parity) * 0.5))
    half = here // 2
    tab_ref[14:15, :] = jnp.where(row_lane == 0, half, jnp.where(row_lane == 1, here, group))

    logits = lax.dot_general(
        temb_ref[...],
        gw_ref[...],
        (((1,), (1,)), ((), ())),
        preferred_element_type=F32,
        precision=HIGHEST,
    )
    ecols = iota((tasks, logits.shape[1]), 1).astype(F32)
    first = jnp.sum(jnp.where(ecols == e_first, logits, 0.0), axis=1, keepdims=True)
    second = jnp.sum(jnp.where(ecols == e_second, logits, 0.0), axis=1, keepdims=True)
    top = jnp.maximum(first, second)
    first, second = jnp.exp(first - top), jnp.exp(second - top)
    denominator = first + second
    gate_ref[...] = jnp.where(
        tlane == 0.0, first / denominator, jnp.where(tlane == 1.0, second / denominator, 0.0)
    )


def norm_stats(values):
    centred = values - jnp.mean(values, axis=-1, keepdims=True)
    scale = lax.rsqrt(jnp.mean(centred * centred, axis=-1, keepdims=True) + 1e-05)
    return centred * scale, scale


def prep_kernel(
    tab, gates, cs0, cs1, cl, csb, clb, xs, xl, gain, bias,
    deo, cb_s, cb_l, ns, nl, xb_s, xb_l,
):
    e = pl.program_id(0)
    span = cs0.shape[1]
    for k, ref in ((0, cs0), (1, cs1)):
        t = tab[10 + k, e]
        keep = iota((span, 1), 0) < tab[1, t]
        deo[0, span * k : span * (k + 1), :] = jnp.where(
            keep, gates[t, k] * ref[0].astype(F32), 0.0
        ).astype(BF16)
    half_rows = cl.shape[1]
    u = tab[13, e]
    gate = gates[tab[5, u], tab[12, e]]
    keep = iota((half_rows, 1), 0) + half_rows * tab[14, 0] < tab[4, u]
    deo[0, 2 * span : 2 * span + half_rows, :] = jnp.where(keep, gate * cl[0].astype(F32), 0.0).astype(BF16)
    parity = (tab[5, 0] % 2).astype(F32)
    deo[0, 2 * span + half_rows :, :] = jnp.full((16, deo.shape[2]), parity, F32).astype(BF16)
    cb_s[...] = csb[...]
    cb_l[...] = clb[...]
    xb_s[...] = xs[...]
    xb_l[...] = xl[...]
    ns[0] = (norm_stats(xs[0].astype(F32))[0] * gain[0:1, :] + bias[0:1, :]).astype(BF16)
    nl[0] = (norm_stats(xl[0].astype(F32))[0] * gain[0:1, :] + bias[0:1, :]).astype(BF16)


def unpack_weights(own, other, w, wo, bqv):
    shards = own.shape[0]
    for h in range(shards):
        cols = slice(128 * h, 128 * (h + 1))
        w[0:HALF_PACK, cols] = own[h]
        w[HALF_PACK:QKV_ROWS, cols] = other[h, 0 : QKV_ROWS - HALF_PACK, :]
        for c in range(4):
            at = QKV_ROWS - HALF_PACK + 128 * c
            wo[128 * h : 128 * (h + 1), 128 * c : 128 * (c + 1)] = other[h, at : at + 128, :]
        at = MISC_ROW - HALF_PACK
        lines = other[h, at : at + 16, :].astype(F32)
        bqv[0:2, cols] = lines[0:2] + lines[2:4]


def pair_masks():
    lanes = iota((1, 128), 1)
    first = (lanes < HEAD_DIM).astype(BF16)
    return first, (1.0 - first.astype(F32)).astype(BF16)


def both_heads(block, masks):
    return jnp.concatenate([block * masks[0], block * masks[1]], axis=0)


def fold_heads(stacked, keys):
    lanes = iota((1, 128), 1)
    return jnp.where(lanes < HEAD_DIM, stacked[:keys], stacked[keys:])


def softmax_pair(scores, visible, keys):
    parts = []
    for part in (scores[:, :keys], scores[:, keys:]):
        part = jnp.where(visible, part, -1e30)
        shifted = jnp.exp(part - jnp.max(part, axis=-1, keepdims=True))
        parts.append(shifted * (1.0 / jnp.sum(shifted, axis=-1, keepdims=True)))
    return jnp.concatenate(parts, axis=1).astype(BF16)


def short_visible(tab, i, span):
    rows, lanes = iota((128, 128), 0), iota((128, 128), 1)
    limit = jnp.where(iota((1, 128), 1) < span, tab[1, 2 * i], tab[1, 2 * i + 1] + span)
    return ((rows // span) == (lanes // span)) & (lanes < limit)


def attend_short(
    tab, norm, x, own, other, gain, bias, bo, q_ref, k_ref, v_ref, p_ref, ctx, mid, send, w, wo, bqv
):
    core = tab[14, 2] % 2

    @pl.when(core == 0)
    def _():
        unpack_weights(own, other, w, wo, bqv)

    @pl.when(core != 0)
    def _():
        unpack_weights(other, own, w, wo, bqv)

    feats = norm.shape[1]
    rows = norm[...]
    q_ref[...] = ((mm(rows, w[0:feats, :]) + bqv[0:1, :]).astype(BF16) * HEAD_DIM ** (-0.5)).astype(BF16)
    k_ref[...] = mm(rows, w[feats : 2 * feats, :]).astype(BF16)
    v_ref[...] = (mm(rows, w[2 * feats : 3 * feats, :]) + bqv[1:2, :]).astype(BF16)
    masks = pair_masks()
    span = send.shape[2]
    for i in range(norm.shape[0] // 128):
        visible = short_visible(tab, i, span)
        r = slice(128 * i, 128 * (i + 1))
        for p in range(feats // 128):
            c = slice(128 * p, 128 * (p + 1))
            scores = mm_nt(q_ref[r, c], both_heads(k_ref[r, c], masks))
            probs = softmax_pair(scores, visible, 128)
            p_ref[i * (feats // 128) + p] = probs
            ctx[r, c] = mm(probs, both_heads(v_ref[r, c], masks)).astype(BF16)
    attn = mm(ctx[...], wo[...]) + bo[...]
    for t in range(send.shape[0]):
        r = slice(span * t, span * (t + 1))
        keep = iota((span, 1), 0) < tab[1, t]
        middle = x[r, :].astype(F32) + jnp.where(keep, attn[r, :], 0.0)
        mid[r, :] = middle
        mixin = (norm_stats(middle)[0] * gain[1:2, :] + bias[1:2, :]).astype(BF16)
        send[tab[8, t], 0] = mixin
        send[tab[9, t], 1] = mixin


def attend_long(tab, norm, x, w, wo, bqv, gain, bias, bo, q_ref, k_ref, v_ref, p_ref, ctx, mid, send, nq):
    feats = norm.shape[1]
    half_rows = send.shape[1]
    span = 2 * half_rows
    units = norm.shape[0] // span
    offset = tab[14, 0] * half_rows
    for u in range(units):
        at = pl.multiple_of(span * u + offset, half_rows)
        nq[half_rows * u : half_rows * (u + 1), :] = norm[pl.ds(at, half_rows), :]
    rows = norm[...]
    q_ref[...] = ((mm(nq[...], w[0:feats, :]) + bqv[0:1, :]).astype(BF16) * HEAD_DIM ** (-0.5)).astype(BF16)
    k_ref[...] = mm(rows, w[feats : 2 * feats, :]).astype(BF16)
    v_ref[...] = (mm(rows, w[2 * feats : 3 * feats, :]) + bqv[1:2, :]).astype(BF16)
    masks = pair_masks()
    for u in range(units):
        visible = iota((1, span), 1) < tab[4, u]
        r = slice(half_rows * u, half_rows * (u + 1))
        kr = slice(span * u, span * (u + 1))
        for p in range(feats // 128):
            c = slice(128 * p, 128 * (p + 1))
            scores = mm_nt(q_ref[r, c], both_heads(k_ref[kr, c], masks))
            probs = softmax_pair(scores, visible, span)
            p_ref[u * (feats // 128) + p] = probs
            ctx[r, c] = mm(probs, both_heads(v_ref[kr, c], masks)).astype(BF16)
    attn = mm(ctx[...], wo[...]) + bo[...]
    for u in range(units):
        r = slice(half_rows * u, half_rows * (u + 1))
        keep = iota((half_rows, 1), 0) + offset < tab[4, u]
        at = pl.multiple_of(span * u + offset, half_rows)
        middle = x[pl.ds(at, half_rows), :].astype(F32) + jnp.where(keep, attn[r, :], 0.0)
        mid[r, :] = middle
        mixin = (norm_stats(middle)[0] * gain[1:2, :] + bias[1:2, :]).astype(BF16)
        t = tab[5, u]
        send[tab[8, t]] = mixin
        send[tab[9, t]] = mixin


GELU_A = 0.7978845608028654
GELU_B = 0.044715


def expert_kernel(first, tab, *refs):
    if first:
        x, d, wu, bu, wd, bd, eo, dx, dw, ga, xt, dt, ea, da, hs, ps = refs
        prev = None
    else:
        x, d, wu, bu, wd, bd, par, prev, ga_in, _, eo, dx, dw, ga, xt, dt, ea, da, hs, ps = refs
    j = pl.program_id(0)
    feats = x.shape[2]
    rows = x.shape[0] * x.shape[1]
    step = 4 * x.shape[1]

    @pl.when(j == 0)
    def _():
        for g in range(x.shape[0]):
            cols = slice(x.shape[1] * g, x.shape[1] * (g + 1))
            xt[:, cols] = x[g].T
            dt[:, cols] = d[g].T
        ea[...] = jnp.broadcast_to(bd[...], ea.shape)
        da[...] = jnp.zeros_like(da)

    @pl.loop(0, rows // step)
    def _(i):
        r = pl.ds(pl.multiple_of(step * i, step), step)
        xr = x[pl.ds(4 * i, 4)].reshape(step, feats)
        dr = d[pl.ds(4 * i, 4)].reshape(step, feats)
        pre = mm(xr, wu[0]) + bu[...]
        square = pre * pre
        half = 0.5 + 0.5 * jnp.tanh(pre * (GELU_A + (GELU_A * GELU_B) * square))
        hidden = (pre * half).astype(BF16)
        half, square = half.astype(BF16), square.astype(BF16)
        slope = half + hidden * (1.0 - half) * (2.0 * GELU_A + (6.0 * GELU_A * GELU_B) * square)
        dpre = mm_nt(dr, wd[0]).astype(BF16) * slope
        hs[r, :] = hidden
        ps[r, :] = dpre
        ea[r, :] += mm(hidden, wd[0])
        da[r, :] += mm_nt(dpre, wu[0])

    wide = wu.shape[2]
    part = feats // 2

    @pl.loop(0, 2)
    def _(i):
        m = pl.ds(pl.multiple_of(part * i, part), part)
        grad_up = mm(xt[m, :], ps[...])
        grad_down = mm(dt[m, :], hs[...]).T
        if prev is not None:
            grad_up += prev[0, m, :].astype(F32)
            grad_down += prev[0, feats : feats + wide, m].astype(F32)
        dw[0, m, :] = grad_up.astype(BF16)
        dw[0, feats : feats + wide, m] = grad_down.astype(BF16)

    ones = jnp.ones((16, rows), BF16)
    up_bias = mm(ones, ps[...])[0:1, :]
    down_bias = mm_nt(ones, dt[...])[0:1, :]
    which = iota((16, 1), 0)
    tail = jnp.where(which == 0, up_bias, jnp.where(which == 1, down_bias, 0.0))
    if prev is not None:
        tail += prev[0, feats + wide :, :].astype(F32)
    dw[0, feats + wide :, :] = tail.astype(BF16)

    @pl.when(j == pl.num_programs(0) - 1)
    def _():
        own = tab[14, 2]
        t_first, t_second = tab[10, own], tab[11, own]
        lanes = iota((1, 128), 1)
        as_first = (lanes == 2 * t_first).astype(F32)
        as_second = (lanes == 2 * t_second + 1).astype(F32)
        rows_each = x.shape[1]
        gate_sums = jnp.zeros((1, 128), F32)
        for g in range(x.shape[0]):
            r = slice(rows_each * g, rows_each * (g + 1))
            out = ea[r, :].astype(BF16)
            eo[g] = out
            dx[g] = da[r, :].astype(BF16)
            prod = out.astype(F32) * d[g].astype(F32)
            if first:
                half_each = rows_each // 2
                gate_sums += as_first * jnp.sum(prod[:half_each], keepdims=True)
                gate_sums += as_second * jnp.sum(prod[half_each:], keepdims=True)
            else:
                odd = par[g, 0:1, 0:128].astype(F32)
                is_first = odd == (t_first % 2).astype(F32)
                gate_sums += jnp.where(is_first, as_first, as_second) * jnp.sum(prod, keepdims=True)
        if not first:
            gate_sums += ga_in[0:1, :]
        ga[...] = jnp.broadcast_to(gate_sums, ga.shape)


def experts_pass(tab, x, deo, part, w_up, b_up, w_down, b_down, prev, ga, eo):
    experts, rows_each, feats = x.shape
    hidden = w_up.shape[2]
    chunk = hidden // 4
    rows = experts * rows_each
    first = prev is None
    in_specs = [
        SM,
        pl.BlockSpec((experts, rows_each, feats), lambda j: (0, 0, 0)),
        pl.BlockSpec((experts, rows_each, feats), lambda j: (0, part, 0)),
        pl.BlockSpec((1, feats, chunk), lambda j: (0, 0, j)),
        pl.BlockSpec((1, chunk), lambda j: (0, j)),
        pl.BlockSpec((1, chunk, feats), lambda j: (0, j, 0)),
        pl.BlockSpec((1, feats), lambda j: (0, 0)),
    ]
    args = [tab, x, deo, w_up, b_up, w_down, b_down]
    if not first:
        in_specs.append(pl.BlockSpec((experts, 16, feats), lambda j: (0, 2 * rows_each // 16, 0)))
        args.append(deo)
        in_specs.append(pl.BlockSpec((1, GRAD_ROWS, feats), lambda j: (j, 0, 0)))
        args.append(prev)
        in_specs.append(pl.BlockSpec((8, 128), lambda j: (0, 0)))
        args.append(ga)
        in_specs.append(ANY)
        args.append(eo)
    return pl.pallas_call(
        functools.partial(expert_kernel, first),
        grid=(4,),
        in_specs=in_specs,
        out_specs=[
            pl.BlockSpec((experts, rows_each, feats), lambda j: (0, part, 0)),
            pl.BlockSpec((experts, rows_each, feats), lambda j: (0, 0, 0)),
            pl.BlockSpec((1, GRAD_ROWS, feats), lambda j: (j, 0, 0)),
            pl.BlockSpec((8, 128), lambda j: (0, 0)),
        ],
        out_shape=[
            jax.ShapeDtypeStruct((experts, 2 * rows_each, feats), BF16),
            jax.ShapeDtypeStruct(x.shape, BF16),
            jax.ShapeDtypeStruct((4, GRAD_ROWS, feats), BF16),
            jax.ShapeDtypeStruct((8, 128), F32),
        ],
        scratch_shapes=[
            pltpu.VMEM((feats, rows), BF16),
            pltpu.VMEM((feats, rows), BF16),
            pltpu.VMEM((rows, feats), F32),
            pltpu.VMEM((rows, feats), F32),
            pltpu.VMEM((rows, chunk), BF16),
            pltpu.VMEM((rows, chunk), BF16),
        ],
        input_output_aliases={} if first else {len(args) - 1: 0},
        compiler_params=params(),
        cost_estimate=cost(25),
        name="experts_short" if first else "experts_long",
    )(*args)


def norm_back(grad, unit, scale, gain):
    scaled = grad * gain
    return scale * (
        scaled
        - jnp.mean(scaled, axis=-1, keepdims=True)
        - unit * jnp.mean(scaled * unit, axis=-1, keepdims=True)
    )


def head_pair_back(probs, dctx, q, kk, vv, keys):
    dprobs = mm_nt(dctx, vv)
    dvalues = fold_heads(mm_tn(probs, dctx), keys)
    wide = probs.astype(F32)
    prod = wide * dprobs
    parts = []
    for part in (slice(0, keys), slice(keys, 2 * keys)):
        parts.append(prod[:, part] - wide[:, part] * jnp.sum(prod[:, part], axis=-1, keepdims=True))
    dscores = jnp.concatenate(parts, axis=1).astype(BF16)
    dqueries = mm(dscores, kk) * HEAD_DIM ** (-0.5)
    dkeys = fold_heads(mm_tn(dscores, q), keys)
    return dqueries.astype(BF16), dkeys.astype(BF16), dvalues.astype(BF16)


def row_sum(values):
    return jnp.sum(values, axis=0, keepdims=True)


def back_short(
    tab, ret, mid, c, x, norm, q_ref, k_ref, v_ref, p_ref, ctx, w, wo, gain, _,
    zsend, dw, small, _out, dmid, dattn, dctx, dq, dk, dv, dnorm,
):
    feats = norm.shape[1]
    span = zsend.shape[1]
    sums = [jnp.zeros((1, feats), F32) for _ in range(5)]
    for t in range(ret.shape[0]):
        r = slice(span * t, span * (t + 1))
        dmix = ret[tab[8, t], 0].astype(F32) + ret[tab[9, t], 1].astype(F32)
        unit, scale = norm_stats(mid[r, :])
        sums[2] += row_sum(dmix * unit)
        sums[3] += row_sum(dmix)
        middle = c[r, :].astype(F32) + norm_back(dmix, unit, scale, gain[1:2, :])
        dmid[r, :] = middle
        masked = jnp.where(iota((span, 1), 0) < tab[1, t], middle, 0.0)
        sums[4] += row_sum(masked)
        dattn[r, :] = masked.astype(BF16)
    dctx[...] = mm_nt(dattn[...], wo[...]).astype(BF16)
    dw[3 * feats : 4 * feats, :] = mm_tn(ctx[...], dattn[...]).astype(BF16)
    masks = pair_masks()
    for i in range(norm.shape[0] // 128):
        r = slice(128 * i, 128 * (i + 1))
        for p in range(feats // 128):
            c_ = slice(128 * p, 128 * (p + 1))
            a, b, d = head_pair_back(
                p_ref[i * (feats // 128) + p],
                dctx[r, c_],
                q_ref[r, c_],
                both_heads(k_ref[r, c_], masks),
                both_heads(v_ref[r, c_], masks),
                128,
            )
            dq[r, c_] = a
            dk[r, c_] = b
            dv[r, c_] = d
    rows = norm[...]
    for index, ref in enumerate((dq, dk, dv)):
        dw[feats * index : feats * (index + 1), :] = mm_tn(rows, ref[...]).astype(BF16)
    dnorm[...] = (
        mm_nt(dq[...], w[0:feats, :])
        + mm_nt(dk[...], w[feats : 2 * feats, :])
        + mm_nt(dv[...], w[2 * feats : 3 * feats, :])
    )
    for t in range(ret.shape[0]):
        r = slice(span * t, span * (t + 1))
        unit, scale = norm_stats(x[r, :].astype(F32))
        grad = dnorm[r, :]
        sums[0] += row_sum(grad * unit)
        sums[1] += row_sum(grad)
        zsend[tab[2, t]] = (dmid[r, :] + norm_back(grad, unit, scale, gain[0:1, :])).astype(BF16)
    sums.append(row_sum(dq[...].astype(F32)))
    sums.append(row_sum(dv[...].astype(F32)))
    for index, value in enumerate(sums):
        small[index : index + 1, :] = value
    small[7:8, :] = jnp.zeros((1, feats), F32)


def back_long(
    tab, ret, mid, c, x, norm, q_ref, k_ref, v_ref, p_ref, ctx, w, wo, gain, dw_in, small_in, ga, z_short,
    z0, z1, z2, z3, packed, zsend, nq, dmid, dattn, dctx, dq, dk, dv, dnorm, full,
):
    feats = norm.shape[1]
    half_rows = ret.shape[1]
    span = 2 * half_rows
    units = norm.shape[0] // span
    offset = tab[14, 0] * half_rows
    sums = [small_in[index : index + 1, :] for index in range(7)]
    for u in range(units):
        r = slice(half_rows * u, half_rows * (u + 1))
        t = tab[5, u]
        at = pl.multiple_of(span * u + offset, half_rows)
        nq[r, :] = norm[pl.ds(at, half_rows), :]
        dmix = ret[tab[8, t]].astype(F32) + ret[tab[9, t]].astype(F32)
        unit, scale = norm_stats(mid[r, :])
        sums[2] += row_sum(dmix * unit)
        sums[3] += row_sum(dmix)
        middle = c[r, :].astype(F32) + norm_back(dmix, unit, scale, gain[1:2, :])
        dmid[r, :] = middle
        masked = jnp.where(iota((half_rows, 1), 0) + offset < tab[4, u], middle, 0.0)
        sums[4] += row_sum(masked)
        dattn[r, :] = masked.astype(BF16)
    dctx[...] = mm_nt(dattn[...], wo[...]).astype(BF16)
    grad_out = mm_tn(ctx[...], dattn[...]) + dw_in[3 * feats : 4 * feats, :].astype(F32)
    shards = packed.shape[1]
    for h in range(shards):
        for s in range(4):
            full[QKV_ROWS + 128 * s : QKV_ROWS + 128 * (s + 1), 128 * h : 128 * (h + 1)] = grad_out[
                128 * h : 128 * (h + 1), 128 * s : 128 * (s + 1)
            ]
    masks = pair_masks()
    for u in range(units):
        r = slice(half_rows * u, half_rows * (u + 1))
        kr = slice(span * u, span * (u + 1))
        for p in range(feats // 128):
            c_ = slice(128 * p, 128 * (p + 1))
            a, b, d = head_pair_back(
                p_ref[u * (feats // 128) + p],
                dctx[r, c_],
                q_ref[r, c_],
                both_heads(k_ref[kr, c_], masks),
                both_heads(v_ref[kr, c_], masks),
                span,
            )
            dq[r, c_] = a
            dk[kr, c_] = b
            dv[kr, c_] = d
    for index, (left, right) in enumerate(((nq, dq), (norm, dk), (norm, dv))):
        r = slice(feats * index, feats * (index + 1))
        full[r, :] = mm_tn(left[...], right[...]) + dw_in[r, :].astype(F32)
    dnorm[...] = mm_nt(dk[...], w[feats : 2 * feats, :]) + mm_nt(dv[...], w[2 * feats : 3 * feats, :])
    from_q = mm_nt(dq[...], w[0:feats, :])
    for u in range(units):
        at = pl.multiple_of(span * u + offset, half_rows)
        dnorm[pl.ds(at, half_rows), :] += from_q[half_rows * u : half_rows * (u + 1), :]
    for u in range(units):
        owner = tab[16, u]
        for s in range(2):
            r = slice(span * u + half_rows * s, span * u + half_rows * (s + 1))
            unit, scale = norm_stats(x[r, :].astype(F32))
            grad = dnorm[r, :]
            sums[0] += row_sum(grad * unit)
            sums[1] += row_sum(grad)
            own_half = tab[14, 0] == s
            direct = jnp.where(own_half, dmid[half_rows * u : half_rows * (u + 1), :], 0.0)
            zsend[owner, half_rows * s : half_rows * (s + 1), :] = (
                direct + norm_back(grad, unit, scale, gain[0:1, :])
            ).astype(BF16)
    at = z0.shape[1] - span
    for d, ref in enumerate((z0, z1, z2, z3)):
        ref[0, 0:at, :] = z_short[2 * d : 2 * d + 2].reshape(at, feats)
        ref[0, at:, :] = zsend[d]
    sums[5] += row_sum(dq[...].astype(F32))
    sums[6] += row_sum(dv[...].astype(F32))
    full[MISC_ROW:, :] = jnp.zeros((full.shape[0] - MISC_ROW, feats), F32)
    full[MISC_ROW : MISC_ROW + 1, :] = sums[5]
    full[MISC_ROW + 1 : MISC_ROW + 2, :] = sums[6]
    for index in range(5):
        for s in range(4):
            at = MISC_ROW + 2 + 4 * index + s
            piece = sums[index][:, 128 * s : 128 * (s + 1)]
            full[at : at + 1, :] = jnp.concatenate([piece] * shards, axis=1)
    for s in range(shards):
        full[MISC_ROW + 22 : MISC_ROW + 23, 128 * s : 128 * (s + 1)] = ga[0:1, :]
    for g in range(packed.shape[0]):
        for h in range(shards):
            packed[g, tab[14, 1] ^ h] = full[
                SLICE_ROWS * g : SLICE_ROWS * (g + 1), 128 * h : 128 * (h + 1)
            ].astype(BF16)


def mix_kernel(tab, gates, ret, mid_s, mid_l, _, z0, z1, z2, z3, _out, zsend):
    experts = ret.shape[0]
    span = mid_s.shape[0] // experts
    half_rows = ret.shape[1] - 2 * span
    for t in range(experts):
        r = slice(span * t, span * (t + 1))
        keep = iota((span, 1), 0) < tab[1, t]
        e0 = ret[tab[8, t], 0:span, :].astype(F32)
        e1 = ret[tab[9, t], span : 2 * span, :].astype(F32)
        mixed = gates[t, 0] * e0 + gates[t, 1] * e1
        slot = tab[2, t]
        at = pl.multiple_of((slot % 2) * span, span)
        zsend[slot // 2, pl.ds(at, span), :] = (mid_s[r, :] + jnp.where(keep, mixed, 0.0)).astype(BF16)
    for u in range(mid_l.shape[0] // half_rows):
        r = slice(half_rows * u, half_rows * (u + 1))
        t = tab[5, u]
        keep = iota((half_rows, 1), 0) + half_rows * tab[14, 0] < tab[4, u]
        e0 = ret[tab[8, t], 2 * span :, :].astype(F32)
        e1 = ret[tab[9, t], 2 * span :, :].astype(F32)
        mixed = gates[t, 0] * e0 + gates[t, 1] * e1
        zsend[tab[16, u], 2 * span :, :] = (mid_l[r, :] + jnp.where(keep, mixed, 0.0)).astype(BF16)
    for d, ref in enumerate((z0, z1, z2, z3)):
        ref[0] = zsend[d]


def each_distance(index, refs, act):
    for d, ref in enumerate(refs):

        @pl.when(index == d)
        def _(ref=ref):
            act(ref)


def place_out(tab, a0, a1, a2, a3, _0, _1, _2, short_out, long_out):
    parts = (a0, a1, a2, a3)
    span = short_out.shape[1]
    for n in range(short_out.shape[0]):
        slot = tab[6, n]
        at = pl.multiple_of((slot % 2) * span, span)

        def copy_short(ref, n=n, at=at):
            short_out[n] = ref[0, pl.ds(at, span), :]

        each_distance(slot // 2, parts, copy_short)
    half = long_out.shape[1] // 2
    for n in range(long_out.shape[0]):
        for index, row in ((0, 7), (1, 15)):

            def copy_long(ref, n=n, index=index):
                long_out[n, half * index : half * (index + 1), :] = ref[0, 2 * span :, :]

            each_distance(tab[row, n], parts, copy_long)


def place_dx(tab, a0, a1, a2, a3, short_dx, long_dx):
    parts = (a0, a1, a2, a3)
    span = short_dx.shape[1]
    for n in range(short_dx.shape[0]):
        slot = tab[6, n]
        at = pl.multiple_of((slot % 2) * span, span)

        def copy_short(ref, n=n, at=at):
            short_dx[n] = ref[0, pl.ds(at, span), :].astype(F32)

        each_distance(slot // 2, parts, copy_short)
    for n in range(long_dx.shape[0]):

        def first(ref, n=n):
            long_dx[n] = ref[0, 2 * span :, :].astype(F32)

        def second(ref, n=n):
            long_dx[n] += ref[0, 2 * span :, :].astype(F32)

        each_distance(tab[7, n], parts, first)
        each_distance(tab[15, n], parts, second)


def finish_kernel(
    g, ids, gates, temb, gw_t, qkv, qv, wo, gain, shift, bo, grad_temb, grad_gw_t
):
    feats = wo.shape[1]
    for j in range(3):
        qkv[j] = g[feats * j : feats * (j + 1), :].astype(F32)
    for c in range(4):
        at = QKV_ROWS + 128 * c
        wo[:, 128 * c : 128 * (c + 1)] = g[at : at + 128, :].astype(F32)
    misc = g[MISC_ROW : MISC_ROW + 32, :].astype(F32)
    qv[...] = misc[0:2, :]

    def line(index):
        at = 2 + 4 * index
        return jnp.concatenate([misc[at + s : at + s + 1, :] for s in range(4)], axis=1)

    gain[0:1, :], gain[1:2, :] = line(0), line(2)
    shift[0:1, :], shift[1:2, :] = line(1), line(3)
    bo[...] = line(4)
    terms = misc[22:23, :]
    tasks = temb.shape[0]
    sub, lane = iota((tasks, 128), 0), iota((tasks, 128), 1)
    first = jnp.sum(jnp.where(lane == 2 * sub, terms, 0.0), axis=1, keepdims=True)
    second = jnp.sum(jnp.where(lane == 2 * sub + 1, terms, 0.0), axis=1, keepdims=True)
    both = first + second
    first = first - gates[:, 0:1] * both
    second = second - gates[:, 1:2] * both
    experts = gw_t.shape[0]
    rows = iota((experts, tasks), 0)
    eye = (iota((tasks, tasks), 0) == iota((tasks, tasks), 1)).astype(F32)
    spread = jnp.zeros((experts, tasks), F32)
    for k, value in ((0, first), (1, second)):
        as_row = jnp.sum(eye * value, axis=0, keepdims=True)
        spread += jnp.where(rows == ids[k : k + 1, :], as_row, 0.0)
    grad_gw_t[...] = lax.dot_general(
        spread, temb[...], (((1,), (0,)), ((), ())), preferred_element_type=F32, precision=HIGHEST
    )
    grad_temb[...] = lax.dot_general(
        spread.T, gw_t[...], (((1,), (0,)), ((), ())), preferred_element_type=F32, precision=HIGHEST
    )


def finish_experts(tab, shard, up, up_b, down, down_b):
    feats = up.shape[1]
    up[0] = shard[0, 0:feats, :].astype(F32)
    down[0] = shard[0, feats : 2 * feats, :].astype(F32)
    tail = shard[0, 2 * feats :, :].astype(F32)
    up_b[...] = tail[0:1, :]
    down_b[...] = jnp.zeros_like(down_b)
    for h in range(feats // 128):

        @pl.when(tab[14, 1] == h)
        def _(h=h):
            down_b[...] = tail[1:2, 128 * h : 128 * (h + 1)]


def collect_kernel(arrived, *refs):
    for d, ref in enumerate(refs[8:12]):
        terms = arrived[0, d].astype(F32)
        for g in range(1, arrived.shape[0]):
            terms += arrived[g, d].astype(F32)
        ref[0] = terms.astype(BF16)


def shape_of(shape, dtype):
    return jax.ShapeDtypeStruct(shape, dtype)


def balanced(short_x, long_x, expert_ids):
    heads = lax.axis_size("head")
    tasks = expert_ids.shape[0]
    return (
        heads == 4
        and lax.axis_size("expert") == tasks == 8
        and short_x.shape[0] == 4 * tasks
        and long_x.shape[0] == tasks
        and short_x.shape[1:] == (64, 512)
        and long_x.shape[1:] == (256, 512)
    )


def per_device(
    short_x,
    long_x,
    short_cot,
    long_cot,
    short_len,
    long_len,
    short_task,
    long_task,
    expert_ids,
    ln_gain,
    ln_bias,
    w_qkv,
    b_qv,
    w_attn_out,
    b_attn_out,
    w_up,
    b_up,
    w_down,
    b_down,
    task_emb,
    gate_w,
):
    if not balanced(short_x, long_x, expert_ids):
        return per_device_wide(
            short_x, long_x, short_cot, long_cot, short_len, long_len, short_task, long_task,
            expert_ids, ln_gain, ln_bias, w_qkv, b_qv, w_attn_out, b_attn_out, w_up, b_up,
            w_down, b_down, task_emb, gate_w,
        )
    heads = lax.axis_size("head")
    experts = lax.axis_size("expert")
    span, feats = short_x.shape[1:]
    long_span = long_x.shape[1]
    half_rows = long_span // 2
    tasks = expert_ids.shape[0]
    units = long_x.shape[0] // 2
    rows_s = tasks * span
    rows_q = units * half_rows
    rows_l = units * long_span
    pairs = feats // 128

    own_half = pl.pallas_call(
        pack_kernel,
        in_specs=[VM] * 3,
        out_specs=VM,
        out_shape=shape_of((HALF_PACK, 128), BF16),
        compiler_params=params(),
        cost_estimate=cost(2),
        name="pack",
    )(w_qkv, b_qv, w_attn_out)
    raw_own = lax.all_gather(own_half, "head", axis=0)
    raw_other = lax.ppermute(raw_own, "expert", [(i, i ^ 1) for i in range(experts)])

    tab, gates = pl.pallas_call(
        route_kernel,
        in_specs=[VM] * 7,
        out_specs=[VM, VM],
        out_shape=[shape_of((24, 128), jnp.int32), shape_of((tasks, 128), F32)],
        compiler_params=params(),
        cost_estimate=cost(4),
        name="route",
    )(
        short_task.reshape(1, -1),
        short_len.reshape(1, -1),
        long_task.reshape(1, -1),
        long_len.reshape(1, -1),
        expert_ids.T,
        task_emb,
        gate_w.T,
    )

    def blk(n, index):
        return pl.BlockSpec((1, n, feats), index)

    deo, cot_s, cot_l, norm_s, norm_l, own_s, own_l = pl.pallas_call(
        prep_kernel,
        grid_spec=pltpu.PrefetchScalarGridSpec(
            num_scalar_prefetch=1,
            grid=(8,),
            in_specs=[
                SM,
                blk(span, lambda e, tab: (tab[0, tab[10, e]], 0, 0)),
                blk(span, lambda e, tab: (tab[0, tab[11, e]], 0, 0)),
                blk(half_rows, lambda e, tab: (tab[3, tab[13, e]], tab[14, 0], 0)),
                blk(span, lambda e, tab: (tab[0, e], 0, 0)),
                blk(span, lambda e, tab: (tab[3, e // 2], tab[14, 0] * 2 + e % 2, 0)),
                blk(span, lambda e, tab: (tab[0, e], 0, 0)),
                blk(half_rows, lambda e, tab: (tab[3, e // 2], e % 2, 0)),
                pl.BlockSpec((2, feats), lambda e, tab: (0, 0)),
                pl.BlockSpec((2, feats), lambda e, tab: (0, 0)),
            ],
            out_specs=[
                blk(2 * span + half_rows + 16, lambda e, tab: (e, 0, 0)),
                blk(span, lambda e, tab: (e, 0, 0)),
                blk(span, lambda e, tab: (e, 0, 0)),
                blk(span, lambda e, tab: (e, 0, 0)),
                blk(half_rows, lambda e, tab: (e, 0, 0)),
                blk(span, lambda e, tab: (e, 0, 0)),
                blk(half_rows, lambda e, tab: (e, 0, 0)),
            ],
        ),
        out_shape=[
            shape_of((experts, 2 * span + half_rows + 16, feats), BF16),
            shape_of((8, span, feats), BF16),
            shape_of((8, span, feats), BF16),
            shape_of((8, span, feats), BF16),
            shape_of((8, half_rows, feats), BF16),
            shape_of((8, span, feats), BF16),
            shape_of((8, half_rows, feats), BF16),
        ],
        compiler_params=params(),
        cost_estimate=cost(9),
        name="prep",
    )(tab, gates, short_cot, short_cot, long_cot, short_cot, long_cot, short_x, long_x, ln_gain, ln_bias)
    cot_s, norm_s, own_s = (a.reshape(rows_s, feats) for a in (cot_s, norm_s, own_s))
    cot_l = cot_l.reshape(rows_q, feats)
    norm_l, own_l = norm_l.reshape(rows_l, feats), own_l.reshape(rows_l, feats)
    deo = lax.all_to_all(deo, "expert", split_axis=0, concat_axis=0, tiled=True)

    bias_out = b_attn_out.reshape(1, feats)
    w_shapes = [
        shape_of((QKV_ROWS, feats), BF16),
        shape_of((feats, feats), BF16),
        shape_of((8, feats), F32),
    ]

    def attention(kernel, operands, key_rows, query_rows, keys, send_shape, more, scratch, name):
        return pl.pallas_call(
            kernel,
            in_specs=[SM] + [VM] * (len(operands) - 1),
            out_specs=[VM] * (7 + len(more)),
            out_shape=[
                shape_of((query_rows, feats), BF16),
                shape_of((key_rows, feats), BF16),
                shape_of((key_rows, feats), BF16),
                shape_of((4 * pairs, 128, 2 * keys), BF16),
                shape_of((query_rows, feats), BF16),
                shape_of((query_rows, feats), F32),
                shape_of(send_shape, BF16),
            ]
            + more,
            scratch_shapes=scratch,
            compiler_params=params(),
            cost_estimate=cost(12),
            name=name,
        )(*operands)

    q_s, k_s, v_s, p_s, ctx_s, mid_s, send_s, w_all, wo_all, bqv_all = attention(
        attend_short,
        (tab, norm_s, own_s, raw_own, raw_other, ln_gain, ln_bias, bias_out),
        rows_s, rows_s, 128, (experts, 2, span, feats), w_shapes, [], "attend_short",
    )
    send_s = send_s.reshape(experts, 2 * span, feats)
    recv_s = lax.all_to_all(send_s, "expert", split_axis=0, concat_axis=0, tiled=True)
    q_l, k_l, v_l, p_l, ctx_l, mid_l, send_l = attention(
        attend_long,
        (tab, norm_l, own_l, w_all, wo_all, bqv_all, ln_gain, ln_bias, bias_out),
        rows_l, rows_q, long_span, (experts, half_rows, feats), [],
        [pltpu.VMEM((rows_q, feats), BF16)], "attend_long",
    )
    recv_l = lax.all_to_all(send_l, "expert", split_axis=0, concat_axis=0, tiled=True)

    eo, dx_s, dw_s, ga_s = experts_pass(
        tab, recv_s, deo, 0, w_up, b_up, w_down, b_down, None, None, None
    )
    ret_s = lax.all_to_all(dx_s, "expert", split_axis=0, concat_axis=0, tiled=True)
    eo, dx_l, dw_l, ga_l = experts_pass(
        tab, recv_l, deo, 1, w_up, b_up, w_down, b_down, dw_s, ga_s, eo
    )
    ret_l = lax.all_to_all(dx_l, "expert", split_axis=0, concat_axis=0, tiled=True)
    expert_grads = lax.psum_scatter(dw_l, "head", scatter_dimension=0, tiled=True)

    def over_head(blocks):
        return [blocks[0]] + [
            lax.ppermute(blocks[d], "head", [(i, i ^ d) for i in range(heads)]) for d in range(1, heads)
        ]

    zsend_s, dw_attn, small, eo = pl.pallas_call(
        back_short,
        in_specs=[SM] + [VM] * 13 + [ANY],
        out_specs=[VM] * 3 + [ANY],
        out_shape=[
            shape_of((2 * heads, span, feats), BF16),
            shape_of((4 * feats, feats), BF16),
            shape_of((8, feats), F32),
            shape_of(eo.shape, BF16),
        ],
        input_output_aliases={14: 3},
        scratch_shapes=[
            pltpu.VMEM((rows_s, feats), F32),
            pltpu.VMEM((rows_s, feats), BF16),
            pltpu.VMEM((rows_s, feats), BF16),
            pltpu.VMEM((rows_s, feats), BF16),
            pltpu.VMEM((rows_s, feats), BF16),
            pltpu.VMEM((rows_s, feats), BF16),
            pltpu.VMEM((rows_s, feats), F32),
        ],
        compiler_params=params(),
        cost_estimate=cost(36),
        name="back_short",
    )(
        tab, ret_s.reshape(experts, 2, span, feats), mid_s, cot_s, own_s, norm_s,
        q_s, k_s, v_s, p_s, ctx_s, w_all, wo_all, ln_gain, eo,
    )
    out_all = lax.all_to_all(eo, "expert", split_axis=0, concat_axis=0, tiled=True)
    *zsend_x, packed = pl.pallas_call(
        back_long,
        in_specs=[SM] + [VM] * 17,
        out_specs=[VM] * (heads + 1),
        out_shape=[shape_of((1, 2 * span + long_span, feats), BF16)] * heads
        + [shape_of((experts, heads, SLICE_ROWS, 128), BF16)],
        scratch_shapes=[
            pltpu.VMEM((heads, long_span, feats), BF16),
            pltpu.VMEM((rows_q, feats), BF16),
            pltpu.VMEM((rows_q, feats), F32),
            pltpu.VMEM((rows_q, feats), BF16),
            pltpu.VMEM((rows_q, feats), BF16),
            pltpu.VMEM((rows_q, feats), BF16),
            pltpu.VMEM((rows_l, feats), BF16),
            pltpu.VMEM((rows_l, feats), BF16),
            pltpu.VMEM((rows_l, feats), F32),
            pltpu.VMEM((experts * SLICE_ROWS, feats), F32),
        ],
        compiler_params=params(),
        cost_estimate=cost(54),
        name="back_long",
    )(
        tab, ret_l, mid_l, cot_l, own_l, norm_l, q_l, k_l, v_l, p_l, ctx_l, w_all, wo_all, ln_gain,
        dw_attn, small, ga_l, zsend_s,
    )
    back_x = over_head(zsend_x)
    *zsend_o, packed = pl.pallas_call(
        mix_kernel,
        in_specs=[SM, SM] + [VM] * 3 + [ANY],
        out_specs=[VM] * heads + [ANY],
        out_shape=[shape_of((1, 2 * span + half_rows, feats), BF16)] * heads
        + [shape_of(packed.shape, BF16)],
        input_output_aliases={5: heads},
        scratch_shapes=[pltpu.VMEM((heads, 2 * span + half_rows, feats), BF16)],
        compiler_params=params(),
        cost_estimate=cost(12),
        name="mix",
    )(tab, gates, out_all, mid_s, mid_l, packed)
    arrived = lax.all_to_all(packed, "expert", split_axis=0, concat_axis=0, tiled=True)
    through = (*back_x, *zsend_o)
    passed = pl.pallas_call(
        collect_kernel,
        in_specs=[VM] + [ANY] * len(through),
        out_specs=[VM] * heads + [ANY] * len(through),
        out_shape=[shape_of((1, SLICE_ROWS, 128), BF16)] * heads
        + [shape_of(a.shape, a.dtype) for a in through],
        input_output_aliases={1 + i: heads + i for i in range(len(through))},
        compiler_params=params(),
        cost_estimate=cost(3),
        name="collect",
    )(arrived, *through)
    terms, back_x, zsend_o = passed[:heads], passed[heads : 2 * heads], passed[2 * heads :]
    terms = sum(part.astype(F32) for part in over_head(terms)).astype(BF16)
    back_o = over_head(zsend_o)
    attn_grads = lax.all_gather(terms[0], "expert", axis=0, tiled=True)

    short_dx, long_dx = pl.pallas_call(
        place_dx,
        in_specs=[SM] + [VM] * 4,
        out_specs=[VM, VM],
        out_shape=[shape_of((8, span, feats), F32), shape_of((2, long_span, feats), F32)],
        compiler_params=params(),
        cost_estimate=cost(4),
        name="place_dx",
    )(tab, *back_x)

    grad_qkv, grad_qv, grad_wo, grad_gain, grad_shift, grad_bo, grad_task, grad_gate = pl.pallas_call(
        finish_kernel,
        in_specs=[VM] * 5,
        out_specs=[VM] * 8,
        out_shape=[
            shape_of((3, feats, 128), F32),
            shape_of((2, 128), F32),
            shape_of((128, feats), F32),
            shape_of((2, feats), F32),
            shape_of((2, feats), F32),
            shape_of((1, feats), F32),
            shape_of((tasks, feats), F32),
            shape_of((experts, feats), F32),
        ],
        compiler_params=params(),
        cost_estimate=cost(3),
        name="finish",
    )(attn_grads, expert_ids.T, gates, task_emb, gate_w.T)
    chunk = w_up.shape[2] // 4
    grad_up, grad_up_b, grad_down, grad_down_b = pl.pallas_call(
        finish_experts,
        in_specs=[SM, VM],
        out_specs=[VM] * 4,
        out_shape=[
            shape_of((1, feats, chunk), F32),
            shape_of((1, chunk), F32),
            shape_of((1, chunk, feats), F32),
            shape_of((1, feats // heads), F32),
        ],
        compiler_params=params(),
        cost_estimate=cost(3),
        name="finish_experts",
    )(tab, expert_grads)
    short_out, long_out = pl.pallas_call(
        place_out,
        in_specs=[SM] + [VM] * 4 + [ANY] * 3,
        out_specs=[VM, VM],
        out_shape=[shape_of((8, span, feats), BF16), shape_of((2, long_span, feats), BF16)],
        compiler_params=params(),
        cost_estimate=cost(3),
        name="place_out",
    )(tab, *back_o, grad_bo, grad_down_b, short_dx)

    return (
        short_out,
        long_out,
        short_dx,
        long_dx,
        grad_gain,
        grad_shift,
        grad_qkv,
        grad_qv,
        grad_wo,
        grad_bo.reshape(feats),
        grad_up,
        grad_up_b,
        grad_down,
        grad_down_b,
        grad_task,
        grad_gate.T,
    )


def solution(mesh):
    return jax.shard_map(
        per_device,
        mesh=mesh,
        in_specs=(
            P("expert", None, None),
            P("expert", None, None),
            P("expert", None, None),
            P("expert", None, None),
            P("expert"),
            P("expert"),
            P("expert"),
            P("expert"),
            P(),
            P(),
            P(),
            P(None, None, "head"),
            P(None, "head"),
            P("head", None),
            P(),
            P("expert", None, None),
            P("expert", None),
            P("expert", None, None),
            P("expert", None),
            P(),
            P(),
        ),
        out_specs=(
            P(("expert", "head"), None, None),
            P(("expert", "head"), None, None),
            P(("expert", "head"), None, None),
            P(("expert", "head"), None, None),
            P(),
            P(),
            P(None, None, "head"),
            P(None, "head"),
            P("head", None),
            P(),
            P("expert", None, "head"),
            P("expert", "head"),
            P("expert", "head", None),
            P("expert", "head"),
            P(),
            P(),
        ),
        check_vma=False,
    )
```
